128 devices in a mesh: slab: 16 (over y, z), img: 8 (over x, core).
Axes of the slice: x: 4, y: 4, z: 4, core: 2. Of those that a mesh axis runs over, the one named last changes fastest.
Arguments:
- images: bfloat16 [16384, 16384], P('img', 'slab'), may hold values from -6 to 6
- volume: bfloat16 [32, 512, 1024], P('slab'), may hold values from -2 to 2
- precision: float32 [16384], P('img'), may hold values from 0.03 to 1
- candidates: int32 [16384, 16], P('img'), may hold values from 0 to 511, all different within a row
- slot_key: int32 [16, 16, 64], replicated, may hold values from -1 to 511, as said below
- slot_voxel: int32 [16, 16, 64], replicated, may hold values from 0 to 1022, as said below
- slot_weight: int32 [16, 16, 64], replicated, may hold values from 0 to 16
Outputs:
- density: float32 [32, 512, 512], P('slab', None, 'img')
- posterior: float32 [16384, 16], P('img')
The draws below stay inside these ranges and needn't reach their ends.
Inputs may be any that keep to these rules, and one draw needn't show every extreme that they name: slot_key[s, d, :] holds keys p + j (pose p, row j of block d) taken from slab s, live slots first and -1 after; every key of every block d stands exactly once over all s; each (s, d) has at most 64 live slots, and every block has a slab with exactly 64. `slot_voxel`: z * 512 + y with z below 2 and y below 511.
All inputs are finite; a program needn't handle non-finite values.
Results may differ from the reference program's by a relative error of at most 0.0096.
Values may be sent and summed in bfloat16 or wider, within the bound.
A program may use at most 64 MiB of HBM per device.

```python
import math
import jax
import jax.numpy as jnp
from jax import lax

BOX = 512
ROWS_DEV = 1
PL_DEV = 2
IMG_PER = 2048
NPOSE = 512
CANDS = 16
WSTEPS = 16
ROWS = 16
ZW = 32
IMAGES = 16384
CAP = 64
N_SLAB = 16
N_IMG = 8


def slot_layout(key):
    total_keys = NPOSE * ROWS_DEV
    mean_count = total_keys // N_SLAB
    half_count = N_SLAB // 2

    def one_block(block_key):
        first_key, second_key, third_key = jax.random.split(block_key, 3)
        offsets = jax.random.randint(first_key, (half_count,), 0, mean_count + 1)
        offsets = offsets.at[0].set(mean_count)
        counts = jnp.concatenate([mean_count + offsets, mean_count - offsets])
        order = jax.random.permutation(second_key, N_SLAB)
        counts = counts[order]
        starts = jnp.cumsum(counts) - counts
        shuffled = jax.random.permutation(third_key, total_keys)
        slots = jnp.arange(CAP, dtype=jnp.int32)
        position = starts[:, None] + slots[None, :]
        living = slots[None, :] < counts[:, None]
        chosen = shuffled[jnp.clip(position, 0, total_keys - 1)]
        return jnp.where(living, chosen, -1).astype(jnp.int32)
    blocks = jax.vmap(one_block)(jax.random.split(key, N_SLAB))
    return jnp.transpose(blocks, (1, 0, 2))


def draw_slot_key(key, part):
    key = jax.random.fold_in(key, 7)
    return slot_layout(key)


def draw_slot_voxel(key, part):
    key = jax.random.fold_in(key, 23)
    plane_key, row_key = jax.random.split(key)
    planes = jax.random.randint(plane_key, (N_SLAB, N_SLAB, CAP), 0, PL_DEV)
    row_ids = jax.random.randint(row_key, (N_SLAB, N_SLAB, CAP), 0, BOX - 1)
    return (planes * BOX + row_ids).astype(jnp.int32)


def draw_precision(key, part):
    key = jax.random.fold_in(key, 5)
    logs = jax.random.uniform(key, (IMAGES,), jnp.float32, math.log(0.03), math.log(0.3))
    return jnp.exp(logs)


def with_ends(drawn, rng, smallest, high):
    place = [jax.random.randint(jax.random.fold_in(rng, axis), (), 0, length) for axis, length in enumerate(drawn.shape)]
    longest = drawn.shape.index(max(drawn.shape))
    beside = place[:longest] + [(place[longest] + 1) % drawn.shape[longest]] + place[longest + 1:]
    return drawn.at[tuple(place)].set(smallest).at[tuple(beside)].set(high)


def block_levels(key, extent, shards, smallest, top_value):
    loudness, own = 1.0, jax.random.fold_in(key, 6)
    for dim, shards_of in shards:
        heights = jnp.exp(jax.random.uniform(jax.random.fold_in(own, dim), (shards_of,), jnp.float32, smallest / len(shards), top_value / len(shards)))
        loudness = loudness * jnp.repeat(heights, extent[dim] // shards_of).reshape([-1 if axis == dim else 1 for axis in range(len(extent))])
    return loudness


def distinct(key, rows, amount, top, lift):
    sequence = jax.random.permutation(jax.random.fold_in(key, 1), amount)
    favour = sequence
    for power in range(3):
        favour = favour * favour // amount
    favour = favour * lift // amount
    chance = jax.random.randint(jax.random.fold_in(key, 2), (rows, amount), 0, 4096) + favour
    sure = jax.random.permutation(jax.random.fold_in(key, 3), rows)[jnp.arange(amount) % rows]
    chance = jnp.where(jnp.arange(rows)[:, None] == sure[None, :], 1 << 14, chance)
    score = chance * amount + jnp.arange(amount)
    return lax.top_k(score.astype(jnp.int32), top)[1].astype(jnp.int32)


def normal_values(key, shape, deviation, bound, cuts=(), kind=jnp.bfloat16):
    drawn = jax.random.normal(key, shape, jnp.float32) * deviation
    if len(cuts) > 0:
        drawn = block_levels(key, shape, cuts, -0.22, 0.18) * drawn
    return jnp.clip(drawn, min=-bound, max=bound).astype(kind)


def setup_inputs(seed: int = 0) -> dict:
    key_of = jax.random.split(jax.random.key(seed), 8)
    return {
        "images": normal_values(key_of[0], (IMAGES, ROWS * 2 * BOX), 1.0, 6.0, ((0, 8), (1, 16))),
        "volume": normal_values(key_of[1], (ZW, BOX, 2 * BOX), (16.0 / (2 * ROWS * BOX) ** 0.5), 2.0, ((0, 16),)),
        "precision": draw_precision(jax.random.fold_in(key_of[7], 71), 0),
        "candidates": distinct(key_of[3], IMAGES, NPOSE, CANDS, 256),
        "slot_key": draw_slot_key(jax.random.fold_in(key_of[7], 71), 0),
        "slot_voxel": draw_slot_voxel(jax.random.fold_in(key_of[7], 71), 0),
        "slot_weight": with_ends(jax.random.randint(key_of[6], (N_SLAB, N_SLAB, CAP), 0, WSTEPS + 1), jax.random.fold_in(key_of[6], 1), 0, WSTEPS).astype(jnp.int32),
    }


ridge = 0.25


def spread_weights(posterior, precision, candidates):
    amounts = posterior * precision[:, None]
    row_ids = jnp.arange(candidates.shape[0], dtype=jnp.int32)[:, None]
    spread_table = jnp.zeros((candidates.shape[0], NPOSE), jnp.float32)
    spread_table = spread_table.at[row_ids, candidates].add(amounts)
    return spread_table.astype(jnp.bfloat16)


def gridding(samples):
    offset = (jnp.arange(samples, dtype=jnp.float32) - samples / 2) / samples
    return 1.0 / jnp.sinc(offset) ** 2


def reference(images, volume, precision, candidates, slot_key, slot_voxel, slot_weight):
    features = ROWS * 2 * BOX
    vol_rows = volume.reshape(ZW * BOX, 2 * BOX).astype(jnp.float32)
    source = jnp.arange(N_SLAB, dtype=jnp.int32)[:, None, None]
    block = jnp.arange(N_SLAB, dtype=jnp.int32)[None, :, None]
    live = slot_key >= 0
    slot_keys = jnp.where(live, slot_key, 0)
    voxels = source * (PL_DEV * BOX) + slot_voxel
    fraction = (slot_weight.astype(jnp.float32) / WSTEPS)[..., None]
    values = fraction * vol_rows[voxels] + (1.0 - fraction) * vol_rows[voxels + 1]
    target = (slot_keys // ROWS_DEV) * ROWS + block * ROWS_DEV + slot_keys % ROWS_DEV
    dropped = jnp.where(live, target, NPOSE * ROWS)
    slices = jnp.zeros((NPOSE * ROWS, 2 * BOX), jnp.bfloat16)
    slices = slices.at[dropped.reshape(-1)].set(values.astype(jnp.bfloat16).reshape(-1, 2 * BOX), mode="drop")
    slices = slices.reshape(NPOSE, features)
    flat = images
    cross = lax.dot_general(flat, slices, (((1,), (1,)), ((), ())), preferred_element_type=jnp.float32)
    power = jnp.sum(jnp.square(slices.astype(jnp.float32)), axis=1)
    score = precision[:, None] * (cross - 0.5 * power[None, :])
    picked = jnp.take_along_axis(score, candidates, axis=1)
    largest = jnp.max(picked, axis=1, keepdims=True)
    exponent = jnp.exp(picked - largest)
    posterior = exponent / jnp.sum(exponent, axis=1, keepdims=True)
    spread = spread_weights(posterior, precision, candidates)
    pose_weight = jnp.sum(spread.astype(jnp.float32), axis=0)
    group_images = flat.reshape(N_IMG, IMG_PER, features)
    group_spread = spread.reshape(N_IMG, IMG_PER, NPOSE)

    def add_group(totals, pieces):
        part = lax.dot_general(pieces[1], pieces[0], (((0,), (0,)), ((), ())), preferred_element_type=jnp.float32)
        rounded = lax.optimization_barrier(part.astype(jnp.bfloat16))
        return totals + rounded.astype(jnp.float32), None

    back, _ = lax.scan(add_group, jnp.zeros((NPOSE, features), jnp.float32), (group_images, group_spread))
    back_rows = back.reshape(NPOSE * ROWS, 2 * BOX)
    safe_target = jnp.where(live, target, 0)
    contrib = jnp.where(live[..., None], back_rows[safe_target], 0.0)
    slot_mass = jnp.where(live, pose_weight[slot_keys // ROWS_DEV], 0.0)
    accumulated = jnp.zeros((ZW * BOX, 2 * BOX), jnp.float32)
    accumulated = accumulated.at[voxels.reshape(-1)].add((fraction * contrib).reshape(-1, 2 * BOX))
    accumulated = accumulated.at[(voxels + 1).reshape(-1)].add(((1.0 - fraction) * contrib).reshape(-1, 2 * BOX))
    level = fraction[..., 0]
    row_mass = jnp.zeros((ZW * BOX,), jnp.float32)
    row_mass = row_mass.at[voxels.reshape(-1)].add((level * slot_mass).reshape(-1))
    row_mass = row_mass.at[(voxels + 1).reshape(-1)].add(((1.0 - level) * slot_mass).reshape(-1))
    fourier = (accumulated / (row_mass[:, None] + ridge)).reshape(ZW, BOX, 2 * BOX)
    field = fourier[:, :, :BOX] + 1j * fourier[:, :, BOX:]
    density = jnp.real(jnp.fft.ifft2(field, axes=(1, 2))) * BOX
    correction = gridding(BOX)
    density = density * correction[None, :, None] * correction[None, None, :]
    return density.astype(jnp.float32), posterior
```

```python
import math

import jax
import jax.numpy as jnp
import numpy as np
from jax import lax
from jax.sharding import PartitionSpec as P

NPOSE = 512
WSTEPS = 16
RIDGE = 0.25


def gridding(samples):
    offset = (np.arange(samples) - samples / 2) / samples
    return 1.0 / np.sinc(offset) ** 2


def angles(length):
    counter = np.arange(length)
    return (counter[:, None] * counter[None, :] % length) * (2.0 * math.pi / length)


def column_table(length, members):
    turn = angles(length)
    cosine, sine = np.cos(turn), np.sin(turn)
    scale = gridding(length)[None, :]
    to_re = np.concatenate([cosine, -sine], axis=0) * scale
    to_im = np.concatenate([sine, cosine], axis=0) * scale
    width = length // members
    both = np.stack([to_re.reshape(-1, members, width), to_im.reshape(-1, members, width)], axis=2)
    return jnp.asarray(both.reshape(2 * length, 2 * length), jnp.bfloat16)


def row_table(length):
    turn = angles(length)
    scale = gridding(length)[:, None] / length
    return jnp.asarray(np.concatenate([np.cos(turn), -np.sin(turn)], axis=1) * scale, jnp.bfloat16)


def per_device(images, volume, precision, candidates, slot_key, slot_voxel, slot_weight):
    members = lax.axis_size("img")
    slabs = lax.axis_size("slab")
    own = lax.axis_index("slab")
    member = lax.axis_index("img")
    planes, edge, width = volume.shape
    cap = slot_key.shape[2]
    deep = cap // members
    share = NPOSE // members
    voxels = planes * edge
    counts = jnp.sum((slot_key >= 0).astype(jnp.int32), axis=2)
    starts = jnp.cumsum(counts, axis=0) - counts

    out_start = lax.dynamic_index_in_dim(starts, own, 0, keepdims=False)
    residue = (jnp.arange(members)[:, None] - out_start[None, :]) % members
    chosen = residue[:, :, None, None] == jnp.arange(members)[None, None, None, :]

    def by_member(table):
        mine = lax.dynamic_index_in_dim(table, own, 0, keepdims=False).reshape(1, slabs, deep, members)
        return jnp.sum(jnp.where(chosen, mine, 0), axis=3).reshape(-1)

    all_key = by_member(slot_key)
    all_voxel = by_member(slot_voxel)
    all_weight = by_member(slot_weight)
    lower = jnp.where(all_key >= 0, all_weight, 0).astype(jnp.float32) / WSTEPS
    upper = jnp.where(all_key >= 0, WSTEPS - all_weight, 0).astype(jnp.float32) / WSTEPS
    places = jnp.arange(voxels)
    spot = all_voxel[None, :]
    weave = jnp.where(spot == places[:, None], lower[None, :], 0.0) + jnp.where(
        spot + 1 == places[:, None], upper[None, :], 0.0
    )
    weave = weave.astype(jnp.bfloat16)

    in_start = lax.dynamic_index_in_dim(starts, own, 1, keepdims=False)
    in_count = lax.dynamic_index_in_dim(counts, own, 1, keepdims=False)
    in_key = lax.dynamic_index_in_dim(slot_key, own, 1, keepdims=False)
    slot = jnp.arange(deep)[None, :] * members + ((member - in_start) % members)[:, None]
    row = jnp.where(slot < in_count[:, None], (in_start[:, None] + slot) // members, -1).reshape(-1)
    pack = (jnp.arange(share)[:, None] == row[None, :]).astype(jnp.bfloat16)
    order = in_start[:, None] + jnp.arange(cap)[None, :]
    order = (order % members) * share + order // members
    pose_row = jnp.sum(
        jnp.where(in_key.reshape(-1, 1) == jnp.arange(NPOSE)[None, :], order.reshape(-1, 1), 0), axis=0
    )

    mine = slabs * deep
    take = lax.dynamic_slice_in_dim(weave, member * mine, mine, 1)
    outgoing = lax.dot_general(
        take, volume.reshape(voxels, width), (((0,), (0,)), ((), ())), preferred_element_type=jnp.float32
    ).astype(jnp.bfloat16)
    received = lax.all_to_all(outgoing.reshape(slabs, deep, width), "slab", 0, 0, tiled=True)
    block = jnp.dot(pack, received.reshape(mine, width), preferred_element_type=jnp.float32).astype(jnp.bfloat16)
    slices = lax.all_gather(block, "img", axis=0, tiled=True)

    score = lax.dot_general(slices, images, (((1,), (1,)), ((), ())), preferred_element_type=jnp.float32)
    power = jnp.sum(jnp.square(slices.astype(jnp.float32)), axis=1)
    score = score - 0.5 * power[:, None]
    poses = candidates.T
    one_hot = poses[:, None, :] == jnp.arange(NPOSE)[None, :, None]
    rows = jnp.sum(jnp.where(one_hot, pose_row[None, :, None], 0), axis=1)
    row_ids = jnp.arange(NPOSE)[:, None]
    picked = jnp.stack(
        [jnp.sum(jnp.where(rows[k][None, :] == row_ids, score, 0.0), axis=0) for k in range(rows.shape[0])]
    )
    picked = lax.psum(picked, "slab") * precision[None, :]
    exponent = jnp.exp(picked - jnp.max(picked, axis=0, keepdims=True))
    posterior = exponent / jnp.sum(exponent, axis=0, keepdims=True)

    amount = posterior * precision[None, :]
    spread = jnp.zeros((NPOSE, images.shape[0]), jnp.float32)
    for k in range(rows.shape[0]):
        spread = jnp.where(rows[k][None, :] == row_ids, amount[k][None, :], spread)
    spread = spread.astype(jnp.bfloat16)
    row_weight = jnp.sum(spread.astype(jnp.float32), axis=1)
    pose_weight = jnp.sum(jnp.where(row_ids == pose_row[None, :], row_weight[:, None], 0.0), axis=0)
    pose_weight = lax.psum(pose_weight, "img")
    back = jnp.dot(spread, images, preferred_element_type=jnp.float32).astype(jnp.bfloat16)
    parts = lax.all_to_all(back.reshape(members, share, width), "img", 0, 0, tiled=True)
    summed = jnp.sum(parts.astype(jnp.float32), axis=0).astype(jnp.bfloat16)
    unpacked = lax.dot_general(
        pack, summed, (((0,), (0,)), ((), ())), preferred_element_type=jnp.float32
    ).astype(jnp.bfloat16)
    returned = lax.all_to_all(unpacked.reshape(slabs, deep, width), "slab", 0, 0, tiled=True)

    turned = jnp.dot(
        returned.reshape(mine, width), column_table(edge, members), preferred_element_type=jnp.float32
    ).astype(jnp.bfloat16)
    turned = turned.reshape(mine, members, width // members).transpose(1, 0, 2)
    crossed = lax.all_to_all(turned, "img", 0, 0, tiled=True).reshape(members * mine, width // members)
    accumulated = jnp.dot(weave, crossed, preferred_element_type=jnp.float32)
    slot_mass = jnp.sum(
        jnp.where(all_key[:, None] == jnp.arange(NPOSE)[None, :], pose_weight[None, :], 0.0), axis=1
    )
    mass = jnp.sum(weave.astype(jnp.float32) * slot_mass[None, :], axis=1)
    fourier = (accumulated / (mass[:, None] + RIDGE)).astype(jnp.bfloat16)
    half = width // members // 2
    fourier = fourier.reshape(planes, edge, 2, half).transpose(0, 2, 1, 3).reshape(planes, 2 * edge, half)
    density = jnp.einsum("yk,zkx->zyx", row_table(edge), fourier, preferred_element_type=jnp.float32)
    return (density, posterior.T)


def solution(mesh):
    placed = (P("img", "slab"), P("slab", None, None), P("img"), P("img", None), P(), P(), P())
    return jax.shard_map(
        per_device,
        mesh=mesh,
        in_specs=placed,
        out_specs=(P("slab", None, "img"), P("img", None)),
        check_vma=False,
    )
```

```python
import functools
import math

import jax
import jax.numpy as jnp
import numpy as np
from jax import lax
from jax.experimental import pallas as pl
from jax.experimental.pallas import tpu as pltpu
from jax.sharding import PartitionSpec as P

NPOSE = 512
WSTEPS = 16
RIDGE = 0.25
LANES = 128
F32 = jnp.float32
BF16 = jnp.bfloat16


def gridding(samples):
    offset = (np.arange(samples) - samples / 2) / samples
    return 1.0 / np.sinc(offset) ** 2


def angles(length):
    counter = np.arange(length)
    return (counter[:, None] * counter[None, :] % length) * (2.0 * math.pi / length)


def column_table(length, members):
    turn = angles(length)
    cosine, sine = np.cos(turn), np.sin(turn)
    scale = gridding(length)[None, :]
    to_re = np.concatenate([cosine, -sine], axis=0) * scale
    to_im = np.concatenate([sine, cosine], axis=0) * scale
    width = length // members
    both = np.stack([to_re.reshape(-1, members, width), to_im.reshape(-1, members, width)], axis=2)
    return jnp.asarray(both.reshape(2 * length, 2 * length), BF16)


def row_table(length):
    turn = angles(length)
    scale = gridding(length)[:, None] / length
    return jnp.asarray(np.concatenate([np.cos(turn), -np.sin(turn)], axis=1) * scale, BF16)


def remote(src, dst, sends, recvs, device):
    return pltpu.make_async_remote_copy(
        src_ref=src,
        dst_ref=dst,
        send_sem=sends,
        recv_sem=recvs,
        device_id=device,
        device_id_type=pl.DeviceIdType.MESH,
    )


def dot(left, right):
    return jnp.dot(left, right, preferred_element_type=F32)


def each(count, step, first=0):
    def body(index, carry):
        step(index)
        return carry

    lax.fori_loop(first, count, body, 0)


def rows_at(start, size):
    return pl.ds(pl.multiple_of(start, size), size)


def iota(shape, axis):
    return lax.broadcasted_iota(jnp.int32, shape, axis)


def pick_row(mask, values):
    return jnp.sum(jnp.where(mask, values, 0.0), axis=0, keepdims=True)


def kernel(
    slabs, members,
    images, volume, columns, rows, precision_in, poses_in, keys_in, voxels_in, weights_in,
    density, posterior,
    images_v, volume_v, columns_v, rows_v, precision, poses, keys, voxel_of, weight_of,
    slot_table, pack_table, pose_row,
    outgoing, incoming, slices, half_power, weave,
    picks, picks_in, shares, spread, row_weight,
    away, away_in, kept, opposite, opposite_in, ring, ring_in,
    masses, inverse, returning, returned, crossing, crossed,
    loads, slab_send, slab_recv, img_send, img_recv,
):
    own = lax.axis_index("slab")
    member = lax.axis_index("img")
    ring_len = members // 2
    chip, core = member // 2, lax.rem(member, 2)
    share = NPOSE // members
    half = share // 2
    side = ring_len * share
    deep = outgoing.shape[1]
    mine = slabs * deep
    cap = keys.shape[2]
    width = volume_v.shape[1]
    voxels = volume_v.shape[0]
    cands = poses.shape[0]
    right = 2 * lax.rem(chip + 1, ring_len) + core
    left = 2 * lax.rem(chip + ring_len - 1, ring_len) + core
    partner = 2 * chip + 1 - core

    def slab_peer(step):
        return lax.rem(own + step, slabs)

    def img_peer(step):
        return lax.rem(member + step, members)

    barrier = pltpu.get_barrier_semaphore()

    def greet(axis, peer):
        pl.semaphore_signal(barrier, inc=1, device_id={axis: peer}, device_id_type=pl.DeviceIdType.MESH)

    sources = [keys_in, voxels_in, weights_in, volume, poses_in, images, precision_in, columns, rows]
    targets = [keys, voxel_of, weight_of, volume_v, poses, images_v, precision, columns_v, rows_v]
    load = [pltpu.make_async_copy(src, dst, loads.at[i]) for i, (src, dst) in enumerate(zip(sources, targets))]
    for index in range(5):
        load[index].start()
    for step in range(1, slabs):
        greet("slab", slab_peer(step))
    for step in range(1, members):
        greet("img", img_peer(step))

    for index in range(3):
        load[index].wait()
    before = jnp.zeros((slabs, cap), F32)
    for slab in range(slabs):
        before += jnp.where(keys[slab] >= 0, 1.0, 0.0) * jnp.where(own > slab, 1.0, 0.0)
    out_start = jnp.sum(before, axis=1, keepdims=True)
    total_slots = slabs * cap
    position = iota((1, total_slots), 1)
    block_sel = iota((slabs, total_slots), 0) == ((position >> 3) & (slabs - 1))
    start_row = pick_row(block_sel, out_start).astype(jnp.int32)
    slot_row = members * (position & 7) + (((position >> 7) - start_row) & 7)
    slot_sel = iota((cap, total_slots), 0) == slot_row
    own_key = keys[own]
    own_code = voxel_of[own] * 32 + jnp.where(own_key >= 0, weight_of[own], 31)
    chooser = jnp.where(block_sel, 1.0, 0.0)

    def ordered(table):
        wide = lax.dot_general(
            table.astype(F32), chooser, (((0,), (0,)), ((), ())),
            precision=lax.Precision.HIGHEST, preferred_element_type=F32,
        )
        return pick_row(slot_sel, wide)

    code_row = ordered(own_code).astype(jnp.int32)
    level = code_row & 31
    alive = level <= WSTEPS
    slot_table[0:1, :] = (code_row >> 5).astype(F32)
    slot_table[1:2, :] = jnp.where(alive, level, 0).astype(F32) * (1.0 / WSTEPS)
    slot_table[2:3, :] = jnp.where(alive, WSTEPS - level, 0).astype(F32) * (1.0 / WSTEPS)
    slot_table[3:4, :] = ordered(own_key)
    slot_table[4:8, :] = jnp.zeros((4, total_slots), F32)

    own_cols = slot_table[:, rows_at(member * mine, mine)].T
    place = iota((mine, voxels), 1)
    spot = own_cols[:, 0:1].astype(jnp.int32)
    take = jnp.where(place == spot, own_cols[:, 1:2], 0.0) + jnp.where(place == spot + 1, own_cols[:, 2:3], 0.0)
    load[3].wait()
    for index in range(5, len(load)):
        load[index].start()
    woven = dot(take.astype(BF16), volume_v[...])
    for block in range(slabs):
        outgoing[block] = woven[block * deep : (block + 1) * deep].astype(BF16)
    pl.semaphore_wait(barrier, slabs - 1 + members - 1)

    def slab_copy(stage, src, dst, step):
        peer = slab_peer(step)
        return remote(
            src.at[peer], dst.at[own], slab_send.at[stage, step], slab_recv.at[stage, step], {"slab": peer}
        )

    def slab_arrival(stage, dst, step):
        peer = slab_peer(slabs - step)
        return remote(
            dst.at[peer], dst.at[peer], slab_send.at[stage, step], slab_recv.at[stage, step], {"slab": peer}
        )

    def slab_exchange(stage, src, dst):
        for step in range(1, slabs):
            slab_copy(stage, src, dst, step).start()

    def slab_arrivals(stage, dst):
        for step in range(1, slabs):
            slab_arrival(stage, dst, step).wait_recv()

    def img_copy(slot, src, dst, device):
        return remote(src, dst, img_send.at[slot], img_recv.at[slot], {"img": device})

    slab_exchange(0, outgoing, incoming)
    incoming[own] = outgoing[own]

    in_key = jnp.concatenate(
        [jnp.sum(jnp.where(iota((slabs, cap), 0) == own, keys[slab], 0), axis=0, keepdims=True) for slab in range(slabs)],
        axis=0,
    )
    live = jnp.where(in_key >= 0, 1.0, 0.0).astype(BF16)
    count = dot(live, jnp.ones((cap, LANES), BF16))
    earlier = jnp.where(iota((slabs, slabs), 1) < iota((slabs, slabs), 0), 1.0, 0.0).astype(BF16)
    start = dot(earlier, count.astype(BF16))
    lane = iota((1, mine), 1)
    slab_sel = iota((slabs, mine), 0) == (lane >> 3)
    in_start = pick_row(slab_sel, start).astype(jnp.int32)
    in_count = pick_row(slab_sel, count).astype(jnp.int32)
    slot = members * (lane & 7) + ((member - in_start) & 7)
    pack_row = jnp.where(slot < in_count, (in_start + slot) >> 3, -1)
    pack_table[...] = jnp.broadcast_to(pack_row, (8, mine)).astype(F32)

    number = start[:, :cap].astype(jnp.int32) + iota((slabs, cap), 1)
    holder = number & (members - 1)
    ahead = ((holder >> 1) - chip) & (ring_len - 1)
    near = jnp.where(ahead == 0, 3, jnp.where(ahead == 1, 1, jnp.where(ahead == 2, 0, 2)))
    row = jnp.where((holder & 1) == core, near, members - 1 - near) * share + (number >> 3)
    key_cols, row_cols = in_key.astype(F32).T, row.astype(F32).T
    pose_ids = iota((cap, NPOSE), 1).astype(F32)
    found_rows = jnp.zeros((cap, NPOSE), F32)
    for slab in range(slabs):
        found_rows += jnp.where(key_cols[:, slab : slab + 1] == pose_ids, row_cols[:, slab : slab + 1], 0.0)
    pose_row[...] = jnp.broadcast_to(jnp.sum(found_rows, axis=0, keepdims=True), (8, NPOSE)).astype(jnp.int32)

    load[4].wait()
    for part in range(poses.shape[1] // LANES):
        for k in range(0, cands, 8):
            at = (slice(k, k + 8), slice(part * LANES, (part + 1) * LANES))
            pose = poses[at]
            low, high = pose & (LANES - 1), pose >> 7
            renamed = jnp.zeros_like(pose)
            for piece in range(NPOSE // LANES):
                table = pose_row[:, piece * LANES : (piece + 1) * LANES]
                found = jnp.take_along_axis(table, low, axis=1, mode="promise_in_bounds")
                renamed = jnp.where(high == piece, found, renamed)
            poses[at] = renamed

    slab_arrivals(0, incoming)
    arrived = jnp.concatenate([incoming[block].astype(F32) for block in range(slabs)], axis=0).astype(BF16)
    pack = jnp.where(iota((share, mine), 0).astype(F32) == pack_table[0:1, :], 1.0, 0.0).astype(BF16)

    def block_of(index, first=0, size=share):
        return slices.at[index * share + first : index * share + first + size]

    FAR, RIGHT, LEFT, HOME = 0, 1, 2, 3
    slices[HOME * share : (HOME + 1) * share, :] = dot(pack, arrived).astype(BF16)

    def other(index):
        return members - 1 - index

    def top(index):
        return block_of(index, 0, half)

    def bottom(index):
        return block_of(index, half, half)

    gathers = [
        img_copy(0, top(HOME), top(LEFT), right),
        img_copy(1, bottom(HOME), bottom(RIGHT), left),
        img_copy(2, block_of(HOME), block_of(other(HOME)), partner),
        img_copy(3, bottom(HOME), bottom(LEFT), right),
        img_copy(4, top(HOME), top(RIGHT), left),
        img_copy(5, top(LEFT), top(FAR), right),
        img_copy(6, bottom(RIGHT), bottom(FAR), left),
        img_copy(7, block_of(LEFT), block_of(other(LEFT)), partner),
        img_copy(8, block_of(RIGHT), block_of(other(RIGHT)), partner),
        img_copy(9, top(FAR), top(other(FAR)), partner),
        img_copy(10, bottom(FAR), bottom(other(FAR)), partner),
    ]
    for index in range(5):
        gathers[index].start()

    def weave_step(index):
        at = iota((LANES, total_slots), 0) + index * LANES
        spots = slot_table[0:1, :].astype(jnp.int32)
        value = jnp.where(spots == at, slot_table[1:2, :], 0.0) + jnp.where(spots + 1 == at, slot_table[2:3, :], 0.0)
        weave[rows_at(index * LANES, LANES), :] = value.astype(BF16)

    each(voxels // LANES, weave_step)
    gathers[0].wait_recv()
    gathers[5].start()
    gathers[1].wait_recv()
    gathers[6].start()
    gathers[3].wait_recv()
    gathers[7].start()
    gathers[4].wait_recv()
    gathers[8].start()
    load[5].wait()

    def power_step(index):
        at = rows_at(index * share, share)
        values = slices[at, :].astype(F32)
        total = 0.5 * jnp.sum(values * values, axis=1, keepdims=True)
        half_power[at, :] = jnp.broadcast_to(total, (share, LANES))

    chunk = 2 * LANES
    chunks = images_v.shape[0] // chunk

    def picks_of(score, pieces, numbers, value):
        for first, offset, size in pieces:
            block = score[offset : offset + size] - half_power[first : first + size, :]
            for group in range(size // 8):
                picked = jnp.take_along_axis(
                    block[group * 8 : (group + 1) * 8], numbers[0], axis=0, mode="promise_in_bounds"
                )
                value[0] = jnp.where(numbers[2] == first // 8 + group, picked, value[0])
                picked = jnp.take_along_axis(
                    block[group * 8 : (group + 1) * 8], numbers[1], axis=0, mode="promise_in_bounds"
                )
                value[1] = jnp.where(numbers[3] == first // 8 + group, picked, value[1])
        return value

    def score_chunk(index, table, pieces, resume):
        score = lax.dot_general(
            table, images_v[rows_at(index * chunk, chunk), :],
            (((1,), (1,)), ((), ())), preferred_element_type=F32,
        )
        for part in range(chunk // LANES):
            number = poses[:, rows_at(index * chunk + part * LANES, LANES)]
            numbers = [number[0:8] & 7, number[8:16] & 7, number[0:8] >> 3, number[8:16] >> 3]
            block = index * (chunk // LANES) + part
            if resume:
                value = [picks[block, 0:8], picks[block, 8:16]]
            else:
                value = [jnp.zeros((8, LANES), F32), jnp.zeros((8, LANES), F32)]
            value = picks_of(score[:, part * LANES : (part + 1) * LANES], pieces, numbers, value)
            picks[block] = jnp.concatenate(value, axis=0)

    def near_step(index):
        score_chunk(index, slices[share : NPOSE - share, :], [(share, 0, NPOSE - 2 * share)], False)

    gathers[2].wait_recv()
    gathers[7].wait_recv()
    gathers[8].wait_recv()
    each(members - 1, power_step, 1)
    each(chunks // 2, near_step)
    gathers[5].wait_recv()
    gathers[9].start()
    gathers[6].wait_recv()
    gathers[10].start()
    each(chunks, near_step, chunks // 2)
    gathers[9].wait_recv()
    gathers[10].wait_recv()
    power_step(0)
    power_step(members - 1)

    def far_chunk(index):
        table = jnp.concatenate([slices[0:share, :], slices[NPOSE - share : NPOSE, :]], axis=0)
        score_chunk(index, table, [(0, 0, share), (NPOSE - share, share, share)], True)

    def pick_copy(peer):
        step = lax.rem(peer - own + slabs, slabs)
        return slab_copy(1, picks, picks_in, step)

    def far_step(turn):
        index = lax.rem(own // 2 + turn, chunks)
        far_chunk(index)
        pick_copy(2 * index).start()
        pick_copy(2 * index + 1).start()

    each(chunks, far_step, 1)
    far_chunk(own // 2)
    sibling = own + 1 - 2 * lax.rem(own, 2)
    pick_copy(sibling).start()
    picks_in[own] = picks[own]
    load[6].wait()
    row_weight[...] = jnp.zeros_like(row_weight)
    slab_arrivals(1, picks_in)
    total = picks_in[0]
    for block in range(1, slabs):
        total = total + picks_in[block]
    total = total * precision[:, rows_at(own * LANES, LANES)]
    exponent = jnp.exp(total - jnp.max(total, axis=0, keepdims=True))
    shares[own] = exponent / jnp.sum(exponent, axis=0, keepdims=True)

    def share_copy(step):
        return remote(
            shares.at[own], shares.at[own], slab_send.at[2, step], slab_recv.at[2, step], {"slab": slab_peer(step)}
        )

    for step in range(1, slabs):
        share_copy(step).start()
    tile = LANES

    def spread_chunk(block):
        at = rows_at(block * LANES, LANES)
        amount = shares[block] * precision[:, at]
        number = poses[:, at]
        for first in range(0, NPOSE, tile):
            row = iota((tile, LANES), 0) + first
            value = jnp.zeros((tile, LANES), F32)
            for k in range(cands):
                value = jnp.where(number[k : k + 1] == row, amount[k : k + 1], value)
            rounded = value.astype(BF16)
            spread[first : first + tile, at] = rounded
            row_weight[first : first + tile, :] += rounded.astype(F32)

    def spread_step(step):
        slab_arrival(2, shares, step).wait_recv()
        spread_chunk(slab_peer(slabs - step))

    spread_chunk(own)
    each(slabs, spread_step, 1)

    stripe = 2 * LANES
    stripes = width // stripe

    def away_copy(index):
        at = rows_at(index * stripe, stripe)
        return img_copy(24 + index, away.at[:, at], away_in.at[:, at], partner)

    def away_step(index):
        at = rows_at(index * stripe, stripe)
        away[:, at] = dot(spread[side : 2 * side, :], images_v[:, at]).astype(BF16)
        away_copy(index).start()

    def kept_step(index):
        at = rows_at(index * stripe, stripe)
        kept[:, at] = dot(spread[0:side, :], images_v[:, at])

    each(stripes, away_step)
    each(stripes, kept_step)
    each(stripes, lambda index: away_copy(index).wait_recv())

    def kept_part(index, first=0, size=share):
        here = index * share + first
        there = (ring_len - 1 - index) * share + first
        return kept[here : here + size, :] + away_in[there : there + size, :].astype(F32)

    opposite[...] = kept_part(FAR).astype(BF16)
    ring_copies = [
        img_copy(11, opposite.at[0:half], opposite_in.at[0:half], right),
        img_copy(12, opposite.at[half:share], opposite_in.at[half:share], left),
        img_copy(13, ring.at[0, half:share], ring_in.at[0, half:share], right),
        img_copy(14, ring.at[1, 0:half], ring_in.at[1, 0:half], left),
        img_copy(15, ring.at[0, 0:half], ring_in.at[0, 0:half], right),
        img_copy(28, ring.at[1, half:share], ring_in.at[1, half:share], left),
    ]
    ring_copies[0].start()
    ring_copies[1].start()
    ring[0, half:share] = kept_part(RIGHT, half, half).astype(BF16)
    ring_copies[2].start()
    ring[1, 0:half] = kept_part(LEFT, 0, half).astype(BF16)
    ring_copies[3].start()
    ring_copies[0].wait_recv()
    ring[0, 0:half] = (kept_part(RIGHT, 0, half) + opposite_in[0:half, :].astype(F32)).astype(BF16)
    ring_copies[4].start()
    ring_copies[1].wait_recv()
    ring[1, half:share] = (kept_part(LEFT, half, half) + opposite_in[half:share, :].astype(F32)).astype(BF16)
    ring_copies[5].start()

    weight = jnp.sum(row_weight[...], axis=1, keepdims=True)
    mass_row = pick_row(iota((NPOSE, NPOSE), 0) == pose_row[0:1, :], weight)
    masses[member] = jnp.broadcast_to(mass_row, (8, NPOSE))

    def mass_copy(step):
        return img_copy(16 + step, masses.at[member], masses.at[member], img_peer(step))

    def mass_arrival(step):
        peer = img_peer(members - step)
        return img_copy(16 + step, masses.at[peer], masses.at[peer], peer)

    for step in range(1, members):
        mass_copy(step).start()
    for block in range(slabs):
        posterior[:, block * LANES : (block + 1) * LANES] = shares[block]
    held = kept_part(HOME)
    for index in range(2, 6):
        ring_copies[index].wait_recv()
    summed = (held + ring_in[0].astype(F32) + ring_in[1].astype(F32)).astype(BF16)

    unpack = jnp.where(pack_table[...].T[:, 0:1] == iota((mine, share), 1).astype(F32), 1.0, 0.0).astype(BF16)
    unpacked = dot(unpack, summed)
    for block in range(slabs):
        returning[block] = unpacked[block * deep : (block + 1) * deep].astype(BF16)
    slab_exchange(3, returning, returned)
    returned[own] = returning[own]

    for step in range(1, members):
        mass_arrival(step).wait_recv()
    mass_total = masses[0]
    for index in range(1, members):
        mass_total = mass_total + masses[index]
    lanes = iota((LANES, LANES), 1)
    mass_cols = []
    for block in range(members):
        key_col = slot_table[:, block * LANES : (block + 1) * LANES].T[:, 3:4]
        matched = key_col == iota((LANES, NPOSE), 1).astype(F32)
        amount = jnp.sum(jnp.where(matched, mass_total[0:1, :], 0.0), axis=1, keepdims=True)
        first = amount.astype(BF16).astype(F32)
        second = (amount - first).astype(BF16).astype(F32)
        third = amount - first - second
        mass_cols.append(
            jnp.where(lanes == 0, first, jnp.where(lanes == 1, second, jnp.where(lanes == 2, third, 0.0))).astype(BF16)
        )
    mass_table = jnp.concatenate(mass_cols, axis=0)

    def mass_step(index):
        at = rows_at(index * LANES, LANES)
        mass = jnp.sum(dot(weave[at, :], mass_table), axis=1, keepdims=True)
        inverse[at, :] = jnp.broadcast_to(1.0 / (mass + RIDGE), (LANES, LANES))

    each(voxels // LANES, mass_step)
    load[7].wait()
    load[8].wait()
    slab_arrivals(3, returned)

    gathered = jnp.concatenate([returned[block].astype(F32) for block in range(slabs)], axis=0).astype(BF16)
    turned = dot(gathered, columns_v[...])
    for block in range(members):
        crossing[block] = turned[:, block * LANES : (block + 1) * LANES].astype(BF16)

    def cross_copy(step):
        peer = img_peer(step)
        return img_copy(32 + step, crossing.at[peer], crossed.at[member], peer)

    def cross_arrival(step):
        peer = img_peer(members - step)
        return img_copy(32 + step, crossed.at[peer], crossed.at[peer], peer)

    for step in range(1, members):
        cross_copy(step).start()
    crossed[member] = crossing[member]

    for step in range(1, slabs):
        slab_copy(0, outgoing, incoming, step).wait_send()
        slab_copy(1, picks, picks_in, step).wait_send()
        share_copy(step).wait_send()
        slab_copy(3, returning, returned, step).wait_send()
    for copy in gathers + ring_copies:
        copy.wait_send()
    each(stripes, lambda index: away_copy(index).wait_send())
    for step in range(1, members):
        mass_copy(step).wait_send()
    for step in range(1, members):
        cross_arrival(step).wait_recv()

    voxel_rows = dot(weave[...], crossed[...].reshape(members * LANES, LANES)) * inverse[...]
    fourier = voxel_rows.astype(BF16)
    edge = density.shape[2]
    columns_out = density.shape[1]
    for plane in range(density.shape[0]):
        field = fourier[plane * edge : (plane + 1) * edge]
        real = dot(rows_v[:, :edge], field)
        imag = dot(rows_v[:, edge:], field)
        density[plane] = (real[:, :columns_out] + imag[:, columns_out:]).T
    for step in range(1, members):
        cross_copy(step).wait_send()


def per_device(images, volume, precision, candidates, slot_key, slot_voxel, slot_weight):
    members = lax.axis_size("img")
    slabs = lax.axis_size("slab")
    planes, edge, width = volume.shape
    particles, cands = candidates.shape
    cap = slot_key.shape[2]
    deep = cap // members
    share = NPOSE // members
    voxels = planes * edge
    mine = slabs * deep
    side = NPOSE // 2
    big = pl.BlockSpec(memory_space=pl.ANY)
    near = pl.BlockSpec(memory_space=pltpu.VMEM)
    scratch = [
        pltpu.VMEM((particles, width), BF16),
        pltpu.VMEM((voxels, width), BF16),
        pltpu.VMEM((width, width), BF16),
        pltpu.VMEM((edge, 2 * edge), BF16),
        pltpu.VMEM((1, particles), F32),
        pltpu.VMEM((cands, particles), jnp.int32),
        pltpu.VMEM(slot_key.shape, jnp.int32),
        pltpu.VMEM(slot_key.shape, jnp.int32),
        pltpu.VMEM(slot_key.shape, jnp.int32),
        pltpu.VMEM((8, slabs * cap), F32),
        pltpu.VMEM((8, mine), F32),
        pltpu.VMEM((8, NPOSE), jnp.int32),
        pltpu.VMEM((slabs, deep, width), BF16),
        pltpu.VMEM((slabs, deep, width), BF16),
        pltpu.VMEM((NPOSE, width), BF16),
        pltpu.VMEM((NPOSE, LANES), F32),
        pltpu.VMEM((voxels, slabs * cap), BF16),
        pltpu.VMEM((slabs, cands, LANES), F32),
        pltpu.VMEM((slabs, cands, LANES), F32),
        pltpu.VMEM((slabs, cands, LANES), F32),
        pltpu.VMEM((NPOSE, particles), BF16),
        pltpu.VMEM((NPOSE, LANES), F32),
        pltpu.VMEM((side, width), BF16),
        pltpu.VMEM((side, width), BF16),
        pltpu.VMEM((side, width), F32),
        pltpu.VMEM((share, width), BF16),
        pltpu.VMEM((share, width), BF16),
        pltpu.VMEM((2, share, width), BF16),
        pltpu.VMEM((2, share, width), BF16),
        pltpu.VMEM((members, 8, NPOSE), F32),
        pltpu.VMEM((voxels, LANES), F32),
        pltpu.VMEM((slabs, deep, width), BF16),
        pltpu.VMEM((slabs, deep, width), BF16),
        pltpu.VMEM((members, mine, LANES), BF16),
        pltpu.VMEM((members, mine, LANES), BF16),
        pltpu.SemaphoreType.DMA((9,)),
        pltpu.SemaphoreType.DMA((4, slabs)),
        pltpu.SemaphoreType.DMA((4, slabs)),
        pltpu.SemaphoreType.DMA((40,)),
        pltpu.SemaphoreType.DMA((40,)),
    ]
    density, posterior = pl.pallas_call(
        functools.partial(kernel, slabs, members),
        out_shape=(
            jax.ShapeDtypeStruct((planes, edge // members, edge), F32),
            jax.ShapeDtypeStruct((cands, particles), F32),
        ),
        in_specs=[big] * 9,
        out_specs=(near, near),
        scratch_shapes=scratch,
        compiler_params=pltpu.CompilerParams(
            collective_id=0, has_side_effects=True, vmem_limit_bytes=56 * 1024 * 1024
        ),
    )(
        images, volume.reshape(voxels, width), column_table(edge, members), row_table(edge),
        precision[None, :], candidates.T, slot_key, slot_voxel, slot_weight,
    )
    return density.transpose(0, 2, 1), posterior.T


def solution(mesh):
    placed = (P("img", "slab"), P("slab", None, None), P("img"), P("img", None), P(), P(), P())
    return jax.shard_map(
        per_device,
        mesh=mesh,
        in_specs=placed,
        out_specs=(P("slab", None, "img"), P("img", None)),
        check_vma=False,
    )
```

```python
import functools
import math

import jax
import jax.numpy as jnp
import numpy as np
from jax import lax
from jax.experimental import pallas as pl
from jax.experimental.pallas import tpu as pltpu
from jax.sharding import PartitionSpec as P

NPOSE = 512
WSTEPS = 16
RIDGE = 0.25
LANES = 128
F32 = jnp.float32
BF16 = jnp.bfloat16


def gridding(samples):
    offset = (np.arange(samples) - samples / 2) / samples
    return 1.0 / np.sinc(offset) ** 2


def angles(length):
    counter = np.arange(length)
    return (counter[:, None] * counter[None, :] % length) * (2.0 * math.pi / length)


def column_table(length, members):
    turn = angles(length)
    cosine, sine = np.cos(turn), np.sin(turn)
    scale = gridding(length)[None, :]
    to_re = np.concatenate([cosine, -sine], axis=0) * scale
    to_im = np.concatenate([sine, cosine], axis=0) * scale
    width = length // members
    both = np.stack([to_re.reshape(-1, members, width), to_im.reshape(-1, members, width)], axis=2)
    return jnp.asarray(both.reshape(2 * length, 2 * length), BF16)


def row_table(length):
    turn = angles(length)
    scale = gridding(length)[:, None] / length
    return jnp.asarray(np.concatenate([np.cos(turn), -np.sin(turn)], axis=1) * scale, BF16)


def remote(src, dst, sends, recvs, device):
    return pltpu.make_async_remote_copy(
        src_ref=src,
        dst_ref=dst,
        send_sem=sends,
        recv_sem=recvs,
        device_id=device,
        device_id_type=pl.DeviceIdType.MESH,
    )


def dot(left, right):
    return jnp.dot(left, right, preferred_element_type=F32)


def each(count, step, first=0):
    def body(index, carry):
        step(index)
        return carry

    lax.fori_loop(first, count, body, 0)


def rows_at(start, size):
    return pl.ds(pl.multiple_of(start, size), size)


def iota(shape, axis):
    return lax.broadcasted_iota(jnp.int32, shape, axis)


def pick_row(mask, values):
    return jnp.sum(jnp.where(mask, values, 0.0), axis=0, keepdims=True)


def kernel(
    slabs, members,
    images, volume, columns, rows, precision_in, poses_in, keys_in, voxels_in, weights_in,
    density, posterior,
    images_v, volume_v, columns_v, rows_v, precision, poses, keys, voxel_of, weight_of,
    slot_table, pack_table, pose_row,
    outgoing, incoming, slices, half_power, weave,
    picks, picks_in, shares, spread, row_weight,
    away, away_in, kept, opposite, opposite_in, ring, ring_in,
    masses, inverse, returning, returned, crossing, crossed,
    loads, slab_send, slab_recv, img_send, img_recv,
):
    own = lax.axis_index("slab")
    member = lax.axis_index("img")
    ring_len = members // 2
    chip, core = member // 2, lax.rem(member, 2)
    share = NPOSE // members
    half = share // 2
    side = ring_len * share
    deep = outgoing.shape[1]
    mine = slabs * deep
    cap = keys.shape[2]
    width = volume_v.shape[1]
    voxels = volume_v.shape[0]
    cands = poses.shape[0]
    right = 2 * lax.rem(chip + 1, ring_len) + core
    left = 2 * lax.rem(chip + ring_len - 1, ring_len) + core
    partner = 2 * chip + 1 - core

    def slab_peer(step):
        return lax.rem(own + step, slabs)

    def img_peer(step):
        return lax.rem(member + step, members)

    barrier = pltpu.get_barrier_semaphore()

    def greet(axis, peer):
        pl.semaphore_signal(barrier, inc=1, device_id={axis: peer}, device_id_type=pl.DeviceIdType.MESH)

    sources = [keys_in, voxels_in, weights_in, volume, poses_in, images, precision_in, columns, rows]
    targets = [keys, voxel_of, weight_of, volume_v, poses, images_v, precision, columns_v, rows_v]
    load = [pltpu.make_async_copy(src, dst, loads.at[i]) for i, (src, dst) in enumerate(zip(sources, targets))]
    for index in range(5):
        load[index].start()
    for step in range(1, slabs):
        greet("slab", slab_peer(step))
    for step in range(1, members):
        greet("img", img_peer(step))

    for index in range(3):
        load[index].wait()
    before = jnp.zeros((slabs, cap), F32)
    for slab in range(slabs):
        before += jnp.where(keys[slab] >= 0, 1.0, 0.0) * jnp.where(own > slab, 1.0, 0.0)
    out_start = jnp.sum(before, axis=1, keepdims=True)
    total_slots = slabs * cap
    own_key = keys[own]
    own_code = voxel_of[own] * 32 + jnp.where(own_key >= 0, weight_of[own], 31)

    def ordered(first, count, tables):
        position = iota((1, count), 1) + first
        block_sel = iota((slabs, count), 0) == ((position >> 3) & (slabs - 1))
        start_row = pick_row(block_sel, out_start).astype(jnp.int32)
        slot_row = members * (position & 7) + (((position >> 7) - start_row) & 7)
        slot_sel = iota((cap, count), 0) == slot_row
        chooser = jnp.where(block_sel, 1.0, 0.0)
        found = []
        for table in tables:
            wide = lax.dot_general(
                table.astype(F32), chooser, (((0,), (0,)), ((), ())),
                precision=lax.Precision.HIGHEST, preferred_element_type=F32,
            )
            found.append(pick_row(slot_sel, wide))
        return found

    def decoded(code):
        code_row = code.astype(jnp.int32)
        level = code_row & 31
        alive = level <= WSTEPS
        spot = (code_row >> 5).astype(F32)
        lower = jnp.where(alive, level, 0).astype(F32) * (1.0 / WSTEPS)
        upper = jnp.where(alive, WSTEPS - level, 0).astype(F32) * (1.0 / WSTEPS)
        return spot, lower, upper

    parts = decoded(ordered(member * mine, mine, [own_code])[0])
    own_cols = jnp.concatenate(list(parts) + [jnp.zeros((5, mine), F32)], axis=0).T
    place = iota((mine, voxels), 1)
    spot = own_cols[:, 0:1].astype(jnp.int32)
    take = jnp.where(place == spot, own_cols[:, 1:2], 0.0) + jnp.where(place == spot + 1, own_cols[:, 2:3], 0.0)
    load[3].wait()
    for index in range(5, len(load)):
        load[index].start()
    woven = dot(take.astype(BF16), volume_v[...])
    for block in range(slabs):
        outgoing[block] = woven[block * deep : (block + 1) * deep].astype(BF16)
    pl.semaphore_wait(barrier, slabs - 1 + members - 1)

    def slab_copy(stage, src, dst, step):
        peer = slab_peer(step)
        return remote(
            src.at[peer], dst.at[own], slab_send.at[stage, step], slab_recv.at[stage, step], {"slab": peer}
        )

    def slab_arrival(stage, dst, step):
        peer = slab_peer(slabs - step)
        return remote(
            dst.at[peer], dst.at[peer], slab_send.at[stage, step], slab_recv.at[stage, step], {"slab": peer}
        )

    def slab_exchange(stage, src, dst):
        for step in range(1, slabs):
            slab_copy(stage, src, dst, step).start()

    def slab_arrivals(stage, dst):
        for step in range(1, slabs):
            slab_arrival(stage, dst, step).wait_recv()

    def img_copy(slot, src, dst, device):
        return remote(src, dst, img_send.at[slot], img_recv.at[slot], {"img": device})

    slab_exchange(0, outgoing, incoming)
    incoming[own] = outgoing[own]

    code, key_row = ordered(0, total_slots, [own_code, own_key])
    for index, value in enumerate(decoded(code) + (key_row,)):
        slot_table[index : index + 1, :] = value
    slot_table[4:8, :] = jnp.zeros((4, total_slots), F32)

    in_key = jnp.concatenate(
        [jnp.sum(jnp.where(iota((slabs, cap), 0) == own, keys[slab], 0), axis=0, keepdims=True) for slab in range(slabs)],
        axis=0,
    )
    live = jnp.where(in_key >= 0, 1.0, 0.0).astype(BF16)
    count = dot(live, jnp.ones((cap, LANES), BF16))
    earlier = jnp.where(iota((slabs, slabs), 1) < iota((slabs, slabs), 0), 1.0, 0.0).astype(BF16)
    start = dot(earlier, count.astype(BF16))
    lane = iota((1, mine), 1)
    slab_sel = iota((slabs, mine), 0) == (lane >> 3)
    in_start = pick_row(slab_sel, start).astype(jnp.int32)
    in_count = pick_row(slab_sel, count).astype(jnp.int32)
    slot = members * (lane & 7) + ((member - in_start) & 7)
    pack_row = jnp.where(slot < in_count, (in_start + slot) >> 3, -1)
    pack_table[...] = jnp.broadcast_to(pack_row, (8, mine)).astype(F32)

    number = start[:, :cap].astype(jnp.int32) + iota((slabs, cap), 1)
    holder = number & (members - 1)
    ahead = ((holder >> 1) - chip) & (ring_len - 1)
    near = jnp.where(ahead == 0, 3, jnp.where(ahead == 1, 1, jnp.where(ahead == 2, 0, 2)))
    row = jnp.where((holder & 1) == core, near, members - 1 - near) * share + (number >> 3)
    key_cols, row_cols = in_key.astype(F32).T, row.astype(F32).T
    pose_ids = iota((cap, NPOSE), 1).astype(F32)
    found_rows = jnp.zeros((cap, NPOSE), F32)
    for slab in range(slabs):
        found_rows += jnp.where(key_cols[:, slab : slab + 1] == pose_ids, row_cols[:, slab : slab + 1], 0.0)
    pose_row[...] = jnp.broadcast_to(jnp.sum(found_rows, axis=0, keepdims=True), (8, NPOSE)).astype(jnp.int32)

    load[4].wait()
    for part in range(poses.shape[1] // LANES):
        for k in range(0, cands, 8):
            at = (slice(k, k + 8), slice(part * LANES, (part + 1) * LANES))
            pose = poses[at]
            low, high = pose & (LANES - 1), pose >> 7
            renamed = jnp.zeros_like(pose)
            for piece in range(NPOSE // LANES):
                table = pose_row[:, piece * LANES : (piece + 1) * LANES]
                found = jnp.take_along_axis(table, low, axis=1, mode="promise_in_bounds")
                renamed = jnp.where(high == piece, found, renamed)
            poses[at] = renamed

    slab_arrivals(0, incoming)
    arrived = jnp.concatenate([incoming[block].astype(F32) for block in range(slabs)], axis=0).astype(BF16)
    pack = jnp.where(iota((share, mine), 0).astype(F32) == pack_table[0:1, :], 1.0, 0.0).astype(BF16)

    def block_of(index, first=0, size=share):
        return slices.at[index * share + first : index * share + first + size]

    FAR, RIGHT, LEFT, HOME = 0, 1, 2, 3
    slices[HOME * share : (HOME + 1) * share, :] = dot(pack, arrived).astype(BF16)

    def other(index):
        return members - 1 - index

    def top(index):
        return block_of(index, 0, half)

    def bottom(index):
        return block_of(index, half, half)

    gathers = [
        img_copy(0, top(HOME), top(LEFT), right),
        img_copy(1, bottom(HOME), bottom(RIGHT), left),
        img_copy(2, block_of(HOME), block_of(other(HOME)), partner),
        img_copy(3, bottom(HOME), bottom(LEFT), right),
        img_copy(4, top(HOME), top(RIGHT), left),
        img_copy(5, top(LEFT), top(FAR), right),
        img_copy(6, bottom(RIGHT), bottom(FAR), left),
        img_copy(7, block_of(LEFT), block_of(other(LEFT)), partner),
        img_copy(8, block_of(RIGHT), block_of(other(RIGHT)), partner),
        img_copy(9, top(FAR), top(other(FAR)), partner),
        img_copy(10, bottom(FAR), bottom(other(FAR)), partner),
    ]
    for index in range(5):
        gathers[index].start()

    def weave_step(index):
        at = iota((LANES, total_slots), 0) + index * LANES
        spots = slot_table[0:1, :].astype(jnp.int32)
        value = jnp.where(spots == at, slot_table[1:2, :], 0.0) + jnp.where(spots + 1 == at, slot_table[2:3, :], 0.0)
        weave[rows_at(index * LANES, LANES), :] = value.astype(BF16)

    each(voxels // LANES, weave_step)
    gathers[0].wait_recv()
    gathers[5].start()
    gathers[1].wait_recv()
    gathers[6].start()
    gathers[3].wait_recv()
    gathers[7].start()
    gathers[4].wait_recv()
    gathers[8].start()
    load[5].wait()

    def power_step(index):
        at = rows_at(index * share, share)
        values = slices[at, :].astype(F32)
        total = 0.5 * jnp.sum(values * values, axis=1, keepdims=True)
        half_power[at, :] = jnp.broadcast_to(total, (share, LANES))

    chunk = 2 * LANES
    chunks = images_v.shape[0] // chunk

    def picks_of(score, pieces, numbers, value):
        for first, offset, size in pieces:
            block = score[offset : offset + size] - half_power[first : first + size, :]
            for group in range(size // 8):
                picked = jnp.take_along_axis(
                    block[group * 8 : (group + 1) * 8], numbers[0], axis=0, mode="promise_in_bounds"
                )
                value[0] = jnp.where(numbers[2] == first // 8 + group, picked, value[0])
                picked = jnp.take_along_axis(
                    block[group * 8 : (group + 1) * 8], numbers[1], axis=0, mode="promise_in_bounds"
                )
                value[1] = jnp.where(numbers[3] == first // 8 + group, picked, value[1])
        return value

    def score_chunk(index, table, pieces, resume):
        score = lax.dot_general(
            table, images_v[rows_at(index * chunk, chunk), :],
            (((1,), (1,)), ((), ())), preferred_element_type=F32,
        )
        for part in range(chunk // LANES):
            number = poses[:, rows_at(index * chunk + part * LANES, LANES)]
            numbers = [number[0:8] & 7, number[8:16] & 7, number[0:8] >> 3, number[8:16] >> 3]
            block = index * (chunk // LANES) + part
            if resume:
                value = [picks[block, 0:8], picks[block, 8:16]]
            else:
                value = [jnp.zeros((8, LANES), F32), jnp.zeros((8, LANES), F32)]
            value = picks_of(score[:, part * LANES : (part + 1) * LANES], pieces, numbers, value)
            picks[block] = jnp.concatenate(value, axis=0)

    def near_step(index):
        score_chunk(index, slices[share : NPOSE - share, :], [(share, 0, NPOSE - 2 * share)], False)

    gathers[2].wait_recv()
    gathers[7].wait_recv()
    gathers[8].wait_recv()
    each(members - 1, power_step, 1)
    each(chunks // 2, near_step)
    gathers[5].wait_recv()
    gathers[9].start()
    gathers[6].wait_recv()
    gathers[10].start()
    each(chunks, near_step, chunks // 2)
    gathers[9].wait_recv()
    gathers[10].wait_recv()
    power_step(0)
    power_step(members - 1)

    def far_chunk(index):
        table = jnp.concatenate([slices[0:share, :], slices[NPOSE - share : NPOSE, :]], axis=0)
        score_chunk(index, table, [(0, 0, share), (NPOSE - share, share, share)], True)

    def pick_copy(peer):
        step = lax.rem(peer - own + slabs, slabs)
        return slab_copy(1, picks, picks_in, step)

    def far_step(turn):
        index = lax.rem(own // 2 + turn, chunks)
        far_chunk(index)
        pick_copy(2 * index).start()
        pick_copy(2 * index + 1).start()

    each(chunks, far_step, 1)
    far_chunk(own // 2)
    sibling = own + 1 - 2 * lax.rem(own, 2)
    pick_copy(sibling).start()
    picks_in[own] = picks[own]
    load[6].wait()
    row_weight[...] = jnp.zeros_like(row_weight)
    slab_arrivals(1, picks_in)
    total = picks_in[0]
    for block in range(1, slabs):
        total = total + picks_in[block]
    total = total * precision[:, rows_at(own * LANES, LANES)]
    exponent = jnp.exp(total - jnp.max(total, axis=0, keepdims=True))
    shares[own] = exponent / jnp.sum(exponent, axis=0, keepdims=True)

    def share_copy(step):
        return remote(
            shares.at[own], shares.at[own], slab_send.at[2, step], slab_recv.at[2, step], {"slab": slab_peer(step)}
        )

    for step in range(1, slabs):
        share_copy(step).start()
    tile = LANES

    def spread_chunk(block):
        at = rows_at(block * LANES, LANES)
        amount = (shares[block] * precision[:, at]).astype(BF16)
        number = poses[:, at].astype(jnp.int16)
        for first in range(0, NPOSE, tile):
            row = (iota((tile, LANES), 0) + first).astype(jnp.int16)
            value = jnp.zeros((tile, LANES), BF16)
            for k in range(cands):
                value = jnp.where(number[k : k + 1] == row, amount[k : k + 1], value)
            spread[first : first + tile, at] = value
            row_weight[first : first + tile, :] += value.astype(F32)

    def spread_step(step):
        slab_arrival(2, shares, step).wait_recv()
        spread_chunk(slab_peer(slabs - step))

    spread_chunk(own)
    each(slabs, spread_step, 1)

    stripe = 2 * LANES
    halves = 2
    wide = width // halves
    per_half = wide // stripe

    def away_copy(index):
        at = slice(index * stripe, (index + 1) * stripe)
        return img_copy(40 + index, away.at[:, at], away_in.at[:, at], partner)

    def back_stripe(index):
        at = slice(index * stripe, (index + 1) * stripe)
        part = dot(spread[...], images_v[:, at])
        away[:, at] = part[side:].astype(BF16)
        away_copy(index).start()
        kept[:, at] = part[:side]

    def columns_of(part):
        return slice(part * wide, (part + 1) * wide)

    def kept_part(index, part, first=0, size=share):
        here = index * share + first
        there = (ring_len - 1 - index) * share + first
        at = columns_of(part)
        return kept[here : here + size, at] + away_in[there : there + size, at].astype(F32)

    def ring_copy(part, index):
        at = columns_of(part)
        low, high = slice(0, half), slice(half, share)
        refs = [
            (opposite.at[low, at], opposite_in.at[low, at], right),
            (opposite.at[high, at], opposite_in.at[high, at], left),
            (ring.at[0, high, at], ring_in.at[0, high, at], right),
            (ring.at[1, low, at], ring_in.at[1, low, at], left),
            (ring.at[0, low, at], ring_in.at[0, low, at], right),
            (ring.at[1, high, at], ring_in.at[1, high, at], left),
        ]
        return img_copy(48 + 6 * part + index, *refs[index])

    def ring_start(part):
        at = columns_of(part)
        for index in range(part * per_half, (part + 1) * per_half):
            away_copy(index).wait_recv()
        opposite[:, at] = kept_part(FAR, part).astype(BF16)
        ring_copy(part, 0).start()
        ring_copy(part, 1).start()
        ring[0, half:share, at] = kept_part(RIGHT, part, half, half).astype(BF16)
        ring_copy(part, 2).start()
        ring[1, 0:half, at] = kept_part(LEFT, part, 0, half).astype(BF16)
        ring_copy(part, 3).start()

    def ring_relay(part):
        at = columns_of(part)
        ring_copy(part, 0).wait_recv()
        ring[0, 0:half, at] = (kept_part(RIGHT, part, 0, half) + opposite_in[0:half, at].astype(F32)).astype(BF16)
        ring_copy(part, 4).start()
        ring_copy(part, 1).wait_recv()
        ring[1, half:share, at] = (
            kept_part(LEFT, part, half, half) + opposite_in[half:share, at].astype(F32)
        ).astype(BF16)
        ring_copy(part, 5).start()

    unpack = jnp.where(pack_table[...].T[:, 0:1] == iota((mine, share), 1).astype(F32), 1.0, 0.0).astype(BF16)

    def ring_finish(part):
        at = columns_of(part)
        held = kept_part(HOME, part)
        for index in range(2, 6):
            ring_copy(part, index).wait_recv()
        summed = (held + ring_in[0, :, at].astype(F32) + ring_in[1, :, at].astype(F32)).astype(BF16)
        unpacked = dot(unpack, summed)
        for block in range(slabs):
            returning[part, block] = unpacked[block * deep : (block + 1) * deep].astype(BF16)
        slab_exchange(3 + part, returning.at[part], returned.at[part])
        returned[part, own] = returning[part, own]

    back_stripe(0)
    back_stripe(1)
    back_stripe(2)
    ring_start(0)
    back_stripe(3)
    ring_relay(0)
    ring_start(1)

    weight = jnp.sum(row_weight[...], axis=1, keepdims=True)
    mass_row = pick_row(iota((NPOSE, NPOSE), 0) == pose_row[0:1, :], weight)
    masses[member] = jnp.broadcast_to(mass_row, (8, NPOSE))

    def mass_copy(step):
        return img_copy(16 + step, masses.at[member], masses.at[member], img_peer(step))

    def mass_arrival(step):
        peer = img_peer(members - step)
        return img_copy(16 + step, masses.at[peer], masses.at[peer], peer)

    for step in range(1, members):
        mass_copy(step).start()
    ring_relay(1)
    ring_finish(0)
    ring_finish(1)
    for block in range(slabs):
        posterior[:, block * LANES : (block + 1) * LANES] = shares[block]

    for step in range(1, members):
        mass_arrival(step).wait_recv()
    mass_total = masses[0]
    for index in range(1, members):
        mass_total = mass_total + masses[index]
    lanes = iota((LANES, LANES), 1)
    mass_cols = []
    for block in range(members):
        key_col = slot_table[:, block * LANES : (block + 1) * LANES].T[:, 3:4]
        matched = key_col == iota((LANES, NPOSE), 1).astype(F32)
        amount = jnp.sum(jnp.where(matched, mass_total[0:1, :], 0.0), axis=1, keepdims=True)
        first = amount.astype(BF16).astype(F32)
        second = (amount - first).astype(BF16).astype(F32)
        third = amount - first - second
        mass_cols.append(
            jnp.where(lanes == 0, first, jnp.where(lanes == 1, second, jnp.where(lanes == 2, third, 0.0))).astype(BF16)
        )
    mass_table = jnp.concatenate(mass_cols, axis=0)

    def mass_step(index):
        at = rows_at(index * LANES, LANES)
        mass = jnp.sum(dot(weave[at, :], mass_table), axis=1, keepdims=True)
        inverse[at, :] = jnp.broadcast_to(1.0 / (mass + RIDGE), (LANES, LANES))

    each(voxels // LANES, mass_step)
    load[7].wait()
    load[8].wait()

    turned = jnp.zeros((mine, width), F32)
    for part in range(halves):
        slab_arrivals(3 + part, returned.at[part])
        gathered = jnp.concatenate([returned[part, block].astype(F32) for block in range(slabs)], axis=0)
        turned += dot(gathered.astype(BF16), columns_v[columns_of(part), :])
    for block in range(members):
        crossing[block] = turned[:, block * LANES : (block + 1) * LANES].astype(BF16)

    def cross_copy(step):
        peer = img_peer(step)
        return img_copy(32 + step, crossing.at[peer], crossed.at[member], peer)

    def cross_arrival(step):
        peer = img_peer(members - step)
        return img_copy(32 + step, crossed.at[peer], crossed.at[peer], peer)

    for step in range(1, members):
        cross_copy(step).start()
    crossed[member] = crossing[member]

    for step in range(1, slabs):
        slab_copy(0, outgoing, incoming, step).wait_send()
        slab_copy(1, picks, picks_in, step).wait_send()
        share_copy(step).wait_send()
        for part in range(halves):
            slab_copy(3 + part, returning.at[part], returned.at[part], step).wait_send()
    for copy in gathers:
        copy.wait_send()
    for index in range(halves * per_half):
        away_copy(index).wait_send()
    for part in range(halves):
        for index in range(6):
            ring_copy(part, index).wait_send()
    for step in range(1, members):
        mass_copy(step).wait_send()
    for step in range(1, members):
        cross_arrival(step).wait_recv()

    voxel_rows = dot(weave[...], crossed[...].reshape(members * LANES, LANES)) * inverse[...]
    fourier = voxel_rows.astype(BF16)
    edge = density.shape[2]
    columns_out = density.shape[1]
    for plane in range(density.shape[0]):
        field = fourier[plane * edge : (plane + 1) * edge]
        real = dot(rows_v[:, :edge], field)
        imag = dot(rows_v[:, edge:], field)
        density[plane] = (real[:, :columns_out] + imag[:, columns_out:]).T
    for step in range(1, members):
        cross_copy(step).wait_send()


def per_device(images, volume, precision, candidates, slot_key, slot_voxel, slot_weight):
    members = lax.axis_size("img")
    slabs = lax.axis_size("slab")
    planes, edge, width = volume.shape
    particles, cands = candidates.shape
    cap = slot_key.shape[2]
    deep = cap // members
    share = NPOSE // members
    voxels = planes * edge
    mine = slabs * deep
    side = NPOSE // 2
    big = pl.BlockSpec(memory_space=pl.ANY)
    near = pl.BlockSpec(memory_space=pltpu.VMEM)
    scratch = [
        pltpu.VMEM((particles, width), BF16),
        pltpu.VMEM((voxels, width), BF16),
        pltpu.VMEM((width, width), BF16),
        pltpu.VMEM((edge, 2 * edge), BF16),
        pltpu.VMEM((1, particles), F32),
        pltpu.VMEM((cands, particles), jnp.int32),
        pltpu.VMEM(slot_key.shape, jnp.int32),
        pltpu.VMEM(slot_key.shape, jnp.int32),
        pltpu.VMEM(slot_key.shape, jnp.int32),
        pltpu.VMEM((8, slabs * cap), F32),
        pltpu.VMEM((8, mine), F32),
        pltpu.VMEM((8, NPOSE), jnp.int32),
        pltpu.VMEM((slabs, deep, width), BF16),
        pltpu.VMEM((slabs, deep, width), BF16),
        pltpu.VMEM((NPOSE, width), BF16),
        pltpu.VMEM((NPOSE, LANES), F32),
        pltpu.VMEM((voxels, slabs * cap), BF16),
        pltpu.VMEM((slabs, cands, LANES), F32),
        pltpu.VMEM((slabs, cands, LANES), F32),
        pltpu.VMEM((slabs, cands, LANES), F32),
        pltpu.VMEM((NPOSE, particles), BF16),
        pltpu.VMEM((NPOSE, LANES), F32),
        pltpu.VMEM((side, width), BF16),
        pltpu.VMEM((side, width), BF16),
        pltpu.VMEM((side, width), F32),
        pltpu.VMEM((share, width), BF16),
        pltpu.VMEM((share, width), BF16),
        pltpu.VMEM((2, share, width), BF16),
        pltpu.VMEM((2, share, width), BF16),
        pltpu.VMEM((members, 8, NPOSE), F32),
        pltpu.VMEM((voxels, LANES), F32),
        pltpu.VMEM((2, slabs, deep, width // 2), BF16),
        pltpu.VMEM((2, slabs, deep, width // 2), BF16),
        pltpu.VMEM((members, mine, LANES), BF16),
        pltpu.VMEM((members, mine, LANES), BF16),
        pltpu.SemaphoreType.DMA((9,)),
        pltpu.SemaphoreType.DMA((5, slabs)),
        pltpu.SemaphoreType.DMA((5, slabs)),
        pltpu.SemaphoreType.DMA((60,)),
        pltpu.SemaphoreType.DMA((60,)),
    ]
    density, posterior = pl.pallas_call(
        functools.partial(kernel, slabs, members),
        out_shape=(
            jax.ShapeDtypeStruct((planes, edge // members, edge), F32),
            jax.ShapeDtypeStruct((cands, particles), F32),
        ),
        in_specs=[big] * 9,
        out_specs=(near, near),
        scratch_shapes=scratch,
        compiler_params=pltpu.CompilerParams(
            collective_id=0, has_side_effects=True, vmem_limit_bytes=56 * 1024 * 1024
        ),
    )(
        images, volume.reshape(voxels, width), column_table(edge, members), row_table(edge),
        precision[None, :], candidates.T, slot_key, slot_voxel, slot_weight,
    )
    return density.transpose(0, 2, 1), posterior.T


def solution(mesh):
    placed = (P("img", "slab"), P("slab", None, None), P("img"), P("img", None), P(), P(), P())
    return jax.shard_map(
        per_device,
        mesh=mesh,
        in_specs=placed,
        out_specs=(P("slab", None, "img"), P("img", None)),
        check_vma=False,
    )
```

```python
import functools
import math

import jax
import jax.numpy as jnp
import numpy as np
from jax import lax
from jax.experimental import pallas as pl
from jax.experimental.pallas import tpu as pltpu
from jax.sharding import PartitionSpec as P

NPOSE = 512
WSTEPS = 16
RIDGE = 0.25
LANES = 128
F32 = jnp.float32
BF16 = jnp.bfloat16


def gridding(samples):
    offset = (np.arange(samples) - samples / 2) / samples
    return 1.0 / np.sinc(offset) ** 2


def angles(length):
    counter = np.arange(length)
    return (counter[:, None] * counter[None, :] % length) * (2.0 * math.pi / length)


def column_table(length, members):
    turn = angles(length)
    cosine, sine = np.cos(turn), np.sin(turn)
    scale = gridding(length)[None, :]
    to_re = np.concatenate([cosine, -sine], axis=0) * scale
    to_im = np.concatenate([sine, cosine], axis=0) * scale
    width = length // members
    both = np.stack([to_re.reshape(-1, members, width), to_im.reshape(-1, members, width)], axis=2)
    return jnp.asarray(both.reshape(2 * length, 2 * length), BF16)


def row_table(length):
    turn = angles(length)
    scale = gridding(length)[:, None] / length
    return jnp.asarray(np.concatenate([np.cos(turn), -np.sin(turn)], axis=1) * scale, BF16)


def remote(src, dst, sends, recvs, device):
    return pltpu.make_async_remote_copy(
        src_ref=src,
        dst_ref=dst,
        send_sem=sends,
        recv_sem=recvs,
        device_id=device,
        device_id_type=pl.DeviceIdType.MESH,
    )


def dot(left, right):
    return jnp.dot(left, right, preferred_element_type=F32)


def each(count, step, first=0):
    def body(index, carry):
        step(index)
        return carry

    lax.fori_loop(first, count, body, 0)


def rows_at(start, size):
    return pl.ds(pl.multiple_of(start, size), size)


def iota(shape, axis):
    return lax.broadcasted_iota(jnp.int32, shape, axis)


def pick_row(mask, values):
    return jnp.sum(jnp.where(mask, values, 0.0), axis=0, keepdims=True)


def kernel(
    slabs, members,
    images, volume, columns, rows, precision_in, poses_in, keys_in, voxels_in, weights_in,
    density, posterior,
    images_v, volume_v, columns_v, rows_v, precision, poses, keys, voxel_of, weight_of,
    slot_table, pack_table, pose_row,
    outgoing, incoming, slices, half_power, weave,
    picks, picks_in, shares, spread, row_weight, partial,
    away, away_in, kept, opposite, opposite_in, ring, ring_in,
    masses, inverse, returning, returned, crossing, crossed,
    loads, slab_send, slab_recv, img_send, img_recv,
):
    own = lax.axis_index("slab")
    member = lax.axis_index("img")
    ring_len = members // 2
    chip, core = member // 2, lax.rem(member, 2)
    share = NPOSE // members
    half = share // 2
    side = ring_len * share
    deep = outgoing.shape[1]
    mine = slabs * deep
    cap = keys.shape[2]
    width = volume_v.shape[1]
    voxels = volume_v.shape[0]
    cands = poses.shape[0]
    right = 2 * lax.rem(chip + 1, ring_len) + core
    left = 2 * lax.rem(chip + ring_len - 1, ring_len) + core
    partner = 2 * chip + 1 - core

    def slab_peer(step):
        return lax.rem(own + step, slabs)

    def img_peer(step):
        return lax.rem(member + step, members)

    barrier = pltpu.get_barrier_semaphore()

    def greet(axis, peer):
        pl.semaphore_signal(barrier, inc=1, device_id={axis: peer}, device_id_type=pl.DeviceIdType.MESH)

    sources = [keys_in, voxels_in, weights_in, volume, poses_in, images, precision_in, columns, rows]
    targets = [keys, voxel_of, weight_of, volume_v, poses, images_v, precision, columns_v, rows_v]
    load = [pltpu.make_async_copy(src, dst, loads.at[i]) for i, (src, dst) in enumerate(zip(sources, targets))]
    for index in range(5):
        load[index].start()
    for step in range(1, slabs):
        greet("slab", slab_peer(step))
    for step in range(1, members):
        greet("img", img_peer(step))

    for index in range(3):
        load[index].wait()
    before = jnp.zeros((slabs, cap), F32)
    for slab in range(slabs):
        before += jnp.where(keys[slab] >= 0, 1.0, 0.0) * jnp.where(own > slab, 1.0, 0.0)
    out_start = jnp.sum(before, axis=1, keepdims=True)
    total_slots = slabs * cap
    own_key = keys[own]
    own_code = voxel_of[own] * 32 + jnp.where(own_key >= 0, weight_of[own], 31)

    def ordered(first, count, tables):
        position = iota((1, count), 1) + first
        block_sel = iota((slabs, count), 0) == ((position >> 3) & (slabs - 1))
        start_row = pick_row(block_sel, out_start).astype(jnp.int32)
        slot_row = members * (position & 7) + (((position >> 7) - start_row) & 7)
        slot_sel = iota((cap, count), 0) == slot_row
        chooser = jnp.where(block_sel, 1.0, 0.0)
        found = []
        for table in tables:
            wide = lax.dot_general(
                table.astype(F32), chooser, (((0,), (0,)), ((), ())),
                precision=lax.Precision.HIGHEST, preferred_element_type=F32,
            )
            found.append(pick_row(slot_sel, wide))
        return found

    def decoded(code):
        code_row = code.astype(jnp.int32)
        level = code_row & 31
        alive = level <= WSTEPS
        spot = (code_row >> 5).astype(F32)
        lower = jnp.where(alive, level, 0).astype(F32) * (1.0 / WSTEPS)
        upper = jnp.where(alive, WSTEPS - level, 0).astype(F32) * (1.0 / WSTEPS)
        return spot, lower, upper

    parts = decoded(ordered(member * mine, mine, [own_code])[0])
    own_cols = jnp.concatenate(list(parts) + [jnp.zeros((5, mine), F32)], axis=0).T
    place = iota((mine, voxels), 1)
    spot = own_cols[:, 0:1].astype(jnp.int32)
    take = jnp.where(place == spot, own_cols[:, 1:2], 0.0) + jnp.where(place == spot + 1, own_cols[:, 2:3], 0.0)
    load[3].wait()
    for index in range(5, len(load)):
        load[index].start()
    woven = dot(take.astype(BF16), volume_v[...])
    for block in range(slabs):
        outgoing[block] = woven[block * deep : (block + 1) * deep].astype(BF16)
    pl.semaphore_wait(barrier, slabs - 1 + members - 1)

    def slab_copy(stage, src, dst, peer):
        return remote(src.at[peer], dst.at[own], slab_send.at[stage], slab_recv.at[stage], {"slab": peer})

    def slab_whole(stage, ref, count):
        blocks = ref.at[0:count]
        return remote(blocks, blocks, slab_send.at[stage], slab_recv.at[stage], {"slab": slab_peer(1)})

    def slab_exchange(stage, src, dst):
        for step in range(1, slabs):
            slab_copy(stage, src, dst, slab_peer(step)).start()

    def slab_arrivals(stage, dst):
        slab_whole(stage, dst, slabs - 1).wait_recv()

    def img_copy(slot, src, dst, device):
        return remote(src, dst, img_send.at[slot], img_recv.at[slot], {"img": device})

    slab_exchange(0, outgoing, incoming)
    incoming[own] = outgoing[own]

    code, key_row = ordered(0, total_slots, [own_code, own_key])
    for index, value in enumerate(decoded(code) + (key_row,)):
        slot_table[index : index + 1, :] = value
    slot_table[4:8, :] = jnp.zeros((4, total_slots), F32)

    in_key = jnp.concatenate(
        [jnp.sum(jnp.where(iota((slabs, cap), 0) == own, keys[slab], 0), axis=0, keepdims=True) for slab in range(slabs)],
        axis=0,
    )
    live = jnp.where(in_key >= 0, 1.0, 0.0).astype(BF16)
    count = dot(live, jnp.ones((cap, LANES), BF16))
    earlier = jnp.where(iota((slabs, slabs), 1) < iota((slabs, slabs), 0), 1.0, 0.0).astype(BF16)
    start = dot(earlier, count.astype(BF16))
    lane = iota((1, mine), 1)
    slab_sel = iota((slabs, mine), 0) == (lane >> 3)
    in_start = pick_row(slab_sel, start).astype(jnp.int32)
    in_count = pick_row(slab_sel, count).astype(jnp.int32)
    slot = members * (lane & 7) + ((member - in_start) & 7)
    pack_row = jnp.where(slot < in_count, (in_start + slot) >> 3, -1)
    pack_table[...] = jnp.broadcast_to(pack_row, (8, mine)).astype(F32)

    number = start[:, :cap].astype(jnp.int32) + iota((slabs, cap), 1)
    holder = number & (members - 1)
    ahead = ((holder >> 1) - chip) & (ring_len - 1)
    near = jnp.where(ahead == 0, 3, jnp.where(ahead == 1, 1, jnp.where(ahead == 2, 0, 2)))
    row = jnp.where((holder & 1) == core, near, members - 1 - near) * share + (number >> 3)
    key_cols, row_cols = in_key.astype(F32).T, row.astype(F32).T
    pose_ids = iota((cap, NPOSE), 1).astype(F32)
    found_rows = jnp.zeros((cap, NPOSE), F32)
    for slab in range(slabs):
        found_rows += jnp.where(key_cols[:, slab : slab + 1] == pose_ids, row_cols[:, slab : slab + 1], 0.0)
    pose_row[...] = jnp.broadcast_to(jnp.sum(found_rows, axis=0, keepdims=True), (8, NPOSE)).astype(jnp.int32)

    load[4].wait()
    for part in range(poses.shape[1] // LANES):
        for k in range(0, cands, 8):
            at = (slice(k, k + 8), slice(part * LANES, (part + 1) * LANES))
            pose = poses[at]
            low, high = pose & (LANES - 1), pose >> 7
            renamed = jnp.zeros_like(pose)
            for piece in range(NPOSE // LANES):
                table = pose_row[:, piece * LANES : (piece + 1) * LANES]
                found = jnp.take_along_axis(table, low, axis=1, mode="promise_in_bounds")
                renamed = jnp.where(high == piece, found, renamed)
            poses[at] = renamed

    slab_arrivals(0, incoming)
    arrived = jnp.concatenate([incoming[block].astype(F32) for block in range(slabs)], axis=0).astype(BF16)
    pack = jnp.where(iota((share, mine), 0).astype(F32) == pack_table[0:1, :], 1.0, 0.0).astype(BF16)

    def block_of(index, first=0, size=share):
        return slices.at[index * share + first : index * share + first + size]

    FAR, RIGHT, LEFT, HOME = 0, 1, 2, 3
    slices[HOME * share : (HOME + 1) * share, :] = dot(pack, arrived).astype(BF16)

    def other(index):
        return members - 1 - index

    def top(index):
        return block_of(index, 0, half)

    def bottom(index):
        return block_of(index, half, half)

    gathers = [
        img_copy(0, top(HOME), top(LEFT), right),
        img_copy(1, bottom(HOME), bottom(RIGHT), left),
        img_copy(2, block_of(HOME), block_of(other(HOME)), partner),
        img_copy(3, bottom(HOME), bottom(LEFT), right),
        img_copy(4, top(HOME), top(RIGHT), left),
        img_copy(5, top(LEFT), top(FAR), right),
        img_copy(6, bottom(RIGHT), bottom(FAR), left),
        img_copy(7, block_of(LEFT), block_of(other(LEFT)), partner),
        img_copy(8, block_of(RIGHT), block_of(other(RIGHT)), partner),
        img_copy(9, top(FAR), top(other(FAR)), partner),
        img_copy(10, bottom(FAR), bottom(other(FAR)), partner),
    ]
    for index in range(5):
        gathers[index].start()

    def weave_step(index):
        at = iota((LANES, total_slots), 0) + index * LANES
        spots = slot_table[0:1, :].astype(jnp.int32)
        value = jnp.where(spots == at, slot_table[1:2, :], 0.0) + jnp.where(spots + 1 == at, slot_table[2:3, :], 0.0)
        weave[rows_at(index * LANES, LANES), :] = value.astype(BF16)

    each(voxels // LANES, weave_step)
    gathers[0].wait_recv()
    gathers[5].start()
    gathers[1].wait_recv()
    gathers[6].start()
    gathers[3].wait_recv()
    gathers[7].start()
    gathers[4].wait_recv()
    gathers[8].start()
    load[5].wait()

    def power_step(index):
        at = rows_at(index * share, share)
        values = slices[at, :].astype(F32)
        total = 0.5 * jnp.sum(values * values, axis=1, keepdims=True)
        half_power[at, :] = jnp.broadcast_to(total, (share, LANES))

    chunk = 2 * LANES
    chunks = images_v.shape[0] // chunk

    def picks_of(score, pieces, numbers, value):
        for first, offset, size in pieces:
            block = score[offset : offset + size] - half_power[first : first + size, :]
            for group in range(size // 8):
                picked = jnp.take_along_axis(
                    block[group * 8 : (group + 1) * 8], numbers[0], axis=0, mode="promise_in_bounds"
                )
                value[0] = jnp.where(numbers[2] == first // 8 + group, picked, value[0])
                picked = jnp.take_along_axis(
                    block[group * 8 : (group + 1) * 8], numbers[1], axis=0, mode="promise_in_bounds"
                )
                value[1] = jnp.where(numbers[3] == first // 8 + group, picked, value[1])
        return value

    def score_chunk(index, table, pieces, resume):
        score = lax.dot_general(
            table, images_v[rows_at(index * chunk, chunk), :],
            (((1,), (1,)), ((), ())), preferred_element_type=F32,
        )
        for part in range(chunk // LANES):
            number = poses[:, rows_at(index * chunk + part * LANES, LANES)]
            numbers = [number[0:8] & 7, number[8:16] & 7, number[0:8] >> 3, number[8:16] >> 3]
            block = index * (chunk // LANES) + part
            if resume:
                value = [picks[block, 0:8], picks[block, 8:16]]
            else:
                value = [jnp.zeros((8, LANES), F32), jnp.zeros((8, LANES), F32)]
            value = picks_of(score[:, part * LANES : (part + 1) * LANES], pieces, numbers, value)
            picks[block] = jnp.concatenate(value, axis=0)

    def near_step(index):
        score_chunk(index, slices[share : NPOSE - share, :], [(share, 0, NPOSE - 2 * share)], False)

    gathers[2].wait_recv()
    gathers[7].wait_recv()
    gathers[8].wait_recv()
    each(members - 1, power_step, 1)
    each(chunks // 2, near_step)
    gathers[5].wait_recv()
    gathers[9].start()
    gathers[6].wait_recv()
    gathers[10].start()
    each(chunks, near_step, chunks // 2)
    gathers[9].wait_recv()
    gathers[10].wait_recv()
    power_step(0)
    power_step(members - 1)

    def far_chunk(index):
        table = jnp.concatenate([slices[0:share, :], slices[NPOSE - share : NPOSE, :]], axis=0)
        score_chunk(index, table, [(0, 0, share), (NPOSE - share, share, share)], True)

    def pick_send(peer):
        @pl.when(peer != own)
        def _():
            slab_copy(1, picks, picks_in, peer).start()

    def far_step(index):
        far_chunk(index)
        pick_send(2 * index)
        pick_send(2 * index + 1)

    each(chunks, far_step)
    picks_in[own] = picks[own]
    load[6].wait()
    row_weight[...] = jnp.zeros_like(row_weight)
    slab_arrivals(1, picks_in)
    total = picks_in[0]
    for block in range(1, slabs):
        total = total + picks_in[block]
    total = total * precision[:, rows_at(own * LANES, LANES)]
    exponent = jnp.exp(total - jnp.max(total, axis=0, keepdims=True))
    shares[own] = exponent / jnp.sum(exponent, axis=0, keepdims=True)
    ahead_of = slabs // 2
    turn = own // ahead_of
    for step in range(1, slabs):
        remote(
            shares.at[own], shares.at[own], slab_send.at[2], slab_recv.at[5 + turn], {"slab": slab_peer(step)}
        ).start()

    def shares_arrive(which):
        @pl.when(turn == which)
        def _():
            slab_whole(5 + which, shares, ahead_of - 1).wait_recv()

        @pl.when(turn != which)
        def _():
            slab_whole(5 + which, shares, ahead_of).wait_recv()

    tile = LANES

    def spread_chunk(block):
        at = rows_at(block * LANES, LANES)
        amount = (shares[block] * precision[:, at]).astype(BF16)
        number = poses[:, at].astype(jnp.int16)
        for first in range(0, NPOSE, tile):
            row = (iota((tile, LANES), 0) + first).astype(jnp.int16)
            value = jnp.zeros((tile, LANES), BF16)
            for k in range(cands):
                value = jnp.where(number[k : k + 1] == row, amount[k : k + 1], value)
            spread[first : first + tile, at] = value
            row_weight[first : first + tile, :] += value.astype(F32)

    stripe = 2 * LANES
    halves = 2
    wide = width // halves
    per_half = wide // stripe

    def away_copy(index):
        at = slice(index * stripe, (index + 1) * stripe)
        return img_copy(40 + index, away.at[:, at], away_in.at[:, at], partner)

    def back_stripe(index):
        at = slice(index * stripe, (index + 1) * stripe)
        part = partial[:, at] + dot(spread[:, early:], images_v[early:, at])
        away[:, at] = part[side:].astype(BF16)
        away_copy(index).start()
        kept[:, at] = part[:side]

    def columns_of(part):
        return slice(part * wide, (part + 1) * wide)

    def kept_part(index, part, first=0, size=share):
        here = index * share + first
        there = (ring_len - 1 - index) * share + first
        at = columns_of(part)
        return kept[here : here + size, at] + away_in[there : there + size, at].astype(F32)

    def ring_copy(part, index):
        at = columns_of(part)
        low, high = slice(0, half), slice(half, share)
        refs = [
            (opposite.at[low, at], opposite_in.at[low, at], right),
            (opposite.at[high, at], opposite_in.at[high, at], left),
            (ring.at[0, high, at], ring_in.at[0, high, at], right),
            (ring.at[1, low, at], ring_in.at[1, low, at], left),
            (ring.at[0, low, at], ring_in.at[0, low, at], right),
            (ring.at[1, high, at], ring_in.at[1, high, at], left),
        ]
        return img_copy(48 + 6 * part + index, *refs[index])

    def ring_start(part):
        at = columns_of(part)
        for index in range(part * per_half, (part + 1) * per_half):
            away_copy(index).wait_recv()
        opposite[:, at] = kept_part(FAR, part).astype(BF16)
        ring_copy(part, 0).start()
        ring_copy(part, 1).start()
        ring[0, half:share, at] = kept_part(RIGHT, part, half, half).astype(BF16)
        ring_copy(part, 2).start()
        ring[1, 0:half, at] = kept_part(LEFT, part, 0, half).astype(BF16)
        ring_copy(part, 3).start()

    def ring_relay(part):
        at = columns_of(part)
        ring_copy(part, 0).wait_recv()
        ring[0, 0:half, at] = (kept_part(RIGHT, part, 0, half) + opposite_in[0:half, at].astype(F32)).astype(BF16)
        ring_copy(part, 4).start()
        ring_copy(part, 1).wait_recv()
        ring[1, half:share, at] = (
            kept_part(LEFT, part, half, half) + opposite_in[half:share, at].astype(F32)
        ).astype(BF16)
        ring_copy(part, 5).start()

    unpack = jnp.where(pack_table[...].T[:, 0:1] == iota((mine, share), 1).astype(F32), 1.0, 0.0).astype(BF16)

    def ring_finish(part):
        at = columns_of(part)
        held = kept_part(HOME, part)
        for index in range(2, 6):
            ring_copy(part, index).wait_recv()
        summed = (held + ring_in[0, :, at].astype(F32) + ring_in[1, :, at].astype(F32)).astype(BF16)
        unpacked = dot(unpack, summed)
        for block in range(slabs):
            returning[part, block] = unpacked[block * deep : (block + 1) * deep].astype(BF16)
        slab_exchange(3 + part, returning.at[part], returned.at[part])
        returned[part, own] = returning[part, own]

    early = images_v.shape[0] // 2

    def early_stripe(index):
        at = rows_at(index * stripe, stripe)
        partial[:, at] = dot(spread[:, :early], images_v[:early, at])

    shares_arrive(0)
    each(ahead_of, spread_chunk)
    each(width // stripe, early_stripe)
    shares_arrive(1)
    each(slabs, spread_chunk, ahead_of)
    back_stripe(0)
    back_stripe(1)
    back_stripe(2)
    ring_start(0)
    back_stripe(3)
    ring_relay(0)
    ring_start(1)

    weight = jnp.sum(row_weight[...], axis=1, keepdims=True)
    mass_row = pick_row(iota((NPOSE, NPOSE), 0) == pose_row[0:1, :], weight)
    masses[member] = jnp.broadcast_to(mass_row, (8, NPOSE))

    def mass_copy(step):
        return img_copy(16, masses.at[member], masses.at[member], img_peer(step))

    def img_whole(slot, ref):
        blocks = ref.at[0 : members - 1]
        return img_copy(slot, blocks, blocks, img_peer(1))

    for step in range(1, members):
        mass_copy(step).start()
    ring_relay(1)
    ring_finish(0)
    ring_finish(1)
    for block in range(slabs):
        posterior[:, block * LANES : (block + 1) * LANES] = shares[block]

    img_whole(16, masses).wait_recv()
    mass_total = masses[0]
    for index in range(1, members):
        mass_total = mass_total + masses[index]
    lanes = iota((LANES, LANES), 1)
    mass_cols = []
    for block in range(members):
        key_col = slot_table[:, block * LANES : (block + 1) * LANES].T[:, 3:4]
        matched = key_col == iota((LANES, NPOSE), 1).astype(F32)
        amount = jnp.sum(jnp.where(matched, mass_total[0:1, :], 0.0), axis=1, keepdims=True)
        first = amount.astype(BF16).astype(F32)
        second = (amount - first).astype(BF16).astype(F32)
        third = amount - first - second
        mass_cols.append(
            jnp.where(lanes == 0, first, jnp.where(lanes == 1, second, jnp.where(lanes == 2, third, 0.0))).astype(BF16)
        )
    mass_table = jnp.concatenate(mass_cols, axis=0)

    def mass_step(index):
        at = rows_at(index * LANES, LANES)
        mass = jnp.sum(dot(weave[at, :], mass_table), axis=1, keepdims=True)
        inverse[at, :] = jnp.broadcast_to(1.0 / (mass + RIDGE), (LANES, LANES))

    each(voxels // LANES, mass_step)
    load[7].wait()
    load[8].wait()

    turned = jnp.zeros((mine, width), F32)
    for part in range(halves):
        slab_arrivals(3 + part, returned.at[part])
        gathered = jnp.concatenate([returned[part, block].astype(F32) for block in range(slabs)], axis=0)
        turned += dot(gathered.astype(BF16), columns_v[columns_of(part), :])
    for block in range(members):
        crossing[block] = turned[:, block * LANES : (block + 1) * LANES].astype(BF16)

    def cross_copy(step):
        peer = img_peer(step)
        return img_copy(17, crossing.at[peer], crossed.at[member], peer)

    for step in range(1, members):
        cross_copy(step).start()
    crossed[member] = crossing[member]

    for stage, ref in ((0, outgoing), (1, picks), (2, shares), (3, returning.at[0]), (4, returning.at[1])):
        slab_whole(stage, ref, slabs - 1).wait_send()
    for copy in gathers:
        copy.wait_send()
    for index in range(halves * per_half):
        away_copy(index).wait_send()
    for part in range(halves):
        for index in range(6):
            ring_copy(part, index).wait_send()
    img_whole(16, masses).wait_send()
    img_whole(17, crossed).wait_recv()

    voxel_rows = dot(weave[...], crossed[...].reshape(members * LANES, LANES)) * inverse[...]
    fourier = voxel_rows.astype(BF16)
    edge = density.shape[2]
    columns_out = density.shape[1]
    for plane in range(density.shape[0]):
        field = fourier[plane * edge : (plane + 1) * edge]
        real = dot(rows_v[:, :edge], field)
        imag = dot(rows_v[:, edge:], field)
        density[plane] = (real[:, :columns_out] + imag[:, columns_out:]).T
    img_whole(17, crossing).wait_send()


def per_device(images, volume, precision, candidates, slot_key, slot_voxel, slot_weight):
    members = lax.axis_size("img")
    slabs = lax.axis_size("slab")
    planes, edge, width = volume.shape
    particles, cands = candidates.shape
    cap = slot_key.shape[2]
    deep = cap // members
    share = NPOSE // members
    voxels = planes * edge
    mine = slabs * deep
    side = NPOSE // 2
    big = pl.BlockSpec(memory_space=pl.ANY)
    near = pl.BlockSpec(memory_space=pltpu.VMEM)
    scratch = [
        pltpu.VMEM((particles, width), BF16),
        pltpu.VMEM((voxels, width), BF16),
        pltpu.VMEM((width, width), BF16),
        pltpu.VMEM((edge, 2 * edge), BF16),
        pltpu.VMEM((1, particles), F32),
        pltpu.VMEM((cands, particles), jnp.int32),
        pltpu.VMEM(slot_key.shape, jnp.int32),
        pltpu.VMEM(slot_key.shape, jnp.int32),
        pltpu.VMEM(slot_key.shape, jnp.int32),
        pltpu.VMEM((8, slabs * cap), F32),
        pltpu.VMEM((8, mine), F32),
        pltpu.VMEM((8, NPOSE), jnp.int32),
        pltpu.VMEM((slabs, deep, width), BF16),
        pltpu.VMEM((slabs, deep, width), BF16),
        pltpu.VMEM((NPOSE, width), BF16),
        pltpu.VMEM((NPOSE, LANES), F32),
        pltpu.VMEM((voxels, slabs * cap), BF16),
        pltpu.VMEM((slabs, cands, LANES), F32),
        pltpu.VMEM((slabs, cands, LANES), F32),
        pltpu.VMEM((slabs, cands, LANES), F32),
        pltpu.VMEM((NPOSE, particles), BF16),
        pltpu.VMEM((NPOSE, LANES), F32),
        pltpu.VMEM((NPOSE, width), F32),
        pltpu.VMEM((side, width), BF16),
        pltpu.VMEM((side, width), BF16),
        pltpu.VMEM((side, width), F32),
        pltpu.VMEM((share, width), BF16),
        pltpu.VMEM((share, width), BF16),
        pltpu.VMEM((2, share, width), BF16),
        pltpu.VMEM((2, share, width), BF16),
        pltpu.VMEM((members, 8, NPOSE), F32),
        pltpu.VMEM((voxels, LANES), F32),
        pltpu.VMEM((2, slabs, deep, width // 2), BF16),
        pltpu.VMEM((2, slabs, deep, width // 2), BF16),
        pltpu.VMEM((members, mine, LANES), BF16),
        pltpu.VMEM((members, mine, LANES), BF16),
        pltpu.SemaphoreType.DMA((9,)),
        pltpu.SemaphoreType.DMA((7,)),
        pltpu.SemaphoreType.DMA((7,)),
        pltpu.SemaphoreType.DMA((60,)),
        pltpu.SemaphoreType.DMA((60,)),
    ]
    density, posterior = pl.pallas_call(
        functools.partial(kernel, slabs, members),
        out_shape=(
            jax.ShapeDtypeStruct((planes, edge // members, edge), F32),
            jax.ShapeDtypeStruct((cands, particles), F32),
        ),
        in_specs=[big] * 9,
        out_specs=(near, near),
        scratch_shapes=scratch,
        compiler_params=pltpu.CompilerParams(
            collective_id=0, has_side_effects=True, vmem_limit_bytes=56 * 1024 * 1024
        ),
    )(
        images, volume.reshape(voxels, width), column_table(edge, members), row_table(edge),
        precision[None, :], candidates.T, slot_key, slot_voxel, slot_weight,
    )
    return density.transpose(0, 2, 1), posterior.T


def solution(mesh):
    placed = (P("img", "slab"), P("slab", None, None), P("img"), P("img", None), P(), P(), P())
    return jax.shard_map(
        per_device,
        mesh=mesh,
        in_specs=placed,
        out_specs=(P("slab", None, "img"), P("img", None)),
        check_vma=False,
    )
```

```python
import functools
import math

import jax
import jax.numpy as jnp
import numpy as np
from jax import lax
from jax.experimental import pallas as pl
from jax.experimental.pallas import tpu as pltpu
from jax.sharding import PartitionSpec as P

NPOSE = 512
WSTEPS = 16
RIDGE = 0.25
LANES = 128
F32 = jnp.float32
BF16 = jnp.bfloat16


def gridding(samples):
    offset = (np.arange(samples) - samples / 2) / samples
    return 1.0 / np.sinc(offset) ** 2


def angles(length):
    counter = np.arange(length)
    return (counter[:, None] * counter[None, :] % length) * (2.0 * math.pi / length)


def column_table(length, members):
    turn = angles(length)
    cosine, sine = np.cos(turn), np.sin(turn)
    scale = gridding(length)[None, :]
    to_re = np.concatenate([cosine, -sine], axis=0) * scale
    to_im = np.concatenate([sine, cosine], axis=0) * scale
    width = length // members
    both = np.stack([to_re.reshape(-1, members, width), to_im.reshape(-1, members, width)], axis=2)
    return jnp.asarray(both.reshape(2 * length, 2 * length), BF16)


def row_table(length):
    turn = angles(length)
    scale = gridding(length)[:, None] / length
    return jnp.asarray(np.concatenate([np.cos(turn), -np.sin(turn)], axis=1) * scale, BF16)


def remote(src, dst, sends, recvs, device):
    return pltpu.make_async_remote_copy(
        src_ref=src,
        dst_ref=dst,
        send_sem=sends,
        recv_sem=recvs,
        device_id=device,
        device_id_type=pl.DeviceIdType.MESH,
    )


def dot(left, right):
    return jnp.dot(left, right, preferred_element_type=F32)


def each(count, step, first=0):
    def body(index, carry):
        step(index)
        return carry

    lax.fori_loop(first, count, body, 0)


def rows_at(start, size):
    return pl.ds(pl.multiple_of(start, size), size)


def iota(shape, axis):
    return lax.broadcasted_iota(jnp.int32, shape, axis)


def pick_row(mask, values):
    return jnp.sum(jnp.where(mask, values, 0.0), axis=0, keepdims=True)


def kernel(
    slabs, members,
    images, volume, columns, rows, precision_in, poses_in, keys_in, voxels_in, weights_in,
    density, posterior,
    images_v, volume_v, columns_v, rows_v, precision, poses, keys, voxel_of, weight_of,
    slot_table, pack_table, pose_row,
    outgoing, incoming, slices, half_power, scores, weave,
    picks, picks_in, shares, spread, row_weight, partial,
    away, away_in, kept, opposite, opposite_in, ring, ring_in,
    masses, inverse, returning, returned, crossing, crossed,
    loads, slab_send, slab_recv, img_send, img_recv,
):
    own = lax.axis_index("slab")
    member = lax.axis_index("img")
    ring_len = members // 2
    chip, core = member // 2, lax.rem(member, 2)
    share = NPOSE // members
    half = share // 2
    side = ring_len * share
    deep = outgoing.shape[2]
    mine = slabs * deep
    cap = keys.shape[2]
    width = volume_v.shape[1]
    voxels = volume_v.shape[0]
    cands = poses.shape[0]
    halves = 2
    wide = width // halves
    right = 2 * lax.rem(chip + 1, ring_len) + core
    left = 2 * lax.rem(chip + ring_len - 1, ring_len) + core
    partner = 2 * chip + 1 - core

    def slab_peer(step):
        return lax.rem(own + step, slabs)

    def img_peer(step):
        return lax.rem(member + step, members)

    barrier = pltpu.get_barrier_semaphore()

    def greet(axis, peer):
        pl.semaphore_signal(barrier, inc=1, device_id={axis: peer}, device_id_type=pl.DeviceIdType.MESH)

    sources = [keys_in, voxels_in, weights_in, volume, poses_in, images, precision_in, columns, rows]
    targets = [keys, voxel_of, weight_of, volume_v, poses, images_v, precision, columns_v, rows_v]
    load = [pltpu.make_async_copy(src, dst, loads.at[i]) for i, (src, dst) in enumerate(zip(sources, targets))]
    for index in range(5):
        load[index].start()
    for step in range(1, slabs):
        greet("slab", slab_peer(step))
    for step in range(1, members):
        greet("img", img_peer(step))

    for index in range(3):
        load[index].wait()
    before = jnp.zeros((slabs, cap), F32)
    for slab in range(slabs):
        before += jnp.where(keys[slab] >= 0, 1.0, 0.0) * jnp.where(own > slab, 1.0, 0.0)
    out_start = jnp.sum(before, axis=1, keepdims=True)
    total_slots = slabs * cap
    own_key = keys[own]
    own_code = voxel_of[own] * 32 + jnp.where(own_key >= 0, weight_of[own], 31)

    def ordered(first, count, tables):
        position = iota((1, count), 1) + first
        block_sel = iota((slabs, count), 0) == ((position >> 3) & (slabs - 1))
        start_row = pick_row(block_sel, out_start).astype(jnp.int32)
        slot_row = members * (position & 7) + (((position >> 7) - start_row) & 7)
        slot_sel = iota((cap, count), 0) == slot_row
        chooser = jnp.where(block_sel, 1.0, 0.0)
        found = []
        for table in tables:
            wide = lax.dot_general(
                table.astype(F32), chooser, (((0,), (0,)), ((), ())),
                precision=lax.Precision.HIGHEST, preferred_element_type=F32,
            )
            found.append(pick_row(slot_sel, wide))
        return found

    def decoded(code):
        code_row = code.astype(jnp.int32)
        level = code_row & 31
        alive = level <= WSTEPS
        spot = (code_row >> 5).astype(F32)
        lower = jnp.where(alive, level, 0).astype(F32) * (1.0 / WSTEPS)
        upper = jnp.where(alive, WSTEPS - level, 0).astype(F32) * (1.0 / WSTEPS)
        return spot, lower, upper

    parts = decoded(ordered(member * mine, mine, [own_code])[0])
    own_cols = jnp.concatenate(list(parts) + [jnp.zeros((5, mine), F32)], axis=0).T
    place = iota((mine, voxels), 1)
    spot = own_cols[:, 0:1].astype(jnp.int32)
    take = jnp.where(place == spot, own_cols[:, 1:2], 0.0) + jnp.where(place == spot + 1, own_cols[:, 2:3], 0.0)
    load[3].wait()
    for index in range(5, len(load)):
        load[index].start()
    def slab_copy(stage, src, dst, peer):
        return remote(src.at[peer], dst.at[own], slab_send.at[stage], slab_recv.at[stage], {"slab": peer})

    def slab_whole(stage, ref, count):
        blocks = ref.at[0:count]
        return remote(blocks, blocks, slab_send.at[stage], slab_recv.at[stage], {"slab": slab_peer(1)})

    def slab_exchange(stage, src, dst):
        for step in range(1, slabs):
            slab_copy(stage, src, dst, slab_peer(step)).start()

    def slab_arrivals(stage, dst):
        slab_whole(stage, dst, slabs - 1).wait_recv()

    def columns_of(part):
        return slice(part * wide, (part + 1) * wide)

    def img_copy(slot, src, dst, device):
        return remote(src, dst, img_send.at[slot], img_recv.at[slot], {"img": device})

    woven_by = take.astype(BF16)
    first_stage = [0, 7]
    for part in range(halves):
        woven = dot(woven_by, volume_v[:, columns_of(part)])
        for block in range(slabs):
            outgoing[part, block] = woven[block * deep : (block + 1) * deep].astype(BF16)
        if part == 0:
            pl.semaphore_wait(barrier, slabs - 1 + members - 1)
        slab_exchange(first_stage[part], outgoing.at[part], incoming.at[part])
        incoming[part, own] = outgoing[part, own]

    code, key_row = ordered(0, total_slots, [own_code, own_key])
    for index, value in enumerate(decoded(code) + (key_row,)):
        slot_table[index : index + 1, :] = value
    slot_table[4:8, :] = jnp.zeros((4, total_slots), F32)

    in_key = jnp.concatenate(
        [jnp.sum(jnp.where(iota((slabs, cap), 0) == own, keys[slab], 0), axis=0, keepdims=True) for slab in range(slabs)],
        axis=0,
    )
    live = jnp.where(in_key >= 0, 1.0, 0.0).astype(BF16)
    count = dot(live, jnp.ones((cap, LANES), BF16))
    earlier = jnp.where(iota((slabs, slabs), 1) < iota((slabs, slabs), 0), 1.0, 0.0).astype(BF16)
    start = dot(earlier, count.astype(BF16))
    lane = iota((1, mine), 1)
    slab_sel = iota((slabs, mine), 0) == (lane >> 3)
    in_start = pick_row(slab_sel, start).astype(jnp.int32)
    in_count = pick_row(slab_sel, count).astype(jnp.int32)
    slot = members * (lane & 7) + ((member - in_start) & 7)
    pack_row = jnp.where(slot < in_count, (in_start + slot) >> 3, -1)
    pack_table[...] = jnp.broadcast_to(pack_row, (8, mine)).astype(F32)

    number = start[:, :cap].astype(jnp.int32) + iota((slabs, cap), 1)
    holder = number & (members - 1)
    ahead = ((holder >> 1) - chip) & (ring_len - 1)
    near = jnp.where(ahead == 0, 3, jnp.where(ahead == 1, 1, jnp.where(ahead == 2, 0, 2)))
    row = jnp.where((holder & 1) == core, near, members - 1 - near) * share + (number >> 3)
    key_cols, row_cols = in_key.astype(F32).T, row.astype(F32).T
    pose_ids = iota((cap, NPOSE), 1).astype(F32)
    found_rows = jnp.zeros((cap, NPOSE), F32)
    for slab in range(slabs):
        found_rows += jnp.where(key_cols[:, slab : slab + 1] == pose_ids, row_cols[:, slab : slab + 1], 0.0)
    pose_row[...] = jnp.broadcast_to(jnp.sum(found_rows, axis=0, keepdims=True), (8, NPOSE)).astype(jnp.int32)

    load[4].wait()
    for part in range(poses.shape[1] // LANES):
        for k in range(0, cands, 8):
            at = (slice(k, k + 8), slice(part * LANES, (part + 1) * LANES))
            pose = poses[at]
            low, high = pose & (LANES - 1), pose >> 7
            renamed = jnp.zeros_like(pose)
            for piece in range(NPOSE // LANES):
                table = pose_row[:, piece * LANES : (piece + 1) * LANES]
                found = jnp.take_along_axis(table, low, axis=1, mode="promise_in_bounds")
                renamed = jnp.where(high == piece, found, renamed)
            poses[at] = renamed

    pack = jnp.where(iota((share, mine), 0).astype(F32) == pack_table[0:1, :], 1.0, 0.0).astype(BF16)

    FAR, RIGHT, LEFT, HOME = 0, 1, 2, 3

    def other(index):
        return members - 1 - index

    def gather_copy(part, index):
        at = columns_of(part)

        def block_of(block, first=0, size=share):
            return slices.at[block * share + first : block * share + first + size, at]

        def top(block):
            return block_of(block, 0, half)

        def bottom(block):
            return block_of(block, half, half)

        refs = [
            (top(HOME), top(LEFT), right),
            (bottom(HOME), bottom(RIGHT), left),
            (block_of(HOME), block_of(other(HOME)), partner),
            (bottom(HOME), bottom(LEFT), right),
            (top(HOME), top(RIGHT), left),
            (top(LEFT), top(FAR), right),
            (bottom(RIGHT), bottom(FAR), left),
            (block_of(LEFT), block_of(other(LEFT)), partner),
            (block_of(RIGHT), block_of(other(RIGHT)), partner),
            (top(FAR), top(other(FAR)), partner),
            (bottom(FAR), bottom(other(FAR)), partner),
        ]
        return img_copy(64 + 11 * part + index, *refs[index])

    def gather_start(part):
        slab_arrivals(first_stage[part], incoming.at[part])
        arrived = jnp.concatenate([incoming[part, block].astype(F32) for block in range(slabs)], axis=0)
        slices[HOME * share : (HOME + 1) * share, columns_of(part)] = dot(pack, arrived.astype(BF16)).astype(BF16)
        for index in range(5):
            gather_copy(part, index).start()

    def gather_near(part):
        for come, go in ((0, 5), (1, 6), (3, 7), (4, 8)):
            gather_copy(part, come).wait_recv()
            gather_copy(part, go).start()

    def gather_far(part):
        for come, go in ((5, 9), (6, 10)):
            gather_copy(part, come).wait_recv()
            gather_copy(part, go).start()

    def gather_end(part):
        for index in (2, 7, 8, 9, 10):
            gather_copy(part, index).wait_recv()

    def weave_step(index):
        at = iota((LANES, total_slots), 0) + index * LANES
        spots = slot_table[0:1, :].astype(jnp.int32)
        value = jnp.where(spots == at, slot_table[1:2, :], 0.0) + jnp.where(spots + 1 == at, slot_table[2:3, :], 0.0)
        weave[rows_at(index * LANES, LANES), :] = value.astype(BF16)

    each(voxels // LANES, weave_step)
    gather_start(0)
    gather_start(1)

    gather_near(0)
    gather_far(0)
    gather_near(1)
    load[5].wait()
    gather_end(0)

    chunk = 2 * LANES
    chunks = images_v.shape[0] // chunk

    def score_of(index, part):
        at = columns_of(part)
        return lax.dot_general(
            slices[:, at], images_v[rows_at(index * chunk, chunk), at],
            (((1,), (1,)), ((), ())), preferred_element_type=F32,
        )

    def first_step(index):
        scores[:, rows_at(index * chunk, chunk)] = score_of(index, 0)

    each(chunks // 2, first_step)
    gather_far(1)
    each(chunks, first_step, chunks // 2)
    gather_end(1)

    def power_step(index):
        at = rows_at(index * share, share)
        values = slices[at, :].astype(F32)
        total = 0.5 * jnp.sum(values * values, axis=1, keepdims=True)
        half_power[at, :] = jnp.broadcast_to(total, (share, LANES))

    each(members, power_step)

    def pick_chunk(index):
        score = score_of(index, 1)
        for piece in range(chunk // LANES):
            at = rows_at(index * chunk + piece * LANES, LANES)
            block = score[:, piece * LANES : (piece + 1) * LANES] + (scores[:, at] - half_power[...])
            number = poses[:, at]
            lows = [number[k : k + 8] & 7 for k in range(0, cands, 8)]
            highs = [number[k : k + 8] >> 3 for k in range(0, cands, 8)]
            value = [jnp.zeros((8, LANES), F32) for _ in lows]
            for group in range(NPOSE // 8):
                rows8 = block[group * 8 : (group + 1) * 8]
                for k, (low, high) in enumerate(zip(lows, highs)):
                    picked = jnp.take_along_axis(rows8, low, axis=0, mode="promise_in_bounds")
                    value[k] = jnp.where(high == group, picked, value[k])
            picks[index * (chunk // LANES) + piece] = jnp.concatenate(value, axis=0)

    def pick_send(peer):
        @pl.when(peer != own)
        def _():
            slab_copy(1, picks, picks_in, peer).start()

    def pick_step(index):
        pick_chunk(index)
        pick_send(2 * index)
        pick_send(2 * index + 1)

    each(chunks, pick_step)
    picks_in[own] = picks[own]
    load[6].wait()
    row_weight[...] = jnp.zeros_like(row_weight)
    masses[member] = jnp.zeros((8, LANES), F32)
    slab_arrivals(1, picks_in)
    total = picks_in[0]
    for block in range(1, slabs):
        total = total + picks_in[block]
    total = total * precision[:, rows_at(own * LANES, LANES)]
    exponent = jnp.exp(total - jnp.max(total, axis=0, keepdims=True))
    shares[own] = exponent / jnp.sum(exponent, axis=0, keepdims=True)
    ahead_of = slabs // 2
    turn = own // ahead_of
    for step in range(1, slabs):
        remote(
            shares.at[own], shares.at[own], slab_send.at[2], slab_recv.at[5 + turn], {"slab": slab_peer(step)}
        ).start()

    def shares_arrive(which):
        @pl.when(turn == which)
        def _():
            slab_whole(5 + which, shares, ahead_of - 1).wait_recv()

        @pl.when(turn != which)
        def _():
            slab_whole(5 + which, shares, ahead_of).wait_recv()

    tile = LANES

    def spread_chunk(block):
        at = rows_at(block * LANES, LANES)
        amount = (shares[block] * precision[:, at]).astype(BF16)
        number = poses[:, at].astype(jnp.int16)
        for first in range(0, NPOSE, tile):
            row = (iota((tile, LANES), 0) + first).astype(jnp.int16)
            value = jnp.zeros((tile, LANES), BF16)
            for k in range(cands):
                value = jnp.where(number[k : k + 1] == row, amount[k : k + 1], value)
            spread[first : first + tile, at] = value
            row_weight[first : first + tile, :] += value.astype(F32)

    stripe = 2 * LANES
    per_half = wide // stripe

    def away_copy(index):
        at = slice(index * stripe, (index + 1) * stripe)
        return img_copy(40 + index, away.at[:, at], away_in.at[:, at], partner)

    def back_stripe(index):
        at = slice(index * stripe, (index + 1) * stripe)
        part = partial[:, at] + dot(spread[:, early:], images_v[early:, at])
        away[:, at] = part[side:].astype(BF16)
        away_copy(index).start()
        kept[:, at] = part[:side]

    def kept_part(index, part, first=0, size=share):
        here = index * share + first
        there = (ring_len - 1 - index) * share + first
        at = columns_of(part)
        return kept[here : here + size, at] + away_in[there : there + size, at].astype(F32)

    def ring_copy(part, index):
        at = columns_of(part)
        low, high = slice(0, half), slice(half, share)
        refs = [
            (opposite.at[low, at], opposite_in.at[low, at], right),
            (opposite.at[high, at], opposite_in.at[high, at], left),
            (ring.at[0, high, at], ring_in.at[0, high, at], right),
            (ring.at[1, low, at], ring_in.at[1, low, at], left),
            (ring.at[0, low, at], ring_in.at[0, low, at], right),
            (ring.at[1, high, at], ring_in.at[1, high, at], left),
        ]
        return img_copy(48 + 6 * part + index, *refs[index])

    def ring_start(part):
        at = columns_of(part)
        for index in range(part * per_half, (part + 1) * per_half):
            away_copy(index).wait_recv()
        opposite[:, at] = kept_part(FAR, part).astype(BF16)
        ring_copy(part, 0).start()
        ring_copy(part, 1).start()
        ring[0, half:share, at] = kept_part(RIGHT, part, half, half).astype(BF16)
        ring_copy(part, 2).start()
        ring[1, 0:half, at] = kept_part(LEFT, part, 0, half).astype(BF16)
        ring_copy(part, 3).start()

    def ring_relay(part):
        at = columns_of(part)
        ring_copy(part, 0).wait_recv()
        ring[0, 0:half, at] = (kept_part(RIGHT, part, 0, half) + opposite_in[0:half, at].astype(F32)).astype(BF16)
        ring_copy(part, 4).start()
        ring_copy(part, 1).wait_recv()
        ring[1, half:share, at] = (
            kept_part(LEFT, part, half, half) + opposite_in[half:share, at].astype(F32)
        ).astype(BF16)
        ring_copy(part, 5).start()

    unpack = jnp.where(pack_table[...].T[:, 0:1] == iota((mine, share), 1).astype(F32), 1.0, 0.0).astype(BF16)

    def ring_finish(part):
        at = columns_of(part)
        held = kept_part(HOME, part)
        for index in range(2, 6):
            ring_copy(part, index).wait_recv()
        summed = (held + ring_in[0, :, at].astype(F32) + ring_in[1, :, at].astype(F32)).astype(BF16)
        unpacked = dot(unpack, summed)
        for block in range(slabs):
            returning[part, block] = unpacked[block * deep : (block + 1) * deep].astype(BF16)
        slab_exchange(3 + part, returning.at[part], returned.at[part])
        returned[part, own] = returning[part, own]

    early = images_v.shape[0] // 2

    def early_stripe(index):
        at = rows_at(index * stripe, stripe)
        partial[:, at] = dot(spread[:, :early], images_v[:early, at])

    shares_arrive(0)
    each(ahead_of, spread_chunk)
    each(width // stripe, early_stripe)
    shares_arrive(1)
    each(slabs, spread_chunk, ahead_of)

    weight = jnp.sum(row_weight[...], axis=1, keepdims=True)
    mass_row = pick_row(iota((NPOSE, NPOSE), 0) == pose_row[0:1, :], weight)
    for piece in range(NPOSE // LANES):
        masses[member, piece : piece + 1, :] = mass_row[:, piece * LANES : (piece + 1) * LANES]

    def mass_copy(step):
        return img_copy(16, masses.at[member], masses.at[member], img_peer(step))

    def img_whole(slot, ref):
        blocks = ref.at[0 : members - 1]
        return img_copy(slot, blocks, blocks, img_peer(1))

    for step in range(1, members):
        mass_copy(step).start()
    back_stripe(0)
    back_stripe(1)
    back_stripe(2)
    ring_start(0)
    back_stripe(3)
    ring_relay(0)
    ring_start(1)
    ring_relay(1)
    ring_finish(0)
    ring_finish(1)
    for block in range(slabs):
        posterior[:, block * LANES : (block + 1) * LANES] = shares[block]

    img_whole(16, masses).wait_recv()
    mass_sum = masses[0]
    for index in range(1, members):
        mass_sum = mass_sum + masses[index]
    mass_total = jnp.concatenate([mass_sum[piece : piece + 1] for piece in range(NPOSE // LANES)], axis=1)
    lanes = iota((LANES, LANES), 1)
    mass_cols = []
    for block in range(members):
        key_col = slot_table[:, block * LANES : (block + 1) * LANES].T[:, 3:4]
        matched = key_col == iota((LANES, NPOSE), 1).astype(F32)
        amount = jnp.sum(jnp.where(matched, mass_total, 0.0), axis=1, keepdims=True)
        first = amount.astype(BF16).astype(F32)
        second = (amount - first).astype(BF16).astype(F32)
        third = amount - first - second
        mass_cols.append(
            jnp.where(lanes == 0, first, jnp.where(lanes == 1, second, jnp.where(lanes == 2, third, 0.0))).astype(BF16)
        )
    mass_table = jnp.concatenate(mass_cols, axis=0)

    def mass_step(index):
        at = rows_at(index * LANES, LANES)
        mass = jnp.sum(dot(weave[at, :], mass_table), axis=1, keepdims=True)
        inverse[at, :] = jnp.broadcast_to(1.0 / (mass + RIDGE), (LANES, LANES))

    each(voxels // LANES, mass_step)
    load[7].wait()
    load[8].wait()

    turned = jnp.zeros((mine, width), F32)
    for part in range(halves):
        slab_arrivals(3 + part, returned.at[part])
        gathered = jnp.concatenate([returned[part, block].astype(F32) for block in range(slabs)], axis=0)
        turned += dot(gathered.astype(BF16), columns_v[columns_of(part), :])
    for block in range(members):
        crossing[block] = turned[:, block * LANES : (block + 1) * LANES].astype(BF16)

    def cross_copy(step):
        peer = img_peer(step)
        return img_copy(17, crossing.at[peer], crossed.at[member], peer)

    for step in range(1, members):
        cross_copy(step).start()
    crossed[member] = crossing[member]

    for stage, ref in ((0, outgoing.at[0]), (7, outgoing.at[1]), (1, picks), (2, shares), (3, returning.at[0]), (4, returning.at[1])):
        slab_whole(stage, ref, slabs - 1).wait_send()
    for part in range(halves):
        for index in range(11):
            gather_copy(part, index).wait_send()
    for index in range(halves * per_half):
        away_copy(index).wait_send()
    for part in range(halves):
        for index in range(6):
            ring_copy(part, index).wait_send()
    img_whole(16, masses).wait_send()
    img_whole(17, crossed).wait_recv()

    voxel_rows = dot(weave[...], crossed[...].reshape(members * LANES, LANES)) * inverse[...]
    fourier = voxel_rows.astype(BF16)
    edge = density.shape[2]
    columns_out = density.shape[1]
    for plane in range(density.shape[0]):
        field = fourier[plane * edge : (plane + 1) * edge]
        real = dot(rows_v[:, :edge], field)
        imag = dot(rows_v[:, edge:], field)
        density[plane] = (real[:, :columns_out] + imag[:, columns_out:]).T
    img_whole(17, crossing).wait_send()


def per_device(images, volume, precision, candidates, slot_key, slot_voxel, slot_weight):
    members = lax.axis_size("img")
    slabs = lax.axis_size("slab")
    planes, edge, width = volume.shape
    particles, cands = candidates.shape
    cap = slot_key.shape[2]
    deep = cap // members
    share = NPOSE // members
    voxels = planes * edge
    mine = slabs * deep
    side = NPOSE // 2
    big = pl.BlockSpec(memory_space=pl.ANY)
    near = pl.BlockSpec(memory_space=pltpu.VMEM)
    scratch = [
        pltpu.VMEM((particles, width), BF16),
        pltpu.VMEM((voxels, width), BF16),
        pltpu.VMEM((width, width), BF16),
        pltpu.VMEM((edge, 2 * edge), BF16),
        pltpu.VMEM((1, particles), F32),
        pltpu.VMEM((cands, particles), jnp.int32),
        pltpu.VMEM(slot_key.shape, jnp.int32),
        pltpu.VMEM(slot_key.shape, jnp.int32),
        pltpu.VMEM(slot_key.shape, jnp.int32),
        pltpu.VMEM((8, slabs * cap), F32),
        pltpu.VMEM((8, mine), F32),
        pltpu.VMEM((8, NPOSE), jnp.int32),
        pltpu.VMEM((2, slabs, deep, width // 2), BF16),
        pltpu.VMEM((2, slabs, deep, width // 2), BF16),
        pltpu.VMEM((NPOSE, width), BF16),
        pltpu.VMEM((NPOSE, LANES), F32),
        pltpu.VMEM((NPOSE, particles), F32),
        pltpu.VMEM((voxels, slabs * cap), BF16),
        pltpu.VMEM((slabs, cands, LANES), F32),
        pltpu.VMEM((slabs, cands, LANES), F32),
        pltpu.VMEM((slabs, cands, LANES), F32),
        pltpu.VMEM((NPOSE, particles), BF16),
        pltpu.VMEM((NPOSE, LANES), F32),
        pltpu.VMEM((NPOSE, width), F32),
        pltpu.VMEM((side, width), BF16),
        pltpu.VMEM((side, width), BF16),
        pltpu.VMEM((side, width), F32),
        pltpu.VMEM((share, width), BF16),
        pltpu.VMEM((share, width), BF16),
        pltpu.VMEM((2, share, width), BF16),
        pltpu.VMEM((2, share, width), BF16),
        pltpu.VMEM((members, 8, LANES), F32),
        pltpu.VMEM((voxels, LANES), F32),
        pltpu.VMEM((2, slabs, deep, width // 2), BF16),
        pltpu.VMEM((2, slabs, deep, width // 2), BF16),
        pltpu.VMEM((members, mine, LANES), BF16),
        pltpu.VMEM((members, mine, LANES), BF16),
        pltpu.SemaphoreType.DMA((9,)),
        pltpu.SemaphoreType.DMA((8,)),
        pltpu.SemaphoreType.DMA((8,)),
        pltpu.SemaphoreType.DMA((86,)),
        pltpu.SemaphoreType.DMA((86,)),
    ]
    density, posterior = pl.pallas_call(
        functools.partial(kernel, slabs, members),
        out_shape=(
            jax.ShapeDtypeStruct((planes, edge // members, edge), F32),
            jax.ShapeDtypeStruct((cands, particles), F32),
        ),
        in_specs=[big] * 9,
        out_specs=(near, near),
        scratch_shapes=scratch,
        compiler_params=pltpu.CompilerParams(
            collective_id=0, has_side_effects=True, vmem_limit_bytes=56 * 1024 * 1024
        ),
    )(
        images, volume.reshape(voxels, width), column_table(edge, members), row_table(edge),
        precision[None, :], candidates.T, slot_key, slot_voxel, slot_weight,
    )
    return density.transpose(0, 2, 1), posterior.T


def solution(mesh):
    placed = (P("img", "slab"), P("slab", None, None), P("img"), P("img", None), P(), P(), P())
    return jax.shard_map(
        per_device,
        mesh=mesh,
        in_specs=placed,
        out_specs=(P("slab", None, "img"), P("img", None)),
        check_vma=False,
    )
```

```python
import functools
import math

import jax
import jax.numpy as jnp
import numpy as np
from jax import lax
from jax.experimental import pallas as pl
from jax.experimental.pallas import tpu as pltpu
from jax.sharding import PartitionSpec as P

NPOSE = 512
WSTEPS = 16
RIDGE = 0.25
LANES = 128
F32 = jnp.float32
BF16 = jnp.bfloat16


def gridding(samples):
    offset = (np.arange(samples) - samples / 2) / samples
    return 1.0 / np.sinc(offset) ** 2


def angles(length):
    counter = np.arange(length)
    return (counter[:, None] * counter[None, :] % length) * (2.0 * math.pi / length)


def column_table(length, members):
    turn = angles(length)
    cosine, sine = np.cos(turn), np.sin(turn)
    scale = gridding(length)[None, :]
    to_re = np.concatenate([cosine, -sine], axis=0) * scale
    to_im = np.concatenate([sine, cosine], axis=0) * scale
    width = length // members
    both = np.stack([to_re.reshape(-1, members, width), to_im.reshape(-1, members, width)], axis=2)
    return jnp.asarray(both.reshape(2 * length, 2 * length), BF16)


def row_table(length):
    turn = angles(length)
    scale = gridding(length)[:, None] / length
    return jnp.asarray(np.concatenate([np.cos(turn), -np.sin(turn)], axis=1) * scale, BF16)


def remote(src, dst, sends, recvs, device):
    return pltpu.make_async_remote_copy(
        src_ref=src,
        dst_ref=dst,
        send_sem=sends,
        recv_sem=recvs,
        device_id=device,
        device_id_type=pl.DeviceIdType.MESH,
    )


def dot(left, right):
    return jnp.dot(left, right, preferred_element_type=F32)


def each(count, step, first=0):
    def body(index, carry):
        step(index)
        return carry

    lax.fori_loop(first, count, body, 0)


def rows_at(start, size):
    return pl.ds(pl.multiple_of(start, size), size)


def iota(shape, axis):
    return lax.broadcasted_iota(jnp.int32, shape, axis)


def pick_row(mask, values):
    return jnp.sum(jnp.where(mask, values, 0.0), axis=0, keepdims=True)


def kernel(
    slabs, members,
    images, volume, columns, rows, precision_in, poses_in, keys_in, voxels_in, weights_in,
    density, posterior,
    images_v, volume_v, columns_v, rows_v, precision, poses, keys, voxel_of, weight_of,
    slot_table, pack_table, pose_row,
    outgoing, incoming, slices, half_power, ranks, weave,
    picks, picks_in, shares, spread, row_weight, partial,
    away, away_in, kept, opposite, opposite_in, ring, ring_in,
    masses, inverse, returning, returned, crossing, crossed,
    loads, slab_send, slab_recv, img_send, img_recv,
):
    own = lax.axis_index("slab")
    member = lax.axis_index("img")
    ring_len = members // 2
    chip, core = member // 2, lax.rem(member, 2)
    share = NPOSE // members
    half = share // 2
    side = ring_len * share
    deep = outgoing.shape[1]
    mine = slabs * deep
    cap = keys.shape[2]
    width = volume_v.shape[1]
    voxels = volume_v.shape[0]
    cands = poses.shape[0]
    right = 2 * lax.rem(chip + 1, ring_len) + core
    left = 2 * lax.rem(chip + ring_len - 1, ring_len) + core
    partner = 2 * chip + 1 - core

    def slab_peer(step):
        return lax.rem(own + step, slabs)

    def img_peer(step):
        return lax.rem(member + step, members)

    barrier = pltpu.get_barrier_semaphore()

    def greet(axis, peer):
        pl.semaphore_signal(barrier, inc=1, device_id={axis: peer}, device_id_type=pl.DeviceIdType.MESH)

    sources = [keys_in, voxels_in, weights_in, volume, poses_in, images, precision_in, columns, rows]
    targets = [keys, voxel_of, weight_of, volume_v, poses, images_v, precision, columns_v, rows_v]
    load = [pltpu.make_async_copy(src, dst, loads.at[i]) for i, (src, dst) in enumerate(zip(sources, targets))]
    for index in range(5):
        load[index].start()
    for step in range(1, slabs):
        greet("slab", slab_peer(step))
    for step in range(1, members):
        greet("img", img_peer(step))

    for index in range(3):
        load[index].wait()
    before = jnp.zeros((slabs, cap), F32)
    for slab in range(slabs):
        before += jnp.where(keys[slab] >= 0, 1.0, 0.0) * jnp.where(own > slab, 1.0, 0.0)
    out_start = jnp.sum(before, axis=1, keepdims=True)
    total_slots = slabs * cap
    own_key = keys[own]
    own_code = voxel_of[own] * 32 + jnp.where(own_key >= 0, weight_of[own], 31)

    def ordered(first, count, tables):
        position = iota((1, count), 1) + first
        block_sel = iota((slabs, count), 0) == ((position >> 3) & (slabs - 1))
        start_row = pick_row(block_sel, out_start).astype(jnp.int32)
        slot_row = members * (position & 7) + (((position >> 7) - start_row) & 7)
        slot_sel = iota((cap, count), 0) == slot_row
        chooser = jnp.where(block_sel, 1.0, 0.0)
        found = []
        for table in tables:
            wide = lax.dot_general(
                table.astype(F32), chooser, (((0,), (0,)), ((), ())),
                precision=lax.Precision.HIGHEST, preferred_element_type=F32,
            )
            found.append(pick_row(slot_sel, wide))
        return found

    def decoded(code):
        code_row = code.astype(jnp.int32)
        level = code_row & 31
        alive = level <= WSTEPS
        spot = (code_row >> 5).astype(F32)
        lower = jnp.where(alive, level, 0).astype(F32) * (1.0 / WSTEPS)
        upper = jnp.where(alive, WSTEPS - level, 0).astype(F32) * (1.0 / WSTEPS)
        return spot, lower, upper

    parts = decoded(ordered(member * mine, mine, [own_code])[0])
    own_cols = jnp.concatenate(list(parts) + [jnp.zeros((5, mine), F32)], axis=0).T
    place = iota((mine, voxels), 1)
    spot = own_cols[:, 0:1].astype(jnp.int32)
    take = jnp.where(place == spot, own_cols[:, 1:2], 0.0) + jnp.where(place == spot + 1, own_cols[:, 2:3], 0.0)
    load[3].wait()
    for index in range(5, len(load)):
        load[index].start()
    woven = dot(take.astype(BF16), volume_v[...])
    for block in range(slabs):
        outgoing[block] = woven[block * deep : (block + 1) * deep].astype(BF16)
    pl.semaphore_wait(barrier, slabs - 1 + members - 1)

    def slab_copy(stage, src, dst, peer):
        return remote(src.at[peer], dst.at[own], slab_send.at[stage], slab_recv.at[stage], {"slab": peer})

    def slab_whole(stage, ref, count):
        blocks = ref.at[0:count]
        return remote(blocks, blocks, slab_send.at[stage], slab_recv.at[stage], {"slab": slab_peer(1)})

    def slab_exchange(stage, src, dst):
        for step in range(1, slabs):
            slab_copy(stage, src, dst, slab_peer(step)).start()

    def slab_arrivals(stage, dst):
        slab_whole(stage, dst, slabs - 1).wait_recv()

    def img_copy(slot, src, dst, device):
        return remote(src, dst, img_send.at[slot], img_recv.at[slot], {"img": device})

    slab_exchange(0, outgoing, incoming)
    incoming[own] = outgoing[own]

    code, key_row = ordered(0, total_slots, [own_code, own_key])
    for index, value in enumerate(decoded(code) + (key_row,)):
        slot_table[index : index + 1, :] = value
    slot_table[4:8, :] = jnp.zeros((4, total_slots), F32)

    in_key = jnp.concatenate(
        [jnp.sum(jnp.where(iota((slabs, cap), 0) == own, keys[slab], 0), axis=0, keepdims=True) for slab in range(slabs)],
        axis=0,
    )
    live = jnp.where(in_key >= 0, 1.0, 0.0).astype(BF16)
    count = dot(live, jnp.ones((cap, LANES), BF16))
    earlier = jnp.where(iota((slabs, slabs), 1) < iota((slabs, slabs), 0), 1.0, 0.0).astype(BF16)
    start = dot(earlier, count.astype(BF16))
    lane = iota((1, mine), 1)
    slab_sel = iota((slabs, mine), 0) == (lane >> 3)
    in_start = pick_row(slab_sel, start).astype(jnp.int32)
    in_count = pick_row(slab_sel, count).astype(jnp.int32)
    slot = members * (lane & 7) + ((member - in_start) & 7)
    pack_row = jnp.where(slot < in_count, (in_start + slot) >> 3, -1)
    pack_table[...] = jnp.broadcast_to(pack_row, (8, mine)).astype(F32)

    number = start[:, :cap].astype(jnp.int32) + iota((slabs, cap), 1)
    holder = number & (members - 1)
    ahead = ((holder >> 1) - chip) & (ring_len - 1)
    near = jnp.where(ahead == 0, 3, jnp.where(ahead == 1, 1, jnp.where(ahead == 2, 0, 2)))
    row = jnp.where((holder & 1) == core, near, members - 1 - near) * share + (number >> 3)
    key_cols, row_cols = in_key.astype(F32).T, row.astype(F32).T
    pose_ids = iota((cap, NPOSE), 1).astype(F32)
    found_rows = jnp.zeros((cap, NPOSE), F32)
    for slab in range(slabs):
        found_rows += jnp.where(key_cols[:, slab : slab + 1] == pose_ids, row_cols[:, slab : slab + 1], 0.0)
    pose_row[...] = jnp.broadcast_to(jnp.sum(found_rows, axis=0, keepdims=True), (8, NPOSE)).astype(jnp.int32)

    load[4].wait()
    for part in range(poses.shape[1] // LANES):
        for k in range(0, cands, 8):
            at = (slice(k, k + 8), slice(part * LANES, (part + 1) * LANES))
            pose = poses[at]
            low, high = pose & (LANES - 1), pose >> 7
            renamed = jnp.zeros_like(pose)
            for piece in range(NPOSE // LANES):
                table = pose_row[:, piece * LANES : (piece + 1) * LANES]
                found = jnp.take_along_axis(table, low, axis=1, mode="promise_in_bounds")
                renamed = jnp.where(high == piece, found, renamed)
            poses[at] = renamed

    ahead_of = slabs // 2
    turn = own // ahead_of

    def rank_chunk(block):
        at = rows_at(block * LANES, LANES)
        number = poses[:, at].astype(jnp.int16)
        for first in range(0, NPOSE, LANES):
            row = (iota((LANES, LANES), 0) + first).astype(jnp.int16)
            value = jnp.full((LANES, LANES), cands, jnp.int16)
            for k in range(cands):
                value = jnp.where(number[k : k + 1] == row, jnp.int16(k), value)
            ranks[first : first + LANES, at] = value.astype(jnp.int32)

    each(slabs, rank_chunk, ahead_of)

    slab_arrivals(0, incoming)
    arrived = jnp.concatenate([incoming[block].astype(F32) for block in range(slabs)], axis=0).astype(BF16)
    pack = jnp.where(iota((share, mine), 0).astype(F32) == pack_table[0:1, :], 1.0, 0.0).astype(BF16)

    def block_of(index, first=0, size=share):
        return slices.at[index * share + first : index * share + first + size]

    FAR, RIGHT, LEFT, HOME = 0, 1, 2, 3
    slices[HOME * share : (HOME + 1) * share, :] = dot(pack, arrived).astype(BF16)

    def other(index):
        return members - 1 - index

    def top(index):
        return block_of(index, 0, half)

    def bottom(index):
        return block_of(index, half, half)

    gathers = [
        img_copy(0, top(HOME), top(LEFT), right),
        img_copy(1, bottom(HOME), bottom(RIGHT), left),
        img_copy(2, block_of(HOME), block_of(other(HOME)), partner),
        img_copy(3, bottom(HOME), bottom(LEFT), right),
        img_copy(4, top(HOME), top(RIGHT), left),
        img_copy(5, top(LEFT), top(FAR), right),
        img_copy(6, bottom(RIGHT), bottom(FAR), left),
        img_copy(7, block_of(LEFT), block_of(other(LEFT)), partner),
        img_copy(8, block_of(RIGHT), block_of(other(RIGHT)), partner),
        img_copy(9, top(FAR), top(other(FAR)), partner),
        img_copy(10, bottom(FAR), bottom(other(FAR)), partner),
    ]
    for index in range(5):
        gathers[index].start()

    def weave_step(index):
        at = iota((LANES, total_slots), 0) + index * LANES
        spots = slot_table[0:1, :].astype(jnp.int32)
        value = jnp.where(spots == at, slot_table[1:2, :], 0.0) + jnp.where(spots + 1 == at, slot_table[2:3, :], 0.0)
        weave[rows_at(index * LANES, LANES), :] = value.astype(BF16)

    each(voxels // LANES, weave_step)
    gathers[0].wait_recv()
    gathers[5].start()
    gathers[1].wait_recv()
    gathers[6].start()
    gathers[3].wait_recv()
    gathers[7].start()
    gathers[4].wait_recv()
    gathers[8].start()
    load[5].wait()

    def power_step(index):
        at = rows_at(index * share, share)
        values = slices[at, :].astype(F32)
        total = 0.5 * jnp.sum(values * values, axis=1, keepdims=True)
        half_power[at, :] = jnp.broadcast_to(total, (share, LANES))

    chunk = 2 * LANES
    chunks = images_v.shape[0] // chunk

    def picks_of(score, pieces, numbers, value):
        for first, offset, size in pieces:
            block = score[offset : offset + size] - half_power[first : first + size, :]
            for group in range(size // 8):
                picked = jnp.take_along_axis(
                    block[group * 8 : (group + 1) * 8], numbers[0], axis=0, mode="promise_in_bounds"
                )
                value[0] = jnp.where(numbers[2] == first // 8 + group, picked, value[0])
                picked = jnp.take_along_axis(
                    block[group * 8 : (group + 1) * 8], numbers[1], axis=0, mode="promise_in_bounds"
                )
                value[1] = jnp.where(numbers[3] == first // 8 + group, picked, value[1])
        return value

    def score_chunk(index, table, pieces, resume):
        score = lax.dot_general(
            table, images_v[rows_at(index * chunk, chunk), :],
            (((1,), (1,)), ((), ())), preferred_element_type=F32,
        )
        for part in range(chunk // LANES):
            number = poses[:, rows_at(index * chunk + part * LANES, LANES)]
            numbers = [number[0:8] & 7, number[8:16] & 7, number[0:8] >> 3, number[8:16] >> 3]
            block = index * (chunk // LANES) + part
            if resume:
                value = [picks[block, 0:8], picks[block, 8:16]]
            else:
                value = [jnp.zeros((8, LANES), F32), jnp.zeros((8, LANES), F32)]
            value = picks_of(score[:, part * LANES : (part + 1) * LANES], pieces, numbers, value)
            picks[block] = jnp.concatenate(value, axis=0)

    def near_step(index):
        score_chunk(index, slices[share : NPOSE - share, :], [(share, 0, NPOSE - 2 * share)], False)

    gathers[2].wait_recv()
    gathers[7].wait_recv()
    gathers[8].wait_recv()
    each(members - 1, power_step, 1)
    each(chunks // 2, near_step)
    gathers[5].wait_recv()
    gathers[9].start()
    gathers[6].wait_recv()
    gathers[10].start()
    each(chunks, near_step, chunks // 2)
    gathers[9].wait_recv()
    gathers[10].wait_recv()
    power_step(0)
    power_step(members - 1)

    def far_chunk(index):
        table = jnp.concatenate([slices[0:share, :], slices[NPOSE - share : NPOSE, :]], axis=0)
        score_chunk(index, table, [(0, 0, share), (NPOSE - share, share, share)], True)

    def pick_send(peer):
        @pl.when(peer != own)
        def _():
            slab_copy(1, picks, picks_in, peer).start()

    def far_step(index):
        far_chunk(index)
        pick_send(2 * index)
        pick_send(2 * index + 1)

    each(chunks, far_step)
    picks_in[own] = picks[own]
    load[6].wait()
    row_weight[...] = jnp.zeros_like(row_weight)
    masses[member] = jnp.zeros((8, LANES), F32)

    def share_out():
        slab_arrivals(1, picks_in)
        total = picks_in[0]
        for block in range(1, slabs):
            total = total + picks_in[block]
        total = total * precision[:, rows_at(own * LANES, LANES)]
        exponent = jnp.exp(total - jnp.max(total, axis=0, keepdims=True))
        shares[own] = exponent / jnp.sum(exponent, axis=0, keepdims=True)
        for step in range(1, slabs):
            remote(
                shares.at[own], shares.at[own], slab_send.at[2], slab_recv.at[5 + turn], {"slab": slab_peer(step)}
            ).start()

    @pl.when(turn == 0)
    def _():
        share_out()

    each(ahead_of, rank_chunk)

    @pl.when(turn != 0)
    def _():
        share_out()

    def shares_arrive(which):
        @pl.when(turn == which)
        def _():
            slab_whole(5 + which, shares, ahead_of - 1).wait_recv()

        @pl.when(turn != which)
        def _():
            slab_whole(5 + which, shares, ahead_of).wait_recv()

    def spread_chunk(block):
        at = rows_at(block * LANES, LANES)
        amount = shares[block] * precision[:, at]
        rounded = amount.astype(BF16).astype(F32)
        low, high = rounded[0:8], rounded[8:16]
        for first in range(0, NPOSE, 16):
            values = []
            for group in (first, first + 8):
                rank = ranks[group : group + 8, at]
                place = rank & 7
                from_low = jnp.take_along_axis(low, place, axis=0, mode="promise_in_bounds")
                from_high = jnp.take_along_axis(high, place, axis=0, mode="promise_in_bounds")
                value = jnp.where(rank < 8, from_low, jnp.where(rank < cands, from_high, 0.0))
                row_weight[group : group + 8, :] += value
                values.append(value)
            spread[first : first + 16, at] = jnp.concatenate(values, axis=0).astype(BF16)

    stripe = 2 * LANES
    halves = 1
    wide = width // halves
    per_half = wide // stripe

    def away_copy(index):
        at = slice(index * stripe, (index + 1) * stripe)
        return img_copy(40 + index, away.at[:, at], away_in.at[:, at], partner)

    def back_stripe(index):
        at = slice(index * stripe, (index + 1) * stripe)
        part = partial[:, at] + dot(spread[:, early:], images_v[early:, at])
        away[:, at] = part[side:].astype(BF16)
        away_copy(index).start()
        kept[:, at] = part[:side]

    def columns_of(part):
        return slice(part * wide, (part + 1) * wide)

    def kept_part(index, part, first=0, size=share):
        here = index * share + first
        there = (ring_len - 1 - index) * share + first
        at = columns_of(part)
        return kept[here : here + size, at] + away_in[there : there + size, at].astype(F32)

    def ring_copy(part, index):
        at = columns_of(part)
        low, high = slice(0, half), slice(half, share)
        refs = [
            (opposite.at[low, at], opposite_in.at[low, at], right),
            (opposite.at[high, at], opposite_in.at[high, at], left),
            (ring.at[0, high, at], ring_in.at[0, high, at], right),
            (ring.at[1, low, at], ring_in.at[1, low, at], left),
            (ring.at[0, low, at], ring_in.at[0, low, at], right),
            (ring.at[1, high, at], ring_in.at[1, high, at], left),
        ]
        return img_copy(48 + 6 * part + index, *refs[index])

    def ring_start(part):
        at = columns_of(part)
        for index in range(part * per_half, (part + 1) * per_half):
            away_copy(index).wait_recv()
        opposite[:, at] = kept_part(FAR, part).astype(BF16)
        ring_copy(part, 0).start()
        ring_copy(part, 1).start()
        ring[0, half:share, at] = kept_part(RIGHT, part, half, half).astype(BF16)
        ring_copy(part, 2).start()
        ring[1, 0:half, at] = kept_part(LEFT, part, 0, half).astype(BF16)
        ring_copy(part, 3).start()

    def ring_relay(part):
        at = columns_of(part)
        ring_copy(part, 0).wait_recv()
        ring[0, 0:half, at] = (kept_part(RIGHT, part, 0, half) + opposite_in[0:half, at].astype(F32)).astype(BF16)
        ring_copy(part, 4).start()
        ring_copy(part, 1).wait_recv()
        ring[1, half:share, at] = (
            kept_part(LEFT, part, half, half) + opposite_in[half:share, at].astype(F32)
        ).astype(BF16)
        ring_copy(part, 5).start()

    unpack = jnp.where(pack_table[...].T[:, 0:1] == iota((mine, share), 1).astype(F32), 1.0, 0.0).astype(BF16)

    def ring_finish(part):
        at = columns_of(part)
        held = kept_part(HOME, part)
        for index in range(2, 6):
            ring_copy(part, index).wait_recv()
        summed = (held + ring_in[0, :, at].astype(F32) + ring_in[1, :, at].astype(F32)).astype(BF16)
        unpacked = dot(unpack, summed)
        for block in range(slabs):
            returning[part, block] = unpacked[block * deep : (block + 1) * deep].astype(BF16)
        slab_exchange(3 + part, returning.at[part], returned.at[part])
        returned[part, own] = returning[part, own]

    early = images_v.shape[0] // 2

    def early_stripe(index):
        at = rows_at(index * stripe, stripe)
        partial[:, at] = dot(spread[:, :early], images_v[:early, at])

    shares_arrive(0)
    each(ahead_of, spread_chunk)
    each(width // stripe, early_stripe)
    shares_arrive(1)
    each(slabs, spread_chunk, ahead_of)

    weight = jnp.sum(row_weight[...], axis=1, keepdims=True)
    mass_row = pick_row(iota((NPOSE, NPOSE), 0) == pose_row[0:1, :], weight)
    for piece in range(NPOSE // LANES):
        masses[member, piece : piece + 1, :] = mass_row[:, piece * LANES : (piece + 1) * LANES]

    def mass_copy(step):
        return img_copy(16, masses.at[member], masses.at[member], img_peer(step))

    def img_whole(slot, ref):
        blocks = ref.at[0 : members - 1]
        return img_copy(slot, blocks, blocks, img_peer(1))

    for step in range(1, members):
        mass_copy(step).start()
    for index in range(width // stripe):
        back_stripe(index)
    ring_start(0)
    ring_relay(0)
    ring_finish(0)
    for block in range(slabs):
        posterior[:, block * LANES : (block + 1) * LANES] = shares[block]

    img_whole(16, masses).wait_recv()
    mass_sum = masses[0]
    for index in range(1, members):
        mass_sum = mass_sum + masses[index]
    mass_total = jnp.concatenate([mass_sum[piece : piece + 1] for piece in range(NPOSE // LANES)], axis=1)
    lanes = iota((LANES, LANES), 1)
    mass_cols = []
    for block in range(members):
        key_col = slot_table[:, block * LANES : (block + 1) * LANES].T[:, 3:4]
        matched = key_col == iota((LANES, NPOSE), 1).astype(F32)
        amount = jnp.sum(jnp.where(matched, mass_total, 0.0), axis=1, keepdims=True)
        first = amount.astype(BF16).astype(F32)
        second = (amount - first).astype(BF16).astype(F32)
        third = amount - first - second
        mass_cols.append(
            jnp.where(lanes == 0, first, jnp.where(lanes == 1, second, jnp.where(lanes == 2, third, 0.0))).astype(BF16)
        )
    mass_table = jnp.concatenate(mass_cols, axis=0)

    def mass_step(index):
        at = rows_at(index * LANES, LANES)
        mass = jnp.sum(dot(weave[at, :], mass_table), axis=1, keepdims=True)
        inverse[at, :] = jnp.broadcast_to(1.0 / (mass + RIDGE), (LANES, LANES))

    each(voxels // LANES, mass_step)
    load[7].wait()
    load[8].wait()

    turned = jnp.zeros((mine, width), F32)
    for part in range(halves):
        slab_arrivals(3 + part, returned.at[part])
        gathered = jnp.concatenate([returned[part, block].astype(F32) for block in range(slabs)], axis=0)
        turned += dot(gathered.astype(BF16), columns_v[columns_of(part), :])
    for block in range(members):
        crossing[block] = turned[:, block * LANES : (block + 1) * LANES].astype(BF16)

    def cross_copy(step):
        peer = img_peer(step)
        return img_copy(17, crossing.at[peer], crossed.at[member], peer)

    for step in range(1, members):
        cross_copy(step).start()
    crossed[member] = crossing[member]

    for stage, ref in ((0, outgoing), (1, picks), (2, shares), (3, returning.at[0])):
        slab_whole(stage, ref, slabs - 1).wait_send()
    for copy in gathers:
        copy.wait_send()
    for index in range(halves * per_half):
        away_copy(index).wait_send()
    for part in range(halves):
        for index in range(6):
            ring_copy(part, index).wait_send()
    img_whole(16, masses).wait_send()
    img_whole(17, crossed).wait_recv()

    voxel_rows = dot(weave[...], crossed[...].reshape(members * LANES, LANES)) * inverse[...]
    fourier = voxel_rows.astype(BF16)
    edge = density.shape[2]
    columns_out = density.shape[1]
    for plane in range(density.shape[0]):
        field = fourier[plane * edge : (plane + 1) * edge]
        real = dot(rows_v[:, :edge], field)
        imag = dot(rows_v[:, edge:], field)
        density[plane] = (real[:, :columns_out] + imag[:, columns_out:]).T
    img_whole(17, crossing).wait_send()


def per_device(images, volume, precision, candidates, slot_key, slot_voxel, slot_weight):
    members = lax.axis_size("img")
    slabs = lax.axis_size("slab")
    planes, edge, width = volume.shape
    particles, cands = candidates.shape
    cap = slot_key.shape[2]
    deep = cap // members
    share = NPOSE // members
    voxels = planes * edge
    mine = slabs * deep
    side = NPOSE // 2
    big = pl.BlockSpec(memory_space=pl.ANY)
    near = pl.BlockSpec(memory_space=pltpu.VMEM)
    scratch = [
        pltpu.VMEM((particles, width), BF16),
        pltpu.VMEM((voxels, width), BF16),
        pltpu.VMEM((width, width), BF16),
        pltpu.VMEM((edge, 2 * edge), BF16),
        pltpu.VMEM((1, particles), F32),
        pltpu.VMEM((cands, particles), jnp.int32),
        pltpu.VMEM(slot_key.shape, jnp.int32),
        pltpu.VMEM(slot_key.shape, jnp.int32),
        pltpu.VMEM(slot_key.shape, jnp.int32),
        pltpu.VMEM((8, slabs * cap), F32),
        pltpu.VMEM((8, mine), F32),
        pltpu.VMEM((8, NPOSE), jnp.int32),
        pltpu.VMEM((slabs, deep, width), BF16),
        pltpu.VMEM((slabs, deep, width), BF16),
        pltpu.VMEM((NPOSE, width), BF16),
        pltpu.VMEM((NPOSE, LANES), F32),
        pltpu.VMEM((NPOSE, particles), jnp.int32),
        pltpu.VMEM((voxels, slabs * cap), BF16),
        pltpu.VMEM((slabs, cands, LANES), F32),
        pltpu.VMEM((slabs, cands, LANES), F32),
        pltpu.VMEM((slabs, cands, LANES), F32),
        pltpu.VMEM((NPOSE, particles), BF16),
        pltpu.VMEM((NPOSE, LANES), F32),
        pltpu.VMEM((NPOSE, width), F32),
        pltpu.VMEM((side, width), BF16),
        pltpu.VMEM((side, width), BF16),
        pltpu.VMEM((side, width), F32),
        pltpu.VMEM((share, width), BF16),
        pltpu.VMEM((share, width), BF16),
        pltpu.VMEM((2, share, width), BF16),
        pltpu.VMEM((2, share, width), BF16),
        pltpu.VMEM((members, 8, LANES), F32),
        pltpu.VMEM((voxels, LANES), F32),
        pltpu.VMEM((1, slabs, deep, width), BF16),
        pltpu.VMEM((1, slabs, deep, width), BF16),
        pltpu.VMEM((members, mine, LANES), BF16),
        pltpu.VMEM((members, mine, LANES), BF16),
        pltpu.SemaphoreType.DMA((9,)),
        pltpu.SemaphoreType.DMA((7,)),
        pltpu.SemaphoreType.DMA((7,)),
        pltpu.SemaphoreType.DMA((60,)),
        pltpu.SemaphoreType.DMA((60,)),
    ]
    density, posterior = pl.pallas_call(
        functools.partial(kernel, slabs, members),
        out_shape=(
            jax.ShapeDtypeStruct((planes, edge // members, edge), F32),
            jax.ShapeDtypeStruct((cands, particles), F32),
        ),
        in_specs=[big] * 9,
        out_specs=(near, near),
        scratch_shapes=scratch,
        compiler_params=pltpu.CompilerParams(
            collective_id=0, has_side_effects=True, vmem_limit_bytes=56 * 1024 * 1024
        ),
    )(
        images, volume.reshape(voxels, width), column_table(edge, members), row_table(edge),
        precision[None, :], candidates.T, slot_key, slot_voxel, slot_weight,
    )
    return density.transpose(0, 2, 1), posterior.T


def solution(mesh):
    placed = (P("img", "slab"), P("slab", None, None), P("img"), P("img", None), P(), P(), P())
    return jax.shard_map(
        per_device,
        mesh=mesh,
        in_specs=placed,
        out_specs=(P("slab", None, "img"), P("img", None)),
        check_vma=False,
    )
```

```python
import functools
import math

import jax
import jax.numpy as jnp
import numpy as np
from jax import lax
from jax.experimental import pallas as pl
from jax.experimental.pallas import tpu as pltpu
from jax.sharding import PartitionSpec as P

NPOSE = 512
WSTEPS = 16
RIDGE = 0.25
LANES = 128
F32 = jnp.float32
BF16 = jnp.bfloat16


def gridding(samples):
    offset = (np.arange(samples) - samples / 2) / samples
    return 1.0 / np.sinc(offset) ** 2


def angles(length):
    counter = np.arange(length)
    return (counter[:, None] * counter[None, :] % length) * (2.0 * math.pi / length)


def column_table(length, members):
    turn = angles(length)
    cosine, sine = np.cos(turn), np.sin(turn)
    scale = gridding(length)[None, :]
    to_re = np.concatenate([cosine, -sine], axis=0) * scale
    to_im = np.concatenate([sine, cosine], axis=0) * scale
    width = length // members
    both = np.stack([to_re.reshape(-1, members, width), to_im.reshape(-1, members, width)], axis=2)
    return jnp.asarray(both.reshape(2 * length, 2 * length), BF16)


def row_table(length):
    turn = angles(length)
    scale = gridding(length)[:, None] / length
    return jnp.asarray(np.concatenate([np.cos(turn), -np.sin(turn)], axis=1) * scale, BF16)


def remote(src, dst, sends, recvs, device):
    return pltpu.make_async_remote_copy(
        src_ref=src,
        dst_ref=dst,
        send_sem=sends,
        recv_sem=recvs,
        device_id=device,
        device_id_type=pl.DeviceIdType.MESH,
    )


def dot(left, right):
    return jnp.dot(left, right, preferred_element_type=F32)


def each(count, step, first=0):
    def body(index, carry):
        step(index)
        return carry

    lax.fori_loop(first, count, body, 0)


def rows_at(start, size):
    return pl.ds(pl.multiple_of(start, size), size)


def iota(shape, axis):
    return lax.broadcasted_iota(jnp.int32, shape, axis)


def pick_row(mask, values):
    return jnp.sum(jnp.where(mask, values, 0.0), axis=0, keepdims=True)


def kernel(
    slabs, members,
    images, volume, columns, rows, precision_in, poses_in, keys_in, voxels_in, weights_in,
    density, posterior,
    images_v, volume_v, columns_v, rows_v, precision, poses, keys, voxel_of, weight_of,
    slot_table, pack_table, pose_row,
    outgoing, incoming, slices, half_power, ranks, weave,
    picks, picks_in, shares, spread, row_weight, partial,
    away, away_in, kept, opposite, opposite_in, ring, ring_in,
    masses, inverse, returning, returned, crossing, crossed,
    loads, slab_send, slab_recv, img_send, img_recv,
):
    own = lax.axis_index("slab")
    member = lax.axis_index("img")
    ring_len = members // 2
    chip, core = member // 2, lax.rem(member, 2)
    share = NPOSE // members
    half = share // 2
    side = ring_len * share
    deep = outgoing.shape[1]
    mine = slabs * deep
    cap = keys.shape[2]
    width = volume_v.shape[1]
    voxels = volume_v.shape[0]
    cands = poses.shape[0]
    right = 2 * lax.rem(chip + 1, ring_len) + core
    left = 2 * lax.rem(chip + ring_len - 1, ring_len) + core
    partner = 2 * chip + 1 - core

    def slab_peer(step):
        return lax.rem(own + step, slabs)

    def img_peer(step):
        return lax.rem(member + step, members)

    barrier = pltpu.get_barrier_semaphore()

    def greet(axis, peer):
        pl.semaphore_signal(barrier, inc=1, device_id={axis: peer}, device_id_type=pl.DeviceIdType.MESH)

    sources = [keys_in, voxels_in, weights_in, volume, poses_in, images, precision_in, columns, rows]
    targets = [keys, voxel_of, weight_of, volume_v, poses, images_v, precision, columns_v, rows_v]
    load = [pltpu.make_async_copy(src, dst, loads.at[i]) for i, (src, dst) in enumerate(zip(sources, targets))]

    def start_load(index):
        src, dst = sources[index], targets[index]
        pieces = 8 if src.shape[0] >= 512 else 1
        size = src.shape[0] // pieces
        for piece in range(pieces):
            at = slice(piece * size, (piece + 1) * size)
            pltpu.make_async_copy(src.at[at], dst.at[at], loads.at[index]).start()

    for index in range(5):
        start_load(index)
    for step in range(1, slabs):
        greet("slab", slab_peer(step))
    for step in range(1, members):
        greet("img", img_peer(step))

    with jax.named_scope("own_slots"):
        for index in range(3):
            load[index].wait()
        before = jnp.zeros((slabs, cap), F32)
        for slab in range(slabs):
            before += jnp.where(keys[slab] >= 0, 1.0, 0.0) * jnp.where(own > slab, 1.0, 0.0)
        out_start = jnp.sum(before, axis=1, keepdims=True)
        total_slots = slabs * cap
        own_key = keys[own]
        own_code = voxel_of[own] * 32 + jnp.where(own_key >= 0, weight_of[own], 31)

        def ordered(first, count, tables):
            position = iota((1, count), 1) + first
            block_sel = iota((slabs, count), 0) == ((position >> 3) & (slabs - 1))
            start_row = pick_row(block_sel, out_start).astype(jnp.int32)
            slot_row = members * (position & 7) + (((position >> 7) - start_row) & 7)
            slot_sel = iota((cap, count), 0) == slot_row
            chooser = jnp.where(block_sel, 1.0, 0.0)
            found = []
            for table in tables:
                wide = lax.dot_general(
                    table.astype(F32), chooser, (((0,), (0,)), ((), ())),
                    precision=lax.Precision.HIGHEST, preferred_element_type=F32,
                )
                found.append(pick_row(slot_sel, wide))
            return found

        def decoded(code):
            code_row = code.astype(jnp.int32)
            level = code_row & 31
            alive = level <= WSTEPS
            spot = (code_row >> 5).astype(F32)
            lower = jnp.where(alive, level, 0).astype(F32) * (1.0 / WSTEPS)
            upper = jnp.where(alive, WSTEPS - level, 0).astype(F32) * (1.0 / WSTEPS)
            return spot, lower, upper

        parts = decoded(ordered(member * mine, mine, [own_code])[0])
        own_cols = jnp.concatenate(list(parts) + [jnp.zeros((5, mine), F32)], axis=0).T
        place = iota((mine, voxels), 1)
        spot = own_cols[:, 0:1].astype(jnp.int32)
        take = jnp.where(place == spot, own_cols[:, 1:2], 0.0) + jnp.where(place == spot + 1, own_cols[:, 2:3], 0.0)
        load[3].wait()
        for index in range(5, len(load)):
            start_load(index)
        woven = dot(take.astype(BF16), volume_v[...])
        for block in range(slabs):
            outgoing[block] = woven[block * deep : (block + 1) * deep].astype(BF16)
        pl.semaphore_wait(barrier, slabs - 1 + members - 1)

        def slab_copy(stage, src, dst, peer):
            return remote(src.at[peer], dst.at[own], slab_send.at[stage], slab_recv.at[stage], {"slab": peer})

        def slab_whole(stage, ref, count):
            blocks = ref.at[0:count]
            return remote(blocks, blocks, slab_send.at[stage], slab_recv.at[stage], {"slab": slab_peer(1)})

        def slab_exchange(stage, src, dst):
            for step in range(1, slabs):
                slab_copy(stage, src, dst, slab_peer(step)).start()

        def slab_arrivals(stage, dst):
            slab_whole(stage, dst, slabs - 1).wait_recv()

        def img_copy(slot, src, dst, device):
            return remote(src, dst, img_send.at[slot], img_recv.at[slot], {"img": device})

    with jax.named_scope("tables"):
        slab_exchange(0, outgoing, incoming)
        incoming[own] = outgoing[own]

        code, key_row = ordered(0, total_slots, [own_code, own_key])
        for index, value in enumerate(decoded(code) + (key_row,)):
            slot_table[index : index + 1, :] = value
        slot_table[4:8, :] = jnp.zeros((4, total_slots), F32)

        in_key = jnp.concatenate(
            [jnp.sum(jnp.where(iota((slabs, cap), 0) == own, keys[slab], 0), axis=0, keepdims=True) for slab in range(slabs)],
            axis=0,
        )
        live = jnp.where(in_key >= 0, 1.0, 0.0).astype(BF16)
        count = dot(live, jnp.ones((cap, LANES), BF16))
        earlier = jnp.where(iota((slabs, slabs), 1) < iota((slabs, slabs), 0), 1.0, 0.0).astype(BF16)
        start = dot(earlier, count.astype(BF16))
        lane = iota((1, mine), 1)
        slab_sel = iota((slabs, mine), 0) == (lane >> 3)
        in_start = pick_row(slab_sel, start).astype(jnp.int32)
        in_count = pick_row(slab_sel, count).astype(jnp.int32)
        slot = members * (lane & 7) + ((member - in_start) & 7)
        pack_row = jnp.where(slot < in_count, (in_start + slot) >> 3, -1)
        pack_table[...] = jnp.broadcast_to(pack_row, (8, mine)).astype(F32)

        number = start[:, :cap].astype(jnp.int32) + iota((slabs, cap), 1)
        holder = number & (members - 1)
        ahead = ((holder >> 1) - chip) & (ring_len - 1)
        near = jnp.where(ahead == 0, 3, jnp.where(ahead == 1, 1, jnp.where(ahead == 2, 0, 2)))
        row = jnp.where((holder & 1) == core, near, members - 1 - near) * share + (number >> 3)
        key_cols, row_cols = in_key.astype(F32).T, row.astype(F32).T
        pose_ids = iota((cap, NPOSE), 1).astype(F32)
        found_rows = jnp.zeros((cap, NPOSE), F32)
        for slab in range(slabs):
            found_rows += jnp.where(key_cols[:, slab : slab + 1] == pose_ids, row_cols[:, slab : slab + 1], 0.0)
        pose_row[...] = jnp.broadcast_to(jnp.sum(found_rows, axis=0, keepdims=True), (8, NPOSE)).astype(jnp.int32)

        load[4].wait()
        for part in range(poses.shape[1] // LANES):
            for k in range(0, cands, 8):
                at = (slice(k, k + 8), slice(part * LANES, (part + 1) * LANES))
                pose = poses[at]
                low, high = pose & (LANES - 1), pose >> 7
                renamed = jnp.zeros_like(pose)
                for piece in range(NPOSE // LANES):
                    table = pose_row[:, piece * LANES : (piece + 1) * LANES]
                    found = jnp.take_along_axis(table, low, axis=1, mode="promise_in_bounds")
                    renamed = jnp.where(high == piece, found, renamed)
                poses[at] = renamed

        ahead_of = slabs // 2
        turn = own // ahead_of

        def rank_chunk(block):
            at = rows_at(block * LANES, LANES)
            number = poses[:, at].astype(jnp.int16)
            for first in range(0, NPOSE, LANES):
                row = (iota((LANES, LANES), 0) + first).astype(jnp.int16)
                value = jnp.full((LANES, LANES), cands, jnp.int16)
                for k in range(cands):
                    value = jnp.where(number[k : k + 1] == row, jnp.int16(k), value)
                ranks[first : first + LANES, at] = value.astype(jnp.int32)

        each(slabs, rank_chunk, ahead_of)

    with jax.named_scope("pack_rows"):
        slab_arrivals(0, incoming)
        arrived = jnp.concatenate([incoming[block].astype(F32) for block in range(slabs)], axis=0).astype(BF16)
        pack = jnp.where(iota((share, mine), 0).astype(F32) == pack_table[0:1, :], 1.0, 0.0).astype(BF16)

        def block_of(index, first=0, size=share):
            return slices.at[index * share + first : index * share + first + size]

        FAR, RIGHT, LEFT, HOME = 0, 1, 2, 3
        slices[HOME * share : (HOME + 1) * share, :] = dot(pack, arrived).astype(BF16)

        def other(index):
            return members - 1 - index

        def top(index):
            return block_of(index, 0, half)

        def bottom(index):
            return block_of(index, half, half)

        gathers = [
            img_copy(0, top(HOME), top(LEFT), right),
            img_copy(1, bottom(HOME), bottom(RIGHT), left),
            img_copy(2, block_of(HOME), block_of(other(HOME)), partner),
            img_copy(3, bottom(HOME), bottom(LEFT), right),
            img_copy(4, top(HOME), top(RIGHT), left),
            img_copy(5, top(LEFT), top(FAR), right),
            img_copy(6, bottom(RIGHT), bottom(FAR), left),
            img_copy(7, block_of(LEFT), block_of(other(LEFT)), partner),
            img_copy(8, block_of(RIGHT), block_of(other(RIGHT)), partner),
            img_copy(9, top(FAR), top(other(FAR)), partner),
            img_copy(10, bottom(FAR), bottom(other(FAR)), partner),
        ]
        for index in range(5):
            gathers[index].start()

    with jax.named_scope("gather_near"):
        def weave_step(index):
            at = iota((LANES, total_slots), 0) + index * LANES
            spots = slot_table[0:1, :].astype(jnp.int32)
            value = jnp.where(spots == at, slot_table[1:2, :], 0.0) + jnp.where(spots + 1 == at, slot_table[2:3, :], 0.0)
            weave[rows_at(index * LANES, LANES), :] = value.astype(BF16)

        each(voxels // LANES, weave_step)
        gathers[0].wait_recv()
        gathers[5].start()
        gathers[1].wait_recv()
        gathers[6].start()
        gathers[3].wait_recv()
        gathers[7].start()
        gathers[4].wait_recv()
        gathers[8].start()
        load[5].wait()

        def power_step(index):
            at = rows_at(index * share, share)
            values = slices[at, :].astype(F32)
            total = 0.5 * jnp.sum(values * values, axis=1, keepdims=True)
            half_power[at, :] = jnp.broadcast_to(total, (share, LANES))

        chunk = 2 * LANES
        chunks = images_v.shape[0] // chunk

        def picks_of(score, pieces, numbers, value):
            for first, offset, size in pieces:
                block = score[offset : offset + size] - half_power[first : first + size, :]
                for group in range(size // 8):
                    picked = jnp.take_along_axis(
                        block[group * 8 : (group + 1) * 8], numbers[0], axis=0, mode="promise_in_bounds"
                    )
                    value[0] = jnp.where(numbers[2] == first // 8 + group, picked, value[0])
                    picked = jnp.take_along_axis(
                        block[group * 8 : (group + 1) * 8], numbers[1], axis=0, mode="promise_in_bounds"
                    )
                    value[1] = jnp.where(numbers[3] == first // 8 + group, picked, value[1])
            return value

        def score_chunk(index, table, pieces, resume):
            score = lax.dot_general(
                table, images_v[rows_at(index * chunk, chunk), :],
                (((1,), (1,)), ((), ())), preferred_element_type=F32,
            )
            for part in range(chunk // LANES):
                number = poses[:, rows_at(index * chunk + part * LANES, LANES)]
                numbers = [number[0:8] & 7, number[8:16] & 7, number[0:8] >> 3, number[8:16] >> 3]
                block = index * (chunk // LANES) + part
                if resume:
                    value = [picks[block, 0:8], picks[block, 8:16]]
                else:
                    value = [jnp.zeros((8, LANES), F32), jnp.zeros((8, LANES), F32)]
                value = picks_of(score[:, part * LANES : (part + 1) * LANES], pieces, numbers, value)
                picks[block] = jnp.concatenate(value, axis=0)

        def near_step(index):
            score_chunk(index, slices[share : NPOSE - share, :], [(share, 0, NPOSE - 2 * share)], False)

        def far_chunk(index):
            table = jnp.concatenate([slices[0:share, :], slices[NPOSE - share : NPOSE, :]], axis=0)
            score_chunk(index, table, [(0, 0, share), (NPOSE - share, share, share)], True)

        def full_chunk(index):
            score_chunk(index, slices[...], [(0, 0, NPOSE)], False)

    with jax.named_scope("scores"):
        gathers[2].wait_recv()
        gathers[7].wait_recv()
        gathers[8].wait_recv()
        each(members - 1, power_step, 1)
        each(chunks // 4, near_step)
        gathers[5].wait_recv()
        gathers[9].start()
        gathers[6].wait_recv()
        gathers[10].start()
        each(chunks // 2, near_step, chunks // 4)
        gathers[9].wait_recv()
        gathers[10].wait_recv()
        power_step(0)
        power_step(members - 1)

        def pick_send(peer):
            @pl.when(peer != own)
            def _():
                slab_copy(1, picks, picks_in, peer).start()

        def far_step(index):
            far_chunk(index)
            pick_send(2 * index)
            pick_send(2 * index + 1)

        def full_step(index):
            full_chunk(index)
            pick_send(2 * index)
            pick_send(2 * index + 1)

        each(chunks // 2, far_step)
        each(chunks, full_step, chunks // 2)
        picks_in[own] = picks[own]
        load[6].wait()
        row_weight[...] = jnp.zeros_like(row_weight)
        masses[member] = jnp.zeros((8, LANES), F32)

        def share_out():
            slab_arrivals(1, picks_in)
            total = picks_in[0]
            for block in range(1, slabs):
                total = total + picks_in[block]
            total = total * precision[:, rows_at(own * LANES, LANES)]
            exponent = jnp.exp(total - jnp.max(total, axis=0, keepdims=True))
            shares[own] = exponent / jnp.sum(exponent, axis=0, keepdims=True)
            for step in range(1, slabs):
                remote(
                    shares.at[own], shares.at[own], slab_send.at[2], slab_recv.at[5 + turn], {"slab": slab_peer(step)}
                ).start()

    with jax.named_scope("sum_scores"):
        @pl.when(turn == 0)
        def _():
            share_out()

        each(ahead_of, rank_chunk)

        @pl.when(turn != 0)
        def _():
            share_out()

        def shares_arrive(which):
            @pl.when(turn == which)
            def _():
                slab_whole(5 + which, shares, ahead_of - 1).wait_recv()

            @pl.when(turn != which)
            def _():
                slab_whole(5 + which, shares, ahead_of).wait_recv()

        def spread_chunk(block):
            at = rows_at(block * LANES, LANES)
            amount = shares[block] * precision[:, at]
            rounded = amount.astype(BF16).astype(F32)
            low, high = rounded[0:8], rounded[8:16]
            for first in range(0, NPOSE, 16):
                values = []
                for group in (first, first + 8):
                    rank = ranks[group : group + 8, at]
                    place = rank & 7
                    from_low = jnp.take_along_axis(low, place, axis=0, mode="promise_in_bounds")
                    from_high = jnp.take_along_axis(high, place, axis=0, mode="promise_in_bounds")
                    value = jnp.where(rank < 8, from_low, jnp.where(rank < cands, from_high, 0.0))
                    row_weight[group : group + 8, :] += value
                    values.append(value)
                spread[first : first + 16, at] = jnp.concatenate(values, axis=0).astype(BF16)

        stripe = 2 * LANES
        halves = 1
        wide = width // halves
        per_half = wide // stripe

        def away_copy(index):
            at = slice(index * stripe, (index + 1) * stripe)
            return img_copy(40 + index, away.at[:, at], away_in.at[:, at], partner)

        def back_stripe(index):
            at = slice(index * stripe, (index + 1) * stripe)
            part = partial[:, at] + dot(spread[:, early:], images_v[early:, at])
            away[:, at] = part[side:].astype(BF16)
            away_copy(index).start()
            kept[:, at] = part[:side]

        def columns_of(part):
            return slice(part * wide, (part + 1) * wide)

        def kept_part(index, part, first=0, size=share):
            here = index * share + first
            there = (ring_len - 1 - index) * share + first
            at = columns_of(part)
            return kept[here : here + size, at] + away_in[there : there + size, at].astype(F32)

        def ring_copy(part, index):
            at = columns_of(part)
            low, high = slice(0, half), slice(half, share)
            refs = [
                (opposite.at[low, at], opposite_in.at[low, at], right),
                (opposite.at[high, at], opposite_in.at[high, at], left),
                (ring.at[0, high, at], ring_in.at[0, high, at], right),
                (ring.at[1, low, at], ring_in.at[1, low, at], left),
                (ring.at[0, low, at], ring_in.at[0, low, at], right),
                (ring.at[1, high, at], ring_in.at[1, high, at], left),
            ]
            return img_copy(48 + 6 * part + index, *refs[index])

        def ring_start(part):
            at = columns_of(part)
            for index in range(part * per_half, (part + 1) * per_half):
                away_copy(index).wait_recv()
            opposite[:, at] = kept_part(FAR, part).astype(BF16)
            ring_copy(part, 0).start()
            ring_copy(part, 1).start()
            ring[0, half:share, at] = kept_part(RIGHT, part, half, half).astype(BF16)
            ring_copy(part, 2).start()
            ring[1, 0:half, at] = kept_part(LEFT, part, 0, half).astype(BF16)
            ring_copy(part, 3).start()

        def ring_relay(part):
            at = columns_of(part)
            ring_copy(part, 0).wait_recv()
            ring[0, 0:half, at] = (kept_part(RIGHT, part, 0, half) + opposite_in[0:half, at].astype(F32)).astype(BF16)
            ring_copy(part, 4).start()
            ring_copy(part, 1).wait_recv()
            ring[1, half:share, at] = (
                kept_part(LEFT, part, half, half) + opposite_in[half:share, at].astype(F32)
            ).astype(BF16)
            ring_copy(part, 5).start()

        unpack = jnp.where(pack_table[...].T[:, 0:1] == iota((mine, share), 1).astype(F32), 1.0, 0.0).astype(BF16)

        def ring_finish(part):
            at = columns_of(part)
            held = kept_part(HOME, part)
            for index in range(2, 6):
                ring_copy(part, index).wait_recv()
            summed = (held + ring_in[0, :, at].astype(F32) + ring_in[1, :, at].astype(F32)).astype(BF16)
            unpacked = dot(unpack, summed)
            for block in range(slabs):
                returning[part, block] = unpacked[block * deep : (block + 1) * deep].astype(BF16)
            slab_exchange(3 + part, returning.at[part], returned.at[part])
            returned[part, own] = returning[part, own]

        early = images_v.shape[0] // 2

        def early_stripe(index):
            at = rows_at(index * stripe, stripe)
            partial[:, at] = dot(spread[:, :early], images_v[:early, at])

    with jax.named_scope("spread_first"):
        shares_arrive(0)
        each(ahead_of, spread_chunk)
        each(width // stripe, early_stripe)

    with jax.named_scope("spread_second"):
        shares_arrive(1)
        each(slabs, spread_chunk, ahead_of)

    with jax.named_scope("stripes"):
        weight = jnp.sum(row_weight[...], axis=1, keepdims=True)
        mass_row = pick_row(iota((NPOSE, NPOSE), 0) == pose_row[0:1, :], weight)
        for piece in range(NPOSE // LANES):
            masses[member, piece : piece + 1, :] = mass_row[:, piece * LANES : (piece + 1) * LANES]

        def mass_copy(step):
            return img_copy(16, masses.at[member], masses.at[member], img_peer(step))

        def img_whole(slot, ref):
            blocks = ref.at[0 : members - 1]
            return img_copy(slot, blocks, blocks, img_peer(1))

        for step in range(1, members):
            mass_copy(step).start()
        for index in range(width // stripe):
            back_stripe(index)

    with jax.named_scope("ring"):
        ring_start(0)
        ring_relay(0)

    with jax.named_scope("unpack"):
        ring_finish(0)
        for block in range(slabs):
            posterior[:, block * LANES : (block + 1) * LANES] = shares[block]

    with jax.named_scope("voxel_masses"):
        img_whole(16, masses).wait_recv()
        mass_sum = masses[0]
        for index in range(1, members):
            mass_sum = mass_sum + masses[index]
        mass_total = jnp.concatenate([mass_sum[piece : piece + 1] for piece in range(NPOSE // LANES)], axis=1)
        lanes = iota((LANES, LANES), 1)
        mass_cols = []
        for block in range(members):
            key_col = slot_table[:, block * LANES : (block + 1) * LANES].T[:, 3:4]
            matched = key_col == iota((LANES, NPOSE), 1).astype(F32)
            amount = jnp.sum(jnp.where(matched, mass_total, 0.0), axis=1, keepdims=True)
            first = amount.astype(BF16).astype(F32)
            second = (amount - first).astype(BF16).astype(F32)
            third = amount - first - second
            mass_cols.append(
                jnp.where(lanes == 0, first, jnp.where(lanes == 1, second, jnp.where(lanes == 2, third, 0.0))).astype(BF16)
            )
        mass_table = jnp.concatenate(mass_cols, axis=0)

        def mass_step(index):
            at = rows_at(index * LANES, LANES)
            mass = jnp.sum(dot(weave[at, :], mass_table), axis=1, keepdims=True)
            inverse[at, :] = jnp.broadcast_to(1.0 / (mass + RIDGE), (LANES, LANES))

        each(voxels // LANES, mass_step)
        load[7].wait()
        load[8].wait()

    with jax.named_scope("transform_x"):
        turned = jnp.zeros((mine, width), F32)
        for part in range(halves):
            slab_arrivals(3 + part, returned.at[part])
            gathered = jnp.concatenate([returned[part, block].astype(F32) for block in range(slabs)], axis=0)
            turned += dot(gathered.astype(BF16), columns_v[columns_of(part), :])
        for block in range(members):
            crossing[block] = turned[:, block * LANES : (block + 1) * LANES].astype(BF16)

        def cross_copy(step):
            peer = img_peer(step)
            return img_copy(17, crossing.at[peer], crossed.at[member], peer)

        for step in range(1, members):
            cross_copy(step).start()
        crossed[member] = crossing[member]

    with jax.named_scope("sends_done"):
        for stage, ref in ((0, outgoing), (1, picks), (2, shares), (3, returning.at[0])):
            slab_whole(stage, ref, slabs - 1).wait_send()
        for copy in gathers:
            copy.wait_send()
        for index in range(halves * per_half):
            away_copy(index).wait_send()
        for part in range(halves):
            for index in range(6):
                ring_copy(part, index).wait_send()
        img_whole(16, masses).wait_send()
        img_whole(17, crossed).wait_recv()

    with jax.named_scope("transform_y"):
        voxel_rows = dot(weave[...], crossed[...].reshape(members * LANES, LANES)) * inverse[...]
        fourier = voxel_rows.astype(BF16)
        edge = density.shape[2]
        columns_out = density.shape[1]
        for plane in range(density.shape[0]):
            field = fourier[plane * edge : (plane + 1) * edge]
            real = dot(rows_v[:, :edge], field)
            imag = dot(rows_v[:, edge:], field)
            density[plane] = (real[:, :columns_out] + imag[:, columns_out:]).T
        img_whole(17, crossing).wait_send()


def per_device(images, volume, precision, candidates, slot_key, slot_voxel, slot_weight):
    members = lax.axis_size("img")
    slabs = lax.axis_size("slab")
    planes, edge, width = volume.shape
    particles, cands = candidates.shape
    cap = slot_key.shape[2]
    deep = cap // members
    share = NPOSE // members
    voxels = planes * edge
    mine = slabs * deep
    side = NPOSE // 2
    big = pl.BlockSpec(memory_space=pl.ANY)
    near = pl.BlockSpec(memory_space=pltpu.VMEM)
    scratch = [
        pltpu.VMEM((particles, width), BF16),
        pltpu.VMEM((voxels, width), BF16),
        pltpu.VMEM((width, width), BF16),
        pltpu.VMEM((edge, 2 * edge), BF16),
        pltpu.VMEM((1, particles), F32),
        pltpu.VMEM((cands, particles), jnp.int32),
        pltpu.VMEM(slot_key.shape, jnp.int32),
        pltpu.VMEM(slot_key.shape, jnp.int32),
        pltpu.VMEM(slot_key.shape, jnp.int32),
        pltpu.VMEM((8, slabs * cap), F32),
        pltpu.VMEM((8, mine), F32),
        pltpu.VMEM((8, NPOSE), jnp.int32),
        pltpu.VMEM((slabs, deep, width), BF16),
        pltpu.VMEM((slabs, deep, width), BF16),
        pltpu.VMEM((NPOSE, width), BF16),
        pltpu.VMEM((NPOSE, LANES), F32),
        pltpu.VMEM((NPOSE, particles), jnp.int32),
        pltpu.VMEM((voxels, slabs * cap), BF16),
        pltpu.VMEM((slabs, cands, LANES), F32),
        pltpu.VMEM((slabs, cands, LANES), F32),
        pltpu.VMEM((slabs, cands, LANES), F32),
        pltpu.VMEM((NPOSE, particles), BF16),
        pltpu.VMEM((NPOSE, LANES), F32),
        pltpu.VMEM((NPOSE, width), F32),
        pltpu.VMEM((side, width), BF16),
        pltpu.VMEM((side, width), BF16),
        pltpu.VMEM((side, width), F32),
        pltpu.VMEM((share, width), BF16),
        pltpu.VMEM((share, width), BF16),
        pltpu.VMEM((2, share, width), BF16),
        pltpu.VMEM((2, share, width), BF16),
        pltpu.VMEM((members, 8, LANES), F32),
        pltpu.VMEM((voxels, LANES), F32),
        pltpu.VMEM((1, slabs, deep, width), BF16),
        pltpu.VMEM((1, slabs, deep, width), BF16),
        pltpu.VMEM((members, mine, LANES), BF16),
        pltpu.VMEM((members, mine, LANES), BF16),
        pltpu.SemaphoreType.DMA((9,)),
        pltpu.SemaphoreType.DMA((7,)),
        pltpu.SemaphoreType.DMA((7,)),
        pltpu.SemaphoreType.DMA((60,)),
        pltpu.SemaphoreType.DMA((60,)),
    ]
    density, posterior = pl.pallas_call(
        functools.partial(kernel, slabs, members),
        out_shape=(
            jax.ShapeDtypeStruct((planes, edge // members, edge), F32),
            jax.ShapeDtypeStruct((cands, particles), F32),
        ),
        in_specs=[big] * 9,
        out_specs=(near, near),
        scratch_shapes=scratch,
        compiler_params=pltpu.CompilerParams(
            collective_id=0, has_side_effects=True, vmem_limit_bytes=56 * 1024 * 1024
        ),
    )(
        images, volume.reshape(voxels, width), column_table(edge, members), row_table(edge),
        precision[None, :], candidates.T, slot_key, slot_voxel, slot_weight,
    )
    return density.transpose(0, 2, 1), posterior.T


def solution(mesh):
    placed = (P("img", "slab"), P("slab", None, None), P("img"), P("img", None), P(), P(), P())
    return jax.shard_map(
        per_device,
        mesh=mesh,
        in_specs=placed,
        out_specs=(P("slab", None, "img"), P("img", None)),
        check_vma=False,
    )
```

```python
import functools
import math

import jax
import jax.numpy as jnp
import numpy as np
from jax import lax
from jax.experimental import pallas as pl
from jax.experimental.pallas import tpu as pltpu
from jax.sharding import PartitionSpec as P

NPOSE = 512
WSTEPS = 16
RIDGE = 0.25
LANES = 128
F32 = jnp.float32
BF16 = jnp.bfloat16


def gridding(samples):
    offset = (np.arange(samples) - samples / 2) / samples
    return 1.0 / np.sinc(offset) ** 2


def angles(length):
    counter = np.arange(length)
    return (counter[:, None] * counter[None, :] % length) * (2.0 * math.pi / length)


def column_table(length, members):
    turn = angles(length)
    cosine, sine = np.cos(turn), np.sin(turn)
    scale = gridding(length)[None, :]
    to_re = np.concatenate([cosine, -sine], axis=0) * scale
    to_im = np.concatenate([sine, cosine], axis=0) * scale
    width = length // members
    both = np.stack([to_re.reshape(-1, members, width), to_im.reshape(-1, members, width)], axis=2)
    return jnp.asarray(both.reshape(2 * length, 2 * length), BF16)


def row_table(length):
    turn = angles(length)
    scale = gridding(length)[:, None] / length
    return jnp.asarray(np.concatenate([np.cos(turn), -np.sin(turn)], axis=1) * scale, BF16)


def remote(src, dst, sends, recvs, device):
    return pltpu.make_async_remote_copy(
        src_ref=src,
        dst_ref=dst,
        send_sem=sends,
        recv_sem=recvs,
        device_id=device,
        device_id_type=pl.DeviceIdType.MESH,
    )


def dot(left, right):
    return jnp.dot(left, right, preferred_element_type=F32)


def each(count, step, first=0):
    def body(index, carry):
        step(index)
        return carry

    lax.fori_loop(first, count, body, 0)


def rows_at(start, size):
    return pl.ds(pl.multiple_of(start, size), size)


def iota(shape, axis):
    return lax.broadcasted_iota(jnp.int32, shape, axis)


def pick_row(mask, values):
    return jnp.sum(jnp.where(mask, values, 0.0), axis=0, keepdims=True)


def kernel(
    slabs, members,
    images, volume, columns, precision_in, poses_in, keys_in, voxels_in, weights_in,
    fourier, shares_out,
    images_v, volume_v, columns_v, precision, poses, keys, voxel_of, weight_of,
    slot_table, pack_table, pose_row,
    outgoing, incoming, slices, half_power, ranks, weave,
    picks, picks_in, shares, spread, row_weight, partial,
    away, away_in, kept, opposite, opposite_in, ring, ring_in,
    masses, inverse, returning, returned, crossing, crossed,
    loads, slab_send, slab_recv, img_send, img_recv,
):
    own = lax.axis_index("slab")
    member = lax.axis_index("img")
    ring_len = members // 2
    chip, core = member // 2, lax.rem(member, 2)
    share = NPOSE // members
    half = share // 2
    side = ring_len * share
    deep = outgoing.shape[1]
    mine = slabs * deep
    cap = keys.shape[2]
    width = volume_v.shape[1]
    voxels = volume_v.shape[0]
    cands = poses.shape[0]
    right = 2 * lax.rem(chip + 1, ring_len) + core
    left = 2 * lax.rem(chip + ring_len - 1, ring_len) + core
    partner = 2 * chip + 1 - core

    def slab_peer(step):
        return lax.rem(own + step, slabs)

    def img_peer(step):
        return lax.rem(member + step, members)

    barrier = pltpu.get_barrier_semaphore()

    def greet(axis, peer):
        pl.semaphore_signal(barrier, inc=1, device_id={axis: peer}, device_id_type=pl.DeviceIdType.MESH)

    sources = [keys_in, voxels_in, weights_in, volume, poses_in, images, precision_in, columns]
    targets = [keys, voxel_of, weight_of, volume_v, poses, images_v, precision, columns_v]
    load = [pltpu.make_async_copy(src, dst, loads.at[i]) for i, (src, dst) in enumerate(zip(sources, targets))]

    def start_load(index):
        src, dst = sources[index], targets[index]
        pieces = 8 if src.shape[0] >= 512 else 1
        size = src.shape[0] // pieces
        for piece in range(pieces):
            at = slice(piece * size, (piece + 1) * size)
            pltpu.make_async_copy(src.at[at], dst.at[at], loads.at[index]).start()

    for index in range(5):
        start_load(index)
    for step in range(1, slabs):
        greet("slab", slab_peer(step))
    for step in range(1, members):
        greet("img", img_peer(step))

    for index in range(3):
        load[index].wait()
    before = jnp.zeros((slabs, cap), F32)
    for slab in range(slabs):
        before += jnp.where(keys[slab] >= 0, 1.0, 0.0) * jnp.where(own > slab, 1.0, 0.0)
    out_start = jnp.sum(before, axis=1, keepdims=True)
    total_slots = slabs * cap
    own_key = keys[own]
    own_code = voxel_of[own] * 32 + jnp.where(own_key >= 0, weight_of[own], 31)

    def ordered(first, count, tables):
        position = iota((1, count), 1) + first
        block_sel = iota((slabs, count), 0) == ((position >> 3) & (slabs - 1))
        start_row = pick_row(block_sel, out_start).astype(jnp.int32)
        slot_row = members * (position & 7) + (((position >> 7) - start_row) & 7)
        slot_sel = iota((cap, count), 0) == slot_row
        chooser = jnp.where(block_sel, 1.0, 0.0)
        found = []
        for table in tables:
            wide = lax.dot_general(
                table.astype(F32), chooser, (((0,), (0,)), ((), ())),
                precision=lax.Precision.HIGHEST, preferred_element_type=F32,
            )
            found.append(pick_row(slot_sel, wide))
        return found

    def decoded(code):
        code_row = code.astype(jnp.int32)
        level = code_row & 31
        alive = level <= WSTEPS
        spot = (code_row >> 5).astype(F32)
        lower = jnp.where(alive, level, 0).astype(F32) * (1.0 / WSTEPS)
        upper = jnp.where(alive, WSTEPS - level, 0).astype(F32) * (1.0 / WSTEPS)
        return spot, lower, upper

    parts = decoded(ordered(member * mine, mine, [own_code])[0])
    own_cols = jnp.concatenate(list(parts) + [jnp.zeros((5, mine), F32)], axis=0).T
    place = iota((mine, voxels), 1)
    spot = own_cols[:, 0:1].astype(jnp.int32)
    take = jnp.where(place == spot, own_cols[:, 1:2], 0.0) + jnp.where(place == spot + 1, own_cols[:, 2:3], 0.0)
    load[3].wait()
    for index in range(5, len(load)):
        start_load(index)
    woven = dot(take.astype(BF16), volume_v[...])
    for block in range(slabs):
        outgoing[block] = woven[block * deep : (block + 1) * deep].astype(BF16)
    pl.semaphore_wait(barrier, slabs - 1 + members - 1)

    def slab_copy(stage, src, dst, peer):
        return remote(src.at[peer], dst.at[own], slab_send.at[stage], slab_recv.at[stage], {"slab": peer})

    def slab_whole(stage, ref, count):
        blocks = ref.at[0:count]
        return remote(blocks, blocks, slab_send.at[stage], slab_recv.at[stage], {"slab": slab_peer(1)})

    def slab_exchange(stage, src, dst):
        for step in range(1, slabs):
            slab_copy(stage, src, dst, slab_peer(step)).start()

    def slab_arrivals(stage, dst):
        slab_whole(stage, dst, slabs - 1).wait_recv()

    def img_copy(slot, src, dst, device):
        return remote(src, dst, img_send.at[slot], img_recv.at[slot], {"img": device})

    slab_exchange(0, outgoing, incoming)
    incoming[own] = outgoing[own]

    code, key_row = ordered(0, total_slots, [own_code, own_key])
    for index, value in enumerate(decoded(code) + (key_row,)):
        slot_table[index : index + 1, :] = value
    slot_table[4:8, :] = jnp.zeros((4, total_slots), F32)

    in_key = jnp.concatenate(
        [jnp.sum(jnp.where(iota((slabs, cap), 0) == own, keys[slab], 0), axis=0, keepdims=True) for slab in range(slabs)],
        axis=0,
    )
    live = jnp.where(in_key >= 0, 1.0, 0.0).astype(BF16)
    count = dot(live, jnp.ones((cap, LANES), BF16))
    earlier = jnp.where(iota((slabs, slabs), 1) < iota((slabs, slabs), 0), 1.0, 0.0).astype(BF16)
    start = dot(earlier, count.astype(BF16))
    lane = iota((1, mine), 1)
    slab_sel = iota((slabs, mine), 0) == (lane >> 3)
    in_start = pick_row(slab_sel, start).astype(jnp.int32)
    in_count = pick_row(slab_sel, count).astype(jnp.int32)
    slot = members * (lane & 7) + ((member - in_start) & 7)
    pack_row = jnp.where(slot < in_count, (in_start + slot) >> 3, -1)
    pack_table[...] = jnp.broadcast_to(pack_row, (8, mine)).astype(F32)

    number = start[:, :cap].astype(jnp.int32) + iota((slabs, cap), 1)
    holder = number & (members - 1)
    ahead = ((holder >> 1) - chip) & (ring_len - 1)
    near = jnp.where(ahead == 0, 3, jnp.where(ahead == 1, 1, jnp.where(ahead == 2, 0, 2)))
    row = jnp.where((holder & 1) == core, near, members - 1 - near) * share + (number >> 3)
    key_cols, row_cols = in_key.astype(F32).T, row.astype(F32).T
    pose_ids = iota((cap, NPOSE), 1).astype(F32)
    found_rows = jnp.zeros((cap, NPOSE), F32)
    for slab in range(slabs):
        found_rows += jnp.where(key_cols[:, slab : slab + 1] == pose_ids, row_cols[:, slab : slab + 1], 0.0)
    pose_row[...] = jnp.broadcast_to(jnp.sum(found_rows, axis=0, keepdims=True), (8, NPOSE)).astype(jnp.int32)

    load[4].wait()
    for part in range(poses.shape[1] // LANES):
        for k in range(0, cands, 8):
            at = (slice(k, k + 8), slice(part * LANES, (part + 1) * LANES))
            pose = poses[at]
            low, high = pose & (LANES - 1), pose >> 7
            renamed = jnp.zeros_like(pose)
            for piece in range(NPOSE // LANES):
                table = pose_row[:, piece * LANES : (piece + 1) * LANES]
                found = jnp.take_along_axis(table, low, axis=1, mode="promise_in_bounds")
                renamed = jnp.where(high == piece, found, renamed)
            poses[at] = renamed

    ahead_of = slabs // 2
    turn = own // ahead_of

    def rank_chunk(block):
        at = rows_at(block * LANES, LANES)
        number = poses[:, at].astype(jnp.int16)
        for first in range(0, NPOSE, LANES):
            row = (iota((LANES, LANES), 0) + first).astype(jnp.int16)
            value = jnp.full((LANES, LANES), cands, jnp.int16)
            for k in range(cands):
                value = jnp.where(number[k : k + 1] == row, jnp.int16(k), value)
            ranks[first : first + LANES, at] = value.astype(jnp.int32)

    each(slabs, rank_chunk, ahead_of)

    slab_arrivals(0, incoming)
    arrived = jnp.concatenate([incoming[block].astype(F32) for block in range(slabs)], axis=0).astype(BF16)
    pack = jnp.where(iota((share, mine), 0).astype(F32) == pack_table[0:1, :], 1.0, 0.0).astype(BF16)

    def block_of(index, first=0, size=share):
        return slices.at[index * share + first : index * share + first + size]

    FAR, RIGHT, LEFT, HOME = 0, 1, 2, 3
    slices[HOME * share : (HOME + 1) * share, :] = dot(pack, arrived).astype(BF16)

    def other(index):
        return members - 1 - index

    def top(index):
        return block_of(index, 0, half)

    def bottom(index):
        return block_of(index, half, half)

    gathers = [
        img_copy(0, top(HOME), top(LEFT), right),
        img_copy(1, bottom(HOME), bottom(RIGHT), left),
        img_copy(2, block_of(HOME), block_of(other(HOME)), partner),
        img_copy(3, bottom(HOME), bottom(LEFT), right),
        img_copy(4, top(HOME), top(RIGHT), left),
        img_copy(5, top(LEFT), top(FAR), right),
        img_copy(6, bottom(RIGHT), bottom(FAR), left),
        img_copy(7, block_of(LEFT), block_of(other(LEFT)), partner),
        img_copy(8, block_of(RIGHT), block_of(other(RIGHT)), partner),
        img_copy(9, top(FAR), top(other(FAR)), partner),
        img_copy(10, bottom(FAR), bottom(other(FAR)), partner),
    ]
    for index in range(5):
        gathers[index].start()

    def weave_step(index):
        at = iota((LANES, total_slots), 0) + index * LANES
        spots = slot_table[0:1, :].astype(jnp.int32)
        value = jnp.where(spots == at, slot_table[1:2, :], 0.0) + jnp.where(spots + 1 == at, slot_table[2:3, :], 0.0)
        weave[rows_at(index * LANES, LANES), :] = value.astype(BF16)

    each(voxels // LANES, weave_step)
    gathers[0].wait_recv()
    gathers[5].start()
    gathers[1].wait_recv()
    gathers[6].start()
    gathers[3].wait_recv()
    gathers[7].start()
    gathers[4].wait_recv()
    gathers[8].start()
    load[5].wait()

    def power_step(index):
        at = rows_at(index * share, share)
        values = slices[at, :].astype(F32)
        total = 0.5 * jnp.sum(values * values, axis=1, keepdims=True)
        half_power[at, :] = jnp.broadcast_to(total, (share, LANES))

    chunk = 2 * LANES
    chunks = images_v.shape[0] // chunk

    def picks_of(score, pieces, numbers, value):
        for first, offset, size in pieces:
            block = score[offset : offset + size] - half_power[first : first + size, :]
            for group in range(size // 8):
                picked = jnp.take_along_axis(
                    block[group * 8 : (group + 1) * 8], numbers[0], axis=0, mode="promise_in_bounds"
                )
                value[0] = jnp.where(numbers[2] == first // 8 + group, picked, value[0])
                picked = jnp.take_along_axis(
                    block[group * 8 : (group + 1) * 8], numbers[1], axis=0, mode="promise_in_bounds"
                )
                value[1] = jnp.where(numbers[3] == first // 8 + group, picked, value[1])
        return value

    def score_chunk(index, table, pieces, resume):
        score = lax.dot_general(
            table, images_v[rows_at(index * chunk, chunk), :],
            (((1,), (1,)), ((), ())), preferred_element_type=F32,
        )
        for part in range(chunk // LANES):
            number = poses[:, rows_at(index * chunk + part * LANES, LANES)]
            numbers = [number[0:8] & 7, number[8:16] & 7, number[0:8] >> 3, number[8:16] >> 3]
            block = index * (chunk // LANES) + part
            if resume:
                value = [picks[block, 0:8], picks[block, 8:16]]
            else:
                value = [jnp.zeros((8, LANES), F32), jnp.zeros((8, LANES), F32)]
            value = picks_of(score[:, part * LANES : (part + 1) * LANES], pieces, numbers, value)
            picks[block] = jnp.concatenate(value, axis=0)

    def near_step(index):
        score_chunk(index, slices[share : NPOSE - share, :], [(share, 0, NPOSE - 2 * share)], False)

    def far_chunk(index):
        table = jnp.concatenate([slices[0:share, :], slices[NPOSE - share : NPOSE, :]], axis=0)
        score_chunk(index, table, [(0, 0, share), (NPOSE - share, share, share)], True)

    def full_chunk(index):
        score_chunk(index, slices[...], [(0, 0, NPOSE)], False)

    gathers[2].wait_recv()
    gathers[7].wait_recv()
    gathers[8].wait_recv()
    each(members - 1, power_step, 1)
    each(chunks // 4, near_step)
    gathers[5].wait_recv()
    gathers[9].start()
    gathers[6].wait_recv()
    gathers[10].start()
    each(chunks // 2, near_step, chunks // 4)
    gathers[9].wait_recv()
    gathers[10].wait_recv()
    power_step(0)
    power_step(members - 1)

    def pick_send(peer):
        @pl.when(peer != own)
        def _():
            slab_copy(1, picks, picks_in, peer).start()

    def far_step(index):
        far_chunk(index)
        pick_send(2 * index)
        pick_send(2 * index + 1)

    def full_step(index):
        full_chunk(index)
        pick_send(2 * index)
        pick_send(2 * index + 1)

    each(chunks // 2, far_step)
    each(chunks, full_step, chunks // 2)
    picks_in[own] = picks[own]
    load[6].wait()
    row_weight[...] = jnp.zeros_like(row_weight)
    masses[member] = jnp.zeros((8, LANES), F32)

    def share_out():
        slab_arrivals(1, picks_in)
        total = picks_in[0]
        for block in range(1, slabs):
            total = total + picks_in[block]
        total = total * precision[:, rows_at(own * LANES, LANES)]
        exponent = jnp.exp(total - jnp.max(total, axis=0, keepdims=True))
        shares[own] = exponent / jnp.sum(exponent, axis=0, keepdims=True)
        for step in range(1, slabs):
            remote(
                shares.at[own], shares.at[own], slab_send.at[2], slab_recv.at[5 + turn], {"slab": slab_peer(step)}
            ).start()

    @pl.when(turn == 0)
    def _():
        share_out()

    each(ahead_of, rank_chunk)

    @pl.when(turn != 0)
    def _():
        share_out()

    def shares_arrive(which):
        @pl.when(turn == which)
        def _():
            slab_whole(5 + which, shares, ahead_of - 1).wait_recv()

        @pl.when(turn != which)
        def _():
            slab_whole(5 + which, shares, ahead_of).wait_recv()

    def spread_chunk(block):
        at = rows_at(block * LANES, LANES)
        amount = shares[block] * precision[:, at]
        rounded = amount.astype(BF16).astype(F32)
        low, high = rounded[0:8], rounded[8:16]
        for first in range(0, NPOSE, 16):
            values = []
            for group in (first, first + 8):
                rank = ranks[group : group + 8, at]
                place = rank & 7
                from_low = jnp.take_along_axis(low, place, axis=0, mode="promise_in_bounds")
                from_high = jnp.take_along_axis(high, place, axis=0, mode="promise_in_bounds")
                value = jnp.where(rank < 8, from_low, jnp.where(rank < cands, from_high, 0.0))
                row_weight[group : group + 8, :] += value
                values.append(value)
            spread[first : first + 16, at] = jnp.concatenate(values, axis=0).astype(BF16)

    stripe = 2 * LANES
    halves = 1
    wide = width // halves
    per_half = wide // stripe

    def away_copy(index):
        at = slice(index * stripe, (index + 1) * stripe)
        return img_copy(40 + index, away.at[:, at], away_in.at[:, at], partner)

    def back_stripe(index):
        at = slice(index * stripe, (index + 1) * stripe)
        part = partial[:, at] + dot(spread[:, early:], images_v[early:, at])
        away[:, at] = part[side:].astype(BF16)
        away_copy(index).start()
        kept[:, at] = part[:side]

    def columns_of(part):
        return slice(part * wide, (part + 1) * wide)

    def kept_part(index, part, first=0, size=share):
        here = index * share + first
        there = (ring_len - 1 - index) * share + first
        at = columns_of(part)
        return kept[here : here + size, at] + away_in[there : there + size, at].astype(F32)

    def ring_copy(part, index):
        at = columns_of(part)
        low, high = slice(0, half), slice(half, share)
        refs = [
            (opposite.at[low, at], opposite_in.at[low, at], right),
            (opposite.at[high, at], opposite_in.at[high, at], left),
            (ring.at[0, high, at], ring_in.at[0, high, at], right),
            (ring.at[1, low, at], ring_in.at[1, low, at], left),
            (ring.at[0, low, at], ring_in.at[0, low, at], right),
            (ring.at[1, high, at], ring_in.at[1, high, at], left),
        ]
        return img_copy(48 + 6 * part + index, *refs[index])

    def ring_start(part):
        at = columns_of(part)
        for index in range(part * per_half, (part + 1) * per_half):
            away_copy(index).wait_recv()
        opposite[:, at] = kept_part(FAR, part).astype(BF16)
        ring_copy(part, 0).start()
        ring_copy(part, 1).start()
        ring[0, half:share, at] = kept_part(RIGHT, part, half, half).astype(BF16)
        ring_copy(part, 2).start()
        ring[1, 0:half, at] = kept_part(LEFT, part, 0, half).astype(BF16)
        ring_copy(part, 3).start()

    def ring_relay(part):
        at = columns_of(part)
        ring_copy(part, 0).wait_recv()
        ring[0, 0:half, at] = (kept_part(RIGHT, part, 0, half) + opposite_in[0:half, at].astype(F32)).astype(BF16)
        ring_copy(part, 4).start()
        ring_copy(part, 1).wait_recv()
        ring[1, half:share, at] = (
            kept_part(LEFT, part, half, half) + opposite_in[half:share, at].astype(F32)
        ).astype(BF16)
        ring_copy(part, 5).start()

    unpack = jnp.where(pack_table[...].T[:, 0:1] == iota((mine, share), 1).astype(F32), 1.0, 0.0).astype(BF16)

    def ring_finish(part):
        at = columns_of(part)
        held = kept_part(HOME, part)
        for index in range(2, 6):
            ring_copy(part, index).wait_recv()
        summed = (held + ring_in[0, :, at].astype(F32) + ring_in[1, :, at].astype(F32)).astype(BF16)
        unpacked = dot(unpack, summed)
        for block in range(slabs):
            returning[part, block] = unpacked[block * deep : (block + 1) * deep].astype(BF16)
        slab_exchange(3 + part, returning.at[part], returned.at[part])
        returned[part, own] = returning[part, own]

    early = images_v.shape[0] // 2

    def early_stripe(index):
        at = rows_at(index * stripe, stripe)
        partial[:, at] = dot(spread[:, :early], images_v[:early, at])

    shares_arrive(0)
    each(ahead_of, spread_chunk)
    each(width // stripe, early_stripe)
    shares_arrive(1)
    each(slabs, spread_chunk, ahead_of)

    weight = jnp.sum(row_weight[...], axis=1, keepdims=True)
    mass_row = pick_row(iota((NPOSE, NPOSE), 0) == pose_row[0:1, :], weight)
    for piece in range(NPOSE // LANES):
        masses[member, piece : piece + 1, :] = mass_row[:, piece * LANES : (piece + 1) * LANES]

    def mass_copy(step):
        return img_copy(16, masses.at[member], masses.at[member], img_peer(step))

    def img_whole(slot, ref):
        blocks = ref.at[0 : members - 1]
        return img_copy(slot, blocks, blocks, img_peer(1))

    for step in range(1, members):
        mass_copy(step).start()
    for index in range(width // stripe):
        back_stripe(index)
    ring_start(0)
    ring_relay(0)
    ring_finish(0)
    shares_copy = pltpu.make_async_copy(shares, shares_out, loads.at[8])
    shares_copy.start()

    img_whole(16, masses).wait_recv()
    mass_sum = masses[0]
    for index in range(1, members):
        mass_sum = mass_sum + masses[index]
    mass_total = jnp.concatenate([mass_sum[piece : piece + 1] for piece in range(NPOSE // LANES)], axis=1)
    lanes = iota((LANES, LANES), 1)
    mass_cols = []
    for block in range(members):
        key_col = slot_table[:, block * LANES : (block + 1) * LANES].T[:, 3:4]
        matched = key_col == iota((LANES, NPOSE), 1).astype(F32)
        amount = jnp.sum(jnp.where(matched, mass_total, 0.0), axis=1, keepdims=True)
        first = amount.astype(BF16).astype(F32)
        second = (amount - first).astype(BF16).astype(F32)
        third = amount - first - second
        mass_cols.append(
            jnp.where(lanes == 0, first, jnp.where(lanes == 1, second, jnp.where(lanes == 2, third, 0.0))).astype(BF16)
        )
    mass_table = jnp.concatenate(mass_cols, axis=0)

    def mass_step(index):
        at = rows_at(index * LANES, LANES)
        mass = jnp.sum(dot(weave[at, :], mass_table), axis=1, keepdims=True)
        inverse[at, :] = jnp.broadcast_to(1.0 / (mass + RIDGE), (LANES, LANES))

    each(voxels // LANES, mass_step)
    load[7].wait()

    turned = jnp.zeros((mine, width), F32)
    for part in range(halves):
        slab_arrivals(3 + part, returned.at[part])
        gathered = jnp.concatenate([returned[part, block].astype(F32) for block in range(slabs)], axis=0)
        turned += dot(gathered.astype(BF16), columns_v[columns_of(part), :])
    for block in range(members):
        crossing[block] = turned[:, block * LANES : (block + 1) * LANES].astype(BF16)

    def cross_copy(step):
        peer = img_peer(step)
        return img_copy(17, crossing.at[peer], crossed.at[member], peer)

    for step in range(1, members):
        cross_copy(step).start()
    crossed[member] = crossing[member]

    for stage, ref in ((0, outgoing), (1, picks), (2, shares), (3, returning.at[0])):
        slab_whole(stage, ref, slabs - 1).wait_send()
    for copy in gathers:
        copy.wait_send()
    for index in range(halves * per_half):
        away_copy(index).wait_send()
    for part in range(halves):
        for index in range(6):
            ring_copy(part, index).wait_send()
    img_whole(16, masses).wait_send()
    img_whole(17, crossed).wait_recv()

    voxel_rows = dot(weave[...], crossed[...].reshape(members * LANES, LANES)) * inverse[...]
    fourier[...] = voxel_rows.astype(BF16)
    shares_copy.wait()
    img_whole(17, crossing).wait_send()


def finish(rows, fourier, shares, density, posterior):
    edge = density.shape[2]
    columns_out = density.shape[1]
    for plane in range(density.shape[0]):
        field = fourier[plane * edge : (plane + 1) * edge, :]
        real = dot(rows[:, :edge], field)
        imag = dot(rows[:, edge:], field)
        density[plane] = (real[:, :columns_out] + imag[:, columns_out:]).T
    for block in range(shares.shape[0]):
        posterior[:, block * LANES : (block + 1) * LANES] = shares[block]


def per_device(images, volume, precision, candidates, slot_key, slot_voxel, slot_weight):
    members = lax.axis_size("img")
    slabs = lax.axis_size("slab")
    planes, edge, width = volume.shape
    particles, cands = candidates.shape
    cap = slot_key.shape[2]
    deep = cap // members
    share = NPOSE // members
    voxels = planes * edge
    mine = slabs * deep
    side = NPOSE // 2
    big = pl.BlockSpec(memory_space=pl.ANY)
    near = pl.BlockSpec(memory_space=pltpu.VMEM)
    scratch = [
        pltpu.VMEM((particles, width), BF16),
        pltpu.VMEM((voxels, width), BF16),
        pltpu.VMEM((width, width), BF16),
        pltpu.VMEM((1, particles), F32),
        pltpu.VMEM((cands, particles), jnp.int32),
        pltpu.VMEM(slot_key.shape, jnp.int32),
        pltpu.VMEM(slot_key.shape, jnp.int32),
        pltpu.VMEM(slot_key.shape, jnp.int32),
        pltpu.VMEM((8, slabs * cap), F32),
        pltpu.VMEM((8, mine), F32),
        pltpu.VMEM((8, NPOSE), jnp.int32),
        pltpu.VMEM((slabs, deep, width), BF16),
        pltpu.VMEM((slabs, deep, width), BF16),
        pltpu.VMEM((NPOSE, width), BF16),
        pltpu.VMEM((NPOSE, LANES), F32),
        pltpu.VMEM((NPOSE, particles), jnp.int32),
        pltpu.VMEM((voxels, slabs * cap), BF16),
        pltpu.VMEM((slabs, cands, LANES), F32),
        pltpu.VMEM((slabs, cands, LANES), F32),
        pltpu.VMEM((slabs, cands, LANES), F32),
        pltpu.VMEM((NPOSE, particles), BF16),
        pltpu.VMEM((NPOSE, LANES), F32),
        pltpu.VMEM((NPOSE, width), F32),
        pltpu.VMEM((side, width), BF16),
        pltpu.VMEM((side, width), BF16),
        pltpu.VMEM((side, width), F32),
        pltpu.VMEM((share, width), BF16),
        pltpu.VMEM((share, width), BF16),
        pltpu.VMEM((2, share, width), BF16),
        pltpu.VMEM((2, share, width), BF16),
        pltpu.VMEM((members, 8, LANES), F32),
        pltpu.VMEM((voxels, LANES), F32),
        pltpu.VMEM((1, slabs, deep, width), BF16),
        pltpu.VMEM((1, slabs, deep, width), BF16),
        pltpu.VMEM((members, mine, LANES), BF16),
        pltpu.VMEM((members, mine, LANES), BF16),
        pltpu.SemaphoreType.DMA((9,)),
        pltpu.SemaphoreType.DMA((7,)),
        pltpu.SemaphoreType.DMA((7,)),
        pltpu.SemaphoreType.DMA((60,)),
        pltpu.SemaphoreType.DMA((60,)),
    ]
    fourier, shares = pl.pallas_call(
        functools.partial(kernel, slabs, members),
        out_shape=(
            jax.ShapeDtypeStruct((voxels, LANES), BF16),
            jax.ShapeDtypeStruct((slabs, cands, LANES), F32),
        ),
        in_specs=[big] * 8,
        out_specs=(near, big),
        scratch_shapes=scratch,
        compiler_params=pltpu.CompilerParams(
            collective_id=0, has_side_effects=True, vmem_limit_bytes=56 * 1024 * 1024
        ),
    )(
        images, volume.reshape(voxels, width), column_table(edge, members),
        precision[None, :], candidates.T, slot_key, slot_voxel, slot_weight,
    )
    density, posterior = pl.pallas_call(
        finish,
        out_shape=(
            jax.ShapeDtypeStruct((planes, edge // members, edge), F32),
            jax.ShapeDtypeStruct((cands, particles), F32),
        ),
        in_specs=[near] * 3,
        out_specs=(near, near),
        compiler_params=pltpu.CompilerParams(vmem_limit_bytes=56 * 1024 * 1024),
    )(row_table(edge), fourier, shares)
    return density.transpose(0, 2, 1), posterior.T


def solution(mesh):
    placed = (P("img", "slab"), P("slab", None, None), P("img"), P("img", None), P(), P(), P())
    return jax.shard_map(
        per_device,
        mesh=mesh,
        in_specs=placed,
        out_specs=(P("slab", None, "img"), P("img", None)),
        check_vma=False,
    )
```

```python
import functools
import math

import jax
import jax.numpy as jnp
import numpy as np
from jax import lax
from jax.experimental import pallas as pl
from jax.experimental.pallas import tpu as pltpu
from jax.sharding import PartitionSpec as P

NPOSE = 512
WSTEPS = 16
RIDGE = 0.25
LANES = 128
F32 = jnp.float32
BF16 = jnp.bfloat16


def gridding(samples):
    offset = (np.arange(samples) - samples / 2) / samples
    return 1.0 / np.sinc(offset) ** 2


def angles(length):
    counter = np.arange(length)
    return (counter[:, None] * counter[None, :] % length) * (2.0 * math.pi / length)


def column_table(length, members):
    turn = angles(length)
    cosine, sine = np.cos(turn), np.sin(turn)
    scale = gridding(length)[None, :]
    to_re = np.concatenate([cosine, -sine], axis=0) * scale
    to_im = np.concatenate([sine, cosine], axis=0) * scale
    width = length // members
    both = np.stack([to_re.reshape(-1, members, width), to_im.reshape(-1, members, width)], axis=2)
    return jnp.asarray(both.reshape(2 * length, 2 * length), BF16)


def row_table(length):
    turn = angles(length)
    scale = gridding(length)[None, :] / length
    return jnp.asarray(np.concatenate([np.cos(turn), -np.sin(turn)], axis=0) * scale, BF16)


def remote(src, dst, sends, recvs, device):
    return pltpu.make_async_remote_copy(
        src_ref=src,
        dst_ref=dst,
        send_sem=sends,
        recv_sem=recvs,
        device_id=device,
        device_id_type=pl.DeviceIdType.MESH,
    )


def dot(left, right):
    return jnp.dot(left, right, preferred_element_type=F32)


def each(count, step, first=0):
    def body(index, carry):
        step(index)
        return carry

    lax.fori_loop(first, count, body, 0)


def rows_at(start, size):
    return pl.ds(pl.multiple_of(start, size), size)


def iota(shape, axis):
    return lax.broadcasted_iota(jnp.int32, shape, axis)


def pick_row(mask, values):
    return jnp.sum(jnp.where(mask, values, 0.0), axis=0, keepdims=True)


def kernel(
    slabs, members,
    images, volume, columns, precision_in, poses_in, keys_in, voxels_in, weights_in,
    fourier, shares_out,
    images_v, volume_v, columns_v, precision, poses, keys, voxel_of, weight_of,
    slot_table, pack_table, pose_row,
    outgoing, incoming, slices, half_power, ranks, weave,
    picks, picks_in, shares, spread_first, spread_middle, spread_last, row_weight, partial,
    away, away_in, kept, opposite, opposite_in, ring, ring_in,
    masses, inverse, returning, returned, crossing, crossed,
    loads, slab_send, slab_recv, img_send, img_recv,
):
    own = lax.axis_index("slab")
    member = lax.axis_index("img")
    ring_len = members // 2
    chip, core = member // 2, lax.rem(member, 2)
    share = NPOSE // members
    half = share // 2
    side = ring_len * share
    deep = outgoing.shape[1]
    mine = slabs * deep
    cap = keys.shape[2]
    width = volume_v.shape[1]
    voxels = volume_v.shape[0]
    cands = poses.shape[0]
    right = 2 * lax.rem(chip + 1, ring_len) + core
    left = 2 * lax.rem(chip + ring_len - 1, ring_len) + core
    partner = 2 * chip + 1 - core

    def slab_peer(step):
        return lax.rem(own + step, slabs)

    def img_peer(step):
        return lax.rem(member + step, members)

    barrier = pltpu.get_barrier_semaphore()

    def greet(axis, peer):
        pl.semaphore_signal(barrier, inc=1, device_id={axis: peer}, device_id_type=pl.DeviceIdType.MESH)

    sources = [keys_in, voxels_in, weights_in, volume, poses_in, images, precision_in, columns]
    targets = [keys, voxel_of, weight_of, volume_v, poses, images_v, precision, columns_v]
    load = [pltpu.make_async_copy(src, dst, loads.at[i]) for i, (src, dst) in enumerate(zip(sources, targets))]

    def start_load(index):
        src, dst = sources[index], targets[index]
        pieces = 8 if src.shape[0] >= 512 else 1
        size = src.shape[0] // pieces
        for piece in range(pieces):
            at = slice(piece * size, (piece + 1) * size)
            pltpu.make_async_copy(src.at[at], dst.at[at], loads.at[index]).start()

    for index in range(5):
        start_load(index)
    for step in range(1, slabs):
        greet("slab", slab_peer(step))
    for step in range(1, members):
        greet("img", img_peer(step))

    for index in range(3):
        load[index].wait()
    before = jnp.zeros((slabs, cap), F32)
    for slab in range(slabs):
        before += jnp.where(keys[slab] >= 0, 1.0, 0.0) * jnp.where(own > slab, 1.0, 0.0)
    out_start = jnp.sum(before, axis=1, keepdims=True)
    total_slots = slabs * cap
    own_key = keys[own]
    own_code = voxel_of[own] * 32 + jnp.where(own_key >= 0, weight_of[own], 31)

    def ordered(first, count, tables):
        position = iota((1, count), 1) + first
        block_sel = iota((slabs, count), 0) == ((position >> 3) & (slabs - 1))
        start_row = pick_row(block_sel, out_start).astype(jnp.int32)
        slot_row = members * (position & 7) + (((position >> 7) - start_row) & 7)
        slot_sel = iota((cap, count), 0) == slot_row
        chooser = jnp.where(block_sel, 1.0, 0.0)
        found = []
        for table in tables:
            wide = lax.dot_general(
                table.astype(F32), chooser, (((0,), (0,)), ((), ())),
                precision=lax.Precision.HIGHEST, preferred_element_type=F32,
            )
            found.append(pick_row(slot_sel, wide))
        return found

    def decoded(code):
        code_row = code.astype(jnp.int32)
        level = code_row & 31
        alive = level <= WSTEPS
        spot = (code_row >> 5).astype(F32)
        lower = jnp.where(alive, level, 0).astype(F32) * (1.0 / WSTEPS)
        upper = jnp.where(alive, WSTEPS - level, 0).astype(F32) * (1.0 / WSTEPS)
        return spot, lower, upper

    parts = decoded(ordered(member * mine, mine, [own_code])[0])
    own_cols = jnp.concatenate(list(parts) + [jnp.zeros((5, mine), F32)], axis=0).T
    place = iota((mine, voxels), 1)
    spot = own_cols[:, 0:1].astype(jnp.int32)
    take = jnp.where(place == spot, own_cols[:, 1:2], 0.0) + jnp.where(place == spot + 1, own_cols[:, 2:3], 0.0)
    load[3].wait()
    for index in range(5, len(load)):
        start_load(index)
    woven = dot(take.astype(BF16), volume_v[...])
    for block in range(slabs):
        outgoing[block] = woven[block * deep : (block + 1) * deep].astype(BF16)
    pl.semaphore_wait(barrier, slabs - 1 + members - 1)

    def slab_copy(stage, src, dst, peer):
        return remote(src.at[peer], dst.at[own], slab_send.at[stage], slab_recv.at[stage], {"slab": peer})

    def slab_whole(stage, ref, count):
        blocks = ref.at[0:count]
        return remote(blocks, blocks, slab_send.at[stage], slab_recv.at[stage], {"slab": slab_peer(1)})

    def slab_exchange(stage, src, dst):
        for step in range(1, slabs):
            slab_copy(stage, src, dst, slab_peer(step)).start()

    def slab_arrivals(stage, dst):
        slab_whole(stage, dst, slabs - 1).wait_recv()

    def img_copy(slot, src, dst, device):
        return remote(src, dst, img_send.at[slot], img_recv.at[slot], {"img": device})

    slab_exchange(0, outgoing, incoming)
    incoming[own] = outgoing[own]

    code, key_row = ordered(0, total_slots, [own_code, own_key])
    for index, value in enumerate(decoded(code) + (key_row,)):
        slot_table[index : index + 1, :] = value
    slot_table[4:8, :] = jnp.zeros((4, total_slots), F32)

    in_key = jnp.concatenate(
        [jnp.sum(jnp.where(iota((slabs, cap), 0) == own, keys[slab], 0), axis=0, keepdims=True) for slab in range(slabs)],
        axis=0,
    )
    live = jnp.where(in_key >= 0, 1.0, 0.0).astype(BF16)
    count = dot(live, jnp.ones((cap, LANES), BF16))
    earlier = jnp.where(iota((slabs, slabs), 1) < iota((slabs, slabs), 0), 1.0, 0.0).astype(BF16)
    start = dot(earlier, count.astype(BF16))
    lane = iota((1, mine), 1)
    slab_sel = iota((slabs, mine), 0) == (lane >> 3)
    in_start = pick_row(slab_sel, start).astype(jnp.int32)
    in_count = pick_row(slab_sel, count).astype(jnp.int32)
    slot = members * (lane & 7) + ((member - in_start) & 7)
    pack_row = jnp.where(slot < in_count, (in_start + slot) >> 3, -1)
    pack_table[...] = jnp.broadcast_to(pack_row, (8, mine)).astype(F32)

    number = start[:, :cap].astype(jnp.int32) + iota((slabs, cap), 1)
    holder = number & (members - 1)
    ahead = ((holder >> 1) - chip) & (ring_len - 1)
    near = jnp.where(ahead == 0, 3, jnp.where(ahead == 1, 1, jnp.where(ahead == 2, 0, 2)))
    row = jnp.where((holder & 1) == core, near, members - 1 - near) * share + (number >> 3)
    key_cols, row_cols = in_key.astype(F32).T, row.astype(F32).T
    pose_ids = iota((cap, NPOSE), 1).astype(F32)
    found_rows = jnp.zeros((cap, NPOSE), F32)
    for slab in range(slabs):
        found_rows += jnp.where(key_cols[:, slab : slab + 1] == pose_ids, row_cols[:, slab : slab + 1], 0.0)
    pose_row[...] = jnp.broadcast_to(jnp.sum(found_rows, axis=0, keepdims=True), (8, NPOSE)).astype(jnp.int32)

    load[4].wait()
    for part in range(poses.shape[1] // LANES):
        for k in range(0, cands, 8):
            at = (slice(k, k + 8), slice(part * LANES, (part + 1) * LANES))
            pose = poses[at]
            low, high = pose & (LANES - 1), pose >> 7
            renamed = jnp.zeros_like(pose)
            for piece in range(NPOSE // LANES):
                table = pose_row[:, piece * LANES : (piece + 1) * LANES]
                found = jnp.take_along_axis(table, low, axis=1, mode="promise_in_bounds")
                renamed = jnp.where(high == piece, found, renamed)
            poses[at] = renamed

    first_chunks = 3
    ahead_of = 2 * first_chunks
    middle = (slabs + ahead_of) // 2
    turn = jnp.where(own >= ahead_of, 1, 0)

    def rank_chunk(block):
        at = rows_at(block * LANES, LANES)
        number = poses[:, at].astype(jnp.int16)
        for first in range(0, NPOSE, LANES):
            row = (iota((LANES, LANES), 0) + first).astype(jnp.int16)
            value = jnp.full((LANES, LANES), cands, jnp.int16)
            for k in range(cands):
                value = jnp.where(number[k : k + 1] == row, jnp.int16(k), value)
            ranks[first : first + LANES, at] = value.astype(jnp.int32)

    each(slabs, rank_chunk, ahead_of)

    slab_arrivals(0, incoming)
    arrived = jnp.concatenate([incoming[block].astype(F32) for block in range(slabs)], axis=0).astype(BF16)
    pack = jnp.where(iota((share, mine), 0).astype(F32) == pack_table[0:1, :], 1.0, 0.0).astype(BF16)

    def block_of(index, first=0, size=share):
        return slices.at[index * share + first : index * share + first + size]

    FAR, RIGHT, LEFT, HOME = 0, 1, 2, 3
    slices[HOME * share : (HOME + 1) * share, :] = dot(pack, arrived).astype(BF16)

    def other(index):
        return members - 1 - index

    def top(index):
        return block_of(index, 0, half)

    def bottom(index):
        return block_of(index, half, half)

    gathers = [
        img_copy(0, top(HOME), top(LEFT), right),
        img_copy(1, bottom(HOME), bottom(RIGHT), left),
        img_copy(2, block_of(HOME), block_of(other(HOME)), partner),
        img_copy(3, bottom(HOME), bottom(LEFT), right),
        img_copy(4, top(HOME), top(RIGHT), left),
        img_copy(5, top(LEFT), top(FAR), right),
        img_copy(6, bottom(RIGHT), bottom(FAR), left),
        img_copy(7, block_of(LEFT), block_of(other(LEFT)), partner),
        img_copy(8, block_of(RIGHT), block_of(other(RIGHT)), partner),
        img_copy(9, top(FAR), top(other(FAR)), partner),
        img_copy(10, bottom(FAR), bottom(other(FAR)), partner),
    ]
    for index in range(5):
        gathers[index].start()

    def weave_step(index):
        at = rows_at(index * LANES, LANES)
        cols = slot_table[:, at].T
        spots = cols[:, 0:1].astype(jnp.int32)
        voxel = iota((LANES, voxels), 1)
        value = jnp.where(voxel == spots, cols[:, 1:2], 0.0) + jnp.where(voxel == spots + 1, cols[:, 2:3], 0.0)
        weave[at, :] = value.astype(BF16)

    each(total_slots // LANES, weave_step)
    gathers[0].wait_recv()
    gathers[5].start()
    gathers[1].wait_recv()
    gathers[6].start()
    gathers[3].wait_recv()
    gathers[7].start()
    gathers[4].wait_recv()
    gathers[8].start()
    load[5].wait()

    def power_step(index):
        at = rows_at(index * share, share)
        values = slices[at, :].astype(F32)
        total = 0.5 * jnp.sum(values * values, axis=1, keepdims=True)
        half_power[at, :] = jnp.broadcast_to(total, (share, LANES))

    chunk = 2 * LANES
    chunks = images_v.shape[0] // chunk

    def picks_of(score, pieces, numbers, value):
        for first, offset, size in pieces:
            block = score[offset : offset + size] - half_power[first : first + size, :]
            for group in range(size // 8):
                picked = jnp.take_along_axis(
                    block[group * 8 : (group + 1) * 8], numbers[0], axis=0, mode="promise_in_bounds"
                )
                value[0] = jnp.where(numbers[2] == first // 8 + group, picked, value[0])
                picked = jnp.take_along_axis(
                    block[group * 8 : (group + 1) * 8], numbers[1], axis=0, mode="promise_in_bounds"
                )
                value[1] = jnp.where(numbers[3] == first // 8 + group, picked, value[1])
        return value

    def score_chunk(index, table, pieces, resume):
        score = lax.dot_general(
            table, images_v[rows_at(index * chunk, chunk), :],
            (((1,), (1,)), ((), ())), preferred_element_type=F32,
        )
        for part in range(chunk // LANES):
            number = poses[:, rows_at(index * chunk + part * LANES, LANES)]
            numbers = [number[0:8] & 7, number[8:16] & 7, number[0:8] >> 3, number[8:16] >> 3]
            block = index * (chunk // LANES) + part
            if resume:
                value = [picks[block, 0:8], picks[block, 8:16]]
            else:
                value = [jnp.zeros((8, LANES), F32), jnp.zeros((8, LANES), F32)]
            value = picks_of(score[:, part * LANES : (part + 1) * LANES], pieces, numbers, value)
            picks[block] = jnp.concatenate(value, axis=0)

    def near_step(index):
        score_chunk(index, slices[share : NPOSE - share, :], [(share, 0, NPOSE - 2 * share)], False)

    def far_chunk(index):
        table = jnp.concatenate([slices[0:share, :], slices[NPOSE - share : NPOSE, :]], axis=0)
        score_chunk(index, table, [(0, 0, share), (NPOSE - share, share, share)], True)

    def full_chunk(index):
        score_chunk(index, slices[...], [(0, 0, NPOSE)], False)

    gathers[2].wait_recv()
    gathers[7].wait_recv()
    gathers[8].wait_recv()
    each(members - 1, power_step, 1)
    each(first_chunks - 1, near_step)
    gathers[5].wait_recv()
    gathers[9].start()
    gathers[6].wait_recv()
    gathers[10].start()
    each(first_chunks, near_step, first_chunks - 1)
    gathers[9].wait_recv()
    gathers[10].wait_recv()
    power_step(0)
    power_step(members - 1)

    def pick_send(peer):
        @pl.when(peer != own)
        def _():
            slab_copy(1, picks, picks_in, peer).start()

    def far_step(index):
        far_chunk(index)
        pick_send(2 * index)
        pick_send(2 * index + 1)

    def full_step(index):
        full_chunk(index)
        pick_send(2 * index)
        pick_send(2 * index + 1)

    each(first_chunks, far_step)
    each(chunks, full_step, first_chunks)
    picks_in[own] = picks[own]
    load[6].wait()
    row_weight[...] = jnp.zeros_like(row_weight)
    masses[member] = jnp.zeros((8, LANES), F32)

    def share_out():
        slab_arrivals(1, picks_in)
        total = picks_in[0]
        for block in range(1, slabs):
            total = total + picks_in[block]
        total = total * precision[:, rows_at(own * LANES, LANES)]
        exponent = jnp.exp(total - jnp.max(total, axis=0, keepdims=True))
        shares[own] = exponent / jnp.sum(exponent, axis=0, keepdims=True)
        for step in range(1, slabs):
            remote(
                shares.at[own], shares.at[own], slab_send.at[2], slab_recv.at[5 + turn], {"slab": slab_peer(step)}
            ).start()

    @pl.when(turn == 0)
    def _():
        share_out()

    each(ahead_of, rank_chunk)

    @pl.when(turn != 0)
    def _():
        share_out()

    def shares_arrive(which):
        group = ahead_of if which == 0 else slabs - ahead_of

        @pl.when(turn == which)
        def _():
            slab_whole(5 + which, shares, group - 1).wait_recv()

        @pl.when(turn != which)
        def _():
            slab_whole(5 + which, shares, group).wait_recv()

    def spread_chunk(block, spread, origin):
        at = rows_at(block * LANES, LANES)
        to = rows_at((block - origin) * LANES, LANES)
        amount = shares[block] * precision[:, at]
        rounded = amount.astype(BF16).astype(F32)
        low, high = rounded[0:8], rounded[8:16]
        for first in range(0, NPOSE, 16):
            values = []
            for group in (first, first + 8):
                rank = ranks[group : group + 8, at]
                place = rank & 7
                from_low = jnp.take_along_axis(low, place, axis=0, mode="promise_in_bounds")
                from_high = jnp.take_along_axis(high, place, axis=0, mode="promise_in_bounds")
                value = jnp.where(rank < 8, from_low, jnp.where(rank < cands, from_high, 0.0))
                row_weight[group : group + 8, :] += value
                values.append(value)
            spread[first : first + 16, to] = jnp.concatenate(values, axis=0).astype(BF16)

    stripe = 2 * LANES
    halves = 1
    wide = width // halves
    per_half = wide // stripe

    def away_copy(index):
        at = slice(index * stripe, (index + 1) * stripe)
        return img_copy(40 + index, away.at[:, at], away_in.at[:, at], partner)

    def back_stripe(index):
        at = slice(index * stripe, (index + 1) * stripe)
        part = partial[:, at] + dot(spread_last[...], images_v[middle * LANES :, at])
        away[:, at] = part[side:].astype(BF16)
        away_copy(index).start()
        kept[:, at] = part[:side]

    def columns_of(part):
        return slice(part * wide, (part + 1) * wide)

    def kept_part(index, part, first=0, size=share):
        here = index * share + first
        there = (ring_len - 1 - index) * share + first
        at = columns_of(part)
        return kept[here : here + size, at] + away_in[there : there + size, at].astype(F32)

    def ring_copy(part, index):
        at = columns_of(part)
        low, high = slice(0, half), slice(half, share)
        refs = [
            (opposite.at[low, at], opposite_in.at[low, at], right),
            (opposite.at[high, at], opposite_in.at[high, at], left),
            (ring.at[0, high, at], ring_in.at[0, high, at], right),
            (ring.at[1, low, at], ring_in.at[1, low, at], left),
            (ring.at[0, low, at], ring_in.at[0, low, at], right),
            (ring.at[1, high, at], ring_in.at[1, high, at], left),
        ]
        return img_copy(48 + 6 * part + index, *refs[index])

    def ring_start(part):
        at = columns_of(part)
        for index in range(part * per_half, (part + 1) * per_half):
            away_copy(index).wait_recv()
        opposite[:, at] = kept_part(FAR, part).astype(BF16)
        ring_copy(part, 0).start()
        ring_copy(part, 1).start()
        ring[0, half:share, at] = kept_part(RIGHT, part, half, half).astype(BF16)
        ring_copy(part, 2).start()
        ring[1, 0:half, at] = kept_part(LEFT, part, 0, half).astype(BF16)
        ring_copy(part, 3).start()

    def ring_relay(part):
        at = columns_of(part)
        ring_copy(part, 0).wait_recv()
        ring[0, 0:half, at] = (kept_part(RIGHT, part, 0, half) + opposite_in[0:half, at].astype(F32)).astype(BF16)
        ring_copy(part, 4).start()
        ring_copy(part, 1).wait_recv()
        ring[1, half:share, at] = (
            kept_part(LEFT, part, half, half) + opposite_in[half:share, at].astype(F32)
        ).astype(BF16)
        ring_copy(part, 5).start()

    unpack = jnp.where(pack_table[...].T[:, 0:1] == iota((mine, share), 1).astype(F32), 1.0, 0.0).astype(BF16)

    def ring_finish(part):
        at = columns_of(part)
        held = kept_part(HOME, part)
        for index in range(2, 6):
            ring_copy(part, index).wait_recv()
        summed = (held + ring_in[0, :, at].astype(F32) + ring_in[1, :, at].astype(F32)).astype(BF16)
        unpacked = dot(unpack, summed)
        for block in range(slabs):
            returning[part, block] = unpacked[block * deep : (block + 1) * deep].astype(BF16)
        slab_exchange(3 + part, returning.at[part], returned.at[part])
        returned[part, own] = returning[part, own]

    def early_stripe(index):
        at = rows_at(index * stripe, stripe)
        partial[:, at] = dot(spread_first[...], images_v[: ahead_of * LANES, at])

    shares_arrive(0)
    each(ahead_of, lambda block: spread_chunk(block, spread_first, 0))
    each(width // stripe, early_stripe)
    shares_arrive(1)
    each(middle, lambda block: spread_chunk(block, spread_middle, ahead_of), ahead_of)
    waiting = list(range(middle, slabs))
    for index in range(width // stripe):
        at = slice(index * stripe, (index + 1) * stripe)
        partial[:, at] += dot(spread_middle[...], images_v[ahead_of * LANES : middle * LANES, at])
        for block in waiting[index :: width // stripe]:
            spread_chunk(block, spread_last, middle)

    weight = jnp.sum(row_weight[...], axis=1, keepdims=True)
    mass_row = pick_row(iota((NPOSE, NPOSE), 0) == pose_row[0:1, :], weight)
    for piece in range(NPOSE // LANES):
        masses[member, piece : piece + 1, :] = mass_row[:, piece * LANES : (piece + 1) * LANES]

    def mass_copy(step):
        return img_copy(16, masses.at[member], masses.at[member], img_peer(step))

    def img_whole(slot, ref):
        blocks = ref.at[0 : members - 1]
        return img_copy(slot, blocks, blocks, img_peer(1))

    for step in range(1, members):
        mass_copy(step).start()
    for index in range(width // stripe):
        back_stripe(index)
    ring_start(0)
    ring_relay(0)
    ring_finish(0)
    shares_copy = pltpu.make_async_copy(shares, shares_out, loads.at[8])
    shares_copy.start()

    img_whole(16, masses).wait_recv()
    mass_sum = masses[0]
    for index in range(1, members):
        mass_sum = mass_sum + masses[index]
    mass_cols = mass_sum.T
    amount = jnp.zeros((1, total_slots), F32)
    for piece in range(NPOSE // LANES):
        pose = (iota((LANES, total_slots), 0) + piece * LANES).astype(F32)
        amount += pick_row(slot_table[3:4, :] == pose, mass_cols[:, piece : piece + 1])
    first = amount.astype(BF16).astype(F32)
    second = (amount - first).astype(BF16).astype(F32)
    pieces = [first, second, amount - first - second, jnp.zeros((13, total_slots), F32)]
    mass = dot(jnp.concatenate(pieces, axis=0).astype(BF16), weave[...])
    inverse[...] = 1.0 / (jnp.sum(mass, axis=0, keepdims=True) + RIDGE)
    load[7].wait()

    turned = jnp.zeros((mine, width), F32)
    for part in range(halves):
        slab_arrivals(3 + part, returned.at[part])
        gathered = jnp.concatenate([returned[part, block].astype(F32) for block in range(slabs)], axis=0)
        turned += dot(gathered.astype(BF16), columns_v[columns_of(part), :])
    for block in range(members):
        crossing[block] = turned[:, block * LANES : (block + 1) * LANES].T.astype(BF16)

    def cross_copy(step):
        peer = img_peer(step)
        return img_copy(17, crossing.at[peer], crossed.at[member], peer)

    for step in range(1, members):
        cross_copy(step).start()
    crossed[member] = crossing[member]

    for stage, ref in ((0, outgoing), (1, picks), (2, shares), (3, returning.at[0])):
        slab_whole(stage, ref, slabs - 1).wait_send()
    for copy in gathers:
        copy.wait_send()
    for index in range(halves * per_half):
        away_copy(index).wait_send()
    for part in range(halves):
        for index in range(6):
            ring_copy(part, index).wait_send()
    img_whole(16, masses).wait_send()
    img_whole(17, crossed).wait_recv()

    slots = jnp.concatenate([crossed[block] for block in range(members)], axis=1)
    fourier[...] = (dot(slots, weave[...]) * inverse[...]).astype(BF16)
    shares_copy.wait()
    img_whole(17, crossing).wait_send()


def finish(rows, fourier, shares, density, posterior):
    planes, columns_out, edge = density.shape
    real = jnp.concatenate([fourier[:columns_out, z * edge : (z + 1) * edge] for z in range(planes)], axis=0)
    imag = jnp.concatenate([fourier[columns_out:, z * edge : (z + 1) * edge] for z in range(planes)], axis=0)
    value = dot(real, rows[:edge, :]) + dot(imag, rows[edge:, :])
    for z in range(planes):
        density[z] = value[z * columns_out : (z + 1) * columns_out]
    for block in range(shares.shape[0]):
        posterior[:, block * LANES : (block + 1) * LANES] = shares[block]


def per_device(images, volume, precision, candidates, slot_key, slot_voxel, slot_weight):
    members = lax.axis_size("img")
    slabs = lax.axis_size("slab")
    planes, edge, width = volume.shape
    particles, cands = candidates.shape
    cap = slot_key.shape[2]
    deep = cap // members
    share = NPOSE // members
    voxels = planes * edge
    mine = slabs * deep
    side = NPOSE // 2
    big = pl.BlockSpec(memory_space=pl.ANY)
    near = pl.BlockSpec(memory_space=pltpu.VMEM)
    scratch = [
        pltpu.VMEM((particles, width), BF16),
        pltpu.VMEM((voxels, width), BF16),
        pltpu.VMEM((width, width), BF16),
        pltpu.VMEM((1, particles), F32),
        pltpu.VMEM((cands, particles), jnp.int32),
        pltpu.VMEM(slot_key.shape, jnp.int32),
        pltpu.VMEM(slot_key.shape, jnp.int32),
        pltpu.VMEM(slot_key.shape, jnp.int32),
        pltpu.VMEM((8, slabs * cap), F32),
        pltpu.VMEM((8, mine), F32),
        pltpu.VMEM((8, NPOSE), jnp.int32),
        pltpu.VMEM((slabs, deep, width), BF16),
        pltpu.VMEM((slabs, deep, width), BF16),
        pltpu.VMEM((NPOSE, width), BF16),
        pltpu.VMEM((NPOSE, LANES), F32),
        pltpu.VMEM((NPOSE, particles), jnp.int32),
        pltpu.VMEM((slabs * cap, voxels), BF16),
        pltpu.VMEM((slabs, cands, LANES), F32),
        pltpu.VMEM((slabs, cands, LANES), F32),
        pltpu.VMEM((slabs, cands, LANES), F32),
        pltpu.VMEM((NPOSE, 6 * LANES), BF16),
        pltpu.VMEM((NPOSE, 5 * LANES), BF16),
        pltpu.VMEM((NPOSE, 5 * LANES), BF16),
        pltpu.VMEM((NPOSE, LANES), F32),
        pltpu.VMEM((NPOSE, width), F32),
        pltpu.VMEM((side, width), BF16),
        pltpu.VMEM((side, width), BF16),
        pltpu.VMEM((side, width), F32),
        pltpu.VMEM((share, width), BF16),
        pltpu.VMEM((share, width), BF16),
        pltpu.VMEM((2, share, width), BF16),
        pltpu.VMEM((2, share, width), BF16),
        pltpu.VMEM((members, 8, LANES), F32),
        pltpu.VMEM((1, voxels), F32),
        pltpu.VMEM((1, slabs, deep, width), BF16),
        pltpu.VMEM((1, slabs, deep, width), BF16),
        pltpu.VMEM((members, mine, LANES), BF16),
        pltpu.VMEM((members, mine, LANES), BF16),
        pltpu.SemaphoreType.DMA((9,)),
        pltpu.SemaphoreType.DMA((7,)),
        pltpu.SemaphoreType.DMA((7,)),
        pltpu.SemaphoreType.DMA((60,)),
        pltpu.SemaphoreType.DMA((60,)),
    ]
    fourier, shares = pl.pallas_call(
        functools.partial(kernel, slabs, members),
        out_shape=(
            jax.ShapeDtypeStruct((LANES, voxels), BF16),
            jax.ShapeDtypeStruct((slabs, cands, LANES), F32),
        ),
        in_specs=[big] * 8,
        out_specs=(near, big),
        scratch_shapes=scratch,
        compiler_params=pltpu.CompilerParams(
            collective_id=0, has_side_effects=True, vmem_limit_bytes=56 * 1024 * 1024
        ),
    )(
        images, volume.reshape(voxels, width), column_table(edge, members),
        precision[None, :], candidates.T, slot_key, slot_voxel, slot_weight,
    )
    density, posterior = pl.pallas_call(
        finish,
        out_shape=(
            jax.ShapeDtypeStruct((planes, edge // members, edge), F32),
            jax.ShapeDtypeStruct((cands, particles), F32),
        ),
        in_specs=[near] * 3,
        out_specs=(near, near),
        compiler_params=pltpu.CompilerParams(vmem_limit_bytes=56 * 1024 * 1024),
    )(row_table(edge), fourier, shares)
    return density.transpose(0, 2, 1), posterior.T


def solution(mesh):
    placed = (P("img", "slab"), P("slab", None, None), P("img"), P("img", None), P(), P(), P())
    return jax.shard_map(
        per_device,
        mesh=mesh,
        in_specs=placed,
        out_specs=(P("slab", None, "img"), P("img", None)),
        check_vma=False,
    )
```

```python
import functools
import math

import jax
import jax.numpy as jnp
import numpy as np
from jax import lax
from jax.experimental import pallas as pl
from jax.experimental.pallas import tpu as pltpu
from jax.sharding import PartitionSpec as P

NPOSE = 512
WSTEPS = 16
RIDGE = 0.25
LANES = 128
F32 = jnp.float32
BF16 = jnp.bfloat16


def gridding(samples):
    offset = (np.arange(samples) - samples / 2) / samples
    return 1.0 / np.sinc(offset) ** 2


def angles(length):
    counter = np.arange(length)
    return (counter[:, None] * counter[None, :] % length) * (2.0 * math.pi / length)


def column_table(length, members):
    turn = angles(length)
    cosine, sine = np.cos(turn), np.sin(turn)
    scale = gridding(length)[None, :]
    to_re = np.concatenate([cosine, -sine], axis=0) * scale
    to_im = np.concatenate([sine, cosine], axis=0) * scale
    width = length // members
    both = np.stack([to_re.reshape(-1, members, width), to_im.reshape(-1, members, width)], axis=2)
    return jnp.asarray(both.reshape(2 * length, 2 * length), BF16)


def row_table(length):
    turn = angles(length)
    scale = gridding(length)[None, :] / length
    return jnp.asarray(np.concatenate([np.cos(turn), -np.sin(turn)], axis=0) * scale, BF16)


def remote(src, dst, sends, recvs, device):
    return pltpu.make_async_remote_copy(
        src_ref=src,
        dst_ref=dst,
        send_sem=sends,
        recv_sem=recvs,
        device_id=device,
        device_id_type=pl.DeviceIdType.MESH,
    )


def dot(left, right):
    return jnp.dot(left, right, preferred_element_type=F32)


def each(count, step, first=0):
    def body(index, carry):
        step(index)
        return carry

    lax.fori_loop(first, count, body, 0)


def rows_at(start, size):
    return pl.ds(pl.multiple_of(start, size), size)


def iota(shape, axis):
    return lax.broadcasted_iota(jnp.int32, shape, axis)


def pick_row(mask, values):
    return jnp.sum(jnp.where(mask, values, 0.0), axis=0, keepdims=True)


def kernel(
    slabs, members,
    images, volume, columns, precision_in, poses_in, keys_in, voxels_in, weights_in,
    fourier, shares_out,
    images_v, volume_v, columns_v, precision, poses, keys, voxel_of, weight_of,
    pack_table, pose_row, named, unpack,
    outgoing, incoming, slices, half_power, ranks, weave,
    picks, picks_in, shares, spread_first, spread_middle, spread_last, row_weight, partial, back,
    away, away_in, kept, opposite, opposite_in, ring, ring_in,
    masses, inverse, returning, returned,
    loads, slab_send, slab_recv, img_send, img_recv,
):
    own = lax.axis_index("slab")
    member = lax.axis_index("img")
    ring_len = members // 2
    chip, core = member // 2, lax.rem(member, 2)
    share = NPOSE // members
    half = share // 2
    side = ring_len * share
    deep = outgoing.shape[1]
    mine = slabs * deep
    cap = keys.shape[2]
    width = volume_v.shape[1]
    voxels = volume_v.shape[0]
    cands = poses.shape[0]
    right = 2 * lax.rem(chip + 1, ring_len) + core
    left = 2 * lax.rem(chip + ring_len - 1, ring_len) + core
    partner = 2 * chip + 1 - core

    def slab_peer(step):
        return lax.rem(own + step, slabs)

    def img_peer(step):
        return lax.rem(member + step, members)

    barrier = pltpu.get_barrier_semaphore()

    def greet(axis, peer):
        pl.semaphore_signal(barrier, inc=1, device_id={axis: peer}, device_id_type=pl.DeviceIdType.MESH)

    sources = [keys_in, voxels_in, weights_in, volume, poses_in, images, precision_in, columns]
    targets = [keys, voxel_of, weight_of, volume_v, poses, images_v, precision, columns_v]
    load = [pltpu.make_async_copy(src, dst, loads.at[i]) for i, (src, dst) in enumerate(zip(sources, targets))]

    def start_load(index):
        src, dst = sources[index], targets[index]
        pieces = 8 if src.shape[0] >= 512 else 1
        size = src.shape[0] // pieces
        for piece in range(pieces):
            at = slice(piece * size, (piece + 1) * size)
            pltpu.make_async_copy(src.at[at], dst.at[at], loads.at[index]).start()

    for index in range(5):
        start_load(index)
    for step in range(1, slabs):
        greet("slab", slab_peer(step))
    for step in range(1, members):
        greet("img", img_peer(step))

    for index in range(3):
        load[index].wait()
    before = jnp.zeros((slabs, cap), F32)
    for slab in range(slabs):
        before += jnp.where(keys[slab] >= 0, 1.0, 0.0) * jnp.where(own > slab, 1.0, 0.0)
    out_start = jnp.sum(before, axis=1, keepdims=True)
    total_slots = slabs * cap
    own_key = keys[own]
    own_code = voxel_of[own] * 32 + jnp.where(own_key >= 0, weight_of[own], 31)

    def ordered(first, count, tables):
        position = iota((1, count), 1) + first
        block_sel = iota((slabs, count), 0) == ((position >> 3) & (slabs - 1))
        start_row = pick_row(block_sel, out_start).astype(jnp.int32)
        slot_row = members * (position & 7) + (((position >> 7) - start_row) & 7)
        slot_sel = iota((cap, count), 0) == slot_row
        chooser = jnp.where(block_sel, 1.0, 0.0)
        found = []
        for table in tables:
            wide = lax.dot_general(
                table.astype(F32), chooser, (((0,), (0,)), ((), ())),
                precision=lax.Precision.HIGHEST, preferred_element_type=F32,
            )
            found.append(pick_row(slot_sel, wide))
        return found

    def decoded(code):
        code_row = code.astype(jnp.int32)
        level = code_row & 31
        alive = level <= WSTEPS
        spot = (code_row >> 5).astype(F32)
        lower = jnp.where(alive, level, 0).astype(F32) * (1.0 / WSTEPS)
        upper = jnp.where(alive, WSTEPS - level, 0).astype(F32) * (1.0 / WSTEPS)
        return spot, lower, upper

    parts = decoded(ordered(member * mine, mine, [own_code])[0])
    own_cols = jnp.concatenate(list(parts) + [jnp.zeros((5, mine), F32)], axis=0).T
    place = iota((mine, voxels), 1)
    spot = own_cols[:, 0:1].astype(jnp.int32)
    take = jnp.where(place == spot, own_cols[:, 1:2], 0.0) + jnp.where(place == spot + 1, own_cols[:, 2:3], 0.0)
    load[3].wait()
    for index in range(5, len(load)):
        start_load(index)
    woven = dot(take.astype(BF16), volume_v[...])
    for block in range(slabs):
        outgoing[block] = woven[block * deep : (block + 1) * deep].astype(BF16)
    pl.semaphore_wait(barrier, slabs - 1 + members - 1)

    def slab_copy(stage, src, dst, peer):
        return remote(src.at[peer], dst.at[own], slab_send.at[stage], slab_recv.at[stage], {"slab": peer})

    def slab_whole(stage, ref, count):
        blocks = ref.at[0:count]
        return remote(blocks, blocks, slab_send.at[stage], slab_recv.at[stage], {"slab": slab_peer(1)})

    def slab_exchange(stage, src, dst):
        for step in range(1, slabs):
            slab_copy(stage, src, dst, slab_peer(step)).start()

    def slab_arrivals(stage, dst):
        slab_whole(stage, dst, slabs - 1).wait_recv()

    def img_copy(slot, src, dst, device):
        return remote(src, dst, img_send.at[slot], img_recv.at[slot], {"img": device})

    slab_exchange(0, outgoing, incoming)
    incoming[own] = outgoing[own]

    in_key = jnp.concatenate(
        [jnp.sum(jnp.where(iota((slabs, cap), 0) == own, keys[slab], 0), axis=0, keepdims=True) for slab in range(slabs)],
        axis=0,
    )
    live = jnp.where(in_key >= 0, 1.0, 0.0).astype(BF16)
    count = dot(live, jnp.ones((cap, LANES), BF16))
    earlier = jnp.where(iota((slabs, slabs), 1) < iota((slabs, slabs), 0), 1.0, 0.0).astype(BF16)
    start = dot(earlier, count.astype(BF16))
    lane = iota((1, mine), 1)
    slab_sel = iota((slabs, mine), 0) == (lane >> 3)
    in_start = pick_row(slab_sel, start).astype(jnp.int32)
    in_count = pick_row(slab_sel, count).astype(jnp.int32)
    slot = members * (lane & 7) + ((member - in_start) & 7)
    pack_row = jnp.where(slot < in_count, (in_start + slot) >> 3, -1)
    pack_table[...] = jnp.broadcast_to(pack_row, (8, mine)).astype(F32)

    number = start[:, :cap].astype(jnp.int32) + iota((slabs, cap), 1)
    holder = number & (members - 1)
    ahead = ((holder >> 1) - chip) & (ring_len - 1)
    near = jnp.where(ahead == 0, 3, jnp.where(ahead == 1, 1, jnp.where(ahead == 2, 0, 2)))
    row = jnp.where((holder & 1) == core, near, members - 1 - near) * share + (number >> 3)
    key_cols, row_cols = in_key.astype(F32).T, row.astype(F32).T
    pose_ids = iota((cap, NPOSE), 1).astype(F32)
    found_rows = jnp.zeros((cap, NPOSE), F32)
    for slab in range(slabs):
        matched = key_cols[:, slab : slab + 1] == pose_ids
        found_rows += jnp.where(matched, row_cols[:, slab : slab + 1], 0.0)
        unpack[slab * cap : (slab + 1) * cap, :] = jnp.where(matched, 1.0, 0.0).astype(BF16)
    pose_row[...] = jnp.broadcast_to(jnp.sum(found_rows, axis=0, keepdims=True), (8, NPOSE)).astype(jnp.int32)

    load[4].wait()
    for part in range(poses.shape[1] // LANES):
        for k in range(0, cands, 8):
            at = (slice(k, k + 8), slice(part * LANES, (part + 1) * LANES))
            pose = poses[at]
            low, high = pose & (LANES - 1), pose >> 7
            renamed = jnp.zeros_like(pose)
            for piece in range(NPOSE // LANES):
                table = pose_row[:, piece * LANES : (piece + 1) * LANES]
                found = jnp.take_along_axis(table, low, axis=1, mode="promise_in_bounds")
                renamed = jnp.where(high == piece, found, renamed)
            named[at] = renamed

    first_chunks = 3
    ahead_of = 2 * first_chunks
    middle = (slabs + ahead_of) // 2
    turn = jnp.where(own >= ahead_of, 1, 0)

    def rank_chunk(block):
        at = rows_at(block * LANES, LANES)
        number = poses[:, at].astype(jnp.int16)
        for first in range(0, NPOSE, LANES):
            row = (iota((LANES, LANES), 0) + first).astype(jnp.int16)
            value = jnp.full((LANES, LANES), cands, jnp.int16)
            for k in range(cands):
                value = jnp.where(number[k : k + 1] == row, jnp.int16(k), value)
            ranks[first : first + LANES, at] = value.astype(jnp.int32)

    each(middle, rank_chunk, ahead_of)

    slab_arrivals(0, incoming)
    arrived = jnp.concatenate([incoming[block].astype(F32) for block in range(slabs)], axis=0).astype(BF16)
    pack = jnp.where(iota((share, mine), 0).astype(F32) == pack_table[0:1, :], 1.0, 0.0).astype(BF16)

    def block_of(index, first=0, size=share):
        return slices.at[index * share + first : index * share + first + size]

    FAR, RIGHT, LEFT, HOME = 0, 1, 2, 3
    slices[HOME * share : (HOME + 1) * share, :] = dot(pack, arrived).astype(BF16)

    def other(index):
        return members - 1 - index

    def top(index):
        return block_of(index, 0, half)

    def bottom(index):
        return block_of(index, half, half)

    gathers = [
        img_copy(0, top(HOME), top(LEFT), right),
        img_copy(1, bottom(HOME), bottom(RIGHT), left),
        img_copy(2, block_of(HOME), block_of(other(HOME)), partner),
        img_copy(3, bottom(HOME), bottom(LEFT), right),
        img_copy(4, top(HOME), top(RIGHT), left),
        img_copy(5, top(LEFT), top(FAR), right),
        img_copy(6, bottom(RIGHT), bottom(FAR), left),
        img_copy(7, block_of(LEFT), block_of(other(LEFT)), partner),
        img_copy(8, block_of(RIGHT), block_of(other(RIGHT)), partner),
        img_copy(9, top(FAR), top(other(FAR)), partner),
        img_copy(10, bottom(FAR), bottom(other(FAR)), partner),
    ]
    for index in range(5):
        gathers[index].start()

    each(slabs, rank_chunk, middle)
    gathers[0].wait_recv()
    gathers[5].start()
    gathers[1].wait_recv()
    gathers[6].start()
    gathers[3].wait_recv()
    gathers[7].start()
    gathers[4].wait_recv()
    gathers[8].start()
    load[5].wait()

    def power_step(index):
        at = rows_at(index * share, share)
        values = slices[at, :].astype(F32)
        total = 0.5 * jnp.sum(values * values, axis=1, keepdims=True)
        half_power[at, :] = jnp.broadcast_to(total, (share, LANES))

    chunk = 2 * LANES
    chunks = images_v.shape[0] // chunk

    def picks_of(score, pieces, numbers, value):
        for first, offset, size in pieces:
            block = score[offset : offset + size] - half_power[first : first + size, :]
            for group in range(size // 8):
                picked = jnp.take_along_axis(
                    block[group * 8 : (group + 1) * 8], numbers[0], axis=0, mode="promise_in_bounds"
                )
                value[0] = jnp.where(numbers[2] == first // 8 + group, picked, value[0])
                picked = jnp.take_along_axis(
                    block[group * 8 : (group + 1) * 8], numbers[1], axis=0, mode="promise_in_bounds"
                )
                value[1] = jnp.where(numbers[3] == first // 8 + group, picked, value[1])
        return value

    def score_chunk(index, table, pieces, resume):
        score = lax.dot_general(
            table, images_v[rows_at(index * chunk, chunk), :],
            (((1,), (1,)), ((), ())), preferred_element_type=F32,
        )
        for part in range(chunk // LANES):
            number = named[:, rows_at(index * chunk + part * LANES, LANES)]
            numbers = [number[0:8] & 7, number[8:16] & 7, number[0:8] >> 3, number[8:16] >> 3]
            block = index * (chunk // LANES) + part
            if resume:
                value = [picks[block, 0:8], picks[block, 8:16]]
            else:
                value = [jnp.zeros((8, LANES), F32), jnp.zeros((8, LANES), F32)]
            value = picks_of(score[:, part * LANES : (part + 1) * LANES], pieces, numbers, value)
            picks[block] = jnp.concatenate(value, axis=0)

    def near_step(index):
        score_chunk(index, slices[share : NPOSE - share, :], [(share, 0, NPOSE - 2 * share)], False)

    def far_chunk(index):
        table = jnp.concatenate([slices[0:share, :], slices[NPOSE - share : NPOSE, :]], axis=0)
        score_chunk(index, table, [(0, 0, share), (NPOSE - share, share, share)], True)

    def full_chunk(index):
        score_chunk(index, slices[...], [(0, 0, NPOSE)], False)

    gathers[2].wait_recv()
    gathers[7].wait_recv()
    gathers[8].wait_recv()
    each(members - 1, power_step, 1)
    each(first_chunks - 1, near_step)
    gathers[5].wait_recv()
    gathers[9].start()
    gathers[6].wait_recv()
    gathers[10].start()
    each(first_chunks, near_step, first_chunks - 1)
    gathers[9].wait_recv()
    gathers[10].wait_recv()
    power_step(0)
    power_step(members - 1)

    def pick_send(peer):
        @pl.when(peer != own)
        def _():
            slab_copy(1, picks, picks_in, peer).start()

    def far_step(index):
        far_chunk(index)
        pick_send(2 * index)
        pick_send(2 * index + 1)

    def full_step(index):
        full_chunk(index)
        pick_send(2 * index)
        pick_send(2 * index + 1)

    each(first_chunks, far_step)
    each(chunks, full_step, first_chunks)
    picks_in[own] = picks[own]
    load[6].wait()
    row_weight[...] = jnp.zeros_like(row_weight)
    masses[member] = jnp.zeros((8, LANES), F32)

    def share_out():
        slab_arrivals(1, picks_in)
        total = picks_in[0]
        for block in range(1, slabs):
            total = total + picks_in[block]
        total = total * precision[:, rows_at(own * LANES, LANES)]
        exponent = jnp.exp(total - jnp.max(total, axis=0, keepdims=True))
        shares[own] = exponent / jnp.sum(exponent, axis=0, keepdims=True)
        for step in range(1, slabs):
            remote(
                shares.at[own], shares.at[own], slab_send.at[2], slab_recv.at[5 + turn], {"slab": slab_peer(step)}
            ).start()

    @pl.when(turn == 0)
    def _():
        share_out()

    each(ahead_of, rank_chunk)

    @pl.when(turn != 0)
    def _():
        share_out()

    def shares_arrive(which):
        group = ahead_of if which == 0 else slabs - ahead_of

        @pl.when(turn == which)
        def _():
            slab_whole(5 + which, shares, group - 1).wait_recv()

        @pl.when(turn != which)
        def _():
            slab_whole(5 + which, shares, group).wait_recv()

    def spread_chunk(block, spread, origin):
        at = rows_at(block * LANES, LANES)
        to = rows_at((block - origin) * LANES, LANES)
        amount = shares[block] * precision[:, at]
        rounded = amount.astype(BF16).astype(F32)
        low, high = rounded[0:8], rounded[8:16]
        for first in range(0, NPOSE, 16):
            values = []
            for group in (first, first + 8):
                rank = ranks[group : group + 8, at]
                place = rank & 7
                from_low = jnp.take_along_axis(low, place, axis=0, mode="promise_in_bounds")
                from_high = jnp.take_along_axis(high, place, axis=0, mode="promise_in_bounds")
                value = jnp.where(rank < 8, from_low, jnp.where(rank < cands, from_high, 0.0))
                row_weight[group : group + 8, :] += value
                values.append(value)
            spread[first : first + 16, to] = jnp.concatenate(values, axis=0).astype(BF16)

    stripe = 2 * LANES

    def early_stripe(index):
        at = rows_at(index * stripe, stripe)
        partial[:, at] = dot(spread_first[...], images_v[: ahead_of * LANES, at])

    shares_arrive(0)
    each(ahead_of, lambda block: spread_chunk(block, spread_first, 0))
    each(width // stripe, early_stripe)
    shares_arrive(1)
    each(middle, lambda block: spread_chunk(block, spread_middle, ahead_of), ahead_of)
    waiting = list(range(middle, slabs))
    for index in range(width // stripe):
        at = slice(index * stripe, (index + 1) * stripe)
        partial[:, at] += dot(spread_middle[...], images_v[ahead_of * LANES : middle * LANES, at])
        for block in waiting[index :: width // stripe]:
            spread_chunk(block, spread_last, middle)

    for piece in range(NPOSE // LANES):
        weight = row_weight[piece * LANES : (piece + 1) * LANES, :].T
        masses[member, piece : piece + 1, :] = jnp.sum(weight, axis=0, keepdims=True)

    def mass_copy(step):
        return img_copy(16, masses.at[member], masses.at[member], img_peer(step))

    def img_whole(slot, ref):
        blocks = ref.at[0 : members - 1]
        return img_copy(slot, blocks, blocks, img_peer(1))

    for step in range(1, members):
        mass_copy(step).start()

    def back_stripe(index):
        at = rows_at(index * stripe, stripe)
        part = partial[:, at] + dot(spread_last[...], images_v[middle * LANES :, at])
        back[:, at] = part.astype(BF16)

    each(width // stripe, back_stripe)
    load[7].wait()
    half_rows = NPOSE // 2

    def away_copy(index):
        return img_copy(40 + index, away.at[index], away_in.at[index], partner)

    def turn_stripe(index, chip_index):
        part = dot(back[...], columns_v[:, rows_at(chip_index * stripe, stripe)])
        first, second = part[:, :LANES], part[:, LANES:]
        kept[index] = jnp.where(core == 0, first, second)
        away[index] = jnp.where(core == 0, second, first).astype(BF16)
        away_copy(index).start()

    def kept_part(index, first=0, size=NPOSE):
        rows = slice(first, first + size)
        return kept[index, rows, :] + away_in[index, rows, :].astype(F32)

    low, high = slice(0, half_rows), slice(half_rows, NPOSE)
    ring_copies = [
        img_copy(48, opposite.at[low], opposite_in.at[low], right),
        img_copy(49, opposite.at[high], opposite_in.at[high], left),
        img_copy(50, ring.at[0, high], ring_in.at[0, high], right),
        img_copy(51, ring.at[1, low], ring_in.at[1, low], left),
        img_copy(52, ring.at[0, low], ring_in.at[0, low], right),
        img_copy(53, ring.at[1, high], ring_in.at[1, high], left),
    ]
    turn_stripe(FAR, lax.rem(chip + 2, ring_len))
    turn_stripe(RIGHT, lax.rem(chip + 1, ring_len))
    away_copy(FAR).wait_recv()
    opposite[...] = kept_part(FAR).astype(BF16)
    ring_copies[0].start()
    ring_copies[1].start()
    turn_stripe(LEFT, lax.rem(chip + ring_len - 1, ring_len))
    away_copy(RIGHT).wait_recv()
    ring[0, high] = kept_part(RIGHT, half_rows, half_rows).astype(BF16)
    ring_copies[2].start()
    turn_stripe(HOME, chip)
    away_copy(LEFT).wait_recv()
    ring[1, low] = kept_part(LEFT, 0, half_rows).astype(BF16)
    ring_copies[3].start()
    ring_copies[0].wait_recv()
    ring[0, low] = (kept_part(RIGHT, 0, half_rows) + opposite_in[low, :].astype(F32)).astype(BF16)
    ring_copies[4].start()
    ring_copies[1].wait_recv()
    ring[1, high] = (kept_part(LEFT, half_rows, half_rows) + opposite_in[high, :].astype(F32)).astype(BF16)
    ring_copies[5].start()
    shares_copy = pltpu.make_async_copy(shares, shares_out, loads.at[8])
    shares_copy.start()
    away_copy(HOME).wait_recv()
    held = kept_part(HOME)
    for index in range(2, 6):
        ring_copies[index].wait_recv()
    summed = (held + ring_in[0].astype(F32) + ring_in[1].astype(F32)).astype(BF16)

    unpacked = dot(unpack[...], summed)
    for slab in range(slabs):
        returning[slab] = unpacked[slab * cap : (slab + 1) * cap].astype(BF16)
    slab_exchange(3, returning, returned)
    returned[own] = returning[own]

    img_whole(16, masses).wait_recv()
    mass_sum = masses[0]
    for index in range(1, members):
        mass_sum = mass_sum + masses[index]
    mass_row = jnp.concatenate([mass_sum[piece : piece + 1] for piece in range(NPOSE // LANES)], axis=1)
    own_keys = keys[own]
    levels = weight_of[own].astype(F32) * (1.0 / WSTEPS)
    alive = jnp.where(own_keys >= 0, 1.0, 0.0)
    spot_cols = voxel_of[own].astype(F32).T.astype(jnp.int32)
    lower_cols, upper_cols = (levels * alive).T, ((1.0 - levels) * alive).T
    own_key_cols = own_keys.astype(F32).T
    voxel = iota((cap, voxels), 1)
    mass = jnp.zeros((1, voxels), F32)
    for block in range(slabs):
        spots, lows, highs, key = (
            table[:, block : block + 1] for table in (spot_cols, lower_cols, upper_cols, own_key_cols)
        )
        value = jnp.where(voxel == spots, lows, 0.0) + jnp.where(voxel == spots + 1, highs, 0.0)
        weave[block * cap : (block + 1) * cap, :] = value.astype(BF16)
        amount = jnp.sum(jnp.where(key == pose_ids, mass_row, 0.0), axis=1, keepdims=True)
        mass += pick_row(value > 0.0, value * amount)
    inverse[...] = 1.0 / (mass + RIDGE)
    slab_arrivals(3, returned)

    for stage, ref in ((0, outgoing), (1, picks), (2, shares), (3, returning)):
        slab_whole(stage, ref, slabs - 1).wait_send()
    for copy in gathers + ring_copies:
        copy.wait_send()
    for index in range(ring_len):
        away_copy(index).wait_send()
    img_whole(16, masses).wait_send()

    pair = LANES // cap
    slots = jnp.concatenate(
        [
            returned[block : block + pair].reshape(LANES, LANES).astype(F32).T.astype(BF16)
            for block in range(0, slabs, pair)
        ],
        axis=1,
    )
    fourier[...] = (dot(slots, weave[...]) * inverse[...]).astype(BF16)
    shares_copy.wait()


def finish(rows, fourier, shares, density, posterior):
    planes, columns_out, edge = density.shape
    real = jnp.concatenate([fourier[:columns_out, z * edge : (z + 1) * edge] for z in range(planes)], axis=0)
    imag = jnp.concatenate([fourier[columns_out:, z * edge : (z + 1) * edge] for z in range(planes)], axis=0)
    value = dot(real, rows[:edge, :]) + dot(imag, rows[edge:, :])
    for z in range(planes):
        density[z] = value[z * columns_out : (z + 1) * columns_out]
    for block in range(shares.shape[0]):
        posterior[:, block * LANES : (block + 1) * LANES] = shares[block]


def per_device(images, volume, precision, candidates, slot_key, slot_voxel, slot_weight):
    members = lax.axis_size("img")
    slabs = lax.axis_size("slab")
    planes, edge, width = volume.shape
    particles, cands = candidates.shape
    cap = slot_key.shape[2]
    deep = cap // members
    share = NPOSE // members
    voxels = planes * edge
    mine = slabs * deep
    side = NPOSE // 2
    big = pl.BlockSpec(memory_space=pl.ANY)
    near = pl.BlockSpec(memory_space=pltpu.VMEM)
    scratch = [
        pltpu.VMEM((particles, width), BF16),
        pltpu.VMEM((voxels, width), BF16),
        pltpu.VMEM((width, width), BF16),
        pltpu.VMEM((1, particles), F32),
        pltpu.VMEM((cands, particles), jnp.int32),
        pltpu.VMEM(slot_key.shape, jnp.int32),
        pltpu.VMEM(slot_key.shape, jnp.int32),
        pltpu.VMEM(slot_key.shape, jnp.int32),
        pltpu.VMEM((8, mine), F32),
        pltpu.VMEM((8, NPOSE), jnp.int32),
        pltpu.VMEM((cands, particles), jnp.int32),
        pltpu.VMEM((slabs * cap, NPOSE), BF16),
        pltpu.VMEM((slabs, deep, width), BF16),
        pltpu.VMEM((slabs, deep, width), BF16),
        pltpu.VMEM((NPOSE, width), BF16),
        pltpu.VMEM((NPOSE, LANES), F32),
        pltpu.VMEM((NPOSE, particles), jnp.int32),
        pltpu.VMEM((slabs * cap, voxels), BF16),
        pltpu.VMEM((slabs, cands, LANES), F32),
        pltpu.VMEM((slabs, cands, LANES), F32),
        pltpu.VMEM((slabs, cands, LANES), F32),
        pltpu.VMEM((NPOSE, 6 * LANES), BF16),
        pltpu.VMEM((NPOSE, 5 * LANES), BF16),
        pltpu.VMEM((NPOSE, 5 * LANES), BF16),
        pltpu.VMEM((NPOSE, LANES), F32),
        pltpu.VMEM((NPOSE, width), F32),
        pltpu.VMEM((NPOSE, width), BF16),
        pltpu.VMEM((members // 2, NPOSE, LANES), BF16),
        pltpu.VMEM((members // 2, NPOSE, LANES), BF16),
        pltpu.VMEM((members // 2, NPOSE, LANES), F32),
        pltpu.VMEM((NPOSE, LANES), BF16),
        pltpu.VMEM((NPOSE, LANES), BF16),
        pltpu.VMEM((2, NPOSE, LANES), BF16),
        pltpu.VMEM((2, NPOSE, LANES), BF16),
        pltpu.VMEM((members, 8, LANES), F32),
        pltpu.VMEM((1, voxels), F32),
        pltpu.VMEM((slabs, cap, LANES), BF16),
        pltpu.VMEM((slabs, cap, LANES), BF16),
        pltpu.SemaphoreType.DMA((9,)),
        pltpu.SemaphoreType.DMA((7,)),
        pltpu.SemaphoreType.DMA((7,)),
        pltpu.SemaphoreType.DMA((60,)),
        pltpu.SemaphoreType.DMA((60,)),
    ]
    fourier, shares = pl.pallas_call(
        functools.partial(kernel, slabs, members),
        out_shape=(
            jax.ShapeDtypeStruct((LANES, voxels), BF16),
            jax.ShapeDtypeStruct((slabs, cands, LANES), F32),
        ),
        in_specs=[big] * 8,
        out_specs=(near, big),
        scratch_shapes=scratch,
        compiler_params=pltpu.CompilerParams(
            collective_id=0, has_side_effects=True, vmem_limit_bytes=56 * 1024 * 1024
        ),
    )(
        images, volume.reshape(voxels, width), column_table(edge, members),
        precision[None, :], candidates.T, slot_key, slot_voxel, slot_weight,
    )
    density, posterior = pl.pallas_call(
        finish,
        out_shape=(
            jax.ShapeDtypeStruct((planes, edge // members, edge), F32),
            jax.ShapeDtypeStruct((cands, particles), F32),
        ),
        in_specs=[near] * 3,
        out_specs=(near, near),
        compiler_params=pltpu.CompilerParams(vmem_limit_bytes=56 * 1024 * 1024),
    )(row_table(edge), fourier, shares)
    return density.transpose(0, 2, 1), posterior.T


def solution(mesh):
    placed = (P("img", "slab"), P("slab", None, None), P("img"), P("img", None), P(), P(), P())
    return jax.shard_map(
        per_device,
        mesh=mesh,
        in_specs=placed,
        out_specs=(P("slab", None, "img"), P("img", None)),
        check_vma=False,
    )
```

```python
import functools
import math

import jax
import jax.numpy as jnp
import numpy as np
from jax import lax
from jax.experimental import pallas as pl
from jax.experimental.pallas import tpu as pltpu
from jax.sharding import PartitionSpec as P

NPOSE = 512
WSTEPS = 16
RIDGE = 0.25
LANES = 128
F32 = jnp.float32
BF16 = jnp.bfloat16


def gridding(samples):
    offset = (np.arange(samples) - samples / 2) / samples
    return 1.0 / np.sinc(offset) ** 2


def angles(length):
    counter = np.arange(length)
    return (counter[:, None] * counter[None, :] % length) * (2.0 * math.pi / length)


def column_table(length, members):
    turn = angles(length)
    cosine, sine = np.cos(turn), np.sin(turn)
    scale = gridding(length)[None, :]
    to_re = np.concatenate([cosine, -sine], axis=0) * scale
    to_im = np.concatenate([sine, cosine], axis=0) * scale
    width = length // members
    both = np.stack([to_re.reshape(-1, members, width), to_im.reshape(-1, members, width)], axis=2)
    return jnp.asarray(both.reshape(2 * length, 2 * length), BF16)


def row_table(length):
    turn = angles(length)
    scale = gridding(length)[None, :] / length
    return jnp.asarray(np.concatenate([np.cos(turn), -np.sin(turn)], axis=0) * scale, BF16)


def remote(src, dst, sends, recvs, device):
    return pltpu.make_async_remote_copy(
        src_ref=src,
        dst_ref=dst,
        send_sem=sends,
        recv_sem=recvs,
        device_id=device,
        device_id_type=pl.DeviceIdType.MESH,
    )


def dot(left, right):
    return jnp.dot(left, right, preferred_element_type=F32)


def each(count, step, first=0):
    def body(index, carry):
        step(index)
        return carry

    lax.fori_loop(first, count, body, 0)


def rows_at(start, size):
    return pl.ds(pl.multiple_of(start, size), size)


def iota(shape, axis):
    return lax.broadcasted_iota(jnp.int32, shape, axis)


def pick_row(mask, values):
    return jnp.sum(jnp.where(mask, values, 0.0), axis=0, keepdims=True)


def kernel(
    slabs, members,
    images, volume, columns, precision_in, poses_in, keys_in, voxels_in, weights_in,
    fourier, shares_out,
    images_v, volume_v, columns_v, precision, poses, keys, voxel_of, weight_of,
    pack_table, pose_row, named, unpack,
    outgoing, incoming, slices, half_power, ranks, weave,
    picks, picks_in, shares, spread_first, spread_middle, spread_last, row_weight, partial, back,
    away, away_in, kept, opposite, opposite_in, ring, ring_in,
    masses, inverse, returning, returned,
    loads, slab_send, slab_recv, img_send, img_recv,
):
    own = lax.axis_index("slab")
    member = lax.axis_index("img")
    ring_len = members // 2
    chip, core = member // 2, lax.rem(member, 2)
    share = NPOSE // members
    half = share // 2
    side = ring_len * share
    deep = outgoing.shape[1]
    mine = slabs * deep
    cap = keys.shape[2]
    width = volume_v.shape[1]
    voxels = volume_v.shape[0]
    cands = poses.shape[0]
    right = 2 * lax.rem(chip + 1, ring_len) + core
    left = 2 * lax.rem(chip + ring_len - 1, ring_len) + core
    partner = 2 * chip + 1 - core

    def slab_peer(step):
        return lax.rem(own + step, slabs)

    def img_peer(step):
        return lax.rem(member + step, members)

    barrier = pltpu.get_barrier_semaphore()

    def greet(axis, peer):
        pl.semaphore_signal(barrier, inc=1, device_id={axis: peer}, device_id_type=pl.DeviceIdType.MESH)

    sources = [keys_in, voxels_in.at[own], weights_in.at[own], volume, poses_in, images, precision_in, columns]
    targets = [keys, voxel_of, weight_of, volume_v, poses, images_v, precision, columns_v]
    load = [pltpu.make_async_copy(src, dst, loads.at[i]) for i, (src, dst) in enumerate(zip(sources, targets))]

    def start_load(index):
        src, dst = sources[index], targets[index]
        pieces = 8 if src.shape[0] >= 512 else 1
        size = src.shape[0] // pieces
        for piece in range(pieces):
            at = slice(piece * size, (piece + 1) * size)
            pltpu.make_async_copy(src.at[at], dst.at[at], loads.at[index]).start()

    for index in range(5):
        start_load(index)
    for step in range(1, slabs):
        greet("slab", slab_peer(step))
    for step in range(1, members):
        greet("img", img_peer(step))

    for index in range(3):
        load[index].wait()
    before = jnp.zeros((slabs, cap), F32)
    for slab in range(slabs):
        before += jnp.where(keys[slab] >= 0, 1.0, 0.0) * jnp.where(own > slab, 1.0, 0.0)
    out_start = jnp.sum(before, axis=1, keepdims=True)
    total_slots = slabs * cap
    own_key = keys[own]
    own_code = voxel_of[...] * 32 + jnp.where(own_key >= 0, weight_of[...], 31)

    def ordered(first, count, tables):
        position = iota((1, count), 1) + first
        block_sel = iota((slabs, count), 0) == ((position >> 3) & (slabs - 1))
        start_row = pick_row(block_sel, out_start).astype(jnp.int32)
        slot_row = members * (position & 7) + (((position >> 7) - start_row) & 7)
        slot_sel = iota((cap, count), 0) == slot_row
        chooser = jnp.where(block_sel, 1.0, 0.0)
        found = []
        for table in tables:
            wide = lax.dot_general(
                table.astype(F32), chooser, (((0,), (0,)), ((), ())),
                precision=lax.Precision.HIGHEST, preferred_element_type=F32,
            )
            found.append(pick_row(slot_sel, wide))
        return found

    def decoded(code):
        code_row = code.astype(jnp.int32)
        level = code_row & 31
        alive = level <= WSTEPS
        spot = (code_row >> 5).astype(F32)
        lower = jnp.where(alive, level, 0).astype(F32) * (1.0 / WSTEPS)
        upper = jnp.where(alive, WSTEPS - level, 0).astype(F32) * (1.0 / WSTEPS)
        return spot, lower, upper

    parts = decoded(ordered(member * mine, mine, [own_code])[0])
    own_cols = jnp.concatenate(list(parts) + [jnp.zeros((5, mine), F32)], axis=0).T
    place = iota((mine, voxels), 1)
    spot = own_cols[:, 0:1].astype(jnp.int32)
    take = jnp.where(place == spot, own_cols[:, 1:2], 0.0) + jnp.where(place == spot + 1, own_cols[:, 2:3], 0.0)
    load[3].wait()
    for index in range(5, len(load)):
        start_load(index)
    woven = dot(take.astype(BF16), volume_v[...])
    for block in range(slabs):
        outgoing[block] = woven[block * deep : (block + 1) * deep].astype(BF16)
    pl.semaphore_wait(barrier, slabs - 1 + members - 1)

    def slab_copy(stage, src, dst, peer):
        return remote(src.at[peer], dst.at[own], slab_send.at[stage], slab_recv.at[stage], {"slab": peer})

    def slab_whole(stage, ref, count):
        blocks = ref.at[0:count]
        return remote(blocks, blocks, slab_send.at[stage], slab_recv.at[stage], {"slab": slab_peer(1)})

    def slab_exchange(stage, src, dst):
        for step in range(1, slabs):
            slab_copy(stage, src, dst, slab_peer(step)).start()

    def slab_arrivals(stage, dst):
        slab_whole(stage, dst, slabs - 1).wait_recv()

    def img_copy(slot, src, dst, device):
        return remote(src, dst, img_send.at[slot], img_recv.at[slot], {"img": device})

    slab_exchange(0, outgoing, incoming)
    incoming[own] = outgoing[own]

    in_key = jnp.concatenate(
        [jnp.sum(jnp.where(iota((slabs, cap), 0) == own, keys[slab], 0), axis=0, keepdims=True) for slab in range(slabs)],
        axis=0,
    )
    live = jnp.where(in_key >= 0, 1.0, 0.0).astype(BF16)
    count = dot(live, jnp.ones((cap, LANES), BF16))
    earlier = jnp.where(iota((slabs, slabs), 1) < iota((slabs, slabs), 0), 1.0, 0.0).astype(BF16)
    start = dot(earlier, count.astype(BF16))
    lane = iota((1, mine), 1)
    slab_sel = iota((slabs, mine), 0) == (lane >> 3)
    in_start = pick_row(slab_sel, start).astype(jnp.int32)
    in_count = pick_row(slab_sel, count).astype(jnp.int32)
    slot = members * (lane & 7) + ((member - in_start) & 7)
    pack_row = jnp.where(slot < in_count, (in_start + slot) >> 3, -1)
    pack_table[...] = jnp.broadcast_to(pack_row, (8, mine)).astype(F32)

    number = start[:, :cap].astype(jnp.int32) + iota((slabs, cap), 1)
    holder = number & (members - 1)
    ahead = ((holder >> 1) - chip) & (ring_len - 1)
    near = jnp.where(ahead == 0, 3, jnp.where(ahead == 1, 1, jnp.where(ahead == 2, 0, 2)))
    row = jnp.where((holder & 1) == core, near, members - 1 - near) * share + (number >> 3)
    key_cols, row_cols = in_key.astype(F32).T, row.astype(F32).T
    pose_ids = iota((cap, NPOSE), 1).astype(F32)
    found_rows = jnp.zeros((cap, NPOSE), F32)
    for slab in range(slabs):
        matched = key_cols[:, slab : slab + 1] == pose_ids
        found_rows += jnp.where(matched, row_cols[:, slab : slab + 1], 0.0)
        unpack[slab * cap : (slab + 1) * cap, :] = jnp.where(matched, 1.0, 0.0).astype(BF16)
    pose_row[...] = jnp.broadcast_to(jnp.sum(found_rows, axis=0, keepdims=True), (8, NPOSE)).astype(jnp.int32)

    load[4].wait()
    for part in range(poses.shape[1] // LANES):
        for k in range(0, cands, 8):
            at = (slice(k, k + 8), slice(part * LANES, (part + 1) * LANES))
            pose = poses[at]
            low, high = pose & (LANES - 1), pose >> 7
            renamed = jnp.zeros_like(pose)
            for piece in range(NPOSE // LANES):
                table = pose_row[:, piece * LANES : (piece + 1) * LANES]
                found = jnp.take_along_axis(table, low, axis=1, mode="promise_in_bounds")
                renamed = jnp.where(high == piece, found, renamed)
            named[at] = renamed

    first_chunks = 3
    ahead_of = 2 * first_chunks
    middle = 2 * ahead_of
    turn = jnp.where(own >= ahead_of, 1, 0)

    def rank_chunk(block):
        at = rows_at(block * LANES, LANES)
        number = poses[:, at].astype(jnp.int16)
        for first in range(0, NPOSE, LANES):
            row = (iota((LANES, LANES), 0) + first).astype(jnp.int16)
            value = jnp.full((LANES, LANES), cands, jnp.int16)
            for k in range(cands):
                value = jnp.where(number[k : k + 1] == row, jnp.int16(k), value)
            ranks[first : first + LANES, at] = value.astype(jnp.int32)

    each(middle, rank_chunk, ahead_of)

    slab_arrivals(0, incoming)
    arrived = jnp.concatenate([incoming[block].astype(F32) for block in range(slabs)], axis=0).astype(BF16)
    pack = jnp.where(iota((share, mine), 0).astype(F32) == pack_table[0:1, :], 1.0, 0.0).astype(BF16)

    def block_of(index, first=0, size=share):
        return slices.at[index * share + first : index * share + first + size]

    FAR, RIGHT, LEFT, HOME = 0, 1, 2, 3
    slices[HOME * share : (HOME + 1) * share, :] = dot(pack, arrived).astype(BF16)

    def other(index):
        return members - 1 - index

    def top(index):
        return block_of(index, 0, half)

    def bottom(index):
        return block_of(index, half, half)

    gathers = [
        img_copy(0, top(HOME), top(LEFT), right),
        img_copy(1, bottom(HOME), bottom(RIGHT), left),
        img_copy(2, block_of(HOME), block_of(other(HOME)), partner),
        img_copy(3, bottom(HOME), bottom(LEFT), right),
        img_copy(4, top(HOME), top(RIGHT), left),
        img_copy(5, top(LEFT), top(FAR), right),
        img_copy(6, bottom(RIGHT), bottom(FAR), left),
        img_copy(7, block_of(LEFT), block_of(other(LEFT)), partner),
        img_copy(8, block_of(RIGHT), block_of(other(RIGHT)), partner),
        img_copy(9, top(FAR), top(other(FAR)), partner),
        img_copy(10, bottom(FAR), bottom(other(FAR)), partner),
    ]
    for index in range(5):
        gathers[index].start()

    each(slabs, rank_chunk, middle)

    def power_step(index):
        at = rows_at(index * share, share)
        values = slices[at, :].astype(F32)
        total = 0.5 * jnp.sum(values * values, axis=1, keepdims=True)
        half_power[at, :] = jnp.broadcast_to(total, (share, LANES))

    power_step(HOME)
    gathers[0].wait_recv()
    gathers[5].start()
    gathers[1].wait_recv()
    gathers[6].start()
    gathers[3].wait_recv()
    gathers[7].start()
    gathers[4].wait_recv()
    gathers[8].start()
    load[5].wait()

    chunk = 2 * LANES
    chunks = images_v.shape[0] // chunk

    def picks_of(score, pieces, numbers, value):
        for first, offset, size in pieces:
            block = score[offset : offset + size] - half_power[first : first + size, :]
            for group in range(size // 8):
                picked = jnp.take_along_axis(
                    block[group * 8 : (group + 1) * 8], numbers[0], axis=0, mode="promise_in_bounds"
                )
                value[0] = jnp.where(numbers[2] == first // 8 + group, picked, value[0])
                picked = jnp.take_along_axis(
                    block[group * 8 : (group + 1) * 8], numbers[1], axis=0, mode="promise_in_bounds"
                )
                value[1] = jnp.where(numbers[3] == first // 8 + group, picked, value[1])
        return value

    def score_chunk(index, table, pieces, resume):
        score = lax.dot_general(
            table, images_v[rows_at(index * chunk, chunk), :],
            (((1,), (1,)), ((), ())), preferred_element_type=F32,
        )
        for part in range(chunk // LANES):
            number = named[:, rows_at(index * chunk + part * LANES, LANES)]
            numbers = [number[0:8] & 7, number[8:16] & 7, number[0:8] >> 3, number[8:16] >> 3]
            block = index * (chunk // LANES) + part
            if resume:
                value = [picks[block, 0:8], picks[block, 8:16]]
            else:
                value = [jnp.zeros((8, LANES), F32), jnp.zeros((8, LANES), F32)]
            value = picks_of(score[:, part * LANES : (part + 1) * LANES], pieces, numbers, value)
            picks[block] = jnp.concatenate(value, axis=0)

    def near_step(index):
        score_chunk(index, slices[share : NPOSE - share, :], [(share, 0, NPOSE - 2 * share)], False)

    def far_chunk(index):
        table = jnp.concatenate([slices[0:share, :], slices[NPOSE - share : NPOSE, :]], axis=0)
        score_chunk(index, table, [(0, 0, share), (NPOSE - share, share, share)], True)

    def full_chunk(index):
        score_chunk(index, slices[...], [(0, 0, NPOSE)], False)

    power_step(LEFT)
    power_step(RIGHT)
    gathers[2].wait_recv()
    power_step(other(HOME))
    gathers[7].wait_recv()
    gathers[8].wait_recv()
    power_step(other(LEFT))
    power_step(other(RIGHT))
    each(first_chunks - 1, near_step)
    gathers[5].wait_recv()
    gathers[9].start()
    gathers[6].wait_recv()
    gathers[10].start()
    each(first_chunks, near_step, first_chunks - 1)
    gathers[9].wait_recv()
    gathers[10].wait_recv()
    power_step(0)
    power_step(members - 1)

    def pick_send(peer):
        @pl.when(peer != own)
        def _():
            slab_copy(1, picks, picks_in, peer).start()

    def far_step(index):
        far_chunk(index)
        pick_send(2 * index)
        pick_send(2 * index + 1)

    def full_step(index):
        full_chunk(index)
        pick_send(2 * index)
        pick_send(2 * index + 1)

    each(first_chunks, far_step)
    each(chunks, full_step, first_chunks)
    picks_in[own] = picks[own]
    load[6].wait()
    row_weight[...] = jnp.zeros_like(row_weight)
    masses[member] = jnp.zeros((8, LANES), F32)

    def share_out():
        slab_arrivals(1, picks_in)
        total = picks_in[0]
        for block in range(1, slabs):
            total = total + picks_in[block]
        total = total * precision[:, rows_at(own * LANES, LANES)]
        exponent = jnp.exp(total - jnp.max(total, axis=0, keepdims=True))
        shares[own] = (exponent / jnp.sum(exponent, axis=0, keepdims=True)).astype(BF16)
        for step in range(1, slabs):
            remote(
                shares.at[own], shares.at[own], slab_send.at[2], slab_recv.at[5 + turn], {"slab": slab_peer(step)}
            ).start()

    @pl.when(turn == 0)
    def _():
        share_out()

    each(ahead_of, rank_chunk)

    @pl.when(turn != 0)
    def _():
        share_out()

    def shares_arrive(which):
        group = ahead_of if which == 0 else slabs - ahead_of

        @pl.when(turn == which)
        def _():
            slab_whole(5 + which, shares, group - 1).wait_recv()

        @pl.when(turn != which)
        def _():
            slab_whole(5 + which, shares, group).wait_recv()

    def spread_chunk(block, spread, origin):
        at = rows_at(block * LANES, LANES)
        to = rows_at((block - origin) * LANES, LANES)
        amount = shares[block].astype(F32) * precision[:, at]
        rounded = amount.astype(BF16).astype(F32)
        low, high = rounded[0:8], rounded[8:16]
        for first in range(0, NPOSE, 16):
            values = []
            for group in (first, first + 8):
                rank = ranks[group : group + 8, at]
                place = rank & 7
                from_low = jnp.take_along_axis(low, place, axis=0, mode="promise_in_bounds")
                from_high = jnp.take_along_axis(high, place, axis=0, mode="promise_in_bounds")
                value = jnp.where(rank < 8, from_low, jnp.where(rank < cands, from_high, 0.0))
                row_weight[group : group + 8, :] += value
                values.append(value)
            spread[first : first + 16, to] = jnp.concatenate(values, axis=0).astype(BF16)

    stripe = 2 * LANES

    def early_stripe(index):
        at = rows_at(index * stripe, stripe)
        partial[:, at] = dot(spread_first[...], images_v[: ahead_of * LANES, at])

    shares_arrive(0)
    each(ahead_of, lambda block: spread_chunk(block, spread_first, 0))
    each(width // stripe, early_stripe)
    shares_arrive(1)
    each(middle, lambda block: spread_chunk(block, spread_middle, ahead_of), ahead_of)
    waiting = list(range(middle, slabs))
    for index in range(width // stripe):
        at = slice(index * stripe, (index + 1) * stripe)
        partial[:, at] += dot(spread_middle[...], images_v[ahead_of * LANES : middle * LANES, at])
        for block in waiting[index :: width // stripe]:
            spread_chunk(block, spread_last, middle)

    for piece in range(NPOSE // LANES):
        weight = row_weight[piece * LANES : (piece + 1) * LANES, :].T
        masses[member, piece : piece + 1, :] = jnp.sum(weight, axis=0, keepdims=True)

    def mass_copy(step):
        return img_copy(16, masses.at[member], masses.at[member], img_peer(step))

    def img_whole(slot, ref):
        blocks = ref.at[0 : members - 1]
        return img_copy(slot, blocks, blocks, img_peer(1))

    for step in range(1, members):
        mass_copy(step).start()

    def back_stripe(index):
        at = rows_at(index * stripe, stripe)
        part = partial[:, at] + dot(spread_last[...], images_v[middle * LANES :, at])
        back[:, at] = part.astype(BF16)

    each(width // stripe, back_stripe)
    load[7].wait()
    half_rows = NPOSE // 2

    def away_copy(index):
        return img_copy(40 + index, away.at[index], away_in.at[index], partner)

    def turn_stripe(index, chip_index):
        part = dot(back[...], columns_v[:, rows_at(chip_index * stripe, stripe)])
        first, second = part[:, :LANES], part[:, LANES:]
        kept[index] = jnp.where(core == 0, first, second)
        away[index] = jnp.where(core == 0, second, first).astype(BF16)
        away_copy(index).start()

    def kept_part(index, first=0, size=NPOSE):
        rows = slice(first, first + size)
        return kept[index, rows, :] + away_in[index, rows, :].astype(F32)

    low, high = slice(0, half_rows), slice(half_rows, NPOSE)
    ring_copies = [
        img_copy(48, opposite.at[low], opposite_in.at[low], right),
        img_copy(49, opposite.at[high], opposite_in.at[high], left),
        img_copy(50, ring.at[0, high], ring_in.at[0, high], right),
        img_copy(51, ring.at[1, low], ring_in.at[1, low], left),
        img_copy(52, ring.at[0, low], ring_in.at[0, low], right),
        img_copy(53, ring.at[1, high], ring_in.at[1, high], left),
    ]
    turn_stripe(FAR, lax.rem(chip + 2, ring_len))
    turn_stripe(RIGHT, lax.rem(chip + 1, ring_len))
    away_copy(FAR).wait_recv()
    opposite[...] = kept_part(FAR).astype(BF16)
    ring_copies[0].start()
    ring_copies[1].start()
    turn_stripe(LEFT, lax.rem(chip + ring_len - 1, ring_len))
    away_copy(RIGHT).wait_recv()
    ring[0, high] = kept_part(RIGHT, half_rows, half_rows).astype(BF16)
    ring_copies[2].start()
    turn_stripe(HOME, chip)
    away_copy(LEFT).wait_recv()
    ring[1, low] = kept_part(LEFT, 0, half_rows).astype(BF16)
    ring_copies[3].start()
    ring_copies[0].wait_recv()
    ring[0, low] = (kept_part(RIGHT, 0, half_rows) + opposite_in[low, :].astype(F32)).astype(BF16)
    ring_copies[4].start()
    ring_copies[1].wait_recv()
    ring[1, high] = (kept_part(LEFT, half_rows, half_rows) + opposite_in[high, :].astype(F32)).astype(BF16)
    ring_copies[5].start()
    shares_copy = pltpu.make_async_copy(shares, shares_out, loads.at[8])
    shares_copy.start()
    away_copy(HOME).wait_recv()
    held = kept_part(HOME)
    for index in range(2, 6):
        ring_copies[index].wait_recv()
    summed = (held + ring_in[0].astype(F32) + ring_in[1].astype(F32)).astype(BF16)

    unpacked = dot(unpack[...], summed)
    for slab in range(slabs):
        returning[slab] = unpacked[slab * cap : (slab + 1) * cap].astype(BF16)
    slab_exchange(3, returning, returned)
    returned[own] = returning[own]

    img_whole(16, masses).wait_recv()
    mass_sum = masses[0]
    for index in range(1, members):
        mass_sum = mass_sum + masses[index]
    mass_row = jnp.concatenate([mass_sum[piece : piece + 1] for piece in range(NPOSE // LANES)], axis=1)
    own_keys = keys[own]
    levels = weight_of[...].astype(F32) * (1.0 / WSTEPS)
    alive = jnp.where(own_keys >= 0, 1.0, 0.0)
    spot_cols = voxel_of[...].astype(F32).T.astype(jnp.int32)
    lower_cols, upper_cols = (levels * alive).T, ((1.0 - levels) * alive).T
    own_key_cols = own_keys.astype(F32).T
    voxel = iota((cap, voxels), 1)
    mass = jnp.zeros((1, voxels), F32)
    for block in range(slabs):
        spots, lows, highs, key = (
            table[:, block : block + 1] for table in (spot_cols, lower_cols, upper_cols, own_key_cols)
        )
        value = jnp.where(voxel == spots, lows, 0.0) + jnp.where(voxel == spots + 1, highs, 0.0)
        weave[block * cap : (block + 1) * cap, :] = value.astype(BF16)
        amount = jnp.sum(jnp.where(key == pose_ids, mass_row, 0.0), axis=1, keepdims=True)
        mass += pick_row(value > 0.0, value * amount)
    inverse[...] = 1.0 / (mass + RIDGE)
    slab_arrivals(3, returned)

    for stage, ref in ((0, outgoing), (1, picks), (2, shares), (3, returning)):
        slab_whole(stage, ref, slabs - 1).wait_send()
    for copy in gathers + ring_copies:
        copy.wait_send()
    for index in range(ring_len):
        away_copy(index).wait_send()
    img_whole(16, masses).wait_send()

    pair = LANES // cap
    slots = jnp.concatenate(
        [
            returned[block : block + pair].reshape(LANES, LANES).astype(F32).T.astype(BF16)
            for block in range(0, slabs, pair)
        ],
        axis=1,
    )
    fourier[...] = (dot(slots, weave[...]) * inverse[...]).astype(BF16)
    shares_copy.wait()


def finish(rows, fourier, shares, density, posterior):
    planes, columns_out, edge = density.shape
    real = jnp.concatenate([fourier[:columns_out, z * edge : (z + 1) * edge] for z in range(planes)], axis=0)
    imag = jnp.concatenate([fourier[columns_out:, z * edge : (z + 1) * edge] for z in range(planes)], axis=0)
    value = dot(real, rows[:edge, :]) + dot(imag, rows[edge:, :])
    for z in range(planes):
        density[z] = value[z * columns_out : (z + 1) * columns_out]
    for block in range(shares.shape[0]):
        posterior[:, block * LANES : (block + 1) * LANES] = shares[block].astype(F32)


def per_device(images, volume, precision, candidates, slot_key, slot_voxel, slot_weight):
    members = lax.axis_size("img")
    slabs = lax.axis_size("slab")
    planes, edge, width = volume.shape
    particles, cands = candidates.shape
    cap = slot_key.shape[2]
    deep = cap // members
    share = NPOSE // members
    voxels = planes * edge
    mine = slabs * deep
    side = NPOSE // 2
    big = pl.BlockSpec(memory_space=pl.ANY)
    near = pl.BlockSpec(memory_space=pltpu.VMEM)
    scratch = [
        pltpu.VMEM((particles, width), BF16),
        pltpu.VMEM((voxels, width), BF16),
        pltpu.VMEM((width, width), BF16),
        pltpu.VMEM((1, particles), F32),
        pltpu.VMEM((cands, particles), jnp.int32),
        pltpu.VMEM(slot_key.shape, jnp.int32),
        pltpu.VMEM(slot_key.shape[1:], jnp.int32),
        pltpu.VMEM(slot_key.shape[1:], jnp.int32),
        pltpu.VMEM((8, mine), F32),
        pltpu.VMEM((8, NPOSE), jnp.int32),
        pltpu.VMEM((cands, particles), jnp.int32),
        pltpu.VMEM((slabs * cap, NPOSE), BF16),
        pltpu.VMEM((slabs, deep, width), BF16),
        pltpu.VMEM((slabs, deep, width), BF16),
        pltpu.VMEM((NPOSE, width), BF16),
        pltpu.VMEM((NPOSE, LANES), F32),
        pltpu.VMEM((NPOSE, particles), jnp.int32),
        pltpu.VMEM((slabs * cap, voxels), BF16),
        pltpu.VMEM((slabs, cands, LANES), F32),
        pltpu.VMEM((slabs, cands, LANES), F32),
        pltpu.VMEM((slabs, cands, LANES), BF16),
        pltpu.VMEM((NPOSE, 6 * LANES), BF16),
        pltpu.VMEM((NPOSE, 6 * LANES), BF16),
        pltpu.VMEM((NPOSE, 4 * LANES), BF16),
        pltpu.VMEM((NPOSE, LANES), F32),
        pltpu.VMEM((NPOSE, width), F32),
        pltpu.VMEM((NPOSE, width), BF16),
        pltpu.VMEM((members // 2, NPOSE, LANES), BF16),
        pltpu.VMEM((members // 2, NPOSE, LANES), BF16),
        pltpu.VMEM((members // 2, NPOSE, LANES), F32),
        pltpu.VMEM((NPOSE, LANES), BF16),
        pltpu.VMEM((NPOSE, LANES), BF16),
        pltpu.VMEM((2, NPOSE, LANES), BF16),
        pltpu.VMEM((2, NPOSE, LANES), BF16),
        pltpu.VMEM((members, 8, LANES), F32),
        pltpu.VMEM((1, voxels), F32),
        pltpu.VMEM((slabs, cap, LANES), BF16),
        pltpu.VMEM((slabs, cap, LANES), BF16),
        pltpu.SemaphoreType.DMA((9,)),
        pltpu.SemaphoreType.DMA((7,)),
        pltpu.SemaphoreType.DMA((7,)),
        pltpu.SemaphoreType.DMA((60,)),
        pltpu.SemaphoreType.DMA((60,)),
    ]
    fourier, shares = pl.pallas_call(
        functools.partial(kernel, slabs, members),
        out_shape=(
            jax.ShapeDtypeStruct((LANES, voxels), BF16),
            jax.ShapeDtypeStruct((slabs, cands, LANES), BF16),
        ),
        in_specs=[big] * 8,
        out_specs=(near, big),
        scratch_shapes=scratch,
        compiler_params=pltpu.CompilerParams(
            collective_id=0, has_side_effects=True, vmem_limit_bytes=56 * 1024 * 1024
        ),
    )(
        images, volume.reshape(voxels, width), column_table(edge, members),
        precision[None, :], candidates.T, slot_key, slot_voxel, slot_weight,
    )
    density, posterior = pl.pallas_call(
        finish,
        out_shape=(
            jax.ShapeDtypeStruct((planes, edge // members, edge), F32),
            jax.ShapeDtypeStruct((cands, particles), F32),
        ),
        in_specs=[near] * 3,
        out_specs=(near, near),
        compiler_params=pltpu.CompilerParams(vmem_limit_bytes=56 * 1024 * 1024),
    )(row_table(edge), fourier, shares)
    return density.transpose(0, 2, 1), posterior.T


def solution(mesh):
    placed = (P("img", "slab"), P("slab", None, None), P("img"), P("img", None), P(), P(), P())
    return jax.shard_map(
        per_device,
        mesh=mesh,
        in_specs=placed,
        out_specs=(P("slab", None, "img"), P("img", None)),
        check_vma=False,
    )
```

```python
import functools
import math

import jax
import jax.numpy as jnp
import numpy as np
from jax import lax
from jax.experimental import pallas as pl
from jax.experimental.pallas import tpu as pltpu
from jax.sharding import PartitionSpec as P

NPOSE = 512
WSTEPS = 16
RIDGE = 0.25
LANES = 128
F32 = jnp.float32
BF16 = jnp.bfloat16


def gridding(samples):
    offset = (np.arange(samples) - samples / 2) / samples
    return 1.0 / np.sinc(offset) ** 2


def angles(length):
    counter = np.arange(length)
    return (counter[:, None] * counter[None, :] % length) * (2.0 * math.pi / length)


def column_table(length, members):
    turn = angles(length)
    cosine, sine = np.cos(turn), np.sin(turn)
    scale = gridding(length)[None, :]
    to_re = np.concatenate([cosine, -sine], axis=0) * scale
    to_im = np.concatenate([sine, cosine], axis=0) * scale
    width = length // members
    both = np.stack([to_re.reshape(-1, members, width), to_im.reshape(-1, members, width)], axis=2)
    return jnp.asarray(both.reshape(2 * length, 2 * length), BF16)


def row_table(length):
    turn = angles(length)
    scale = gridding(length)[None, :] / length
    return jnp.asarray(np.concatenate([np.cos(turn), -np.sin(turn)], axis=0) * scale, BF16)


def remote(src, dst, sends, recvs, device):
    return pltpu.make_async_remote_copy(
        src_ref=src,
        dst_ref=dst,
        send_sem=sends,
        recv_sem=recvs,
        device_id=device,
        device_id_type=pl.DeviceIdType.MESH,
    )


def dot(left, right):
    return jnp.dot(left, right, preferred_element_type=F32)


def each(count, step, first=0):
    def body(index, carry):
        step(index)
        return carry

    lax.fori_loop(first, count, body, 0)


def rows_at(start, size):
    return pl.ds(pl.multiple_of(start, size), size)


def iota(shape, axis):
    return lax.broadcasted_iota(jnp.int32, shape, axis)


def pick_row(mask, values):
    return jnp.sum(jnp.where(mask, values, 0.0), axis=0, keepdims=True)


def kernel(
    slabs, members,
    images, volume, columns, precision_in, poses_in, keys_in, voxels_in, weights_in,
    fourier, shares_out,
    images_v, volume_v, columns_v, precision, poses, keys, voxel_of, weight_of,
    pack_table, pose_row, named, unpack,
    outgoing, incoming, slices, half_power, ranks, weave,
    picks, picks_in, shares, spread_first, spread_middle, spread_last, row_weight, partial, turned,
    away, away_in, kept, opposite, opposite_in, ring, ring_in,
    masses, inverse, returning, returned,
    loads, slab_send, slab_recv, img_send, img_recv,
):
    own = lax.axis_index("slab")
    member = lax.axis_index("img")
    ring_len = members // 2
    chip, core = member // 2, lax.rem(member, 2)
    share = NPOSE // members
    half = share // 2
    side = ring_len * share
    deep = outgoing.shape[1]
    mine = slabs * deep
    cap = keys.shape[2]
    width = volume_v.shape[1]
    voxels = volume_v.shape[0]
    cands = poses.shape[0]
    right = 2 * lax.rem(chip + 1, ring_len) + core
    left = 2 * lax.rem(chip + ring_len - 1, ring_len) + core
    partner = 2 * chip + 1 - core

    def slab_peer(step):
        return lax.rem(own + step, slabs)

    def img_peer(step):
        return lax.rem(member + step, members)

    barrier = pltpu.get_barrier_semaphore()

    def greet(axis, peer):
        pl.semaphore_signal(barrier, inc=1, device_id={axis: peer}, device_id_type=pl.DeviceIdType.MESH)

    sources = [keys_in, voxels_in.at[own], weights_in.at[own], volume, poses_in, images, columns, precision_in]
    targets = [keys, voxel_of, weight_of, volume_v, poses, images_v, columns_v, precision]
    load = [pltpu.make_async_copy(src, dst, loads.at[i]) for i, (src, dst) in enumerate(zip(sources, targets))]

    def start_load(index):
        src, dst = sources[index], targets[index]
        pieces = 8 if src.shape[0] >= 512 else 1
        size = src.shape[0] // pieces
        for piece in range(pieces):
            at = slice(piece * size, (piece + 1) * size)
            pltpu.make_async_copy(src.at[at], dst.at[at], loads.at[index]).start()

    for index in range(5):
        start_load(index)
    for step in range(1, slabs):
        greet("slab", slab_peer(step))
    for step in range(1, members):
        greet("img", img_peer(step))

    for index in range(3):
        load[index].wait()
    before = jnp.zeros((slabs, cap), F32)
    for slab in range(slabs):
        before += jnp.where(keys[slab] >= 0, 1.0, 0.0) * jnp.where(own > slab, 1.0, 0.0)
    out_start = jnp.sum(before, axis=1, keepdims=True)
    total_slots = slabs * cap
    own_key = keys[own]
    own_code = voxel_of[...] * 32 + jnp.where(own_key >= 0, weight_of[...], 31)

    def ordered(first, count, tables):
        position = iota((1, count), 1) + first
        block_sel = iota((slabs, count), 0) == ((position >> 3) & (slabs - 1))
        start_row = pick_row(block_sel, out_start).astype(jnp.int32)
        slot_row = members * (position & 7) + (((position >> 7) - start_row) & 7)
        slot_sel = iota((cap, count), 0) == slot_row
        chooser = jnp.where(block_sel, 1.0, 0.0)
        found = []
        for table in tables:
            wide = lax.dot_general(
                table.astype(F32), chooser, (((0,), (0,)), ((), ())),
                precision=lax.Precision.HIGHEST, preferred_element_type=F32,
            )
            found.append(pick_row(slot_sel, wide))
        return found

    def decoded(code):
        code_row = code.astype(jnp.int32)
        level = code_row & 31
        alive = level <= WSTEPS
        spot = (code_row >> 5).astype(F32)
        lower = jnp.where(alive, level, 0).astype(F32) * (1.0 / WSTEPS)
        upper = jnp.where(alive, WSTEPS - level, 0).astype(F32) * (1.0 / WSTEPS)
        return spot, lower, upper

    parts = decoded(ordered(member * mine, mine, [own_code])[0])
    own_cols = jnp.concatenate(list(parts) + [jnp.zeros((5, mine), F32)], axis=0).T
    place = iota((mine, voxels), 1)
    spot = own_cols[:, 0:1].astype(jnp.int32)
    take = jnp.where(place == spot, own_cols[:, 1:2], 0.0) + jnp.where(place == spot + 1, own_cols[:, 2:3], 0.0)
    load[3].wait()
    for index in range(5, len(load)):
        start_load(index)
    woven = dot(take.astype(BF16), volume_v[...])
    for block in range(slabs):
        outgoing[block] = woven[block * deep : (block + 1) * deep].astype(BF16)
    pl.semaphore_wait(barrier, slabs - 1 + members - 1)

    def slab_copy(stage, src, dst, peer):
        return remote(src.at[peer], dst.at[own], slab_send.at[stage], slab_recv.at[stage], {"slab": peer})

    def slab_whole(stage, ref, count):
        blocks = ref.at[0:count]
        return remote(blocks, blocks, slab_send.at[stage], slab_recv.at[stage], {"slab": slab_peer(1)})

    def slab_exchange(stage, src, dst):
        for step in range(1, slabs):
            slab_copy(stage, src, dst, slab_peer(step)).start()

    def slab_arrivals(stage, dst):
        slab_whole(stage, dst, slabs - 1).wait_recv()

    def img_copy(slot, src, dst, device):
        return remote(src, dst, img_send.at[slot], img_recv.at[slot], {"img": device})

    slab_exchange(0, outgoing, incoming)
    incoming[own] = outgoing[own]

    in_key = jnp.concatenate(
        [jnp.sum(jnp.where(iota((slabs, cap), 0) == own, keys[slab], 0), axis=0, keepdims=True) for slab in range(slabs)],
        axis=0,
    )
    live = jnp.where(in_key >= 0, 1.0, 0.0).astype(BF16)
    count = dot(live, jnp.ones((cap, LANES), BF16))
    earlier = jnp.where(iota((slabs, slabs), 1) < iota((slabs, slabs), 0), 1.0, 0.0).astype(BF16)
    start = dot(earlier, count.astype(BF16))
    lane = iota((1, mine), 1)
    slab_sel = iota((slabs, mine), 0) == (lane >> 3)
    in_start = pick_row(slab_sel, start).astype(jnp.int32)
    in_count = pick_row(slab_sel, count).astype(jnp.int32)
    slot = members * (lane & 7) + ((member - in_start) & 7)
    pack_row = jnp.where(slot < in_count, (in_start + slot) >> 3, -1)
    pack_table[...] = jnp.broadcast_to(pack_row, (8, mine)).astype(F32)

    number = start[:, :cap].astype(jnp.int32) + iota((slabs, cap), 1)
    holder = number & (members - 1)
    ahead = ((holder >> 1) - chip) & (ring_len - 1)
    near = jnp.where(ahead == 0, 3, jnp.where(ahead == 1, 1, jnp.where(ahead == 2, 0, 2)))
    row = jnp.where((holder & 1) == core, near, members - 1 - near) * share + (number >> 3)
    key_cols, row_cols = in_key.astype(F32).T, row.astype(F32).T
    pose_ids = iota((cap, NPOSE), 1).astype(F32)
    found_rows = jnp.zeros((cap, NPOSE), F32)
    for slab in range(slabs):
        matched = key_cols[:, slab : slab + 1] == pose_ids
        found_rows += jnp.where(matched, row_cols[:, slab : slab + 1], 0.0)
        unpack[slab * cap : (slab + 1) * cap, :] = jnp.where(matched, 1.0, 0.0).astype(BF16)
    pose_row[...] = jnp.broadcast_to(jnp.sum(found_rows, axis=0, keepdims=True), (8, NPOSE)).astype(jnp.int32)

    load[4].wait()
    for part in range(poses.shape[1] // LANES):
        for k in range(0, cands, 8):
            at = (slice(k, k + 8), slice(part * LANES, (part + 1) * LANES))
            pose = poses[at]
            low, high = pose & (LANES - 1), pose >> 7
            renamed = jnp.zeros_like(pose)
            for piece in range(NPOSE // LANES):
                table = pose_row[:, piece * LANES : (piece + 1) * LANES]
                found = jnp.take_along_axis(table, low, axis=1, mode="promise_in_bounds")
                renamed = jnp.where(high == piece, found, renamed)
            named[at] = renamed

    first_chunks = 3
    ahead_of = 2 * first_chunks
    middle = 2 * ahead_of
    turn = jnp.where(own >= ahead_of, 1, 0)

    def rank_chunk(block):
        at = rows_at(block * LANES, LANES)
        number = poses[:, at].astype(jnp.int16)
        for first in range(0, NPOSE, LANES):
            row = (iota((LANES, LANES), 0) + first).astype(jnp.int16)
            value = jnp.full((LANES, LANES), cands, jnp.int16)
            for k in range(cands):
                value = jnp.where(number[k : k + 1] == row, jnp.int16(k), value)
            ranks[first : first + LANES, at] = value.astype(jnp.int32)

    stripe = 2 * LANES
    stripes = width // stripe
    slabful = images_v.shape[0] // stripes

    def prepare(step):
        block = rows_at(lax.div(step, stripes) * slabful, slabful)
        at = rows_at(lax.rem(step, stripes) * stripe, stripe)
        turned[block, at] = dot(images_v[block, :], columns_v[:, at]).astype(BF16)
        rank_chunk(lax.rem(step + ahead_of, slabs))

    load[5].wait()
    load[6].wait()
    each(6, prepare)

    slab_arrivals(0, incoming)
    arrived = jnp.concatenate([incoming[block].astype(F32) for block in range(slabs)], axis=0).astype(BF16)
    pack = jnp.where(iota((share, mine), 0).astype(F32) == pack_table[0:1, :], 1.0, 0.0).astype(BF16)

    def block_of(index, first=0, size=share):
        return slices.at[index * share + first : index * share + first + size]

    FAR, RIGHT, LEFT, HOME = 0, 1, 2, 3
    slices[HOME * share : (HOME + 1) * share, :] = dot(pack, arrived).astype(BF16)

    def other(index):
        return members - 1 - index

    def top(index):
        return block_of(index, 0, half)

    def bottom(index):
        return block_of(index, half, half)

    gathers = [
        img_copy(0, top(HOME), top(LEFT), right),
        img_copy(1, bottom(HOME), bottom(RIGHT), left),
        img_copy(2, block_of(HOME), block_of(other(HOME)), partner),
        img_copy(3, bottom(HOME), bottom(LEFT), right),
        img_copy(4, top(HOME), top(RIGHT), left),
        img_copy(5, top(LEFT), top(FAR), right),
        img_copy(6, bottom(RIGHT), bottom(FAR), left),
        img_copy(7, block_of(LEFT), block_of(other(LEFT)), partner),
        img_copy(8, block_of(RIGHT), block_of(other(RIGHT)), partner),
        img_copy(9, top(FAR), top(other(FAR)), partner),
        img_copy(10, bottom(FAR), bottom(other(FAR)), partner),
    ]
    for index in range(5):
        gathers[index].start()

    each(10, prepare, 6)

    def power_step(index):
        at = rows_at(index * share, share)
        values = slices[at, :].astype(F32)
        total = 0.5 * jnp.sum(values * values, axis=1, keepdims=True)
        half_power[at, :] = jnp.broadcast_to(total, (share, LANES))

    power_step(HOME)
    gathers[0].wait_recv()
    gathers[5].start()
    gathers[1].wait_recv()
    gathers[6].start()
    gathers[3].wait_recv()
    gathers[7].start()
    gathers[4].wait_recv()
    gathers[8].start()

    chunk = 2 * LANES
    chunks = images_v.shape[0] // chunk

    def picks_of(score, pieces, numbers, value):
        for first, offset, size in pieces:
            block = score[offset : offset + size] - half_power[first : first + size, :]
            for group in range(size // 8):
                picked = jnp.take_along_axis(
                    block[group * 8 : (group + 1) * 8], numbers[0], axis=0, mode="promise_in_bounds"
                )
                value[0] = jnp.where(numbers[2] == first // 8 + group, picked, value[0])
                picked = jnp.take_along_axis(
                    block[group * 8 : (group + 1) * 8], numbers[1], axis=0, mode="promise_in_bounds"
                )
                value[1] = jnp.where(numbers[3] == first // 8 + group, picked, value[1])
        return value

    def score_chunk(index, table, pieces, resume):
        score = lax.dot_general(
            table, images_v[rows_at(index * chunk, chunk), :],
            (((1,), (1,)), ((), ())), preferred_element_type=F32,
        )
        for part in range(chunk // LANES):
            number = named[:, rows_at(index * chunk + part * LANES, LANES)]
            numbers = [number[0:8] & 7, number[8:16] & 7, number[0:8] >> 3, number[8:16] >> 3]
            block = index * (chunk // LANES) + part
            if resume:
                value = [picks[block, 0:8], picks[block, 8:16]]
            else:
                value = [jnp.zeros((8, LANES), F32), jnp.zeros((8, LANES), F32)]
            value = picks_of(score[:, part * LANES : (part + 1) * LANES], pieces, numbers, value)
            picks[block] = jnp.concatenate(value, axis=0)

    def near_step(index):
        score_chunk(index, slices[share : NPOSE - share, :], [(share, 0, NPOSE - 2 * share)], False)

    def far_chunk(index):
        table = jnp.concatenate([slices[0:share, :], slices[NPOSE - share : NPOSE, :]], axis=0)
        score_chunk(index, table, [(0, 0, share), (NPOSE - share, share, share)], True)

    def full_chunk(index):
        score_chunk(index, slices[...], [(0, 0, NPOSE)], False)

    each(12, prepare, 10)
    power_step(LEFT)
    power_step(RIGHT)
    gathers[2].wait_recv()
    power_step(other(HOME))
    gathers[7].wait_recv()
    gathers[8].wait_recv()
    power_step(other(LEFT))
    power_step(other(RIGHT))
    each(first_chunks - 1, near_step)
    gathers[5].wait_recv()
    gathers[9].start()
    gathers[6].wait_recv()
    gathers[10].start()
    each(first_chunks, near_step, first_chunks - 1)
    gathers[9].wait_recv()
    gathers[10].wait_recv()
    power_step(0)
    power_step(members - 1)

    def pick_send(peer):
        @pl.when(peer != own)
        def _():
            slab_copy(1, picks, picks_in, peer).start()

    def far_step(index):
        far_chunk(index)
        pick_send(2 * index)
        pick_send(2 * index + 1)

    def full_step(index):
        full_chunk(index)
        pick_send(2 * index)
        pick_send(2 * index + 1)

    each(first_chunks, far_step)
    each(chunks, full_step, first_chunks)
    picks_in[own] = picks[own]
    load[7].wait()
    row_weight[...] = jnp.zeros_like(row_weight)
    masses[member] = jnp.zeros((8, LANES), F32)

    def share_out():
        slab_arrivals(1, picks_in)
        total = picks_in[0]
        for block in range(1, slabs):
            total = total + picks_in[block]
        total = total * precision[:, rows_at(own * LANES, LANES)]
        exponent = jnp.exp(total - jnp.max(total, axis=0, keepdims=True))
        shares[own] = (exponent / jnp.sum(exponent, axis=0, keepdims=True)).astype(BF16)
        for step in range(1, slabs):
            remote(
                shares.at[own], shares.at[own], slab_send.at[2], slab_recv.at[5 + turn], {"slab": slab_peer(step)}
            ).start()

    @pl.when(turn == 0)
    def _():
        share_out()

    each(slabs, prepare, 12)

    @pl.when(turn != 0)
    def _():
        share_out()

    def shares_arrive(which):
        group = ahead_of if which == 0 else slabs - ahead_of

        @pl.when(turn == which)
        def _():
            slab_whole(5 + which, shares, group - 1).wait_recv()

        @pl.when(turn != which)
        def _():
            slab_whole(5 + which, shares, group).wait_recv()

    def spread_chunk(block, spread, origin):
        at = rows_at(block * LANES, LANES)
        to = rows_at((block - origin) * LANES, LANES)
        amount = shares[block].astype(F32) * precision[:, at]
        rounded = amount.astype(BF16).astype(F32)
        low, high = rounded[0:8], rounded[8:16]
        for first in range(0, NPOSE, 16):
            values = []
            for group in (first, first + 8):
                rank = ranks[group : group + 8, at]
                place = rank & 7
                from_low = jnp.take_along_axis(low, place, axis=0, mode="promise_in_bounds")
                from_high = jnp.take_along_axis(high, place, axis=0, mode="promise_in_bounds")
                value = jnp.where(rank < 8, from_low, jnp.where(rank < cands, from_high, 0.0))
                row_weight[group : group + 8, :] += value
                values.append(value)
            spread[first : first + 16, to] = jnp.concatenate(values, axis=0).astype(BF16)

    def early_stripe(index):
        at = rows_at(index * stripe, stripe)
        partial[:, at] = dot(spread_first[...], turned[: ahead_of * LANES, at])

    shares_arrive(0)
    each(ahead_of, lambda block: spread_chunk(block, spread_first, 0))
    each(width // stripe, early_stripe)
    shares_arrive(1)
    each(middle, lambda block: spread_chunk(block, spread_middle, ahead_of), ahead_of)
    waiting = list(range(middle, slabs))
    for index in range(width // stripe):
        at = slice(index * stripe, (index + 1) * stripe)
        partial[:, at] += dot(spread_middle[...], turned[ahead_of * LANES : middle * LANES, at])
        for block in waiting[index :: width // stripe]:
            spread_chunk(block, spread_last, middle)

    for piece in range(NPOSE // LANES):
        weight = row_weight[piece * LANES : (piece + 1) * LANES, :].T
        masses[member, piece : piece + 1, :] = jnp.sum(weight, axis=0, keepdims=True)

    def mass_copy(step):
        return img_copy(16, masses.at[member], masses.at[member], img_peer(step))

    def img_whole(slot, ref):
        blocks = ref.at[0 : members - 1]
        return img_copy(slot, blocks, blocks, img_peer(1))

    for step in range(1, members):
        mass_copy(step).start()

    half_rows = NPOSE // 2

    def away_copy(index):
        return img_copy(40 + index, away.at[index], away_in.at[index], partner)

    def turn_stripe(index, chip_index):
        at = rows_at(chip_index * stripe, stripe)
        part = partial[:, at] + dot(spread_last[...], turned[middle * LANES :, at])
        first, second = part[:, :LANES], part[:, LANES:]
        kept[index] = jnp.where(core == 0, first, second)
        away[index] = jnp.where(core == 0, second, first).astype(BF16)
        away_copy(index).start()

    def kept_part(index, first=0, size=NPOSE):
        rows = slice(first, first + size)
        return kept[index, rows, :] + away_in[index, rows, :].astype(F32)

    low, high = slice(0, half_rows), slice(half_rows, NPOSE)
    ring_copies = [
        img_copy(48, opposite.at[low], opposite_in.at[low], right),
        img_copy(49, opposite.at[high], opposite_in.at[high], left),
        img_copy(50, ring.at[0, high], ring_in.at[0, high], right),
        img_copy(51, ring.at[1, low], ring_in.at[1, low], left),
        img_copy(52, ring.at[0, low], ring_in.at[0, low], right),
        img_copy(53, ring.at[1, high], ring_in.at[1, high], left),
    ]
    turn_stripe(FAR, lax.rem(chip + 2, ring_len))
    turn_stripe(RIGHT, lax.rem(chip + 1, ring_len))
    away_copy(FAR).wait_recv()
    opposite[...] = kept_part(FAR).astype(BF16)
    ring_copies[0].start()
    ring_copies[1].start()
    turn_stripe(LEFT, lax.rem(chip + ring_len - 1, ring_len))
    away_copy(RIGHT).wait_recv()
    ring[0, high] = kept_part(RIGHT, half_rows, half_rows).astype(BF16)
    ring_copies[2].start()
    turn_stripe(HOME, chip)
    away_copy(LEFT).wait_recv()
    ring[1, low] = kept_part(LEFT, 0, half_rows).astype(BF16)
    ring_copies[3].start()
    ring_copies[0].wait_recv()
    ring[0, low] = (kept_part(RIGHT, 0, half_rows) + opposite_in[low, :].astype(F32)).astype(BF16)
    ring_copies[4].start()
    ring_copies[1].wait_recv()
    ring[1, high] = (kept_part(LEFT, half_rows, half_rows) + opposite_in[high, :].astype(F32)).astype(BF16)
    ring_copies[5].start()
    shares_copy = pltpu.make_async_copy(shares, shares_out, loads.at[8])
    shares_copy.start()
    away_copy(HOME).wait_recv()
    held = kept_part(HOME)
    for index in range(2, 6):
        ring_copies[index].wait_recv()
    summed = (held + ring_in[0].astype(F32) + ring_in[1].astype(F32)).astype(BF16)

    unpacked = dot(unpack[...], summed)
    for slab in range(slabs):
        returning[slab] = unpacked[slab * cap : (slab + 1) * cap].astype(BF16)
    slab_exchange(3, returning, returned)
    returned[own] = returning[own]

    img_whole(16, masses).wait_recv()
    mass_sum = masses[0]
    for index in range(1, members):
        mass_sum = mass_sum + masses[index]
    mass_row = jnp.concatenate([mass_sum[piece : piece + 1] for piece in range(NPOSE // LANES)], axis=1)
    own_keys = keys[own]
    levels = weight_of[...].astype(F32) * (1.0 / WSTEPS)
    alive = jnp.where(own_keys >= 0, 1.0, 0.0)
    spot_cols = voxel_of[...].astype(F32).T.astype(jnp.int32)
    lower_cols, upper_cols = (levels * alive).T, ((1.0 - levels) * alive).T
    own_key_cols = own_keys.astype(F32).T
    voxel = iota((cap, voxels), 1)
    mass = jnp.zeros((1, voxels), F32)
    for block in range(slabs):
        spots, lows, highs, key = (
            table[:, block : block + 1] for table in (spot_cols, lower_cols, upper_cols, own_key_cols)
        )
        value = jnp.where(voxel == spots, lows, 0.0) + jnp.where(voxel == spots + 1, highs, 0.0)
        weave[block * cap : (block + 1) * cap, :] = value.astype(BF16)
        amount = jnp.sum(jnp.where(key == pose_ids, mass_row, 0.0), axis=1, keepdims=True)
        mass += pick_row(value > 0.0, value * amount)
    inverse[...] = 1.0 / (mass + RIDGE)
    slab_arrivals(3, returned)

    for stage, ref in ((0, outgoing), (1, picks), (2, shares), (3, returning)):
        slab_whole(stage, ref, slabs - 1).wait_send()
    for copy in gathers + ring_copies:
        copy.wait_send()
    for index in range(ring_len):
        away_copy(index).wait_send()
    img_whole(16, masses).wait_send()

    pair = LANES // cap
    slots = jnp.concatenate(
        [
            returned[block : block + pair].reshape(LANES, LANES).astype(F32).T.astype(BF16)
            for block in range(0, slabs, pair)
        ],
        axis=1,
    )
    fourier[...] = (dot(slots, weave[...]) * inverse[...]).astype(BF16)
    shares_copy.wait()


def finish(rows, fourier, shares, density, posterior):
    planes, columns_out, edge = density.shape
    real = jnp.concatenate([fourier[:columns_out, z * edge : (z + 1) * edge] for z in range(planes)], axis=0)
    imag = jnp.concatenate([fourier[columns_out:, z * edge : (z + 1) * edge] for z in range(planes)], axis=0)
    value = dot(real, rows[:edge, :]) + dot(imag, rows[edge:, :])
    for z in range(planes):
        density[z] = value[z * columns_out : (z + 1) * columns_out]
    for block in range(shares.shape[0]):
        posterior[:, block * LANES : (block + 1) * LANES] = shares[block].astype(F32)


def per_device(images, volume, precision, candidates, slot_key, slot_voxel, slot_weight):
    members = lax.axis_size("img")
    slabs = lax.axis_size("slab")
    planes, edge, width = volume.shape
    particles, cands = candidates.shape
    cap = slot_key.shape[2]
    deep = cap // members
    share = NPOSE // members
    voxels = planes * edge
    mine = slabs * deep
    side = NPOSE // 2
    big = pl.BlockSpec(memory_space=pl.ANY)
    near = pl.BlockSpec(memory_space=pltpu.VMEM)
    scratch = [
        pltpu.VMEM((particles, width), BF16),
        pltpu.VMEM((voxels, width), BF16),
        pltpu.VMEM((width, width), BF16),
        pltpu.VMEM((1, particles), F32),
        pltpu.VMEM((cands, particles), jnp.int32),
        pltpu.VMEM(slot_key.shape, jnp.int32),
        pltpu.VMEM(slot_key.shape[1:], jnp.int32),
        pltpu.VMEM(slot_key.shape[1:], jnp.int32),
        pltpu.VMEM((8, mine), F32),
        pltpu.VMEM((8, NPOSE), jnp.int32),
        pltpu.VMEM((cands, particles), jnp.int32),
        pltpu.VMEM((slabs * cap, NPOSE), BF16),
        pltpu.VMEM((slabs, deep, width), BF16),
        pltpu.VMEM((slabs, deep, width), BF16),
        pltpu.VMEM((NPOSE, width), BF16),
        pltpu.VMEM((NPOSE, LANES), F32),
        pltpu.VMEM((NPOSE, particles), jnp.int32),
        pltpu.VMEM((slabs * cap, voxels), BF16),
        pltpu.VMEM((slabs, cands, LANES), F32),
        pltpu.VMEM((slabs, cands, LANES), F32),
        pltpu.VMEM((slabs, cands, LANES), BF16),
        pltpu.VMEM((NPOSE, 6 * LANES), BF16),
        pltpu.VMEM((NPOSE, 6 * LANES), BF16),
        pltpu.VMEM((NPOSE, 4 * LANES), BF16),
        pltpu.VMEM((NPOSE, LANES), F32),
        pltpu.VMEM((NPOSE, width), F32),
        pltpu.VMEM((particles, width), BF16),
        pltpu.VMEM((members // 2, NPOSE, LANES), BF16),
        pltpu.VMEM((members // 2, NPOSE, LANES), BF16),
        pltpu.VMEM((members // 2, NPOSE, LANES), F32),
        pltpu.VMEM((NPOSE, LANES), BF16),
        pltpu.VMEM((NPOSE, LANES), BF16),
        pltpu.VMEM((2, NPOSE, LANES), BF16),
        pltpu.VMEM((2, NPOSE, LANES), BF16),
        pltpu.VMEM((members, 8, LANES), F32),
        pltpu.VMEM((1, voxels), F32),
        pltpu.VMEM((slabs, cap, LANES), BF16),
        pltpu.VMEM((slabs, cap, LANES), BF16),
        pltpu.SemaphoreType.DMA((9,)),
        pltpu.SemaphoreType.DMA((7,)),
        pltpu.SemaphoreType.DMA((7,)),
        pltpu.SemaphoreType.DMA((60,)),
        pltpu.SemaphoreType.DMA((60,)),
    ]
    fourier, shares = pl.pallas_call(
        functools.partial(kernel, slabs, members),
        out_shape=(
            jax.ShapeDtypeStruct((LANES, voxels), BF16),
            jax.ShapeDtypeStruct((slabs, cands, LANES), BF16),
        ),
        in_specs=[big] * 8,
        out_specs=(near, big),
        scratch_shapes=scratch,
        compiler_params=pltpu.CompilerParams(
            collective_id=0, has_side_effects=True, vmem_limit_bytes=56 * 1024 * 1024
        ),
    )(
        images, volume.reshape(voxels, width), column_table(edge, members),
        precision[None, :], candidates.T, slot_key, slot_voxel, slot_weight,
    )
    density, posterior = pl.pallas_call(
        finish,
        out_shape=(
            jax.ShapeDtypeStruct((planes, edge // members, edge), F32),
            jax.ShapeDtypeStruct((cands, particles), F32),
        ),
        in_specs=[near] * 3,
        out_specs=(near, near),
        compiler_params=pltpu.CompilerParams(vmem_limit_bytes=56 * 1024 * 1024),
    )(row_table(edge), fourier, shares)
    return density.transpose(0, 2, 1), posterior.T


def solution(mesh):
    placed = (P("img", "slab"), P("slab", None, None), P("img"), P("img", None), P(), P(), P())
    return jax.shard_map(
        per_device,
        mesh=mesh,
        in_specs=placed,
        out_specs=(P("slab", None, "img"), P("img", None)),
        check_vma=False,
    )
```

```python
import functools
import math

import jax
import jax.numpy as jnp
import numpy as np
from jax import lax
from jax.experimental import pallas as pl
from jax.experimental.pallas import tpu as pltpu
from jax.sharding import PartitionSpec as P

NPOSE = 512
WSTEPS = 16
RIDGE = 0.25
LANES = 128
F32 = jnp.float32
BF16 = jnp.bfloat16


def gridding(samples):
    offset = (np.arange(samples) - samples / 2) / samples
    return 1.0 / np.sinc(offset) ** 2


def angles(length):
    counter = np.arange(length)
    return (counter[:, None] * counter[None, :] % length) * (2.0 * math.pi / length)


def column_table(length, members):
    turn = angles(length)
    cosine, sine = np.cos(turn), np.sin(turn)
    scale = gridding(length)[None, :]
    to_re = np.concatenate([cosine, -sine], axis=0) * scale
    to_im = np.concatenate([sine, cosine], axis=0) * scale
    width = length // members
    both = np.stack([to_re.reshape(-1, members, width), to_im.reshape(-1, members, width)], axis=2)
    return jnp.asarray(both.reshape(2 * length, 2 * length), BF16)


def row_table(length):
    turn = angles(length)
    scale = gridding(length)[None, :] / length
    return jnp.asarray(np.concatenate([np.cos(turn), -np.sin(turn)], axis=0) * scale, BF16)


def remote(src, dst, sends, recvs, device):
    return pltpu.make_async_remote_copy(
        src_ref=src,
        dst_ref=dst,
        send_sem=sends,
        recv_sem=recvs,
        device_id=device,
        device_id_type=pl.DeviceIdType.MESH,
    )


def dot(left, right):
    return jnp.dot(left, right, preferred_element_type=F32)


def each(count, step, first=0):
    def body(index, carry):
        step(index)
        return carry

    lax.fori_loop(first, count, body, 0)


def rows_at(start, size):
    return pl.ds(pl.multiple_of(start, size), size)


def iota(shape, axis):
    return lax.broadcasted_iota(jnp.int32, shape, axis)


def pick_row(mask, values):
    return jnp.sum(jnp.where(mask, values, 0.0), axis=0, keepdims=True)


def kernel(
    slabs, members,
    images, volume, columns, precision_in, poses_in, keys_in, voxels_in, weights_in,
    fourier, shares_out,
    images_v, volume_v, columns_v, precision, poses, keys, voxel_of, weight_of,
    pack_table, pose_row, named, unpack,
    outgoing, incoming, slices, half_power, ranks, weave,
    picks, picks_in, shares, spread_first, spread_middle, spread_last, row_weight, partial, turned,
    away, away_in, kept, opposite, opposite_in, ring, ring_in,
    masses, inverse, returning, returned,
    loads, slab_send, slab_recv, img_send, img_recv,
):
    own = lax.axis_index("slab")
    member = lax.axis_index("img")
    ring_len = members // 2
    chip, core = member // 2, lax.rem(member, 2)
    share = NPOSE // members
    half = share // 2
    side = ring_len * share
    deep = outgoing.shape[1]
    mine = slabs * deep
    cap = keys.shape[2]
    width = volume_v.shape[1]
    voxels = volume_v.shape[0]
    cands = poses.shape[0]
    right = 2 * lax.rem(chip + 1, ring_len) + core
    left = 2 * lax.rem(chip + ring_len - 1, ring_len) + core
    partner = 2 * chip + 1 - core

    def slab_peer(step):
        return lax.rem(own + step, slabs)

    def img_peer(step):
        return lax.rem(member + step, members)

    barrier = pltpu.get_barrier_semaphore()

    def greet(axis, peer):
        pl.semaphore_signal(barrier, inc=1, device_id={axis: peer}, device_id_type=pl.DeviceIdType.MESH)

    for step in range(1, slabs):
        greet("slab", slab_peer(step))
    for step in range(1, members):
        greet("img", img_peer(step))
    sources = [keys_in, voxels_in.at[own], weights_in.at[own], volume, poses_in, images, columns, precision_in]
    targets = [keys, voxel_of, weight_of, volume_v, poses, images_v, columns_v, precision]
    load = [pltpu.make_async_copy(src, dst, loads.at[i]) for i, (src, dst) in enumerate(zip(sources, targets))]

    def start_load(index):
        src, dst = sources[index], targets[index]
        pieces = 8 if src.shape[0] >= 512 else 1
        size = src.shape[0] // pieces
        for piece in range(pieces):
            at = slice(piece * size, (piece + 1) * size)
            pltpu.make_async_copy(src.at[at], dst.at[at], loads.at[index]).start()

    for index in range(5):
        start_load(index)

    for index in range(3):
        load[index].wait()
    before = jnp.zeros((slabs, cap), F32)
    for slab in range(slabs):
        before += jnp.where(keys[slab] >= 0, 1.0, 0.0) * jnp.where(own > slab, 1.0, 0.0)
    out_start = jnp.sum(before, axis=1, keepdims=True)
    total_slots = slabs * cap
    own_key = keys[own]
    own_code = voxel_of[...] * 32 + jnp.where(own_key >= 0, weight_of[...], 31)

    def ordered(first, count, tables):
        position = iota((1, count), 1) + first
        block_sel = iota((slabs, count), 0) == ((position >> 3) & (slabs - 1))
        start_row = pick_row(block_sel, out_start).astype(jnp.int32)
        slot_row = members * (position & 7) + (((position >> 7) - start_row) & 7)
        slot_sel = iota((cap, count), 0) == slot_row
        chooser = jnp.where(block_sel, 1.0, 0.0)
        found = []
        for table in tables:
            wide = lax.dot_general(
                table.astype(F32), chooser, (((0,), (0,)), ((), ())),
                precision=lax.Precision.HIGHEST, preferred_element_type=F32,
            )
            found.append(pick_row(slot_sel, wide))
        return found

    def decoded(code):
        code_row = code.astype(jnp.int32)
        level = code_row & 31
        alive = level <= WSTEPS
        spot = (code_row >> 5).astype(F32)
        lower = jnp.where(alive, level, 0).astype(F32) * (1.0 / WSTEPS)
        upper = jnp.where(alive, WSTEPS - level, 0).astype(F32) * (1.0 / WSTEPS)
        return spot, lower, upper

    parts = decoded(ordered(member * mine, mine, [own_code])[0])
    own_cols = jnp.concatenate(list(parts) + [jnp.zeros((5, mine), F32)], axis=0).T
    place = iota((mine, voxels), 1)
    spot = own_cols[:, 0:1].astype(jnp.int32)
    take = jnp.where(place == spot, own_cols[:, 1:2], 0.0) + jnp.where(place == spot + 1, own_cols[:, 2:3], 0.0)
    load[3].wait()
    for index in range(5, len(load)):
        start_load(index)
    woven = dot(take.astype(BF16), volume_v[...])
    for block in range(slabs):
        outgoing[block] = woven[block * deep : (block + 1) * deep].astype(BF16)
    pl.semaphore_wait(barrier, slabs - 1 + members - 1)

    def slab_copy(stage, src, dst, peer):
        return remote(src.at[peer], dst.at[own], slab_send.at[stage], slab_recv.at[stage], {"slab": peer})

    def slab_whole(stage, ref, count):
        blocks = ref.at[0:count]
        return remote(blocks, blocks, slab_send.at[stage], slab_recv.at[stage], {"slab": slab_peer(1)})

    def slab_exchange(stage, src, dst):
        for step in range(1, slabs):
            slab_copy(stage, src, dst, slab_peer(step)).start()

    def slab_arrivals(stage, dst):
        slab_whole(stage, dst, slabs - 1).wait_recv()

    def img_copy(slot, src, dst, device):
        return remote(src, dst, img_send.at[slot], img_recv.at[slot], {"img": device})

    slab_exchange(0, outgoing, incoming)
    incoming[own] = outgoing[own]

    in_key = jnp.concatenate(
        [jnp.sum(jnp.where(iota((slabs, cap), 0) == own, keys[slab], 0), axis=0, keepdims=True) for slab in range(slabs)],
        axis=0,
    )
    live = jnp.where(in_key >= 0, 1.0, 0.0).astype(BF16)
    count = dot(live, jnp.ones((cap, LANES), BF16))
    earlier = jnp.where(iota((slabs, slabs), 1) < iota((slabs, slabs), 0), 1.0, 0.0).astype(BF16)
    start = dot(earlier, count.astype(BF16))
    lane = iota((1, mine), 1)
    slab_sel = iota((slabs, mine), 0) == (lane >> 3)
    in_start = pick_row(slab_sel, start).astype(jnp.int32)
    in_count = pick_row(slab_sel, count).astype(jnp.int32)
    slot = members * (lane & 7) + ((member - in_start) & 7)
    pack_row = jnp.where(slot < in_count, (in_start + slot) >> 3, -1)
    pack_table[...] = jnp.broadcast_to(pack_row, (8, mine)).astype(F32)

    number = start[:, :cap].astype(jnp.int32) + iota((slabs, cap), 1)
    holder = number & (members - 1)
    ahead = ((holder >> 1) - chip) & (ring_len - 1)
    near = jnp.where(ahead == 0, 3, jnp.where(ahead == 1, 1, jnp.where(ahead == 2, 0, 2)))
    row = jnp.where((holder & 1) == core, near, members - 1 - near) * share + (number >> 3)
    key_cols, row_cols = in_key.astype(F32).T, row.astype(F32).T
    pose_ids = iota((cap, NPOSE), 1).astype(F32)
    found_rows = jnp.zeros((cap, NPOSE), F32)
    for slab in range(slabs):
        matched = key_cols[:, slab : slab + 1] == pose_ids
        found_rows += jnp.where(matched, row_cols[:, slab : slab + 1], 0.0)
        unpack[slab * cap : (slab + 1) * cap, :] = jnp.where(matched, 1.0, 0.0).astype(BF16)
    pose_row[...] = jnp.broadcast_to(jnp.sum(found_rows, axis=0, keepdims=True), (8, NPOSE)).astype(jnp.int32)

    load[4].wait()
    for part in range(poses.shape[1] // LANES):
        for k in range(0, cands, 8):
            at = (slice(k, k + 8), slice(part * LANES, (part + 1) * LANES))
            pose = poses[at]
            low, high = pose & (LANES - 1), pose >> 7
            renamed = jnp.zeros_like(pose)
            for piece in range(NPOSE // LANES):
                table = pose_row[:, piece * LANES : (piece + 1) * LANES]
                found = jnp.take_along_axis(table, low, axis=1, mode="promise_in_bounds")
                renamed = jnp.where(high == piece, found, renamed)
            named[at] = renamed

    first_chunks = 3
    ahead_of = 2 * first_chunks
    middle = 2 * ahead_of
    turn = jnp.where(own >= middle, 2, jnp.where(own >= ahead_of, 1, 0))

    def rank_chunk(block):
        at = rows_at(block * LANES, LANES)
        number = poses[:, at].astype(jnp.int16)
        for first in range(0, NPOSE, LANES):
            row = (iota((LANES, LANES), 0) + first).astype(jnp.int16)
            value = jnp.full((LANES, LANES), cands, jnp.int16)
            for k in range(cands):
                value = jnp.where(number[k : k + 1] == row, jnp.int16(k), value)
            ranks[first : first + LANES, at] = value.astype(jnp.int32)

    stripe = 2 * LANES
    stripes = width // stripe
    slabful = images_v.shape[0] // stripes

    def prepare(step):
        block = rows_at(lax.div(step, stripes) * slabful, slabful)
        at = rows_at(lax.rem(step, stripes) * stripe, stripe)
        turned[block, at] = dot(images_v[block, :], columns_v[:, at]).astype(BF16)
        rank_chunk(lax.rem(step + ahead_of, slabs))

    load[5].wait()
    load[6].wait()
    each(6, prepare)

    slab_arrivals(0, incoming)
    arrived = jnp.concatenate([incoming[block].astype(F32) for block in range(slabs)], axis=0).astype(BF16)
    pack = jnp.where(iota((share, mine), 0).astype(F32) == pack_table[0:1, :], 1.0, 0.0).astype(BF16)

    def block_of(index, first=0, size=share):
        return slices.at[index * share + first : index * share + first + size]

    FAR, RIGHT, LEFT, HOME = 0, 1, 2, 3
    slices[HOME * share : (HOME + 1) * share, :] = dot(pack, arrived).astype(BF16)

    def other(index):
        return members - 1 - index

    def top(index):
        return block_of(index, 0, half)

    def bottom(index):
        return block_of(index, half, half)

    gathers = [
        img_copy(0, top(HOME), top(LEFT), right),
        img_copy(1, bottom(HOME), bottom(RIGHT), left),
        img_copy(2, block_of(HOME), block_of(other(HOME)), partner),
        img_copy(3, bottom(HOME), bottom(LEFT), right),
        img_copy(4, top(HOME), top(RIGHT), left),
        img_copy(5, top(LEFT), top(FAR), right),
        img_copy(6, bottom(RIGHT), bottom(FAR), left),
        img_copy(7, block_of(LEFT), block_of(other(LEFT)), partner),
        img_copy(8, block_of(RIGHT), block_of(other(RIGHT)), partner),
        img_copy(9, top(FAR), top(other(FAR)), partner),
        img_copy(10, bottom(FAR), bottom(other(FAR)), partner),
    ]
    for index in range(5):
        gathers[index].start()

    each(10, prepare, 6)

    def power_step(index):
        at = rows_at(index * share, share)
        values = slices[at, :].astype(F32)
        total = 0.5 * jnp.sum(values * values, axis=1, keepdims=True)
        half_power[at, :] = jnp.broadcast_to(total, (share, LANES))

    power_step(HOME)
    gathers[0].wait_recv()
    gathers[5].start()
    gathers[1].wait_recv()
    gathers[6].start()
    gathers[3].wait_recv()
    gathers[7].start()
    gathers[4].wait_recv()
    gathers[8].start()

    chunk = 2 * LANES
    chunks = images_v.shape[0] // chunk

    def picks_of(score, pieces, numbers, value):
        for first, offset, size in pieces:
            block = score[offset : offset + size] - half_power[first : first + size, :]
            for group in range(size // 8):
                picked = jnp.take_along_axis(
                    block[group * 8 : (group + 1) * 8], numbers[0], axis=0, mode="promise_in_bounds"
                )
                value[0] = jnp.where(numbers[2] == first // 8 + group, picked, value[0])
                picked = jnp.take_along_axis(
                    block[group * 8 : (group + 1) * 8], numbers[1], axis=0, mode="promise_in_bounds"
                )
                value[1] = jnp.where(numbers[3] == first // 8 + group, picked, value[1])
        return value

    def score_chunk(index, table, pieces, resume):
        score = lax.dot_general(
            table, images_v[rows_at(index * chunk, chunk), :],
            (((1,), (1,)), ((), ())), preferred_element_type=F32,
        )
        for part in range(chunk // LANES):
            number = named[:, rows_at(index * chunk + part * LANES, LANES)]
            numbers = [number[0:8] & 7, number[8:16] & 7, number[0:8] >> 3, number[8:16] >> 3]
            block = index * (chunk // LANES) + part
            if resume:
                value = [picks[block, 0:8], picks[block, 8:16]]
            else:
                value = [jnp.zeros((8, LANES), F32), jnp.zeros((8, LANES), F32)]
            value = picks_of(score[:, part * LANES : (part + 1) * LANES], pieces, numbers, value)
            picks[block] = jnp.concatenate(value, axis=0)

    def near_step(index):
        score_chunk(index, slices[share : NPOSE - share, :], [(share, 0, NPOSE - 2 * share)], False)

    def far_chunk(index):
        table = jnp.concatenate([slices[0:share, :], slices[NPOSE - share : NPOSE, :]], axis=0)
        score_chunk(index, table, [(0, 0, share), (NPOSE - share, share, share)], True)

    def full_chunk(index):
        score_chunk(index, slices[...], [(0, 0, NPOSE)], False)

    each(12, prepare, 10)
    power_step(LEFT)
    power_step(RIGHT)
    gathers[2].wait_recv()
    power_step(other(HOME))
    gathers[7].wait_recv()
    gathers[8].wait_recv()
    power_step(other(LEFT))
    power_step(other(RIGHT))
    each(first_chunks - 1, near_step)
    gathers[5].wait_recv()
    gathers[9].start()
    gathers[6].wait_recv()
    gathers[10].start()
    each(first_chunks, near_step, first_chunks - 1)
    gathers[9].wait_recv()
    gathers[10].wait_recv()
    power_step(0)
    power_step(members - 1)

    def pick_send(peer):
        @pl.when(peer != own)
        def _():
            slab_copy(1, picks, picks_in, peer).start()

    def far_step(index):
        far_chunk(index)
        pick_send(2 * index)
        pick_send(2 * index + 1)

    def full_step(index):
        full_chunk(index)
        pick_send(2 * index)
        pick_send(2 * index + 1)

    each(first_chunks, far_step)
    each(chunks, full_step, first_chunks)
    picks_in[own] = picks[own]
    load[7].wait()
    row_weight[...] = jnp.zeros_like(row_weight)
    masses[member] = jnp.zeros((8, LANES), F32)

    def share_out():
        slab_arrivals(1, picks_in)
        total = picks_in[0]
        for block in range(1, slabs):
            total = total + picks_in[block]
        total = total * precision[:, rows_at(own * LANES, LANES)]
        exponent = jnp.exp(total - jnp.max(total, axis=0, keepdims=True))
        shares[own] = (exponent / jnp.sum(exponent, axis=0, keepdims=True)).astype(BF16)
        for step in range(1, slabs):
            remote(
                shares.at[own], shares.at[own], slab_send.at[2], slab_recv.at[5 + turn], {"slab": slab_peer(step)}
            ).start()

    @pl.when(turn == 0)
    def _():
        share_out()

    each(slabs, prepare, 12)

    @pl.when(turn != 0)
    def _():
        share_out()

    def shares_arrive(which):
        group = (ahead_of, middle - ahead_of, slabs - middle)[which]

        @pl.when(turn == which)
        def _():
            slab_whole(5 + which, shares, group - 1).wait_recv()

        @pl.when(turn != which)
        def _():
            slab_whole(5 + which, shares, group).wait_recv()

    def spread_chunk(block, spread, origin):
        at = rows_at(block * LANES, LANES)
        to = rows_at((block - origin) * LANES, LANES)
        amount = shares[block].astype(F32) * precision[:, at]
        rounded = amount.astype(BF16).astype(F32)
        low, high = rounded[0:8], rounded[8:16]
        for first in range(0, NPOSE, 16):
            values = []
            for group in (first, first + 8):
                rank = ranks[group : group + 8, at]
                place = rank & 7
                from_low = jnp.take_along_axis(low, place, axis=0, mode="promise_in_bounds")
                from_high = jnp.take_along_axis(high, place, axis=0, mode="promise_in_bounds")
                value = jnp.where(rank < 8, from_low, jnp.where(rank < cands, from_high, 0.0))
                row_weight[group : group + 8, :] += value
                values.append(value)
            spread[first : first + 16, to] = jnp.concatenate(values, axis=0).astype(BF16)

    def early_stripe(index):
        at = rows_at(index * stripe, stripe)
        partial[:, at] = dot(spread_first[...], turned[: ahead_of * LANES, at])

    shares_arrive(0)
    each(ahead_of, lambda block: spread_chunk(block, spread_first, 0))
    each(width // stripe, early_stripe)
    shares_arrive(1)
    each(middle, lambda block: spread_chunk(block, spread_middle, ahead_of), ahead_of)
    shares_arrive(2)
    waiting = list(range(middle, slabs))
    for index in range(width // stripe):
        at = slice(index * stripe, (index + 1) * stripe)
        partial[:, at] += dot(spread_middle[...], turned[ahead_of * LANES : middle * LANES, at])
        for block in waiting[index :: width // stripe]:
            spread_chunk(block, spread_last, middle)

    for piece in range(NPOSE // LANES):
        weight = row_weight[piece * LANES : (piece + 1) * LANES, :].T
        masses[member, piece : piece + 1, :] = jnp.sum(weight, axis=0, keepdims=True)

    def mass_copy(step):
        return img_copy(16, masses.at[member], masses.at[member], img_peer(step))

    def img_whole(slot, ref):
        blocks = ref.at[0 : members - 1]
        return img_copy(slot, blocks, blocks, img_peer(1))

    for step in range(1, members):
        mass_copy(step).start()

    half_rows = NPOSE // 2

    def away_copy(index):
        return img_copy(40 + index, away.at[index], away_in.at[index], partner)

    def turn_stripe(index, chip_index):
        at = rows_at(chip_index * stripe, stripe)
        part = partial[:, at] + dot(spread_last[...], turned[middle * LANES :, at])
        first, second = part[:, :LANES], part[:, LANES:]
        kept[index] = jnp.where(core == 0, first, second)
        away[index] = jnp.where(core == 0, second, first).astype(BF16)
        away_copy(index).start()

    def kept_part(index, first=0, size=NPOSE):
        rows = slice(first, first + size)
        return kept[index, rows, :] + away_in[index, rows, :].astype(F32)

    low, high = slice(0, half_rows), slice(half_rows, NPOSE)
    ring_copies = [
        img_copy(48, opposite.at[low], opposite_in.at[low], right),
        img_copy(49, opposite.at[high], opposite_in.at[high], left),
        img_copy(50, ring.at[0, high], ring_in.at[0, high], right),
        img_copy(51, ring.at[1, low], ring_in.at[1, low], left),
        img_copy(52, ring.at[0, low], ring_in.at[0, low], right),
        img_copy(53, ring.at[1, high], ring_in.at[1, high], left),
    ]
    turn_stripe(FAR, lax.rem(chip + 2, ring_len))
    turn_stripe(RIGHT, lax.rem(chip + 1, ring_len))
    away_copy(FAR).wait_recv()
    opposite[...] = kept_part(FAR).astype(BF16)
    ring_copies[0].start()
    ring_copies[1].start()
    turn_stripe(LEFT, lax.rem(chip + ring_len - 1, ring_len))
    away_copy(RIGHT).wait_recv()
    ring[0, high] = kept_part(RIGHT, half_rows, half_rows).astype(BF16)
    ring_copies[2].start()
    turn_stripe(HOME, chip)
    away_copy(LEFT).wait_recv()
    ring[1, low] = kept_part(LEFT, 0, half_rows).astype(BF16)
    ring_copies[3].start()
    ring_copies[0].wait_recv()
    ring[0, low] = (kept_part(RIGHT, 0, half_rows) + opposite_in[low, :].astype(F32)).astype(BF16)
    ring_copies[4].start()
    ring_copies[1].wait_recv()
    ring[1, high] = (kept_part(LEFT, half_rows, half_rows) + opposite_in[high, :].astype(F32)).astype(BF16)
    ring_copies[5].start()
    shares_copy = pltpu.make_async_copy(shares, shares_out, loads.at[8])
    shares_copy.start()
    away_copy(HOME).wait_recv()
    held = kept_part(HOME)
    for index in range(2, 6):
        ring_copies[index].wait_recv()
    summed = (held + ring_in[0].astype(F32) + ring_in[1].astype(F32)).astype(BF16)

    unpacked = dot(unpack[...], summed)
    for slab in range(slabs):
        returning[slab] = unpacked[slab * cap : (slab + 1) * cap].astype(BF16)
    slab_exchange(3, returning, returned)
    returned[own] = returning[own]

    img_whole(16, masses).wait_recv()
    mass_sum = masses[0]
    for index in range(1, members):
        mass_sum = mass_sum + masses[index]
    mass_row = jnp.concatenate([mass_sum[piece : piece + 1] for piece in range(NPOSE // LANES)], axis=1)
    own_keys = keys[own]
    levels = weight_of[...].astype(F32) * (1.0 / WSTEPS)
    alive = jnp.where(own_keys >= 0, 1.0, 0.0)
    spot_cols = voxel_of[...].astype(F32).T.astype(jnp.int32)
    lower_cols, upper_cols = (levels * alive).T, ((1.0 - levels) * alive).T
    own_key_cols = own_keys.astype(F32).T
    voxel = iota((cap, voxels), 1)
    mass = jnp.zeros((1, voxels), F32)
    for block in range(slabs):
        spots, lows, highs, key = (
            table[:, block : block + 1] for table in (spot_cols, lower_cols, upper_cols, own_key_cols)
        )
        value = jnp.where(voxel == spots, lows, 0.0) + jnp.where(voxel == spots + 1, highs, 0.0)
        weave[block * cap : (block + 1) * cap, :] = value.astype(BF16)
        amount = jnp.sum(jnp.where(key == pose_ids, mass_row, 0.0), axis=1, keepdims=True)
        mass += pick_row(value > 0.0, value * amount)
    inverse[...] = 1.0 / (mass + RIDGE)
    for stage, ref in ((0, outgoing), (1, picks), (2, shares)):
        slab_whole(stage, ref, slabs - 1).wait_send()
    for copy in gathers + ring_copies:
        copy.wait_send()
    for index in range(ring_len):
        away_copy(index).wait_send()
    img_whole(16, masses).wait_send()
    slab_arrivals(3, returned)

    pair = LANES // cap
    slots = jnp.concatenate(
        [
            returned[block : block + pair].reshape(LANES, LANES).astype(F32).T.astype(BF16)
            for block in range(0, slabs, pair)
        ],
        axis=1,
    )
    fourier[...] = (dot(slots, weave[...]) * inverse[...]).astype(BF16)
    shares_copy.wait()
    slab_whole(3, returning, slabs - 1).wait_send()


def finish(rows, fourier, shares, density, posterior):
    planes, columns_out, edge = density.shape
    real = jnp.concatenate([fourier[:columns_out, z * edge : (z + 1) * edge] for z in range(planes)], axis=0)
    imag = jnp.concatenate([fourier[columns_out:, z * edge : (z + 1) * edge] for z in range(planes)], axis=0)
    value = dot(real, rows[:edge, :]) + dot(imag, rows[edge:, :])
    for z in range(planes):
        density[z] = value[z * columns_out : (z + 1) * columns_out]
    for block in range(shares.shape[0]):
        posterior[:, block * LANES : (block + 1) * LANES] = shares[block].astype(F32)


def per_device(images, volume, precision, candidates, slot_key, slot_voxel, slot_weight):
    members = lax.axis_size("img")
    slabs = lax.axis_size("slab")
    planes, edge, width = volume.shape
    particles, cands = candidates.shape
    cap = slot_key.shape[2]
    deep = cap // members
    share = NPOSE // members
    voxels = planes * edge
    mine = slabs * deep
    side = NPOSE // 2
    big = pl.BlockSpec(memory_space=pl.ANY)
    near = pl.BlockSpec(memory_space=pltpu.VMEM)
    scratch = [
        pltpu.VMEM((particles, width), BF16),
        pltpu.VMEM((voxels, width), BF16),
        pltpu.VMEM((width, width), BF16),
        pltpu.VMEM((1, particles), F32),
        pltpu.VMEM((cands, particles), jnp.int32),
        pltpu.VMEM(slot_key.shape, jnp.int32),
        pltpu.VMEM(slot_key.shape[1:], jnp.int32),
        pltpu.VMEM(slot_key.shape[1:], jnp.int32),
        pltpu.VMEM((8, mine), F32),
        pltpu.VMEM((8, NPOSE), jnp.int32),
        pltpu.VMEM((cands, particles), jnp.int32),
        pltpu.VMEM((slabs * cap, NPOSE), BF16),
        pltpu.VMEM((slabs, deep, width), BF16),
        pltpu.VMEM((slabs, deep, width), BF16),
        pltpu.VMEM((NPOSE, width), BF16),
        pltpu.VMEM((NPOSE, LANES), F32),
        pltpu.VMEM((NPOSE, particles), jnp.int32),
        pltpu.VMEM((slabs * cap, voxels), BF16),
        pltpu.VMEM((slabs, cands, LANES), F32),
        pltpu.VMEM((slabs, cands, LANES), F32),
        pltpu.VMEM((slabs, cands, LANES), BF16),
        pltpu.VMEM((NPOSE, 6 * LANES), BF16),
        pltpu.VMEM((NPOSE, 6 * LANES), BF16),
        pltpu.VMEM((NPOSE, 4 * LANES), BF16),
        pltpu.VMEM((NPOSE, LANES), F32),
        pltpu.VMEM((NPOSE, width), F32),
        pltpu.VMEM((particles, width), BF16),
        pltpu.VMEM((members // 2, NPOSE, LANES), BF16),
        pltpu.VMEM((members // 2, NPOSE, LANES), BF16),
        pltpu.VMEM((members // 2, NPOSE, LANES), F32),
        pltpu.VMEM((NPOSE, LANES), BF16),
        pltpu.VMEM((NPOSE, LANES), BF16),
        pltpu.VMEM((2, NPOSE, LANES), BF16),
        pltpu.VMEM((2, NPOSE, LANES), BF16),
        pltpu.VMEM((members, 8, LANES), F32),
        pltpu.VMEM((1, voxels), F32),
        pltpu.VMEM((slabs, cap, LANES), BF16),
        pltpu.VMEM((slabs, cap, LANES), BF16),
        pltpu.SemaphoreType.DMA((9,)),
        pltpu.SemaphoreType.DMA((8,)),
        pltpu.SemaphoreType.DMA((8,)),
        pltpu.SemaphoreType.DMA((60,)),
        pltpu.SemaphoreType.DMA((60,)),
    ]
    fourier, shares = pl.pallas_call(
        functools.partial(kernel, slabs, members),
        out_shape=(
            jax.ShapeDtypeStruct((LANES, voxels), BF16),
            jax.ShapeDtypeStruct((slabs, cands, LANES), BF16),
        ),
        in_specs=[big] * 8,
        out_specs=(near, big),
        scratch_shapes=scratch,
        compiler_params=pltpu.CompilerParams(
            collective_id=0, has_side_effects=True, vmem_limit_bytes=56 * 1024 * 1024
        ),
    )(
        images, volume.reshape(voxels, width), column_table(edge, members),
        precision[None, :], candidates.T, slot_key, slot_voxel, slot_weight,
    )
    density, posterior = pl.pallas_call(
        finish,
        out_shape=(
            jax.ShapeDtypeStruct((planes, edge // members, edge), F32),
            jax.ShapeDtypeStruct((cands, particles), F32),
        ),
        in_specs=[near] * 3,
        out_specs=(near, near),
        compiler_params=pltpu.CompilerParams(vmem_limit_bytes=56 * 1024 * 1024),
    )(row_table(edge), fourier, shares)
    return density.transpose(0, 2, 1), posterior.T


def solution(mesh):
    placed = (P("img", "slab"), P("slab", None, None), P("img"), P("img", None), P(), P(), P())
    return jax.shard_map(
        per_device,
        mesh=mesh,
        in_specs=placed,
        out_specs=(P("slab", None, "img"), P("img", None)),
        check_vma=False,
    )
```

```python
import functools
import math

import jax
import jax.numpy as jnp
import numpy as np
from jax import lax
from jax.experimental import pallas as pl
from jax.experimental.pallas import tpu as pltpu
from jax.sharding import PartitionSpec as P

NPOSE = 512
WSTEPS = 16
RIDGE = 0.25
LANES = 128
F32 = jnp.float32
BF16 = jnp.bfloat16


def gridding(samples):
    offset = (np.arange(samples) - samples / 2) / samples
    return 1.0 / np.sinc(offset) ** 2


def angles(length):
    counter = np.arange(length)
    return (counter[:, None] * counter[None, :] % length) * (2.0 * math.pi / length)


def column_table(length, members):
    turn = angles(length)
    cosine, sine = np.cos(turn), np.sin(turn)
    scale = gridding(length)[None, :]
    to_re = np.concatenate([cosine, -sine], axis=0) * scale
    to_im = np.concatenate([sine, cosine], axis=0) * scale
    width = length // members
    both = np.stack([to_re.reshape(-1, members, width), to_im.reshape(-1, members, width)], axis=2)
    return jnp.asarray(both.reshape(2 * length, 2 * length), BF16)


def row_table(length):
    turn = angles(length)
    scale = gridding(length)[None, :] / length
    return jnp.asarray(np.concatenate([np.cos(turn), -np.sin(turn)], axis=0) * scale, BF16)


def remote(src, dst, sends, recvs, device):
    return pltpu.make_async_remote_copy(
        src_ref=src,
        dst_ref=dst,
        send_sem=sends,
        recv_sem=recvs,
        device_id=device,
        device_id_type=pl.DeviceIdType.MESH,
    )


def dot(left, right):
    return jnp.dot(left, right, preferred_element_type=F32)


def each(count, step, first=0):
    def body(index, carry):
        step(index)
        return carry

    lax.fori_loop(first, count, body, 0)


def rows_at(start, size):
    return pl.ds(pl.multiple_of(start, size), size)


def iota(shape, axis):
    return lax.broadcasted_iota(jnp.int32, shape, axis)


def pick_row(mask, values):
    return jnp.sum(jnp.where(mask, values, 0.0), axis=0, keepdims=True)


def kernel(
    slabs, members,
    images, volume, columns, precision_in, poses_in, keys_in, voxels_in, weights_in,
    fourier, shares_out,
    images_v, volume_v, columns_v, precision, poses, keys, voxel_of, weight_of,
    pack_table, pose_row, named, unpack,
    outgoing, incoming, slices, half_power, ranks, weave,
    picks, picks_in, shares, spread_first, spread_middle, spread_last, row_weight, partial, turned,
    away, away_in, kept, opposite, opposite_in, ring, ring_in,
    masses, inverse, returning, returned,
    loads, slab_send, slab_recv, img_send, img_recv,
):
    own = lax.axis_index("slab")
    member = lax.axis_index("img")
    ring_len = members // 2
    chip, core = member // 2, lax.rem(member, 2)
    share = NPOSE // members
    half = share // 2
    side = ring_len * share
    deep = outgoing.shape[1]
    mine = slabs * deep
    cap = keys.shape[2]
    width = volume_v.shape[1]
    voxels = volume_v.shape[0]
    cands = poses.shape[0]
    right = 2 * lax.rem(chip + 1, ring_len) + core
    left = 2 * lax.rem(chip + ring_len - 1, ring_len) + core
    partner = 2 * chip + 1 - core

    def slab_peer(step):
        return lax.rem(own + step, slabs)

    def img_peer(step):
        return lax.rem(member + step, members)

    barrier = pltpu.get_barrier_semaphore()

    def greet(axis, peer):
        pl.semaphore_signal(barrier, inc=1, device_id={axis: peer}, device_id_type=pl.DeviceIdType.MESH)

    for step in range(1, slabs):
        greet("slab", slab_peer(step))
    for step in range(1, members):
        greet("img", img_peer(step))
    sources = [keys_in, voxels_in.at[own], weights_in.at[own], volume, poses_in, images, columns, precision_in]
    targets = [keys, voxel_of, weight_of, volume_v, poses, images_v, columns_v, precision]
    load = [pltpu.make_async_copy(src, dst, loads.at[i]) for i, (src, dst) in enumerate(zip(sources, targets))]

    def start_load(index):
        src, dst = sources[index], targets[index]
        pieces = 8 if src.shape[0] >= 512 else 1
        size = src.shape[0] // pieces
        for piece in range(pieces):
            at = slice(piece * size, (piece + 1) * size)
            pltpu.make_async_copy(src.at[at], dst.at[at], loads.at[index]).start()

    for index in range(5):
        start_load(index)

    for index in range(3):
        load[index].wait()
    before = jnp.zeros((slabs, cap), F32)
    for slab in range(slabs):
        before += jnp.where(keys[slab] >= 0, 1.0, 0.0) * jnp.where(own > slab, 1.0, 0.0)
    out_start = jnp.sum(before, axis=1, keepdims=True)
    total_slots = slabs * cap
    own_key = keys[own]
    own_code = voxel_of[...] * 32 + jnp.where(own_key >= 0, weight_of[...], 31)

    def ordered(first, count, tables):
        position = iota((1, count), 1) + first
        block_sel = iota((slabs, count), 0) == ((position >> 3) & (slabs - 1))
        start_row = pick_row(block_sel, out_start).astype(jnp.int32)
        slot_row = members * (position & 7) + (((position >> 7) - start_row) & 7)
        slot_sel = iota((cap, count), 0) == slot_row
        chooser = jnp.where(block_sel, 1.0, 0.0)
        found = []
        for table in tables:
            wide = lax.dot_general(
                table.astype(F32), chooser, (((0,), (0,)), ((), ())),
                precision=lax.Precision.HIGHEST, preferred_element_type=F32,
            )
            found.append(pick_row(slot_sel, wide))
        return found

    def decoded(code):
        code_row = code.astype(jnp.int32)
        level = code_row & 31
        alive = level <= WSTEPS
        spot = (code_row >> 5).astype(F32)
        lower = jnp.where(alive, level, 0).astype(F32) * (1.0 / WSTEPS)
        upper = jnp.where(alive, WSTEPS - level, 0).astype(F32) * (1.0 / WSTEPS)
        return spot, lower, upper

    parts = decoded(ordered(member * mine, mine, [own_code])[0])
    own_cols = jnp.concatenate(list(parts) + [jnp.zeros((5, mine), F32)], axis=0).T
    place = iota((mine, voxels), 1)
    spot = own_cols[:, 0:1].astype(jnp.int32)
    take = jnp.where(place == spot, own_cols[:, 1:2], 0.0) + jnp.where(place == spot + 1, own_cols[:, 2:3], 0.0)
    load[3].wait()
    for index in range(5, len(load)):
        start_load(index)
    woven = dot(take.astype(BF16), volume_v[...])
    for block in range(slabs):
        outgoing[block] = woven[block * deep : (block + 1) * deep].astype(BF16)
    pl.semaphore_wait(barrier, slabs - 1 + members - 1)

    def slab_copy(stage, src, dst, peer):
        return remote(src.at[peer], dst.at[own], slab_send.at[stage], slab_recv.at[stage], {"slab": peer})

    def slab_whole(stage, ref, count):
        blocks = ref.at[0:count]
        return remote(blocks, blocks, slab_send.at[stage], slab_recv.at[stage], {"slab": slab_peer(1)})

    def slab_exchange(stage, src, dst):
        for step in range(1, slabs):
            slab_copy(stage, src, dst, slab_peer(step)).start()

    def slab_arrivals(stage, dst):
        slab_whole(stage, dst, slabs - 1).wait_recv()

    def img_copy(slot, src, dst, device):
        return remote(src, dst, img_send.at[slot], img_recv.at[slot], {"img": device})

    slab_exchange(0, outgoing, incoming)
    incoming[own] = outgoing[own]

    in_key = jnp.concatenate(
        [jnp.sum(jnp.where(iota((slabs, cap), 0) == own, keys[slab], 0), axis=0, keepdims=True) for slab in range(slabs)],
        axis=0,
    )
    live = jnp.where(in_key >= 0, 1.0, 0.0).astype(BF16)
    count = dot(live, jnp.ones((cap, LANES), BF16))
    earlier = jnp.where(iota((slabs, slabs), 1) < iota((slabs, slabs), 0), 1.0, 0.0).astype(BF16)
    start = dot(earlier, count.astype(BF16))
    lane = iota((1, mine), 1)
    slab_sel = iota((slabs, mine), 0) == (lane >> 3)
    in_start = pick_row(slab_sel, start).astype(jnp.int32)
    in_count = pick_row(slab_sel, count).astype(jnp.int32)
    slot = members * (lane & 7) + ((member - in_start) & 7)
    pack_row = jnp.where(slot < in_count, (in_start + slot) >> 3, -1)
    pack_table[...] = jnp.broadcast_to(pack_row, (8, mine)).astype(F32)

    number = start[:, :cap].astype(jnp.int32) + iota((slabs, cap), 1)
    holder = number & (members - 1)
    ahead = ((holder >> 1) - chip) & (ring_len - 1)
    near = jnp.where(ahead == 0, 3, jnp.where(ahead == 1, 1, jnp.where(ahead == 2, 0, 2)))
    row = jnp.where((holder & 1) == core, near, members - 1 - near) * share + (number >> 3)
    key_cols, row_cols = in_key.astype(F32).T, row.astype(F32).T
    pose_ids = iota((cap, NPOSE), 1).astype(F32)
    found_rows = jnp.zeros((cap, NPOSE), F32)
    for slab in range(slabs):
        matched = key_cols[:, slab : slab + 1] == pose_ids
        found_rows += jnp.where(matched, row_cols[:, slab : slab + 1], 0.0)
        unpack[slab * cap : (slab + 1) * cap, :] = jnp.where(matched, 1.0, 0.0).astype(BF16)
    pose_row[...] = jnp.broadcast_to(jnp.sum(found_rows, axis=0, keepdims=True), (8, NPOSE)).astype(jnp.int32)

    load[4].wait()
    for part in range(poses.shape[1] // LANES):
        for k in range(0, cands, 8):
            at = (slice(k, k + 8), slice(part * LANES, (part + 1) * LANES))
            pose = poses[at]
            low, high = pose & (LANES - 1), pose >> 7
            renamed = jnp.zeros_like(pose)
            for piece in range(NPOSE // LANES):
                table = pose_row[:, piece * LANES : (piece + 1) * LANES]
                found = jnp.take_along_axis(table, low, axis=1, mode="promise_in_bounds")
                renamed = jnp.where(high == piece, found, renamed)
            named[at] = renamed

    first_chunks = 3
    ahead_of = 2 * first_chunks
    middle = 2 * ahead_of
    turn = jnp.where(own >= middle, 2, jnp.where(own >= ahead_of, 1, 0))

    def rank_chunk(block):
        at = rows_at(block * LANES, LANES)
        number = poses[:, at].astype(jnp.int16)
        for first in range(0, NPOSE, LANES):
            row = (iota((LANES, LANES), 0) + first).astype(jnp.int16)
            value = jnp.full((LANES, LANES), cands, jnp.int16)
            for k in range(cands):
                value = jnp.where(number[k : k + 1] == row, jnp.int16(k), value)
            ranks[first : first + LANES, at] = value.astype(jnp.int32)

    stripe = 2 * LANES
    stripes = width // stripe
    slabful = images_v.shape[0] // stripes

    def prepare(step):
        block = rows_at(lax.div(step, stripes) * slabful, slabful)
        at = rows_at(lax.rem(step, stripes) * stripe, stripe)
        turned[block, at] = dot(images_v[block, :], columns_v[:, at]).astype(BF16)
        rank_chunk(lax.rem(step + ahead_of, slabs))

    load[5].wait()
    load[6].wait()
    each(6, prepare)

    slab_arrivals(0, incoming)
    arrived = jnp.concatenate([incoming[block].astype(F32) for block in range(slabs)], axis=0).astype(BF16)
    pack = jnp.where(iota((share, mine), 0).astype(F32) == pack_table[0:1, :], 1.0, 0.0).astype(BF16)

    def block_of(index, first=0, size=share):
        return slices.at[index * share + first : index * share + first + size]

    FAR, RIGHT, LEFT, HOME = 0, 1, 2, 3
    slices[HOME * share : (HOME + 1) * share, :] = dot(pack, arrived).astype(BF16)

    def other(index):
        return members - 1 - index

    def top(index):
        return block_of(index, 0, half)

    def bottom(index):
        return block_of(index, half, half)

    gathers = [
        img_copy(0, top(HOME), top(LEFT), right),
        img_copy(1, bottom(HOME), bottom(RIGHT), left),
        img_copy(2, block_of(HOME), block_of(other(HOME)), partner),
        img_copy(3, bottom(HOME), bottom(LEFT), right),
        img_copy(4, top(HOME), top(RIGHT), left),
        img_copy(5, top(LEFT), top(FAR), right),
        img_copy(6, bottom(RIGHT), bottom(FAR), left),
        img_copy(7, block_of(LEFT), block_of(other(LEFT)), partner),
        img_copy(8, block_of(RIGHT), block_of(other(RIGHT)), partner),
        img_copy(9, top(FAR), top(other(FAR)), partner),
        img_copy(10, bottom(FAR), bottom(other(FAR)), partner),
    ]
    for index in range(5):
        gathers[index].start()

    each(10, prepare, 6)

    def power_step(index):
        at = rows_at(index * share, share)
        values = slices[at, :].astype(F32)
        total = 0.5 * jnp.sum(values * values, axis=1, keepdims=True)
        half_power[at, :] = jnp.broadcast_to(total, (share, LANES))

    power_step(HOME)
    gathers[0].wait_recv()
    gathers[5].start()
    gathers[1].wait_recv()
    gathers[6].start()
    gathers[3].wait_recv()
    gathers[7].start()
    gathers[4].wait_recv()
    gathers[8].start()

    chunk = 2 * LANES
    chunks = images_v.shape[0] // chunk

    def picks_of(score, pieces, numbers, value):
        for first, offset, size in pieces:
            block = score[offset : offset + size] - half_power[first : first + size, :]
            for group in range(size // 8):
                picked = jnp.take_along_axis(
                    block[group * 8 : (group + 1) * 8], numbers[0], axis=0, mode="promise_in_bounds"
                )
                value[0] = jnp.where(numbers[2] == first // 8 + group, picked, value[0])
                picked = jnp.take_along_axis(
                    block[group * 8 : (group + 1) * 8], numbers[1], axis=0, mode="promise_in_bounds"
                )
                value[1] = jnp.where(numbers[3] == first // 8 + group, picked, value[1])
        return value

    def score_chunk(index, table, pieces, resume):
        score = lax.dot_general(
            table, images_v[rows_at(index * chunk, chunk), :],
            (((1,), (1,)), ((), ())), preferred_element_type=F32,
        )
        for part in range(chunk // LANES):
            number = named[:, rows_at(index * chunk + part * LANES, LANES)]
            numbers = [number[0:8] & 7, number[8:16] & 7, number[0:8] >> 3, number[8:16] >> 3]
            block = index * (chunk // LANES) + part
            if resume:
                value = [picks[block, 0:8], picks[block, 8:16]]
            else:
                value = [jnp.zeros((8, LANES), F32), jnp.zeros((8, LANES), F32)]
            value = picks_of(score[:, part * LANES : (part + 1) * LANES], pieces, numbers, value)
            picks[block] = jnp.concatenate(value, axis=0)

    def near_step(index):
        score_chunk(index, slices[share : NPOSE - share, :], [(share, 0, NPOSE - 2 * share)], False)

    def far_chunk(index):
        table = jnp.concatenate([slices[0:share, :], slices[NPOSE - share : NPOSE, :]], axis=0)
        score_chunk(index, table, [(0, 0, share), (NPOSE - share, share, share)], True)

    def full_chunk(index):
        score_chunk(index, slices[...], [(0, 0, NPOSE)], False)

    each(12, prepare, 10)
    power_step(LEFT)
    power_step(RIGHT)
    gathers[2].wait_recv()
    power_step(other(HOME))
    gathers[7].wait_recv()
    gathers[8].wait_recv()
    power_step(other(LEFT))
    power_step(other(RIGHT))
    each(first_chunks - 1, near_step)
    gathers[5].wait_recv()
    gathers[9].start()
    gathers[6].wait_recv()
    gathers[10].start()
    each(first_chunks, near_step, first_chunks - 1)
    gathers[9].wait_recv()
    gathers[10].wait_recv()
    power_step(0)
    power_step(members - 1)

    def pick_send(peer):
        @pl.when(peer != own)
        def _():
            slab_copy(1, picks, picks_in, peer).start()

    def far_step(index):
        far_chunk(index)
        pick_send(2 * index)
        pick_send(2 * index + 1)

    def full_step(index):
        full_chunk(index)
        pick_send(2 * index)
        pick_send(2 * index + 1)

    each(first_chunks, far_step)
    each(chunks, full_step, first_chunks)
    picks_in[own] = picks[own]
    load[7].wait()
    row_weight[...] = jnp.zeros_like(row_weight)
    masses[member] = jnp.zeros((8, LANES), F32)

    def share_out():
        slab_arrivals(1, picks_in)
        total = picks_in[0]
        for block in range(1, slabs):
            total = total + picks_in[block]
        total = total * precision[:, rows_at(own * LANES, LANES)]
        exponent = jnp.exp(total - jnp.max(total, axis=0, keepdims=True))
        shares[own] = (exponent / jnp.sum(exponent, axis=0, keepdims=True)).astype(BF16)
        for step in range(1, slabs):
            remote(
                shares.at[own], shares.at[own], slab_send.at[2], slab_recv.at[5 + turn], {"slab": slab_peer(step)}
            ).start()

    @pl.when(turn == 0)
    def _():
        share_out()

    each(slabs, prepare, 12)

    @pl.when(turn != 0)
    def _():
        share_out()

    def shares_arrive(which):
        group = (ahead_of, middle - ahead_of, slabs - middle)[which]

        @pl.when(turn == which)
        def _():
            slab_whole(5 + which, shares, group - 1).wait_recv()

        @pl.when(turn != which)
        def _():
            slab_whole(5 + which, shares, group).wait_recv()

    def spread_chunk(block, spread, origin):
        at = rows_at(block * LANES, LANES)
        to = rows_at((block - origin) * LANES, LANES)
        amount = shares[block].astype(F32) * precision[:, at]
        rounded = amount.astype(BF16).astype(F32)
        low, high = rounded[0:8], rounded[8:16]
        for first in range(0, NPOSE, 16):
            values = []
            for group in (first, first + 8):
                rank = ranks[group : group + 8, at]
                place = rank & 7
                from_low = jnp.take_along_axis(low, place, axis=0, mode="promise_in_bounds")
                from_high = jnp.take_along_axis(high, place, axis=0, mode="promise_in_bounds")
                value = jnp.where(rank < 8, from_low, jnp.where(rank < cands, from_high, 0.0))
                row_weight[group : group + 8, :] += value
                values.append(value)
            spread[first : first + 16, to] = jnp.concatenate(values, axis=0).astype(BF16)

    def early_stripe(index):
        at = rows_at(index * stripe, stripe)
        partial[:, at] = dot(spread_first[...], turned[: ahead_of * LANES, at])

    shares_arrive(0)
    each(ahead_of, lambda block: spread_chunk(block, spread_first, 0))
    each(width // stripe, early_stripe)
    shares_arrive(1)
    each(middle, lambda block: spread_chunk(block, spread_middle, ahead_of), ahead_of)
    shares_arrive(2)
    waiting = list(range(middle, slabs))
    for index in range(width // stripe):
        at = slice(index * stripe, (index + 1) * stripe)
        partial[:, at] += dot(spread_middle[...], turned[ahead_of * LANES : middle * LANES, at])
        for block in waiting[index :: width // stripe]:
            spread_chunk(block, spread_last, middle)

    for piece in range(NPOSE // LANES):
        weight = row_weight[piece * LANES : (piece + 1) * LANES, :].T
        masses[member, piece : piece + 1, :] = jnp.sum(weight, axis=0, keepdims=True)

    def mass_copy(step):
        return img_copy(16, masses.at[member], masses.at[member], img_peer(step))

    def img_whole(slot, ref):
        blocks = ref.at[0 : members - 1]
        return img_copy(slot, blocks, blocks, img_peer(1))

    for step in range(1, members):
        mass_copy(step).start()

    half_rows = NPOSE // 2

    def away_copy(index):
        return img_copy(40 + index, away.at[index], away_in.at[index], partner)

    def turn_stripe(index, chip_index):
        at = rows_at(chip_index * stripe, stripe)
        part = partial[:, at] + dot(spread_last[...], turned[middle * LANES :, at])
        first, second = part[:, :LANES], part[:, LANES:]
        kept[index] = jnp.where(core == 0, first, second)
        away[index] = jnp.where(core == 0, second, first).astype(BF16)
        away_copy(index).start()

    def kept_part(index, first=0, size=NPOSE):
        rows = slice(first, first + size)
        return kept[index, rows, :] + away_in[index, rows, :].astype(F32)

    low, high = slice(0, half_rows), slice(half_rows, NPOSE)
    ring_copies = [
        img_copy(48, opposite.at[low], opposite_in.at[low], right),
        img_copy(49, opposite.at[high], opposite_in.at[high], left),
        img_copy(50, ring.at[0, high], ring_in.at[0, high], right),
        img_copy(51, ring.at[1, low], ring_in.at[1, low], left),
        img_copy(52, ring.at[0, low], ring_in.at[0, low], right),
        img_copy(53, ring.at[1, high], ring_in.at[1, high], left),
    ]
    turn_stripe(FAR, lax.rem(chip + 2, ring_len))
    turn_stripe(RIGHT, lax.rem(chip + 1, ring_len))
    away_copy(FAR).wait_recv()
    opposite[...] = kept_part(FAR).astype(BF16)
    ring_copies[0].start()
    ring_copies[1].start()
    turn_stripe(LEFT, lax.rem(chip + ring_len - 1, ring_len))
    away_copy(RIGHT).wait_recv()
    ring[0, high] = kept_part(RIGHT, half_rows, half_rows).astype(BF16)
    ring_copies[2].start()
    turn_stripe(HOME, chip)
    away_copy(LEFT).wait_recv()
    ring[1, low] = kept_part(LEFT, 0, half_rows).astype(BF16)
    ring_copies[3].start()
    ring_copies[0].wait_recv()
    ring[0, low] = (kept_part(RIGHT, 0, half_rows) + opposite_in[low, :].astype(F32)).astype(BF16)
    ring_copies[4].start()
    ring_copies[1].wait_recv()
    ring[1, high] = (kept_part(LEFT, half_rows, half_rows) + opposite_in[high, :].astype(F32)).astype(BF16)
    ring_copies[5].start()
    shares_copy = pltpu.make_async_copy(shares, shares_out, loads.at[8])
    shares_copy.start()
    away_copy(HOME).wait_recv()
    held = kept_part(HOME)
    for index in range(2, 6):
        ring_copies[index].wait_recv()
    summed = (held + ring_in[0].astype(F32) + ring_in[1].astype(F32)).astype(BF16)

    unpacked = dot(unpack[...], summed)
    for slab in range(slabs):
        returning[slab] = unpacked[slab * cap : (slab + 1) * cap].astype(BF16)
    slab_exchange(3, returning, returned)
    returned[own] = returning[own]

    img_whole(16, masses).wait_recv()
    mass_sum = masses[0]
    for index in range(1, members):
        mass_sum = mass_sum + masses[index]
    mass_row = jnp.concatenate([mass_sum[piece : piece + 1] for piece in range(NPOSE // LANES)], axis=1)
    own_keys = keys[own]
    levels = weight_of[...].astype(F32) * (1.0 / WSTEPS)
    alive = jnp.where(own_keys >= 0, 1.0, 0.0)
    spot_cols = voxel_of[...].astype(F32).T.astype(jnp.int32)
    lower_cols, upper_cols = (levels * alive).T, ((1.0 - levels) * alive).T
    own_key_cols = own_keys.astype(F32).T
    voxel = iota((cap, voxels), 1)
    mass = jnp.zeros((1, voxels), F32)
    for block in range(slabs):
        spots, lows, highs, key = (
            table[:, block : block + 1] for table in (spot_cols, lower_cols, upper_cols, own_key_cols)
        )
        value = jnp.where(voxel == spots, lows, 0.0) + jnp.where(voxel == spots + 1, highs, 0.0)
        weave[block * cap : (block + 1) * cap, :] = value.astype(BF16)
        amount = jnp.sum(jnp.where(key == pose_ids, mass_row, 0.0), axis=1, keepdims=True)
        mass += pick_row(value > 0.0, value * amount)
    inverse[...] = 1.0 / (mass + RIDGE)
    for stage, ref in ((0, outgoing), (1, picks), (2, shares)):
        slab_whole(stage, ref, slabs - 1).wait_send()
    for copy in gathers + ring_copies:
        copy.wait_send()
    for index in range(ring_len):
        away_copy(index).wait_send()
    img_whole(16, masses).wait_send()
    slab_arrivals(3, returned)

    pair = LANES // cap
    slots = jnp.concatenate(
        [
            returned[block : block + pair].reshape(LANES, LANES).astype(F32).T.astype(BF16)
            for block in range(0, slabs, pair)
        ],
        axis=1,
    )
    fourier[...] = (dot(slots, weave[...]) * inverse[...]).astype(BF16)
    shares_copy.wait()
    slab_whole(3, returning, slabs - 1).wait_send()


def finish(rows, fourier, shares, density, posterior):
    planes, columns_out, edge = density.shape
    real = jnp.concatenate([fourier[:columns_out, z * edge : (z + 1) * edge] for z in range(planes)], axis=0)
    imag = jnp.concatenate([fourier[columns_out:, z * edge : (z + 1) * edge] for z in range(planes)], axis=0)
    value = dot(real, rows[:edge, :]) + dot(imag, rows[edge:, :])
    for z in range(planes):
        density[z] = value[z * columns_out : (z + 1) * columns_out]
    for block in range(shares.shape[0]):
        posterior[:, block * LANES : (block + 1) * LANES] = shares[block].astype(F32)


def per_device(images, volume, precision, candidates, slot_key, slot_voxel, slot_weight):
    members = lax.axis_size("img")
    slabs = lax.axis_size("slab")
    planes, edge, width = volume.shape
    particles, cands = candidates.shape
    cap = slot_key.shape[2]
    deep = cap // members
    share = NPOSE // members
    voxels = planes * edge
    mine = slabs * deep
    side = NPOSE // 2
    big = pl.BlockSpec(memory_space=pl.ANY)
    near = pl.BlockSpec(memory_space=pltpu.VMEM)
    scratch = [
        pltpu.VMEM((particles, width), BF16),
        pltpu.VMEM((voxels, width), BF16),
        pltpu.VMEM((width, width), BF16),
        pltpu.VMEM((1, particles), F32),
        pltpu.VMEM((cands, particles), jnp.int32),
        pltpu.VMEM(slot_key.shape, jnp.int32),
        pltpu.VMEM(slot_key.shape[1:], jnp.int32),
        pltpu.VMEM(slot_key.shape[1:], jnp.int32),
        pltpu.VMEM((8, mine), F32),
        pltpu.VMEM((8, NPOSE), jnp.int32),
        pltpu.VMEM((cands, particles), jnp.int32),
        pltpu.VMEM((slabs * cap, NPOSE), BF16),
        pltpu.VMEM((slabs, deep, width), BF16),
        pltpu.VMEM((slabs, deep, width), BF16),
        pltpu.VMEM((NPOSE, width), BF16),
        pltpu.VMEM((NPOSE, LANES), F32),
        pltpu.VMEM((NPOSE, particles), jnp.int32),
        pltpu.VMEM((slabs * cap, voxels), BF16),
        pltpu.VMEM((slabs, cands, LANES), F32),
        pltpu.VMEM((slabs, cands, LANES), F32),
        pltpu.VMEM((slabs, cands, LANES), BF16),
        pltpu.VMEM((NPOSE, 6 * LANES), BF16),
        pltpu.VMEM((NPOSE, 6 * LANES), BF16),
        pltpu.VMEM((NPOSE, 4 * LANES), BF16),
        pltpu.VMEM((NPOSE, LANES), F32),
        pltpu.VMEM((NPOSE, width), F32),
        pltpu.VMEM((particles, width), BF16),
        pltpu.VMEM((members // 2, NPOSE, LANES), BF16),
        pltpu.VMEM((members // 2, NPOSE, LANES), BF16),
        pltpu.VMEM((members // 2, NPOSE, LANES), F32),
        pltpu.VMEM((NPOSE, LANES), BF16),
        pltpu.VMEM((NPOSE, LANES), BF16),
        pltpu.VMEM((2, NPOSE, LANES), BF16),
        pltpu.VMEM((2, NPOSE, LANES), BF16),
        pltpu.VMEM((members, 8, LANES), F32),
        pltpu.VMEM((1, voxels), F32),
        pltpu.VMEM((slabs, cap, LANES), BF16),
        pltpu.VMEM((slabs, cap, LANES), BF16),
        pltpu.SemaphoreType.DMA((9,)),
        pltpu.SemaphoreType.DMA((8,)),
        pltpu.SemaphoreType.DMA((8,)),
        pltpu.SemaphoreType.DMA((60,)),
        pltpu.SemaphoreType.DMA((60,)),
    ]
    fourier, shares = pl.pallas_call(
        functools.partial(kernel, slabs, members),
        out_shape=(
            jax.ShapeDtypeStruct((LANES, voxels), BF16),
            jax.ShapeDtypeStruct((slabs, cands, LANES), BF16),
        ),
        in_specs=[big] * 8,
        out_specs=(near, big),
        scratch_shapes=scratch,
        compiler_params=pltpu.CompilerParams(
            collective_id=0, has_side_effects=True, vmem_limit_bytes=52 * 1024 * 1024
        ),
    )(
        images, volume.reshape(voxels, width), column_table(edge, members),
        precision[None, :], candidates.T, slot_key, slot_voxel, slot_weight,
    )
    density, posterior = pl.pallas_call(
        finish,
        out_shape=(
            jax.ShapeDtypeStruct((planes, edge // members, edge), F32),
            jax.ShapeDtypeStruct((cands, particles), F32),
        ),
        in_specs=[near] * 3,
        out_specs=(near, near),
        compiler_params=pltpu.CompilerParams(vmem_limit_bytes=52 * 1024 * 1024),
    )(row_table(edge), fourier, shares)
    return density.transpose(0, 2, 1), posterior.T


def solution(mesh):
    placed = (P("img", "slab"), P("slab", None, None), P("img"), P("img", None), P(), P(), P())
    return jax.shard_map(
        per_device,
        mesh=mesh,
        in_specs=placed,
        out_specs=(P("slab", None, "img"), P("img", None)),
        check_vma=False,
    )
```

```python
import functools
import math

import jax
import jax.numpy as jnp
import numpy as np
from jax import lax
from jax.experimental import pallas as pl
from jax.experimental.pallas import tpu as pltpu
from jax.sharding import PartitionSpec as P

NPOSE = 512
WSTEPS = 16
RIDGE = 0.25
LANES = 128
F32 = jnp.float32
BF16 = jnp.bfloat16


def gridding(samples):
    offset = (np.arange(samples) - samples / 2) / samples
    return 1.0 / np.sinc(offset) ** 2


def angles(length):
    counter = np.arange(length)
    return (counter[:, None] * counter[None, :] % length) * (2.0 * math.pi / length)


def column_table(length, members):
    turn = angles(length)
    cosine, sine = np.cos(turn), np.sin(turn)
    scale = gridding(length)[None, :]
    to_re = np.concatenate([cosine, -sine], axis=0) * scale
    to_im = np.concatenate([sine, cosine], axis=0) * scale
    width = length // members
    both = np.stack([to_re.reshape(-1, members, width), to_im.reshape(-1, members, width)], axis=2)
    return jnp.asarray(both.reshape(2 * length, 2 * length), BF16)


def row_table(length):
    turn = angles(length)
    scale = gridding(length)[None, :] / length
    return jnp.asarray(np.concatenate([np.cos(turn), -np.sin(turn)], axis=0) * scale, BF16)


def remote(src, dst, sends, recvs, device):
    return pltpu.make_async_remote_copy(
        src_ref=src,
        dst_ref=dst,
        send_sem=sends,
        recv_sem=recvs,
        device_id=device,
        device_id_type=pl.DeviceIdType.MESH,
    )


def dot(left, right):
    return jnp.dot(left, right, preferred_element_type=F32)


def each(count, step, first=0):
    def body(index, carry):
        step(index)
        return carry

    lax.fori_loop(first, count, body, 0)


def rows_at(start, size):
    return pl.ds(pl.multiple_of(start, size), size)


def iota(shape, axis):
    return lax.broadcasted_iota(jnp.int32, shape, axis)


def pick_row(mask, values):
    return jnp.sum(jnp.where(mask, values, 0.0), axis=0, keepdims=True)


def kernel(
    slabs, members,
    images, volume, columns, precision_in, poses_in, keys_in, voxels_in, weights_in,
    fourier, shares_out,
    images_v, volume_v, columns_v, precision, poses, keys, voxel_of, weight_of,
    pack_table, pose_row, named, unpack,
    outgoing, incoming, slices, half_power, ranks, weave,
    picks, picks_in, shares, spread_first, spread_middle, spread_last, row_weight, partial, turned,
    away, away_in, kept, opposite, opposite_in, ring, ring_in,
    masses, inverse, returning, returned,
    loads, slab_send, slab_recv, img_send, img_recv,
):
    own = lax.axis_index("slab")
    member = lax.axis_index("img")
    ring_len = members // 2
    chip, core = member // 2, lax.rem(member, 2)
    share = NPOSE // members
    half = share // 2
    side = ring_len * share
    deep = outgoing.shape[1]
    mine = slabs * deep
    cap = keys.shape[2]
    width = volume_v.shape[1]
    voxels = volume_v.shape[0]
    cands = poses.shape[0]
    right = 2 * lax.rem(chip + 1, ring_len) + core
    left = 2 * lax.rem(chip + ring_len - 1, ring_len) + core
    partner = 2 * chip + 1 - core

    def slab_peer(step):
        return lax.rem(own + step, slabs)

    def img_peer(step):
        return lax.rem(member + step, members)

    barrier = pltpu.get_barrier_semaphore()

    def greet(axis, peer):
        pl.semaphore_signal(barrier, inc=1, device_id={axis: peer}, device_id_type=pl.DeviceIdType.MESH)

    for step in range(1, slabs):
        greet("slab", slab_peer(step))
    for step in range(1, members):
        greet("img", img_peer(step))
    sources = [keys_in, voxels_in.at[own], weights_in.at[own], volume, poses_in, images, columns, precision_in]
    targets = [keys, voxel_of, weight_of, volume_v, poses, images_v, columns_v, precision]
    load = [pltpu.make_async_copy(src, dst, loads.at[i]) for i, (src, dst) in enumerate(zip(sources, targets))]

    def start_load(index):
        src, dst = sources[index], targets[index]
        pieces = 8 if src.shape[0] >= 512 else 1
        size = src.shape[0] // pieces
        for piece in range(pieces):
            at = slice(piece * size, (piece + 1) * size)
            pltpu.make_async_copy(src.at[at], dst.at[at], loads.at[index]).start()

    for index in range(5):
        start_load(index)

    for index in range(3):
        load[index].wait()
    before = jnp.zeros((slabs, cap), F32)
    for slab in range(slabs):
        before += jnp.where(keys[slab] >= 0, 1.0, 0.0) * jnp.where(own > slab, 1.0, 0.0)
    out_start = jnp.sum(before, axis=1, keepdims=True)
    total_slots = slabs * cap
    own_key = keys[own]
    own_code = voxel_of[...] * 32 + jnp.where(own_key >= 0, weight_of[...], 31)

    def ordered(first, count, tables):
        position = iota((1, count), 1) + first
        block_sel = iota((slabs, count), 0) == ((position >> 3) & (slabs - 1))
        start_row = pick_row(block_sel, out_start).astype(jnp.int32)
        slot_row = members * (position & 7) + (((position >> 7) - start_row) & 7)
        slot_sel = iota((cap, count), 0) == slot_row
        chooser = jnp.where(block_sel, 1.0, 0.0)
        found = []
        for table in tables:
            wide = lax.dot_general(
                table.astype(F32), chooser, (((0,), (0,)), ((), ())),
                precision=lax.Precision.HIGHEST, preferred_element_type=F32,
            )
            found.append(pick_row(slot_sel, wide))
        return found

    def decoded(code):
        code_row = code.astype(jnp.int32)
        level = code_row & 31
        alive = level <= WSTEPS
        spot = (code_row >> 5).astype(F32)
        lower = jnp.where(alive, level, 0).astype(F32) * (1.0 / WSTEPS)
        upper = jnp.where(alive, WSTEPS - level, 0).astype(F32) * (1.0 / WSTEPS)
        return spot, lower, upper

    parts = decoded(ordered(member * mine, mine, [own_code])[0])
    own_cols = jnp.concatenate(list(parts) + [jnp.zeros((5, mine), F32)], axis=0).T
    place = iota((mine, voxels), 1)
    spot = own_cols[:, 0:1].astype(jnp.int32)
    take = jnp.where(place == spot, own_cols[:, 1:2], 0.0) + jnp.where(place == spot + 1, own_cols[:, 2:3], 0.0)
    load[3].wait()
    for index in range(5, len(load)):
        start_load(index)
    woven = dot(take.astype(BF16), volume_v[...])
    for block in range(slabs):
        outgoing[block] = woven[block * deep : (block + 1) * deep].astype(BF16)
    pl.semaphore_wait(barrier, slabs - 1 + members - 1)

    def slab_copy(stage, src, dst, peer):
        return remote(src.at[peer], dst.at[own], slab_send.at[stage], slab_recv.at[stage], {"slab": peer})

    def slab_whole(stage, ref, count):
        blocks = ref.at[0:count]
        return remote(blocks, blocks, slab_send.at[stage], slab_recv.at[stage], {"slab": slab_peer(1)})

    def slab_exchange(stage, src, dst):
        for step in range(1, slabs):
            slab_copy(stage, src, dst, slab_peer(step)).start()

    def slab_arrivals(stage, dst):
        slab_whole(stage, dst, slabs - 1).wait_recv()

    def img_copy(slot, src, dst, device):
        return remote(src, dst, img_send.at[slot], img_recv.at[slot], {"img": device})

    slab_exchange(0, outgoing, incoming)
    incoming[own] = outgoing[own]

    in_key = jnp.concatenate(
        [jnp.sum(jnp.where(iota((slabs, cap), 0) == own, keys[slab], 0), axis=0, keepdims=True) for slab in range(slabs)],
        axis=0,
    )
    live = jnp.where(in_key >= 0, 1.0, 0.0).astype(BF16)
    count = dot(live, jnp.ones((cap, LANES), BF16))
    earlier = jnp.where(iota((slabs, slabs), 1) < iota((slabs, slabs), 0), 1.0, 0.0).astype(BF16)
    start = dot(earlier, count.astype(BF16))
    lane = iota((1, mine), 1)
    slab_sel = iota((slabs, mine), 0) == (lane >> 3)
    in_start = pick_row(slab_sel, start).astype(jnp.int32)
    in_count = pick_row(slab_sel, count).astype(jnp.int32)
    slot = members * (lane & 7) + ((member - in_start) & 7)
    pack_row = jnp.where(slot < in_count, (in_start + slot) >> 3, -1)
    pack_table[...] = jnp.broadcast_to(pack_row, (8, mine)).astype(F32)

    number = start[:, :cap].astype(jnp.int32) + iota((slabs, cap), 1)
    holder = number & (members - 1)
    ahead = ((holder >> 1) - chip) & (ring_len - 1)
    near = jnp.where(ahead == 0, 3, jnp.where(ahead == 1, 1, jnp.where(ahead == 2, 0, 2)))
    row = jnp.where((holder & 1) == core, near, members - 1 - near) * share + (number >> 3)
    key_cols, row_cols = in_key.astype(F32).T, row.astype(F32).T
    pose_ids = iota((cap, NPOSE), 1).astype(F32)
    found_rows = jnp.zeros((cap, NPOSE), F32)
    for slab in range(slabs):
        matched = key_cols[:, slab : slab + 1] == pose_ids
        found_rows += jnp.where(matched, row_cols[:, slab : slab + 1], 0.0)
        unpack[slab * cap : (slab + 1) * cap, :] = jnp.where(matched, 1.0, 0.0).astype(BF16)
    pose_row[...] = jnp.broadcast_to(jnp.sum(found_rows, axis=0, keepdims=True), (8, NPOSE)).astype(jnp.int32)

    load[4].wait()
    for part in range(poses.shape[1] // LANES):
        for k in range(0, cands, 8):
            at = (slice(k, k + 8), slice(part * LANES, (part + 1) * LANES))
            pose = poses[at]
            low, high = pose & (LANES - 1), pose >> 7
            renamed = jnp.zeros_like(pose)
            for piece in range(NPOSE // LANES):
                table = pose_row[:, piece * LANES : (piece + 1) * LANES]
                found = jnp.take_along_axis(table, low, axis=1, mode="promise_in_bounds")
                renamed = jnp.where(high == piece, found, renamed)
            named[at] = renamed

    first_chunks = 3
    ahead_of = 2 * first_chunks
    middle = 2 * ahead_of
    turn = jnp.where(own >= middle, 2, jnp.where(own >= ahead_of, 1, 0))

    def rank_chunk(block):
        at = rows_at(block * LANES, LANES)
        number = poses[:, at].astype(jnp.int16)
        for first in range(0, NPOSE, LANES):
            row = (iota((LANES, LANES), 0) + first).astype(jnp.int16)
            value = jnp.full((LANES, LANES), cands, jnp.int16)
            for k in range(cands):
                value = jnp.where(number[k : k + 1] == row, jnp.int16(k), value)
            ranks[first : first + LANES, at] = value.astype(jnp.int32)

    stripe = 2 * LANES
    stripes = width // stripe
    slabful = images_v.shape[0] // stripes

    def prepare(step):
        block = rows_at(lax.div(step, stripes) * slabful, slabful)
        at = rows_at(lax.rem(step, stripes) * stripe, stripe)
        turned[block, at] = dot(images_v[block, :], columns_v[:, at]).astype(BF16)
        rank_chunk(lax.rem(step + ahead_of, slabs))

    load[5].wait()
    load[6].wait()
    each(6, prepare)

    slab_arrivals(0, incoming)
    arrived = jnp.concatenate([incoming[block].astype(F32) for block in range(slabs)], axis=0).astype(BF16)
    pack = jnp.where(iota((share, mine), 0).astype(F32) == pack_table[0:1, :], 1.0, 0.0).astype(BF16)

    def block_of(index, first=0, size=share):
        return slices.at[index * share + first : index * share + first + size]

    FAR, RIGHT, LEFT, HOME = 0, 1, 2, 3
    slices[HOME * share : (HOME + 1) * share, :] = dot(pack, arrived).astype(BF16)

    def other(index):
        return members - 1 - index

    def top(index):
        return block_of(index, 0, half)

    def bottom(index):
        return block_of(index, half, half)

    gathers = [
        img_copy(0, top(HOME), top(LEFT), right),
        img_copy(1, bottom(HOME), bottom(RIGHT), left),
        img_copy(2, block_of(HOME), block_of(other(HOME)), partner),
        img_copy(3, bottom(HOME), bottom(LEFT), right),
        img_copy(4, top(HOME), top(RIGHT), left),
        img_copy(5, top(LEFT), top(FAR), right),
        img_copy(6, bottom(RIGHT), bottom(FAR), left),
        img_copy(7, block_of(LEFT), block_of(other(LEFT)), partner),
        img_copy(8, block_of(RIGHT), block_of(other(RIGHT)), partner),
        img_copy(9, top(FAR), top(other(FAR)), partner),
        img_copy(10, bottom(FAR), bottom(other(FAR)), partner),
    ]
    for index in range(5):
        gathers[index].start()

    each(10, prepare, 6)

    def power_step(index):
        at = rows_at(index * share, share)
        values = slices[at, :].astype(F32)
        total = 0.5 * jnp.sum(values * values, axis=1, keepdims=True)
        half_power[at, :] = jnp.broadcast_to(total, (share, LANES))

    power_step(HOME)
    gathers[0].wait_recv()
    gathers[5].start()
    gathers[1].wait_recv()
    gathers[6].start()
    gathers[3].wait_recv()
    gathers[7].start()
    gathers[4].wait_recv()
    gathers[8].start()

    chunk = 2 * LANES
    chunks = images_v.shape[0] // chunk

    def picks_of(score, pieces, numbers, value):
        for first, offset, size in pieces:
            block = score[offset : offset + size] - half_power[first : first + size, :]
            for group in range(size // 8):
                picked = jnp.take_along_axis(
                    block[group * 8 : (group + 1) * 8], numbers[0], axis=0, mode="promise_in_bounds"
                )
                value[0] = jnp.where(numbers[2] == first // 8 + group, picked, value[0])
                picked = jnp.take_along_axis(
                    block[group * 8 : (group + 1) * 8], numbers[1], axis=0, mode="promise_in_bounds"
                )
                value[1] = jnp.where(numbers[3] == first // 8 + group, picked, value[1])
        return value

    def score_chunk(index, table, pieces, resume):
        score = lax.dot_general(
            table, images_v[rows_at(index * chunk, chunk), :],
            (((1,), (1,)), ((), ())), preferred_element_type=F32,
        )
        for part in range(chunk // LANES):
            number = named[:, rows_at(index * chunk + part * LANES, LANES)]
            numbers = [number[0:8] & 7, number[8:16] & 7, number[0:8] >> 3, number[8:16] >> 3]
            block = index * (chunk // LANES) + part
            if resume:
                value = [picks[block, 0:8], picks[block, 8:16]]
            else:
                value = [jnp.zeros((8, LANES), F32), jnp.zeros((8, LANES), F32)]
            value = picks_of(score[:, part * LANES : (part + 1) * LANES], pieces, numbers, value)
            picks[block] = jnp.concatenate(value, axis=0)

    def near_step(index):
        score_chunk(index, slices[share : NPOSE - share, :], [(share, 0, NPOSE - 2 * share)], False)

    def far_chunk(index):
        table = jnp.concatenate([slices[0:share, :], slices[NPOSE - share : NPOSE, :]], axis=0)
        score_chunk(index, table, [(0, 0, share), (NPOSE - share, share, share)], True)

    def full_chunk(index):
        score_chunk(index, slices[...], [(0, 0, NPOSE)], False)

    each(12, prepare, 10)
    power_step(LEFT)
    power_step(RIGHT)
    gathers[2].wait_recv()
    power_step(other(HOME))
    gathers[7].wait_recv()
    gathers[8].wait_recv()
    power_step(other(LEFT))
    power_step(other(RIGHT))
    each(first_chunks - 1, near_step)
    gathers[5].wait_recv()
    gathers[9].start()
    gathers[6].wait_recv()
    gathers[10].start()
    each(first_chunks, near_step, first_chunks - 1)
    gathers[9].wait_recv()
    gathers[10].wait_recv()
    power_step(0)
    power_step(members - 1)

    def pick_send(peer):
        @pl.when(peer != own)
        def _():
            slab_copy(1, picks, picks_in, peer).start()

    def far_step(index):
        far_chunk(index)
        pick_send(2 * index)
        pick_send(2 * index + 1)

    def full_step(index):
        full_chunk(index)
        pick_send(2 * index)
        pick_send(2 * index + 1)

    each(first_chunks, far_step)
    each(chunks, full_step, first_chunks)
    picks_in[own] = picks[own]
    load[7].wait()
    row_weight[...] = jnp.zeros_like(row_weight)
    masses[member] = jnp.zeros((8, LANES), F32)

    def share_out():
        slab_arrivals(1, picks_in)
        total = picks_in[0]
        for block in range(1, slabs):
            total = total + picks_in[block]
        total = total * precision[:, rows_at(own * LANES, LANES)]
        exponent = jnp.exp(total - jnp.max(total, axis=0, keepdims=True))
        shares[own] = (exponent / jnp.sum(exponent, axis=0, keepdims=True)).astype(BF16)
        for step in range(1, slabs):
            remote(
                shares.at[own], shares.at[own], slab_send.at[2], slab_recv.at[5 + turn], {"slab": slab_peer(step)}
            ).start()

    @pl.when(turn == 0)
    def _():
        share_out()

    each(slabs, prepare, 12)

    @pl.when(turn != 0)
    def _():
        share_out()

    def shares_arrive(which):
        group = (ahead_of, middle - ahead_of, slabs - middle)[which]

        @pl.when(turn == which)
        def _():
            slab_whole(5 + which, shares, group - 1).wait_recv()

        @pl.when(turn != which)
        def _():
            slab_whole(5 + which, shares, group).wait_recv()

    def spread_chunk(block, spread, origin):
        at = rows_at(block * LANES, LANES)
        to = rows_at((block - origin) * LANES, LANES)
        amount = shares[block].astype(F32) * precision[:, at]
        rounded = amount.astype(BF16).astype(F32)
        low, high = rounded[0:8], rounded[8:16]
        for first in range(0, NPOSE, 16):
            values = []
            for group in (first, first + 8):
                rank = ranks[group : group + 8, at]
                place = rank & 7
                from_low = jnp.take_along_axis(low, place, axis=0, mode="promise_in_bounds")
                from_high = jnp.take_along_axis(high, place, axis=0, mode="promise_in_bounds")
                value = jnp.where(rank < 8, from_low, jnp.where(rank < cands, from_high, 0.0))
                row_weight[group : group + 8, :] += value
                values.append(value)
            spread[first : first + 16, to] = jnp.concatenate(values, axis=0).astype(BF16)

    def early_stripe(index):
        at = rows_at(index * stripe, stripe)
        partial[:, at] = dot(spread_first[...], turned[: ahead_of * LANES, at])

    shares_arrive(0)
    each(ahead_of, lambda block: spread_chunk(block, spread_first, 0))
    each(width // stripe, early_stripe)
    shares_arrive(1)
    each(middle, lambda block: spread_chunk(block, spread_middle, ahead_of), ahead_of)
    shares_arrive(2)
    waiting = list(range(middle, slabs))
    for index in range(width // stripe):
        at = slice(index * stripe, (index + 1) * stripe)
        partial[:, at] += dot(spread_middle[...], turned[ahead_of * LANES : middle * LANES, at])
        for block in waiting[index :: width // stripe]:
            spread_chunk(block, spread_last, middle)

    for piece in range(NPOSE // LANES):
        weight = row_weight[piece * LANES : (piece + 1) * LANES, :].T
        masses[member, piece : piece + 1, :] = jnp.sum(weight, axis=0, keepdims=True)

    def mass_copy(step):
        return img_copy(16, masses.at[member], masses.at[member], img_peer(step))

    def img_whole(slot, ref):
        blocks = ref.at[0 : members - 1]
        return img_copy(slot, blocks, blocks, img_peer(1))

    for step in range(1, members):
        mass_copy(step).start()

    half_rows = NPOSE // 2

    def away_copy(index):
        return img_copy(40 + index, away.at[index], away_in.at[index], partner)

    def turn_stripe(index, chip_index):
        at = rows_at(chip_index * stripe, stripe)
        part = partial[:, at] + dot(spread_last[...], turned[middle * LANES :, at])
        first, second = part[:, :LANES], part[:, LANES:]
        kept[index] = jnp.where(core == 0, first, second)
        away[index] = jnp.where(core == 0, second, first).astype(BF16)
        away_copy(index).start()

    def kept_part(index, first=0, size=NPOSE):
        rows = slice(first, first + size)
        return kept[index, rows, :] + away_in[index, rows, :].astype(F32)

    low, high = slice(0, half_rows), slice(half_rows, NPOSE)
    ring_copies = [
        img_copy(48, opposite.at[low], opposite_in.at[low], right),
        img_copy(49, opposite.at[high], opposite_in.at[high], left),
        img_copy(50, ring.at[0, high], ring_in.at[0, high], right),
        img_copy(51, ring.at[1, low], ring_in.at[1, low], left),
        img_copy(52, ring.at[0, low], ring_in.at[0, low], right),
        img_copy(53, ring.at[1, high], ring_in.at[1, high], left),
    ]
    turn_stripe(FAR, lax.rem(chip + 2, ring_len))
    turn_stripe(RIGHT, lax.rem(chip + 1, ring_len))
    away_copy(FAR).wait_recv()
    opposite[...] = kept_part(FAR).astype(BF16)
    ring_copies[0].start()
    ring_copies[1].start()
    turn_stripe(LEFT, lax.rem(chip + ring_len - 1, ring_len))
    away_copy(RIGHT).wait_recv()
    ring[0, high] = kept_part(RIGHT, half_rows, half_rows).astype(BF16)
    ring_copies[2].start()
    turn_stripe(HOME, chip)
    away_copy(LEFT).wait_recv()
    ring[1, low] = kept_part(LEFT, 0, half_rows).astype(BF16)
    ring_copies[3].start()
    ring_copies[0].wait_recv()
    ring[0, low] = (kept_part(RIGHT, 0, half_rows) + opposite_in[low, :].astype(F32)).astype(BF16)
    ring_copies[4].start()
    ring_copies[1].wait_recv()
    ring[1, high] = (kept_part(LEFT, half_rows, half_rows) + opposite_in[high, :].astype(F32)).astype(BF16)
    ring_copies[5].start()
    shares_copy = pltpu.make_async_copy(shares, shares_out, loads.at[8])
    shares_copy.start()
    away_copy(HOME).wait_recv()
    held = kept_part(HOME)
    for index in range(2, 6):
        ring_copies[index].wait_recv()
    summed = (held + ring_in[0].astype(F32) + ring_in[1].astype(F32)).astype(BF16)

    unpacked = dot(unpack[...], summed)
    for slab in range(slabs):
        returning[slab] = unpacked[slab * cap : (slab + 1) * cap].astype(BF16)
    slab_exchange(3, returning, returned)
    returned[own] = returning[own]

    img_whole(16, masses).wait_recv()
    mass_sum = masses[0]
    for index in range(1, members):
        mass_sum = mass_sum + masses[index]
    mass_row = jnp.concatenate([mass_sum[piece : piece + 1] for piece in range(NPOSE // LANES)], axis=1)
    own_keys = keys[own]
    levels = weight_of[...].astype(F32) * (1.0 / WSTEPS)
    alive = jnp.where(own_keys >= 0, 1.0, 0.0)
    spot_cols = voxel_of[...].astype(F32).T.astype(jnp.int32)
    lower_cols, upper_cols = (levels * alive).T, ((1.0 - levels) * alive).T
    own_key_cols = own_keys.astype(F32).T
    voxel = iota((cap, voxels), 1)
    mass = jnp.zeros((1, voxels), F32)
    for block in range(slabs):
        spots, lows, highs, key = (
            table[:, block : block + 1] for table in (spot_cols, lower_cols, upper_cols, own_key_cols)
        )
        value = jnp.where(voxel == spots, lows, 0.0) + jnp.where(voxel == spots + 1, highs, 0.0)
        weave[block * cap : (block + 1) * cap, :] = value.astype(BF16)
        amount = jnp.sum(jnp.where(key == pose_ids, mass_row, 0.0), axis=1, keepdims=True)
        mass += pick_row(value > 0.0, value * amount)
    inverse[...] = 1.0 / (mass + RIDGE)
    for stage, ref in ((0, outgoing), (1, picks), (2, shares)):
        slab_whole(stage, ref, slabs - 1).wait_send()
    for copy in gathers + ring_copies:
        copy.wait_send()
    for index in range(ring_len):
        away_copy(index).wait_send()
    img_whole(16, masses).wait_send()
    slab_arrivals(3, returned)

    pair = LANES // cap
    slots = jnp.concatenate(
        [
            returned[block : block + pair].reshape(LANES, LANES).astype(F32).T.astype(BF16)
            for block in range(0, slabs, pair)
        ],
        axis=1,
    )
    fourier[...] = (dot(slots, weave[...]) * inverse[...]).astype(BF16)
    shares_copy.wait()
    slab_whole(3, returning, slabs - 1).wait_send()


def finish(rows, fourier, shares, density, posterior):
    planes, columns_out, edge = density.shape
    real = jnp.concatenate([fourier[:columns_out, z * edge : (z + 1) * edge] for z in range(planes)], axis=0)
    imag = jnp.concatenate([fourier[columns_out:, z * edge : (z + 1) * edge] for z in range(planes)], axis=0)
    value = dot(real, rows[:edge, :]) + dot(imag, rows[edge:, :])
    for z in range(planes):
        density[z] = value[z * columns_out : (z + 1) * columns_out]
    for block in range(shares.shape[0]):
        posterior[:, block * LANES : (block + 1) * LANES] = shares[block].astype(F32)


def per_device(images, volume, precision, candidates, slot_key, slot_voxel, slot_weight):
    members = lax.axis_size("img")
    slabs = lax.axis_size("slab")
    planes, edge, width = volume.shape
    particles, cands = candidates.shape
    cap = slot_key.shape[2]
    deep = cap // members
    share = NPOSE // members
    voxels = planes * edge
    mine = slabs * deep
    side = NPOSE // 2
    big = pl.BlockSpec(memory_space=pl.ANY)
    near = pl.BlockSpec(memory_space=pltpu.VMEM)
    scratch = [
        pltpu.VMEM((particles, width), BF16),
        pltpu.VMEM((voxels, width), BF16),
        pltpu.VMEM((width, width), BF16),
        pltpu.VMEM((1, particles), F32),
        pltpu.VMEM((cands, particles), jnp.int32),
        pltpu.VMEM(slot_key.shape, jnp.int32),
        pltpu.VMEM(slot_key.shape[1:], jnp.int32),
        pltpu.VMEM(slot_key.shape[1:], jnp.int32),
        pltpu.VMEM((8, mine), F32),
        pltpu.VMEM((8, NPOSE), jnp.int32),
        pltpu.VMEM((cands, particles), jnp.int32),
        pltpu.VMEM((slabs * cap, NPOSE), BF16),
        pltpu.VMEM((slabs, deep, width), BF16),
        pltpu.VMEM((slabs, deep, width), BF16),
        pltpu.VMEM((NPOSE, width), BF16),
        pltpu.VMEM((NPOSE, LANES), F32),
        pltpu.VMEM((NPOSE, particles), jnp.int32),
        pltpu.VMEM((slabs * cap, voxels), BF16),
        pltpu.VMEM((slabs, cands, LANES), F32),
        pltpu.VMEM((slabs, cands, LANES), F32),
        pltpu.VMEM((slabs, cands, LANES), BF16),
        pltpu.VMEM((NPOSE, 6 * LANES), BF16),
        pltpu.VMEM((NPOSE, 6 * LANES), BF16),
        pltpu.VMEM((NPOSE, 4 * LANES), BF16),
        pltpu.VMEM((NPOSE, LANES), F32),
        pltpu.VMEM((NPOSE, width), F32),
        pltpu.VMEM((particles, width), BF16),
        pltpu.VMEM((members // 2, NPOSE, LANES), BF16),
        pltpu.VMEM((members // 2, NPOSE, LANES), BF16),
        pltpu.VMEM((members // 2, NPOSE, LANES), F32),
        pltpu.VMEM((NPOSE, LANES), BF16),
        pltpu.VMEM((NPOSE, LANES), BF16),
        pltpu.VMEM((2, NPOSE, LANES), BF16),
        pltpu.VMEM((2, NPOSE, LANES), BF16),
        pltpu.VMEM((members, 8, LANES), F32),
        pltpu.VMEM((1, voxels), F32),
        pltpu.VMEM((slabs, cap, LANES), BF16),
        pltpu.VMEM((slabs, cap, LANES), BF16),
        pltpu.SemaphoreType.DMA((9,)),
        pltpu.SemaphoreType.DMA((8,)),
        pltpu.SemaphoreType.DMA((8,)),
        pltpu.SemaphoreType.DMA((60,)),
        pltpu.SemaphoreType.DMA((60,)),
    ]
    fourier, shares = pl.pallas_call(
        functools.partial(kernel, slabs, members),
        out_shape=(
            pltpu.VMEM((LANES, voxels), BF16),
            pltpu.VMEM((slabs, cands, LANES), BF16),
        ),
        in_specs=[big] * 8,
        out_specs=(near, big),
        scratch_shapes=scratch,
        compiler_params=pltpu.CompilerParams(
            collective_id=0, has_side_effects=True, vmem_limit_bytes=52 * 1024 * 1024
        ),
    )(*(
        pltpu.with_memory_space_constraint(operand, pltpu.HBM)
        for operand in (
            images, volume.reshape(voxels, width), column_table(edge, members),
            precision[None, :], candidates.T, slot_key, slot_voxel, slot_weight,
        )
    ))
    density, posterior = pl.pallas_call(
        finish,
        out_shape=(
            jax.ShapeDtypeStruct((planes, edge // members, edge), F32),
            jax.ShapeDtypeStruct((cands, particles), F32),
        ),
        in_specs=[near] * 3,
        out_specs=(near, near),
        compiler_params=pltpu.CompilerParams(vmem_limit_bytes=16 * 1024 * 1024),
    )(row_table(edge), fourier, shares)
    return density.transpose(0, 2, 1), posterior.T


def solution(mesh):
    placed = (P("img", "slab"), P("slab", None, None), P("img"), P("img", None), P(), P(), P())
    return jax.shard_map(
        per_device,
        mesh=mesh,
        in_specs=placed,
        out_specs=(P("slab", None, "img"), P("img", None)),
        check_vma=False,
    )
```

```python
import functools
import math

import jax
import jax.numpy as jnp
import numpy as np
from jax import lax
from jax.experimental import pallas as pl
from jax.experimental.pallas import tpu as pltpu
from jax.sharding import PartitionSpec as P

NPOSE = 512
WSTEPS = 16
RIDGE = 0.25
LANES = 128
F32 = jnp.float32
BF16 = jnp.bfloat16


def gridding(samples):
    offset = (np.arange(samples) - samples / 2) / samples
    return 1.0 / np.sinc(offset) ** 2


def angles(length):
    counter = np.arange(length)
    return (counter[:, None] * counter[None, :] % length) * (2.0 * math.pi / length)


def column_table(length, members):
    turn = angles(length)
    cosine, sine = np.cos(turn), np.sin(turn)
    scale = gridding(length)[None, :]
    to_re = np.concatenate([cosine, -sine], axis=0) * scale
    to_im = np.concatenate([sine, cosine], axis=0) * scale
    width = length // members
    both = np.stack([to_re.reshape(-1, members, width), to_im.reshape(-1, members, width)], axis=2)
    return jnp.asarray(both.reshape(2 * length, 2 * length), BF16)


def row_table(length):
    turn = angles(length)
    scale = gridding(length)[None, :] / length
    return jnp.asarray(np.concatenate([np.cos(turn), -np.sin(turn)], axis=0) * scale, BF16)


def remote(src, dst, sends, recvs, device):
    return pltpu.make_async_remote_copy(
        src_ref=src,
        dst_ref=dst,
        send_sem=sends,
        recv_sem=recvs,
        device_id=device,
        device_id_type=pl.DeviceIdType.MESH,
    )


def dot(left, right):
    return jnp.dot(left, right, preferred_element_type=F32)


def each(count, step, first=0):
    def body(index, carry):
        step(index)
        return carry

    lax.fori_loop(first, count, body, 0)


def rows_at(start, size):
    return pl.ds(pl.multiple_of(start, size), size)


def iota(shape, axis):
    return lax.broadcasted_iota(jnp.int32, shape, axis)


def pick_row(mask, values):
    return jnp.sum(jnp.where(mask, values, 0.0), axis=0, keepdims=True)


def kernel(
    slabs, members,
    images, volume, columns, precision_in, poses_in, keys_in, voxels_in, weights_in,
    fourier, shares_out,
    images_v, volume_v, columns_v, precision, poses, keys, voxel_of, weight_of,
    pack_table, pose_row, named, unpack,
    outgoing, incoming, slices, half_power, ranks, weave,
    picks, picks_in, shares, spread_first, spread_middle, spread_last, row_weight, partial, turned,
    away, away_in, kept, opposite, opposite_in, ring, ring_in,
    masses, inverse, returning, returned,
    loads, slab_send, slab_recv, img_send, img_recv,
):
    own = lax.axis_index("slab")
    member = lax.axis_index("img")
    ring_len = members // 2
    chip, core = member // 2, lax.rem(member, 2)
    share = NPOSE // members
    half = share // 2
    side = ring_len * share
    deep = outgoing.shape[1]
    mine = slabs * deep
    cap = keys.shape[2]
    width = volume_v.shape[1]
    voxels = volume_v.shape[0]
    cands = poses.shape[0]
    right = 2 * lax.rem(chip + 1, ring_len) + core
    left = 2 * lax.rem(chip + ring_len - 1, ring_len) + core
    partner = 2 * chip + 1 - core

    def slab_peer(step):
        return lax.rem(own + step, slabs)

    def img_peer(step):
        return lax.rem(member + step, members)

    barrier = pltpu.get_barrier_semaphore()

    def greet(axis, peer):
        pl.semaphore_signal(barrier, inc=1, device_id={axis: peer}, device_id_type=pl.DeviceIdType.MESH)

    for step in range(1, slabs):
        greet("slab", slab_peer(step))
    for step in range(1, members):
        greet("img", img_peer(step))
    sources = [keys_in, voxels_in.at[own], weights_in.at[own], volume, poses_in, images, columns, precision_in]
    targets = [keys, voxel_of, weight_of, volume_v, poses, images_v, columns_v, precision]
    load = [pltpu.make_async_copy(src, dst, loads.at[i]) for i, (src, dst) in enumerate(zip(sources, targets))]

    def start_load(index):
        src, dst = sources[index], targets[index]
        pieces = 8 if src.shape[0] >= 512 else 1
        size = src.shape[0] // pieces
        for piece in range(pieces):
            at = slice(piece * size, (piece + 1) * size)
            pltpu.make_async_copy(src.at[at], dst.at[at], loads.at[index]).start()

    for index in range(5):
        start_load(index)

    for index in range(3):
        load[index].wait()
    before = jnp.zeros((slabs, cap), F32)
    for slab in range(slabs):
        before += jnp.where(keys[slab] >= 0, 1.0, 0.0) * jnp.where(own > slab, 1.0, 0.0)
    out_start = jnp.sum(before, axis=1, keepdims=True)
    total_slots = slabs * cap
    own_key = keys[own]
    own_code = voxel_of[...] * 32 + jnp.where(own_key >= 0, weight_of[...], 31)

    def ordered(first, count, tables):
        position = iota((1, count), 1) + first
        block_sel = iota((slabs, count), 0) == ((position >> 3) & (slabs - 1))
        start_row = pick_row(block_sel, out_start).astype(jnp.int32)
        slot_row = members * (position & 7) + (((position >> 7) - start_row) & 7)
        slot_sel = iota((cap, count), 0) == slot_row
        chooser = jnp.where(block_sel, 1.0, 0.0)
        found = []
        for table in tables:
            wide = lax.dot_general(
                table.astype(F32), chooser, (((0,), (0,)), ((), ())),
                precision=lax.Precision.HIGHEST, preferred_element_type=F32,
            )
            found.append(pick_row(slot_sel, wide))
        return found

    def decoded(code):
        code_row = code.astype(jnp.int32)
        level = code_row & 31
        alive = level <= WSTEPS
        spot = (code_row >> 5).astype(F32)
        lower = jnp.where(alive, level, 0).astype(F32) * (1.0 / WSTEPS)
        upper = jnp.where(alive, WSTEPS - level, 0).astype(F32) * (1.0 / WSTEPS)
        return spot, lower, upper

    parts = decoded(ordered(member * mine, mine, [own_code])[0])
    own_cols = jnp.concatenate(list(parts) + [jnp.zeros((5, mine), F32)], axis=0).T
    place = iota((mine, voxels), 1)
    spot = own_cols[:, 0:1].astype(jnp.int32)
    take = jnp.where(place == spot, own_cols[:, 1:2], 0.0) + jnp.where(place == spot + 1, own_cols[:, 2:3], 0.0)
    load[3].wait()
    for index in range(5, len(load)):
        start_load(index)
    woven = dot(take.astype(BF16), volume_v[...])
    for block in range(slabs):
        outgoing[block] = woven[block * deep : (block + 1) * deep].astype(BF16)
    pl.semaphore_wait(barrier, slabs - 1 + members - 1)

    def slab_copy(stage, src, dst, peer):
        return remote(src.at[peer], dst.at[own], slab_send.at[stage], slab_recv.at[stage], {"slab": peer})

    def slab_whole(stage, ref, count):
        blocks = ref.at[0:count]
        return remote(blocks, blocks, slab_send.at[stage], slab_recv.at[stage], {"slab": slab_peer(1)})

    def slab_exchange(stage, src, dst):
        for step in range(1, slabs):
            slab_copy(stage, src, dst, slab_peer(step)).start()

    def slab_arrivals(stage, dst):
        slab_whole(stage, dst, slabs - 1).wait_recv()

    def img_copy(slot, src, dst, device):
        return remote(src, dst, img_send.at[slot], img_recv.at[slot], {"img": device})

    slab_exchange(0, outgoing, incoming)
    incoming[own] = outgoing[own]

    in_key = jnp.concatenate(
        [jnp.sum(jnp.where(iota((slabs, cap), 0) == own, keys[slab], 0), axis=0, keepdims=True) for slab in range(slabs)],
        axis=0,
    )
    live = jnp.where(in_key >= 0, 1.0, 0.0).astype(BF16)
    count = dot(live, jnp.ones((cap, LANES), BF16))
    earlier = jnp.where(iota((slabs, slabs), 1) < iota((slabs, slabs), 0), 1.0, 0.0).astype(BF16)
    start = dot(earlier, count.astype(BF16))
    lane = iota((1, mine), 1)
    slab_sel = iota((slabs, mine), 0) == (lane >> 3)
    in_start = pick_row(slab_sel, start).astype(jnp.int32)
    in_count = pick_row(slab_sel, count).astype(jnp.int32)
    slot = members * (lane & 7) + ((member - in_start) & 7)
    pack_row = jnp.where(slot < in_count, (in_start + slot) >> 3, -1)
    pack_table[...] = jnp.broadcast_to(pack_row, (8, mine)).astype(F32)

    number = start[:, :cap].astype(jnp.int32) + iota((slabs, cap), 1)
    holder = number & (members - 1)
    ahead = ((holder >> 1) - chip) & (ring_len - 1)
    near = jnp.where(ahead == 0, 3, jnp.where(ahead == 1, 1, jnp.where(ahead == 2, 0, 2)))
    row = jnp.where((holder & 1) == core, near, members - 1 - near) * share + (number >> 3)
    key_cols, row_cols = in_key.astype(F32).T, row.astype(F32).T
    pose_ids = iota((cap, NPOSE), 1).astype(F32)
    found_rows = jnp.zeros((cap, NPOSE), F32)
    for slab in range(slabs):
        matched = key_cols[:, slab : slab + 1] == pose_ids
        found_rows += jnp.where(matched, row_cols[:, slab : slab + 1], 0.0)
        unpack[slab * cap : (slab + 1) * cap, :] = jnp.where(matched, 1.0, 0.0).astype(BF16)
    pose_row[...] = jnp.broadcast_to(jnp.sum(found_rows, axis=0, keepdims=True), (8, NPOSE)).astype(jnp.int32)

    load[4].wait()
    for part in range(poses.shape[1] // LANES):
        for k in range(0, cands, 8):
            at = (slice(k, k + 8), slice(part * LANES, (part + 1) * LANES))
            pose = poses[at]
            low, high = pose & (LANES - 1), pose >> 7
            renamed = jnp.zeros_like(pose)
            for piece in range(NPOSE // LANES):
                table = pose_row[:, piece * LANES : (piece + 1) * LANES]
                found = jnp.take_along_axis(table, low, axis=1, mode="promise_in_bounds")
                renamed = jnp.where(high == piece, found, renamed)
            named[at] = renamed

    first_chunks = 3
    ahead_of = 2 * first_chunks
    middle = 2 * ahead_of
    turn = jnp.where(own >= middle, 2, jnp.where(own >= ahead_of, 1, 0))

    def rank_chunk(block):
        at = rows_at(block * LANES, LANES)
        number = poses[:, at].astype(jnp.int16)
        for first in range(0, NPOSE, LANES):
            row = (iota((LANES, LANES), 0) + first).astype(jnp.int16)
            value = jnp.full((LANES, LANES), cands, jnp.int16)
            for k in range(cands):
                value = jnp.where(number[k : k + 1] == row, jnp.int16(k), value)
            ranks[first : first + LANES, at] = value.astype(jnp.int32)

    stripe = 2 * LANES
    stripes = width // stripe
    slabful = images_v.shape[0] // stripes

    def prepare(step):
        block = rows_at(lax.div(step, stripes) * slabful, slabful)
        at = rows_at(lax.rem(step, stripes) * stripe, stripe)
        turned[block, at] = dot(images_v[block, :], columns_v[:, at]).astype(BF16)
        rank_chunk(step)

    load[5].wait()
    load[6].wait()
    each(5, prepare)

    slab_arrivals(0, incoming)
    arrived = jnp.concatenate([incoming[block].astype(F32) for block in range(slabs)], axis=0).astype(BF16)
    pack = jnp.where(iota((share, mine), 0).astype(F32) == pack_table[0:1, :], 1.0, 0.0).astype(BF16)

    def block_of(index, first=0, size=share):
        return slices.at[index * share + first : index * share + first + size]

    FAR, RIGHT, LEFT, HOME = 0, 1, 2, 3
    slices[HOME * share : (HOME + 1) * share, :] = dot(pack, arrived).astype(BF16)

    def other(index):
        return members - 1 - index

    def top(index):
        return block_of(index, 0, half)

    def bottom(index):
        return block_of(index, half, half)

    gathers = [
        img_copy(0, top(HOME), top(LEFT), right),
        img_copy(1, bottom(HOME), bottom(RIGHT), left),
        img_copy(2, block_of(HOME), block_of(other(HOME)), partner),
        img_copy(3, bottom(HOME), bottom(LEFT), right),
        img_copy(4, top(HOME), top(RIGHT), left),
        img_copy(5, top(LEFT), top(FAR), right),
        img_copy(6, bottom(RIGHT), bottom(FAR), left),
        img_copy(7, block_of(LEFT), block_of(other(LEFT)), partner),
        img_copy(8, block_of(RIGHT), block_of(other(RIGHT)), partner),
        img_copy(9, top(FAR), top(other(FAR)), partner),
        img_copy(10, bottom(FAR), bottom(other(FAR)), partner),
    ]
    for index in range(5):
        gathers[index].start()

    each(9, prepare, 5)

    def power_step(index):
        at = rows_at(index * share, share)
        values = slices[at, :].astype(F32)
        total = 0.5 * jnp.sum(values * values, axis=1, keepdims=True)
        half_power[at, :] = jnp.broadcast_to(total, (share, LANES))

    power_step(HOME)
    gathers[0].wait_recv()
    gathers[5].start()
    gathers[1].wait_recv()
    gathers[6].start()
    gathers[3].wait_recv()
    gathers[7].start()
    gathers[4].wait_recv()
    gathers[8].start()

    chunk = 2 * LANES
    chunks = images_v.shape[0] // chunk

    def picks_of(score, pieces, numbers, value):
        for first, offset, size in pieces:
            block = score[offset : offset + size] - half_power[first : first + size, :]
            for group in range(size // 8):
                picked = jnp.take_along_axis(
                    block[group * 8 : (group + 1) * 8], numbers[0], axis=0, mode="promise_in_bounds"
                )
                value[0] = jnp.where(numbers[2] == first // 8 + group, picked, value[0])
                picked = jnp.take_along_axis(
                    block[group * 8 : (group + 1) * 8], numbers[1], axis=0, mode="promise_in_bounds"
                )
                value[1] = jnp.where(numbers[3] == first // 8 + group, picked, value[1])
        return value

    def score_chunk(index, table, pieces, resume):
        score = lax.dot_general(
            table, images_v[rows_at(index * chunk, chunk), :],
            (((1,), (1,)), ((), ())), preferred_element_type=F32,
        )
        for part in range(chunk // LANES):
            number = named[:, rows_at(index * chunk + part * LANES, LANES)]
            numbers = [number[0:8] & 7, number[8:16] & 7, number[0:8] >> 3, number[8:16] >> 3]
            block = index * (chunk // LANES) + part
            if resume:
                value = [picks[block, 0:8], picks[block, 8:16]]
            else:
                value = [jnp.zeros((8, LANES), F32), jnp.zeros((8, LANES), F32)]
            value = picks_of(score[:, part * LANES : (part + 1) * LANES], pieces, numbers, value)
            picks[block] = jnp.concatenate(value, axis=0)

    def near_step(index):
        score_chunk(index, slices[share : NPOSE - share, :], [(share, 0, NPOSE - 2 * share)], False)

    def far_chunk(index):
        table = jnp.concatenate([slices[0:share, :], slices[NPOSE - share : NPOSE, :]], axis=0)
        score_chunk(index, table, [(0, 0, share), (NPOSE - share, share, share)], True)

    def full_chunk(index):
        score_chunk(index, slices[...], [(0, 0, NPOSE)], False)

    each(11, prepare, 9)
    power_step(LEFT)
    power_step(RIGHT)
    gathers[2].wait_recv()
    power_step(other(HOME))
    gathers[7].wait_recv()
    gathers[8].wait_recv()
    power_step(other(LEFT))
    power_step(other(RIGHT))
    each(first_chunks - 1, near_step)
    gathers[5].wait_recv()
    gathers[9].start()
    gathers[6].wait_recv()
    gathers[10].start()
    each(first_chunks, near_step, first_chunks - 1)
    gathers[9].wait_recv()
    gathers[10].wait_recv()
    power_step(0)
    power_step(members - 1)

    def pick_send(peer):
        @pl.when(peer != own)
        def _():
            slab_copy(1, picks, picks_in, peer).start()

    def far_step(index):
        far_chunk(index)
        pick_send(2 * index)
        pick_send(2 * index + 1)

    def full_step(index):
        full_chunk(index)
        pick_send(2 * index)
        pick_send(2 * index + 1)

    each(first_chunks, far_step)
    each(chunks, full_step, first_chunks)
    picks_in[own] = picks[own]
    load[7].wait()
    row_weight[...] = jnp.zeros_like(row_weight)
    masses[member] = jnp.zeros((8, LANES), F32)

    def share_out():
        slab_arrivals(1, picks_in)
        total = picks_in[0]
        for block in range(1, slabs):
            total = total + picks_in[block]
        total = total * precision[:, rows_at(own * LANES, LANES)]
        exponent = jnp.exp(total - jnp.max(total, axis=0, keepdims=True))
        shares[own] = (exponent / jnp.sum(exponent, axis=0, keepdims=True)).astype(BF16)
        for step in range(1, slabs):
            remote(
                shares.at[own], shares.at[own], slab_send.at[2], slab_recv.at[5 + turn], {"slab": slab_peer(step)}
            ).start()

    @pl.when(turn == 0)
    def _():
        share_out()

    each(slabs, prepare, 11)

    @pl.when(turn != 0)
    def _():
        share_out()

    def shares_arrive(which):
        group = (ahead_of, middle - ahead_of, slabs - middle)[which]

        @pl.when(turn == which)
        def _():
            slab_whole(5 + which, shares, group - 1).wait_recv()

        @pl.when(turn != which)
        def _():
            slab_whole(5 + which, shares, group).wait_recv()

    def spread_chunk(block, spread, origin):
        at = rows_at(block * LANES, LANES)
        to = rows_at((block - origin) * LANES, LANES)
        amount = shares[block].astype(F32) * precision[:, at]
        rounded = amount.astype(BF16).astype(F32)
        low, high = rounded[0:8], rounded[8:16]
        for first in range(0, NPOSE, 16):
            values = []
            for group in (first, first + 8):
                rank = ranks[group : group + 8, at]
                place = rank & 7
                from_low = jnp.take_along_axis(low, place, axis=0, mode="promise_in_bounds")
                from_high = jnp.take_along_axis(high, place, axis=0, mode="promise_in_bounds")
                value = jnp.where(rank < 8, from_low, jnp.where(rank < cands, from_high, 0.0))
                row_weight[group : group + 8, :] += value
                values.append(value)
            spread[first : first + 16, to] = jnp.concatenate(values, axis=0).astype(BF16)

    def early_stripe(index):
        at = rows_at(index * stripe, stripe)
        partial[:, at] = dot(spread_first[...], turned[: ahead_of * LANES, at])

    shares_arrive(0)
    each(ahead_of, lambda block: spread_chunk(block, spread_first, 0))
    each(width // stripe, early_stripe)
    shares_arrive(1)
    each(middle, lambda block: spread_chunk(block, spread_middle, ahead_of), ahead_of)
    shares_arrive(2)
    waiting = list(range(middle, slabs))
    for index in range(width // stripe):
        at = slice(index * stripe, (index + 1) * stripe)
        partial[:, at] += dot(spread_middle[...], turned[ahead_of * LANES : middle * LANES, at])
        for block in waiting[index :: width // stripe]:
            spread_chunk(block, spread_last, middle)

    for piece in range(NPOSE // LANES):
        weight = row_weight[piece * LANES : (piece + 1) * LANES, :].T
        masses[member, piece : piece + 1, :] = jnp.sum(weight, axis=0, keepdims=True)

    def mass_copy(step):
        return img_copy(16, masses.at[member], masses.at[member], img_peer(step))

    def img_whole(slot, ref):
        blocks = ref.at[0 : members - 1]
        return img_copy(slot, blocks, blocks, img_peer(1))

    for step in range(1, members):
        mass_copy(step).start()

    half_rows = NPOSE // 2

    def away_copy(index):
        return img_copy(40 + index, away.at[index], away_in.at[index], partner)

    def turn_stripe(index, chip_index):
        at = rows_at(chip_index * stripe, stripe)
        part = partial[:, at] + dot(spread_last[...], turned[middle * LANES :, at])
        first, second = part[:, :LANES], part[:, LANES:]
        kept[index] = jnp.where(core == 0, first, second)
        away[index] = jnp.where(core == 0, second, first).astype(BF16)
        away_copy(index).start()

    def kept_part(index, first=0, size=NPOSE):
        rows = slice(first, first + size)
        return kept[index, rows, :] + away_in[index, rows, :].astype(F32)

    low, high = slice(0, half_rows), slice(half_rows, NPOSE)
    ring_copies = [
        img_copy(48, opposite.at[low], opposite_in.at[low], right),
        img_copy(49, opposite.at[high], opposite_in.at[high], left),
        img_copy(50, ring.at[0, high], ring_in.at[0, high], right),
        img_copy(51, ring.at[1, low], ring_in.at[1, low], left),
        img_copy(52, ring.at[0, low], ring_in.at[0, low], right),
        img_copy(53, ring.at[1, high], ring_in.at[1, high], left),
    ]
    turn_stripe(FAR, lax.rem(chip + 2, ring_len))
    turn_stripe(RIGHT, lax.rem(chip + 1, ring_len))
    away_copy(FAR).wait_recv()
    opposite[...] = kept_part(FAR).astype(BF16)
    ring_copies[0].start()
    ring_copies[1].start()
    turn_stripe(LEFT, lax.rem(chip + ring_len - 1, ring_len))
    away_copy(RIGHT).wait_recv()
    ring[0, high] = kept_part(RIGHT, half_rows, half_rows).astype(BF16)
    ring_copies[2].start()
    turn_stripe(HOME, chip)
    away_copy(LEFT).wait_recv()
    ring[1, low] = kept_part(LEFT, 0, half_rows).astype(BF16)
    ring_copies[3].start()
    ring_copies[0].wait_recv()
    ring[0, low] = (kept_part(RIGHT, 0, half_rows) + opposite_in[low, :].astype(F32)).astype(BF16)
    ring_copies[4].start()
    ring_copies[1].wait_recv()
    ring[1, high] = (kept_part(LEFT, half_rows, half_rows) + opposite_in[high, :].astype(F32)).astype(BF16)
    ring_copies[5].start()
    shares_copy = pltpu.make_async_copy(shares, shares_out, loads.at[8])
    shares_copy.start()
    away_copy(HOME).wait_recv()
    held = kept_part(HOME)
    for index in range(2, 6):
        ring_copies[index].wait_recv()
    summed = (held + ring_in[0].astype(F32) + ring_in[1].astype(F32)).astype(BF16)

    unpacked = dot(unpack[...], summed)
    for slab in range(slabs):
        returning[slab] = unpacked[slab * cap : (slab + 1) * cap].astype(BF16)
    slab_exchange(3, returning, returned)
    returned[own] = returning[own]

    img_whole(16, masses).wait_recv()
    mass_sum = masses[0]
    for index in range(1, members):
        mass_sum = mass_sum + masses[index]
    mass_row = jnp.concatenate([mass_sum[piece : piece + 1] for piece in range(NPOSE // LANES)], axis=1)
    own_keys = keys[own]
    levels = weight_of[...].astype(F32) * (1.0 / WSTEPS)
    alive = jnp.where(own_keys >= 0, 1.0, 0.0)
    spot_cols = voxel_of[...].astype(F32).T.astype(jnp.int32)
    lower_cols, upper_cols = (levels * alive).T, ((1.0 - levels) * alive).T
    own_key_cols = own_keys.astype(F32).T
    voxel = iota((cap, voxels), 1)
    mass = jnp.zeros((1, voxels), F32)
    for block in range(slabs):
        spots, lows, highs, key = (
            table[:, block : block + 1] for table in (spot_cols, lower_cols, upper_cols, own_key_cols)
        )
        value = jnp.where(voxel == spots, lows, 0.0) + jnp.where(voxel == spots + 1, highs, 0.0)
        weave[block * cap : (block + 1) * cap, :] = value.astype(BF16)
        amount = jnp.sum(jnp.where(key == pose_ids, mass_row, 0.0), axis=1, keepdims=True)
        mass += pick_row(value > 0.0, value * amount)
    inverse[...] = 1.0 / (mass + RIDGE)
    for stage, ref in ((0, outgoing), (1, picks), (2, shares)):
        slab_whole(stage, ref, slabs - 1).wait_send()
    for copy in gathers + ring_copies:
        copy.wait_send()
    for index in range(ring_len):
        away_copy(index).wait_send()
    img_whole(16, masses).wait_send()
    slab_arrivals(3, returned)

    pair = LANES // cap
    slots = jnp.concatenate(
        [
            returned[block : block + pair].reshape(LANES, LANES).astype(F32).T.astype(BF16)
            for block in range(0, slabs, pair)
        ],
        axis=1,
    )
    fourier[...] = (dot(slots, weave[...]) * inverse[...]).astype(BF16)
    shares_copy.wait()
    slab_whole(3, returning, slabs - 1).wait_send()


def finish(rows, fourier, shares, density, posterior):
    planes, columns_out, edge = density.shape
    real = jnp.concatenate([fourier[:columns_out, z * edge : (z + 1) * edge] for z in range(planes)], axis=0)
    imag = jnp.concatenate([fourier[columns_out:, z * edge : (z + 1) * edge] for z in range(planes)], axis=0)
    value = dot(real, rows[:edge, :]) + dot(imag, rows[edge:, :])
    for z in range(planes):
        density[z] = value[z * columns_out : (z + 1) * columns_out]
    for block in range(shares.shape[0]):
        posterior[:, block * LANES : (block + 1) * LANES] = shares[block].astype(F32)


def per_device(images, volume, precision, candidates, slot_key, slot_voxel, slot_weight):
    members = lax.axis_size("img")
    slabs = lax.axis_size("slab")
    planes, edge, width = volume.shape
    particles, cands = candidates.shape
    cap = slot_key.shape[2]
    deep = cap // members
    share = NPOSE // members
    voxels = planes * edge
    mine = slabs * deep
    side = NPOSE // 2
    big = pl.BlockSpec(memory_space=pl.ANY)
    near = pl.BlockSpec(memory_space=pltpu.VMEM)
    scratch = [
        pltpu.VMEM((particles, width), BF16),
        pltpu.VMEM((voxels, width), BF16),
        pltpu.VMEM((width, width), BF16),
        pltpu.VMEM((1, particles), F32),
        pltpu.VMEM((cands, particles), jnp.int32),
        pltpu.VMEM(slot_key.shape, jnp.int32),
        pltpu.VMEM(slot_key.shape[1:], jnp.int32),
        pltpu.VMEM(slot_key.shape[1:], jnp.int32),
        pltpu.VMEM((8, mine), F32),
        pltpu.VMEM((8, NPOSE), jnp.int32),
        pltpu.VMEM((cands, particles), jnp.int32),
        pltpu.VMEM((slabs * cap, NPOSE), BF16),
        pltpu.VMEM((slabs, deep, width), BF16),
        pltpu.VMEM((slabs, deep, width), BF16),
        pltpu.VMEM((NPOSE, width), BF16),
        pltpu.VMEM((NPOSE, LANES), F32),
        pltpu.VMEM((NPOSE, particles), jnp.int32),
        pltpu.VMEM((slabs * cap, voxels), BF16),
        pltpu.VMEM((slabs, cands, LANES), F32),
        pltpu.VMEM((slabs, cands, LANES), F32),
        pltpu.VMEM((slabs, cands, LANES), BF16),
        pltpu.VMEM((NPOSE, 6 * LANES), BF16),
        pltpu.VMEM((NPOSE, 6 * LANES), BF16),
        pltpu.VMEM((NPOSE, 4 * LANES), BF16),
        pltpu.VMEM((NPOSE, LANES), F32),
        pltpu.VMEM((NPOSE, width), F32),
        pltpu.VMEM((particles, width), BF16),
        pltpu.VMEM((members // 2, NPOSE, LANES), BF16),
        pltpu.VMEM((members // 2, NPOSE, LANES), BF16),
        pltpu.VMEM((members // 2, NPOSE, LANES), F32),
        pltpu.VMEM((NPOSE, LANES), BF16),
        pltpu.VMEM((NPOSE, LANES), BF16),
        pltpu.VMEM((2, NPOSE, LANES), BF16),
        pltpu.VMEM((2, NPOSE, LANES), BF16),
        pltpu.VMEM((members, 8, LANES), F32),
        pltpu.VMEM((1, voxels), F32),
        pltpu.VMEM((slabs, cap, LANES), BF16),
        pltpu.VMEM((slabs, cap, LANES), BF16),
        pltpu.SemaphoreType.DMA((9,)),
        pltpu.SemaphoreType.DMA((8,)),
        pltpu.SemaphoreType.DMA((8,)),
        pltpu.SemaphoreType.DMA((60,)),
        pltpu.SemaphoreType.DMA((60,)),
    ]
    fourier, shares = pl.pallas_call(
        functools.partial(kernel, slabs, members),
        out_shape=(
            pltpu.VMEM((LANES, voxels), BF16),
            pltpu.VMEM((slabs, cands, LANES), BF16),
        ),
        in_specs=[big] * 8,
        out_specs=(near, big),
        scratch_shapes=scratch,
        compiler_params=pltpu.CompilerParams(
            collective_id=0, has_side_effects=True, vmem_limit_bytes=52 * 1024 * 1024
        ),
    )(*(
        pltpu.with_memory_space_constraint(operand, pltpu.HBM)
        for operand in (
            images, volume.reshape(voxels, width), column_table(edge, members),
            precision[None, :], candidates.T, slot_key, slot_voxel, slot_weight,
        )
    ))
    density, posterior = pl.pallas_call(
        finish,
        out_shape=(
            jax.ShapeDtypeStruct((planes, edge // members, edge), F32),
            jax.ShapeDtypeStruct((cands, particles), F32),
        ),
        in_specs=[near] * 3,
        out_specs=(near, near),
        compiler_params=pltpu.CompilerParams(vmem_limit_bytes=16 * 1024 * 1024),
    )(row_table(edge), fourier, shares)
    return density.transpose(0, 2, 1), posterior.T


def solution(mesh):
    placed = (P("img", "slab"), P("slab", None, None), P("img"), P("img", None), P(), P(), P())
    return jax.shard_map(
        per_device,
        mesh=mesh,
        in_specs=placed,
        out_specs=(P("slab", None, "img"), P("img", None)),
        check_vma=False,
    )
```

```python
import functools
import math

import jax
import jax.numpy as jnp
import numpy as np
from jax import lax
from jax.experimental import pallas as pl
from jax.experimental.pallas import tpu as pltpu
from jax.sharding import PartitionSpec as P

NPOSE = 512
WSTEPS = 16
RIDGE = 0.25
LANES = 128
F32 = jnp.float32
BF16 = jnp.bfloat16


def gridding(samples):
    offset = (np.arange(samples) - samples / 2) / samples
    return 1.0 / np.sinc(offset) ** 2


def angles(length):
    counter = np.arange(length)
    return (counter[:, None] * counter[None, :] % length) * (2.0 * math.pi / length)


def column_table(length, members):
    turn = angles(length)
    cosine, sine = np.cos(turn), np.sin(turn)
    scale = gridding(length)[None, :]
    to_re = np.concatenate([cosine, -sine], axis=0) * scale
    to_im = np.concatenate([sine, cosine], axis=0) * scale
    width = length // members
    both = np.stack([to_re.reshape(-1, members, width), to_im.reshape(-1, members, width)], axis=2)
    return jnp.asarray(both.reshape(2 * length, 2 * length), BF16)


def row_table(length):
    turn = angles(length)
    scale = gridding(length)[None, :] / length
    return jnp.asarray(np.concatenate([np.cos(turn), -np.sin(turn)], axis=0) * scale, BF16)


def remote(src, dst, sends, recvs, device):
    return pltpu.make_async_remote_copy(
        src_ref=src,
        dst_ref=dst,
        send_sem=sends,
        recv_sem=recvs,
        device_id=device,
        device_id_type=pl.DeviceIdType.MESH,
    )


def dot(left, right):
    return jnp.dot(left, right, preferred_element_type=F32)


def each(count, step, first=0):
    def body(index, carry):
        step(index)
        return carry

    lax.fori_loop(first, count, body, 0)


def rows_at(start, size):
    return pl.ds(pl.multiple_of(start, size), size)


def iota(shape, axis):
    return lax.broadcasted_iota(jnp.int32, shape, axis)


def pick_row(mask, values):
    return jnp.sum(jnp.where(mask, values, 0.0), axis=0, keepdims=True)


def kernel(
    slabs, members,
    images, volume, columns, precision_in, poses_in, keys_in, voxels_in, weights_in,
    fourier, shares_out,
    images_v, volume_v, columns_v, precision, poses, keys, voxel_of, weight_of,
    pack_table, pose_row, named, unpack,
    outgoing, incoming, slices, half_power, ranks, weave,
    picks, picks_in, shares, spread_first, spread_middle, spread_last, row_weight, partial, turned,
    away, away_in, kept, opposite, opposite_in, ring, ring_in,
    masses, inverse, returning, returned,
    loads, slab_send, slab_recv, img_send, img_recv,
):
    own = lax.axis_index("slab")
    member = lax.axis_index("img")
    ring_len = members // 2
    chip, core = member // 2, lax.rem(member, 2)
    share = NPOSE // members
    half = share // 2
    side = ring_len * share
    deep = outgoing.shape[1]
    mine = slabs * deep
    cap = keys.shape[2]
    width = volume_v.shape[1]
    voxels = volume_v.shape[0]
    cands = poses.shape[0]
    right = 2 * lax.rem(chip + 1, ring_len) + core
    left = 2 * lax.rem(chip + ring_len - 1, ring_len) + core
    partner = 2 * chip + 1 - core
    across = 2 * lax.rem(chip + 2, ring_len) + core

    def slab_peer(step):
        return lax.rem(own + step, slabs)

    def img_peer(step):
        return lax.rem(member + step, members)

    barrier = pltpu.get_barrier_semaphore()

    def greet(axis, peer):
        pl.semaphore_signal(barrier, inc=1, device_id={axis: peer}, device_id_type=pl.DeviceIdType.MESH)

    for step in range(1, slabs):
        greet("slab", slab_peer(step))
    for step in range(1, members):
        greet("img", img_peer(step))
    sources = [keys_in, voxels_in.at[own], weights_in.at[own], volume, poses_in, images, columns, precision_in]
    targets = [keys, voxel_of, weight_of, volume_v, poses, images_v, columns_v, precision]
    load = [pltpu.make_async_copy(src, dst, loads.at[i]) for i, (src, dst) in enumerate(zip(sources, targets))]

    def start_load(index):
        src, dst = sources[index], targets[index]
        pieces = 8 if src.shape[0] >= 512 else 1
        size = src.shape[0] // pieces
        for piece in range(pieces):
            at = slice(piece * size, (piece + 1) * size)
            pltpu.make_async_copy(src.at[at], dst.at[at], loads.at[index]).start()

    for index in range(5):
        start_load(index)

    for index in range(3):
        load[index].wait()
    before = jnp.zeros((slabs, cap), F32)
    for slab in range(slabs):
        before += jnp.where(keys[slab] >= 0, 1.0, 0.0) * jnp.where(own > slab, 1.0, 0.0)
    out_start = jnp.sum(before, axis=1, keepdims=True)
    total_slots = slabs * cap
    own_key = keys[own]
    own_code = voxel_of[...] * 32 + jnp.where(own_key >= 0, weight_of[...], 31)

    def ordered(first, count, tables):
        position = iota((1, count), 1) + first
        block_sel = iota((slabs, count), 0) == ((position >> 3) & (slabs - 1))
        start_row = pick_row(block_sel, out_start).astype(jnp.int32)
        slot_row = members * (position & 7) + (((position >> 7) - start_row) & 7)
        slot_sel = iota((cap, count), 0) == slot_row
        chooser = jnp.where(block_sel, 1.0, 0.0)
        found = []
        for table in tables:
            wide = lax.dot_general(
                table.astype(F32), chooser, (((0,), (0,)), ((), ())),
                precision=lax.Precision.HIGHEST, preferred_element_type=F32,
            )
            found.append(pick_row(slot_sel, wide))
        return found

    def decoded(code):
        code_row = code.astype(jnp.int32)
        level = code_row & 31
        alive = level <= WSTEPS
        spot = (code_row >> 5).astype(F32)
        lower = jnp.where(alive, level, 0).astype(F32) * (1.0 / WSTEPS)
        upper = jnp.where(alive, WSTEPS - level, 0).astype(F32) * (1.0 / WSTEPS)
        return spot, lower, upper

    parts = decoded(ordered(member * mine, mine, [own_code])[0])
    own_cols = jnp.concatenate(list(parts) + [jnp.zeros((5, mine), F32)], axis=0).T
    place = iota((mine, voxels), 1)
    spot = own_cols[:, 0:1].astype(jnp.int32)
    take = jnp.where(place == spot, own_cols[:, 1:2], 0.0) + jnp.where(place == spot + 1, own_cols[:, 2:3], 0.0)
    load[3].wait()
    for index in range(5, len(load)):
        start_load(index)
    woven = dot(take.astype(BF16), volume_v[...])
    for block in range(slabs):
        outgoing[block] = woven[block * deep : (block + 1) * deep].astype(BF16)
    pl.semaphore_wait(barrier, slabs - 1 + members - 1)

    def slab_copy(stage, src, dst, peer):
        return remote(src.at[peer], dst.at[own], slab_send.at[stage], slab_recv.at[stage], {"slab": peer})

    def slab_whole(stage, ref, count):
        blocks = ref.at[0:count]
        return remote(blocks, blocks, slab_send.at[stage], slab_recv.at[stage], {"slab": slab_peer(1)})

    def slab_exchange(stage, src, dst):
        for step in range(1, slabs):
            slab_copy(stage, src, dst, slab_peer(step)).start()

    def slab_arrivals(stage, dst):
        slab_whole(stage, dst, slabs - 1).wait_recv()

    def img_copy(slot, src, dst, device):
        return remote(src, dst, img_send.at[slot], img_recv.at[slot], {"img": device})

    slab_exchange(0, outgoing, incoming)
    incoming[own] = outgoing[own]

    in_key = jnp.concatenate(
        [jnp.sum(jnp.where(iota((slabs, cap), 0) == own, keys[slab], 0), axis=0, keepdims=True) for slab in range(slabs)],
        axis=0,
    )
    live = jnp.where(in_key >= 0, 1.0, 0.0).astype(BF16)
    count = dot(live, jnp.ones((cap, LANES), BF16))
    earlier = jnp.where(iota((slabs, slabs), 1) < iota((slabs, slabs), 0), 1.0, 0.0).astype(BF16)
    start = dot(earlier, count.astype(BF16))
    lane = iota((1, mine), 1)
    slab_sel = iota((slabs, mine), 0) == (lane >> 3)
    in_start = pick_row(slab_sel, start).astype(jnp.int32)
    in_count = pick_row(slab_sel, count).astype(jnp.int32)
    slot = members * (lane & 7) + ((member - in_start) & 7)
    pack_row = jnp.where(slot < in_count, (in_start + slot) >> 3, -1)
    pack_table[...] = jnp.broadcast_to(pack_row, (8, mine)).astype(F32)

    number = start[:, :cap].astype(jnp.int32) + iota((slabs, cap), 1)
    holder = number & (members - 1)
    ahead = ((holder >> 1) - chip) & (ring_len - 1)
    near = jnp.where(ahead == 0, 3, jnp.where(ahead == 1, 1, jnp.where(ahead == 2, 0, 2)))
    row = jnp.where((holder & 1) == core, near, members - 1 - near) * share + (number >> 3)
    key_cols, row_cols = in_key.astype(F32).T, row.astype(F32).T
    pose_ids = iota((cap, NPOSE), 1).astype(F32)
    found_rows = jnp.zeros((cap, NPOSE), F32)
    for slab in range(slabs):
        matched = key_cols[:, slab : slab + 1] == pose_ids
        found_rows += jnp.where(matched, row_cols[:, slab : slab + 1], 0.0)
        unpack[slab * cap : (slab + 1) * cap, :] = jnp.where(matched, 1.0, 0.0).astype(BF16)
    pose_row[...] = jnp.broadcast_to(jnp.sum(found_rows, axis=0, keepdims=True), (8, NPOSE)).astype(jnp.int32)

    load[4].wait()
    for part in range(poses.shape[1] // LANES):
        for k in range(0, cands, 8):
            at = (slice(k, k + 8), slice(part * LANES, (part + 1) * LANES))
            pose = poses[at]
            low, high = pose & (LANES - 1), pose >> 7
            renamed = jnp.zeros_like(pose)
            for piece in range(NPOSE // LANES):
                table = pose_row[:, piece * LANES : (piece + 1) * LANES]
                found = jnp.take_along_axis(table, low, axis=1, mode="promise_in_bounds")
                renamed = jnp.where(high == piece, found, renamed)
            named[at] = renamed

    first_chunks = 3
    ahead_of = 2 * first_chunks
    middle = 2 * ahead_of
    turn = jnp.where(own >= middle, 2, jnp.where(own >= ahead_of, 1, 0))

    def rank_chunk(block):
        at = rows_at(block * LANES, LANES)
        number = poses[:, at].astype(jnp.int16)
        for first in range(0, NPOSE, LANES):
            row = (iota((LANES, LANES), 0) + first).astype(jnp.int16)
            value = jnp.full((LANES, LANES), cands, jnp.int16)
            for k in range(cands):
                value = jnp.where(number[k : k + 1] == row, jnp.int16(k), value)
            ranks[first : first + LANES, at] = value.astype(jnp.int32)

    stripe = 2 * LANES
    stripes = width // stripe
    slabful = images_v.shape[0] // stripes

    def prepare(step):
        block = rows_at(lax.div(step, stripes) * slabful, slabful)
        at = rows_at(lax.rem(step, stripes) * stripe, stripe)
        turned[block, at] = dot(images_v[block, :], columns_v[:, at]).astype(BF16)
        rank_chunk(step)

    load[5].wait()
    load[6].wait()
    each(5, prepare)

    slab_arrivals(0, incoming)
    arrived = jnp.concatenate([incoming[block].astype(F32) for block in range(slabs)], axis=0).astype(BF16)
    pack = jnp.where(iota((share, mine), 0).astype(F32) == pack_table[0:1, :], 1.0, 0.0).astype(BF16)

    def block_of(index, first=0, size=share):
        return slices.at[index * share + first : index * share + first + size]

    FAR, RIGHT, LEFT, HOME = 0, 1, 2, 3
    slices[HOME * share : (HOME + 1) * share, :] = dot(pack, arrived).astype(BF16)

    def other(index):
        return members - 1 - index

    def top(index):
        return block_of(index, 0, half)

    def bottom(index):
        return block_of(index, half, half)

    gathers = [
        img_copy(0, top(HOME), top(LEFT), right),
        img_copy(1, bottom(HOME), bottom(RIGHT), left),
        img_copy(2, block_of(HOME), block_of(other(HOME)), partner),
        img_copy(3, bottom(HOME), bottom(LEFT), right),
        img_copy(4, top(HOME), top(RIGHT), left),
        img_copy(5, top(HOME), top(FAR), across),
        img_copy(6, bottom(HOME), bottom(FAR), across),
        img_copy(7, block_of(LEFT), block_of(other(LEFT)), partner),
        img_copy(8, block_of(RIGHT), block_of(other(RIGHT)), partner),
        img_copy(9, top(FAR), top(other(FAR)), partner),
        img_copy(10, bottom(FAR), bottom(other(FAR)), partner),
    ]
    for index in range(7):
        gathers[index].start()

    each(9, prepare, 5)

    def power_step(index):
        at = rows_at(index * share, share)
        values = slices[at, :].astype(F32)
        total = 0.5 * jnp.sum(values * values, axis=1, keepdims=True)
        half_power[at, :] = jnp.broadcast_to(total, (share, LANES))

    power_step(HOME)
    gathers[0].wait_recv()
    gathers[1].wait_recv()
    gathers[3].wait_recv()
    gathers[7].start()
    gathers[4].wait_recv()
    gathers[8].start()

    chunk = 2 * LANES
    chunks = images_v.shape[0] // chunk

    def picks_of(score, pieces, numbers, value):
        for first, offset, size in pieces:
            block = score[offset : offset + size] - half_power[first : first + size, :]
            for group in range(size // 8):
                picked = jnp.take_along_axis(
                    block[group * 8 : (group + 1) * 8], numbers[0], axis=0, mode="promise_in_bounds"
                )
                value[0] = jnp.where(numbers[2] == first // 8 + group, picked, value[0])
                picked = jnp.take_along_axis(
                    block[group * 8 : (group + 1) * 8], numbers[1], axis=0, mode="promise_in_bounds"
                )
                value[1] = jnp.where(numbers[3] == first // 8 + group, picked, value[1])
        return value

    def score_chunk(index, table, pieces, resume):
        score = lax.dot_general(
            table, images_v[rows_at(index * chunk, chunk), :],
            (((1,), (1,)), ((), ())), preferred_element_type=F32,
        )
        for part in range(chunk // LANES):
            number = named[:, rows_at(index * chunk + part * LANES, LANES)]
            numbers = [number[0:8] & 7, number[8:16] & 7, number[0:8] >> 3, number[8:16] >> 3]
            block = index * (chunk // LANES) + part
            if resume:
                value = [picks[block, 0:8], picks[block, 8:16]]
            else:
                value = [jnp.zeros((8, LANES), F32), jnp.zeros((8, LANES), F32)]
            value = picks_of(score[:, part * LANES : (part + 1) * LANES], pieces, numbers, value)
            picks[block] = jnp.concatenate(value, axis=0)

    def near_step(index):
        score_chunk(index, slices[share : NPOSE - share, :], [(share, 0, NPOSE - 2 * share)], False)

    def far_chunk(index):
        table = jnp.concatenate([slices[0:share, :], slices[NPOSE - share : NPOSE, :]], axis=0)
        score_chunk(index, table, [(0, 0, share), (NPOSE - share, share, share)], True)

    def full_chunk(index):
        score_chunk(index, slices[...], [(0, 0, NPOSE)], False)

    each(11, prepare, 9)
    power_step(LEFT)
    power_step(RIGHT)
    gathers[2].wait_recv()
    power_step(other(HOME))
    gathers[7].wait_recv()
    gathers[8].wait_recv()
    power_step(other(LEFT))
    power_step(other(RIGHT))
    each(first_chunks - 1, near_step)
    gathers[5].wait_recv()
    gathers[9].start()
    gathers[6].wait_recv()
    gathers[10].start()
    each(first_chunks, near_step, first_chunks - 1)
    gathers[9].wait_recv()
    gathers[10].wait_recv()
    power_step(0)
    power_step(members - 1)

    def pick_send(peer):
        @pl.when(peer != own)
        def _():
            slab_copy(1, picks, picks_in, peer).start()

    def far_step(index):
        far_chunk(index)
        pick_send(2 * index)
        pick_send(2 * index + 1)

    def full_step(index):
        full_chunk(index)
        pick_send(2 * index)
        pick_send(2 * index + 1)

    each(first_chunks, far_step)
    each(chunks, full_step, first_chunks)
    picks_in[own] = picks[own]
    load[7].wait()
    row_weight[...] = jnp.zeros_like(row_weight)
    masses[member] = jnp.zeros((8, LANES), F32)

    def share_out():
        slab_arrivals(1, picks_in)
        total = picks_in[0]
        for block in range(1, slabs):
            total = total + picks_in[block]
        total = total * precision[:, rows_at(own * LANES, LANES)]
        exponent = jnp.exp(total - jnp.max(total, axis=0, keepdims=True))
        shares[own] = (exponent / jnp.sum(exponent, axis=0, keepdims=True)).astype(BF16)
        for step in range(1, slabs):
            remote(
                shares.at[own], shares.at[own], slab_send.at[2], slab_recv.at[5 + turn], {"slab": slab_peer(step)}
            ).start()

    @pl.when(turn == 0)
    def _():
        share_out()

    each(slabs, prepare, 11)

    @pl.when(turn != 0)
    def _():
        share_out()

    def shares_arrive(which):
        group = (ahead_of, middle - ahead_of, slabs - middle)[which]

        @pl.when(turn == which)
        def _():
            slab_whole(5 + which, shares, group - 1).wait_recv()

        @pl.when(turn != which)
        def _():
            slab_whole(5 + which, shares, group).wait_recv()

    def spread_chunk(block, spread, origin):
        at = rows_at(block * LANES, LANES)
        to = rows_at((block - origin) * LANES, LANES)
        amount = shares[block].astype(F32) * precision[:, at]
        rounded = amount.astype(BF16).astype(F32)
        low, high = rounded[0:8], rounded[8:16]
        for first in range(0, NPOSE, 16):
            values = []
            for group in (first, first + 8):
                rank = ranks[group : group + 8, at]
                place = rank & 7
                from_low = jnp.take_along_axis(low, place, axis=0, mode="promise_in_bounds")
                from_high = jnp.take_along_axis(high, place, axis=0, mode="promise_in_bounds")
                value = jnp.where(rank < 8, from_low, jnp.where(rank < cands, from_high, 0.0))
                row_weight[group : group + 8, :] += value
                values.append(value)
            spread[first : first + 16, to] = jnp.concatenate(values, axis=0).astype(BF16)

    def early_stripe(index):
        at = rows_at(index * stripe, stripe)
        partial[:, at] = dot(spread_first[...], turned[: ahead_of * LANES, at])

    shares_arrive(0)
    each(ahead_of, lambda block: spread_chunk(block, spread_first, 0))
    each(width // stripe, early_stripe)
    shares_arrive(1)
    each(middle, lambda block: spread_chunk(block, spread_middle, ahead_of), ahead_of)
    shares_arrive(2)
    waiting = list(range(middle, slabs))
    for index in range(width // stripe):
        at = slice(index * stripe, (index + 1) * stripe)
        partial[:, at] += dot(spread_middle[...], turned[ahead_of * LANES : middle * LANES, at])
        for block in waiting[index :: width // stripe]:
            spread_chunk(block, spread_last, middle)

    for piece in range(NPOSE // LANES):
        weight = row_weight[piece * LANES : (piece + 1) * LANES, :].T
        masses[member, piece : piece + 1, :] = jnp.sum(weight, axis=0, keepdims=True)

    def mass_copy(step):
        return img_copy(16, masses.at[member], masses.at[member], img_peer(step))

    def img_whole(slot, ref):
        blocks = ref.at[0 : members - 1]
        return img_copy(slot, blocks, blocks, img_peer(1))

    for step in range(1, members):
        mass_copy(step).start()


    def away_copy(index):
        return img_copy(40 + index, away.at[index], away_in.at[index], partner)

    def turn_stripe(index, chip_index):
        at = rows_at(chip_index * stripe, stripe)
        part = partial[:, at] + dot(spread_last[...], turned[middle * LANES :, at])
        first, second = part[:, :LANES], part[:, LANES:]
        kept[index] = jnp.where(core == 0, first, second)
        away[index] = jnp.where(core == 0, second, first).astype(BF16)
        away_copy(index).start()

    def kept_part(index, first=0, size=NPOSE):
        rows = slice(first, first + size)
        return kept[index, rows, :] + away_in[index, rows, :].astype(F32)

    ring_copies = [
        img_copy(48, opposite, opposite_in, across),
        img_copy(50, ring.at[0], ring_in.at[0], right),
        img_copy(51, ring.at[1], ring_in.at[1], left),
    ]
    turn_stripe(FAR, lax.rem(chip + 2, ring_len))
    turn_stripe(RIGHT, lax.rem(chip + 1, ring_len))
    away_copy(FAR).wait_recv()
    opposite[...] = kept_part(FAR).astype(BF16)
    ring_copies[0].start()
    turn_stripe(LEFT, lax.rem(chip + ring_len - 1, ring_len))
    away_copy(RIGHT).wait_recv()
    ring[0] = kept_part(RIGHT).astype(BF16)
    ring_copies[1].start()
    turn_stripe(HOME, chip)
    away_copy(LEFT).wait_recv()
    ring[1] = kept_part(LEFT).astype(BF16)
    ring_copies[2].start()
    shares_copy = pltpu.make_async_copy(shares, shares_out, loads.at[8])
    shares_copy.start()
    away_copy(HOME).wait_recv()
    held = kept_part(HOME)
    for copy in ring_copies:
        copy.wait_recv()
    summed = (held + ring_in[0].astype(F32) + ring_in[1].astype(F32) + opposite_in[...].astype(F32)).astype(BF16)

    unpacked = dot(unpack[...], summed)
    for slab in range(slabs):
        returning[slab] = unpacked[slab * cap : (slab + 1) * cap].astype(BF16)
    slab_exchange(3, returning, returned)
    returned[own] = returning[own]

    img_whole(16, masses).wait_recv()
    mass_sum = masses[0]
    for index in range(1, members):
        mass_sum = mass_sum + masses[index]
    mass_row = jnp.concatenate([mass_sum[piece : piece + 1] for piece in range(NPOSE // LANES)], axis=1)
    own_keys = keys[own]
    levels = weight_of[...].astype(F32) * (1.0 / WSTEPS)
    alive = jnp.where(own_keys >= 0, 1.0, 0.0)
    spot_cols = voxel_of[...].astype(F32).T.astype(jnp.int32)
    lower_cols, upper_cols = (levels * alive).T, ((1.0 - levels) * alive).T
    own_key_cols = own_keys.astype(F32).T
    voxel = iota((cap, voxels), 1)
    mass = jnp.zeros((1, voxels), F32)
    for block in range(slabs):
        spots, lows, highs, key = (
            table[:, block : block + 1] for table in (spot_cols, lower_cols, upper_cols, own_key_cols)
        )
        value = jnp.where(voxel == spots, lows, 0.0) + jnp.where(voxel == spots + 1, highs, 0.0)
        weave[block * cap : (block + 1) * cap, :] = value.astype(BF16)
        amount = jnp.sum(jnp.where(key == pose_ids, mass_row, 0.0), axis=1, keepdims=True)
        mass += pick_row(value > 0.0, value * amount)
    inverse[...] = 1.0 / (mass + RIDGE)
    for stage, ref in ((0, outgoing), (1, picks), (2, shares)):
        slab_whole(stage, ref, slabs - 1).wait_send()
    for copy in gathers + ring_copies:
        copy.wait_send()
    for index in range(ring_len):
        away_copy(index).wait_send()
    img_whole(16, masses).wait_send()
    slab_arrivals(3, returned)

    pair = LANES // cap
    slots = jnp.concatenate(
        [
            returned[block : block + pair].reshape(LANES, LANES).astype(F32).T.astype(BF16)
            for block in range(0, slabs, pair)
        ],
        axis=1,
    )
    fourier[...] = (dot(slots, weave[...]) * inverse[...]).astype(BF16)
    shares_copy.wait()
    slab_whole(3, returning, slabs - 1).wait_send()


def finish(rows, fourier, shares, density, posterior):
    planes, columns_out, edge = density.shape
    real = jnp.concatenate([fourier[:columns_out, z * edge : (z + 1) * edge] for z in range(planes)], axis=0)
    imag = jnp.concatenate([fourier[columns_out:, z * edge : (z + 1) * edge] for z in range(planes)], axis=0)
    value = dot(real, rows[:edge, :]) + dot(imag, rows[edge:, :])
    for z in range(planes):
        density[z] = value[z * columns_out : (z + 1) * columns_out]
    for block in range(shares.shape[0]):
        posterior[:, block * LANES : (block + 1) * LANES] = shares[block].astype(F32)


def per_device(images, volume, precision, candidates, slot_key, slot_voxel, slot_weight):
    members = lax.axis_size("img")
    slabs = lax.axis_size("slab")
    planes, edge, width = volume.shape
    particles, cands = candidates.shape
    cap = slot_key.shape[2]
    deep = cap // members
    share = NPOSE // members
    voxels = planes * edge
    mine = slabs * deep
    side = NPOSE // 2
    big = pl.BlockSpec(memory_space=pl.ANY)
    near = pl.BlockSpec(memory_space=pltpu.VMEM)
    scratch = [
        pltpu.VMEM((particles, width), BF16),
        pltpu.VMEM((voxels, width), BF16),
        pltpu.VMEM((width, width), BF16),
        pltpu.VMEM((1, particles), F32),
        pltpu.VMEM((cands, particles), jnp.int32),
        pltpu.VMEM(slot_key.shape, jnp.int32),
        pltpu.VMEM(slot_key.shape[1:], jnp.int32),
        pltpu.VMEM(slot_key.shape[1:], jnp.int32),
        pltpu.VMEM((8, mine), F32),
        pltpu.VMEM((8, NPOSE), jnp.int32),
        pltpu.VMEM((cands, particles), jnp.int32),
        pltpu.VMEM((slabs * cap, NPOSE), BF16),
        pltpu.VMEM((slabs, deep, width), BF16),
        pltpu.VMEM((slabs, deep, width), BF16),
        pltpu.VMEM((NPOSE, width), BF16),
        pltpu.VMEM((NPOSE, LANES), F32),
        pltpu.VMEM((NPOSE, particles), jnp.int32),
        pltpu.VMEM((slabs * cap, voxels), BF16),
        pltpu.VMEM((slabs, cands, LANES), F32),
        pltpu.VMEM((slabs, cands, LANES), F32),
        pltpu.VMEM((slabs, cands, LANES), BF16),
        pltpu.VMEM((NPOSE, 6 * LANES), BF16),
        pltpu.VMEM((NPOSE, 6 * LANES), BF16),
        pltpu.VMEM((NPOSE, 4 * LANES), BF16),
        pltpu.VMEM((NPOSE, LANES), F32),
        pltpu.VMEM((NPOSE, width), F32),
        pltpu.VMEM((particles, width), BF16),
        pltpu.VMEM((members // 2, NPOSE, LANES), BF16),
        pltpu.VMEM((members // 2, NPOSE, LANES), BF16),
        pltpu.VMEM((members // 2, NPOSE, LANES), F32),
        pltpu.VMEM((NPOSE, LANES), BF16),
        pltpu.VMEM((NPOSE, LANES), BF16),
        pltpu.VMEM((2, NPOSE, LANES), BF16),
        pltpu.VMEM((2, NPOSE, LANES), BF16),
        pltpu.VMEM((members, 8, LANES), F32),
        pltpu.VMEM((1, voxels), F32),
        pltpu.VMEM((slabs, cap, LANES), BF16),
        pltpu.VMEM((slabs, cap, LANES), BF16),
        pltpu.SemaphoreType.DMA((9,)),
        pltpu.SemaphoreType.DMA((8,)),
        pltpu.SemaphoreType.DMA((8,)),
        pltpu.SemaphoreType.DMA((60,)),
        pltpu.SemaphoreType.DMA((60,)),
    ]
    fourier, shares = pl.pallas_call(
        functools.partial(kernel, slabs, members),
        out_shape=(
            pltpu.VMEM((LANES, voxels), BF16),
            pltpu.VMEM((slabs, cands, LANES), BF16),
        ),
        in_specs=[big] * 8,
        out_specs=(near, big),
        scratch_shapes=scratch,
        compiler_params=pltpu.CompilerParams(
            collective_id=0, has_side_effects=True, vmem_limit_bytes=52 * 1024 * 1024
        ),
    )(*(
        pltpu.with_memory_space_constraint(operand, pltpu.HBM)
        for operand in (
            images, volume.reshape(voxels, width), column_table(edge, members),
            precision[None, :], candidates.T, slot_key, slot_voxel, slot_weight,
        )
    ))
    density, posterior = pl.pallas_call(
        finish,
        out_shape=(
            jax.ShapeDtypeStruct((planes, edge // members, edge), F32),
            jax.ShapeDtypeStruct((cands, particles), F32),
        ),
        in_specs=[near] * 3,
        out_specs=(near, near),
        compiler_params=pltpu.CompilerParams(vmem_limit_bytes=16 * 1024 * 1024),
    )(row_table(edge), fourier, shares)
    return density.transpose(0, 2, 1), posterior.T


def solution(mesh):
    placed = (P("img", "slab"), P("slab", None, None), P("img"), P("img", None), P(), P(), P())
    return jax.shard_map(
        per_device,
        mesh=mesh,
        in_specs=placed,
        out_specs=(P("slab", None, "img"), P("img", None)),
        check_vma=False,
    )
```
